32 devices in a mesh: dp: 8 (over z, y), seq: 4 (over x, core).
Axes of the slice: x: 2, y: 2, z: 4, core: 2. Of those that a mesh axis runs over, the one named last changes fastest.
Arguments:
- inputs: bfloat16 [32, 1024, 768], P('dp', 'seq'), may hold values from -6 to 6
- segments: int32 [32, 1024], P('dp', 'seq'), may hold values from 0 to 7, as said below
- teacher: bfloat16 [32, 1024, 768], P('dp', 'seq'), may hold values from -12 to 12
- mixing_weight: float32 [768, 2304], P('dp'), may hold values from -0.15625 to 0.15625
- output_weight: float32 [768, 768], P('dp'), may hold values from -1.75 to 1.75
- expand_weight: float32 [768, 3072], P('dp'), may hold values from -0.21875 to 0.21875
- shrink_weight: float32 [3072, 768], P('dp'), may hold values from -0.109375 to 0.109375
- vectors: float32 [9216], P('dp'), may hold values from -0.6 to 3.9
- mixing_first: float32 [768, 2304], P('dp'), may hold values from -0.3125 to 0.3125
- output_first: float32 [768, 768], P('dp'), may hold values from -0.3125 to 0.3125
- expand_first: float32 [768, 3072], P('dp'), may hold values from -0.3125 to 0.3125
- shrink_first: float32 [3072, 768], P('dp'), may hold values from -0.3125 to 0.3125
- vectors_first: float32 [9216], P('dp'), may hold values from -1.25 to 1.25
- mixing_second: float32 [768, 2304], P('dp'), may hold values from 0.00025 to 0.001
- output_second: float32 [768, 768], P('dp'), may hold values from 0.00025 to 0.001
- expand_second: float32 [768, 3072], P('dp'), may hold values from 0.00025 to 0.001
- shrink_second: float32 [3072, 768], P('dp'), may hold values from 0.00025 to 0.001
- vectors_second: float32 [9216], P('dp'), may hold values from 0.004 to 0.016
Outputs:
- block_output: bfloat16 [32, 1024, 768], P('dp', 'seq')
- input_grad: bfloat16 [32, 1024, 768], P('dp', 'seq')
- grad_norm: float32 [], replicated
- mixing_updated: float32 [768, 2304], P('dp')
- output_updated: float32 [768, 768], P('dp')
- expand_updated: float32 [768, 3072], P('dp')
- shrink_updated: float32 [3072, 768], P('dp')
- vectors_updated: float32 [9216], P('dp')
- mixing_momentum: float32 [768, 2304], P('dp')
- output_momentum: float32 [768, 768], P('dp')
- expand_momentum: float32 [768, 3072], P('dp')
- shrink_momentum: float32 [3072, 768], P('dp')
- vectors_momentum: float32 [9216], P('dp')
- mixing_variance: float32 [768, 2304], P('dp')
- output_variance: float32 [768, 768], P('dp')
- expand_variance: float32 [768, 3072], P('dp')
- shrink_variance: float32 [3072, 768], P('dp')
- vectors_variance: float32 [9216], P('dp')
The draws below stay inside these ranges and needn't reach their ends.
Inputs may be any that keep to these rules, and one draw needn't show every extreme that they name: `segments`: along each packed row the ids never fall and number its documents from 0 in order; of the packed rows of each index of dp, one holds a single document and the others hold 8 documents each.
All inputs are finite; a program needn't handle non-finite values.
Results may differ from the reference program's by a relative error of at most 0.018.
The reference program's roundings to bfloat16 on the way count: a program that leaves them out, or rounds other values in their place, can miss the bound.
Values may be sent and summed in bfloat16 or wider, within the bound.
A program may use at most 256 MiB of HBM per device.

```python
import math
import jax
import jax.numpy as jnp
from jax import lax

D = 768
HEADS = 12
HD = 64
FF = 3072
LEN = 1024
NDOC = 8
STEP = 10
SEQ_DEV = 4
SEQS = 32
PV = 9216


def draw_segments(key, part):
    key = jax.random.fold_in(key, 11)
    row_keys = jax.random.split(key, SEQS + 1)

    def one_row(row_key):
        cuts = jax.random.permutation(row_key, LEN - 1)[:NDOC - 1].astype(jnp.int32) + 1
        places = jnp.arange(LEN, dtype=jnp.int32)
        return jnp.sum((places[:, None] >= cuts[None, :]).astype(jnp.int32), axis=1)
    packed_rows = jax.vmap(one_row)(row_keys[:SEQS])
    single = jax.random.randint(row_keys[SEQS], (SEQS // SEQ_DEV,), 0, SEQ_DEV)
    chosen = jnp.arange(SEQS, dtype=jnp.int32) % SEQ_DEV == jnp.repeat(single, SEQ_DEV)
    return jnp.where(chosen[:, None], 0, packed_rows).astype(jnp.int32)


def draw_vectors(key, part):
    key = jax.random.fold_in(key, 5)
    gain_key, bias_key = jax.random.split(key, 2)
    ramp = jnp.arange(D, dtype=jnp.float32) / (D - 1)
    rising = 1.0 + 2.0 * ramp
    wobble = jax.random.uniform(gain_key, (2, D), jnp.float32, 0.8, 1.2)
    biases = 0.3 * jax.random.truncated_normal(bias_key, -2.0, 2.0, (6 * D + FF,), jnp.float32)
    gains = rising[None, :] * wobble
    return jnp.concatenate([gains[0], biases[:4 * D], gains[1], biases[4 * D:]]).astype(jnp.float32)


def shard_levels(own_key, shape, shards, low, largest):
    level, own = 1.0, jax.random.fold_in(own_key, 6)
    for position, blocks in shards:
        draws = jnp.exp(jax.random.uniform(jax.random.fold_in(own, position), (blocks,), jnp.float32, low / len(shards), largest / len(shards)))
        level = level * jnp.repeat(draws, shape[position] // blocks).reshape([-1 if axis == position else 1 for axis in range(len(shape))])
    return level


def centred(key, extent, width, most, cuts=(), held_as=jnp.bfloat16):
    array = width * jax.random.normal(key, extent, jnp.float32)
    if cuts:
        array = array * shard_levels(key, extent, cuts, -0.22, 0.18)
    return jnp.clip(array, -most, most).astype(held_as)


def setup_inputs(seed: int = 0) -> dict:
    key_of = jax.random.split(jax.random.key(seed), 19)
    inputs = centred(key_of[0], (SEQS, LEN, D), 1.0, 6.0, ((0, 8), (1, 4)))
    segments = draw_segments(jax.random.fold_in(key_of[18], 71), 0)
    teacher = centred(key_of[2], (SEQS, LEN, D), 2.0, 12.0, ((0, 8), (1, 4)))
    mixing_weight = centred(key_of[3], (D, 3 * D), (2 * D) ** -0.5, 0.15625, ((0, 8),), jnp.float32)
    output_weight = centred(key_of[4], (D, D), (max(1, 2 * D * NDOC // LEN)) ** -0.5, 1.75, ((0, 8),), jnp.float32)
    expand_weight = centred(key_of[5], (D, FF), D ** -0.5, 0.21875, ((0, 8),), jnp.float32)
    shrink_weight = centred(key_of[6], (FF, D), FF ** -0.5, 0.109375, ((0, 8),), jnp.float32)
    vectors = draw_vectors(jax.random.fold_in(key_of[18], 71), 0)
    mixing_first = centred(key_of[8], (D, 3 * D), 0.0556, 0.3125, ((0, 8),), jnp.float32)
    output_first = centred(key_of[9], (D, D), 0.0556, 0.3125, ((0, 8),), jnp.float32)
    expand_first = centred(key_of[10], (D, FF), 0.0556, 0.3125, ((0, 8),), jnp.float32)
    shrink_first = centred(key_of[11], (FF, D), 0.0556, 0.3125, ((0, 8),), jnp.float32)
    vectors_first = centred(key_of[12], (PV,), 0.222, 1.25, ((0, 8),), jnp.float32)
    mixing_second = jnp.clip(jnp.exp(math.log(0.001) - 1.3862944 * jax.random.uniform(key_of[13], (D, 3 * D), jnp.float32) ** shard_levels(key_of[13], (D, 3 * D), ((0, 8),), -0.2, 0.2)), 0.00025, 0.001)
    output_second = jnp.clip(jnp.exp(math.log(0.001) - 1.3862944 * jax.random.uniform(key_of[14], (D, D), jnp.float32) ** shard_levels(key_of[14], (D, D), ((0, 8),), -0.2, 0.2)), 0.00025, 0.001)
    expand_second = jnp.clip(jnp.exp(math.log(0.001) - 1.3862944 * jax.random.uniform(key_of[15], (D, FF), jnp.float32) ** shard_levels(key_of[15], (D, FF), ((0, 8),), -0.2, 0.2)), 0.00025, 0.001)
    shrink_second = jnp.clip(jnp.exp(math.log(0.001) - 1.3862944 * jax.random.uniform(key_of[16], (FF, D), jnp.float32) ** shard_levels(key_of[16], (FF, D), ((0, 8),), -0.2, 0.2)), 0.00025, 0.001)
    vectors_second = jnp.clip(jnp.exp(math.log(0.016) - 1.3862944 * jax.random.uniform(key_of[17], (PV,), jnp.float32) ** shard_levels(key_of[17], (PV,), ((0, 8),), -0.2, 0.2)), 0.004, 0.016)
    return {"inputs": inputs, "segments": segments, "teacher": teacher, "mixing_weight": mixing_weight, "output_weight": output_weight, "expand_weight": expand_weight, "shrink_weight": shrink_weight, "vectors": vectors, "mixing_first": mixing_first, "output_first": output_first, "expand_first": expand_first, "shrink_first": shrink_first, "vectors_first": vectors_first, "mixing_second": mixing_second, "output_second": output_second, "expand_second": expand_second, "shrink_second": shrink_second, "vectors_second": vectors_second}


@jax.custom_vjp
def low(v):
    return lax.optimization_barrier(v.astype(jnp.bfloat16)).astype(jnp.float32)

@jax.custom_vjp
def low_back(v):
    return v

def low_keep(v):
    return (low(v), None)

def low_pass(kept, grad):
    return (grad,)

def back_keep(v):
    return (v, None)

def back_low(kept, grad):
    return (low(grad),)
low.defvjp(low_keep, low_pass)
low_back.defvjp(back_keep, back_low)
NEGATIVE = -1e+30
NORM_EPS = 1e-05
BETA_ONE = 0.9
BETA_TWO = 0.999
ADAM_EPS = 1e-08
WEIGHT_DECAY = 0.01

def layer_norm(values, norm_gain, norm_shift):
    center = values - lax.optimization_barrier(jnp.mean(values, axis=-1, keepdims=True))
    spread = lax.optimization_barrier(jnp.mean(center * center, axis=-1, keepdims=True))
    return center * lax.rsqrt(spread + NORM_EPS) * norm_gain + norm_shift

def gelu_tanh(values):
    return jax.nn.gelu(values, approximate=True)

def split_vectors(packed):
    return jnp.split(packed, [D, 2 * D, 3 * D, 4 * D, 5 * D, 6 * D, 7 * D, 7 * D + FF])

def adamw(master, first, second, gradient, rate):
    first_new = BETA_ONE * first + (1.0 - BETA_ONE) * gradient
    second_new = BETA_TWO * second + (1.0 - BETA_TWO) * gradient * gradient
    first_hat = first_new / (1.0 - BETA_ONE ** STEP)
    second_hat = second_new / (1.0 - BETA_TWO ** STEP)
    updated = master - rate * (first_hat / (jnp.sqrt(second_hat) + ADAM_EPS) + WEIGHT_DECAY * master)
    return (updated, first_new, second_new)

def learn_rates():
    return (1.0 / math.sqrt(2 * D), 1.0 / math.sqrt(max(1, 2 * D * NDOC // LEN)), 1.0 / math.sqrt(D), 1.0 / math.sqrt(FF), 0.3)

def clip_level():
    return 0.5 * math.sqrt(4 * D * D + 2 * D * FF + 8 * D + FF)

def matmul(left, right):
    return jnp.dot(left, right, precision=lax.Precision.HIGHEST, preferred_element_type=jnp.float32)

def row_forward(parameters, row_input, row_segments, row_teacher):
    mixing, output, expand, shrink, gain_one, shift_one, bias_query, bias_value, bias_output, gain_two, shift_two, bias_expand, bias_shrink = parameters
    scale = 1.0 / math.sqrt(HD)
    normed = low(layer_norm(row_input, gain_one, shift_one))
    projected = matmul(normed, mixing)
    queries = low_back(low((projected[:, :D] + bias_query) * scale))
    keys_all = low_back(low(projected[:, D:2 * D]))
    values_all = low_back(low(projected[:, 2 * D:] + bias_value))
    positions = jnp.arange(LEN, dtype=jnp.int32)
    allowed = (positions[None, :] <= positions[:, None]) & (row_segments[None, :] == row_segments[:, None])
    scores = jnp.einsum('qhd,khd->hqk', queries.reshape(LEN, HEADS, HD), keys_all.reshape(LEN, HEADS, HD), precision=lax.Precision.HIGHEST)
    scores = low_back(jnp.where(allowed[None], scores, NEGATIVE))
    probability = low(jax.nn.softmax(scores, axis=-1))
    attended = jnp.einsum('hqk,khd->qhd', probability, values_all.reshape(LEN, HEADS, HD), precision=lax.Precision.HIGHEST).reshape(LEN, D)
    attended = low_back(low(attended))
    middle = row_input + low_back(matmul(attended, output)) + bias_output
    normed_two = low(layer_norm(middle, gain_two, shift_two))
    hidden = low_back(matmul(normed_two, expand) + bias_expand)
    active = low_back(low(gelu_tanh(hidden)))
    result = middle + low_back(matmul(active, shrink)) + bias_shrink
    target_log = jax.nn.log_softmax(row_teacher, axis=-1)
    student_log = jax.nn.log_softmax(result, axis=-1)
    loss_row = D * jnp.sum(jnp.exp(target_log) * (target_log - student_log))
    return (result, loss_row)

def reference(inputs, segments, teacher, mixing_weight, output_weight, expand_weight, shrink_weight, vectors, mixing_first, output_first, expand_first, shrink_first, vectors_first, mixing_second, output_second, expand_second, shrink_second, vectors_second):
    masters = (mixing_weight, output_weight, expand_weight, shrink_weight, vectors)
    states = inputs.astype(jnp.float32)
    targets = teacher.astype(jnp.float32)

    def total_loss(weights, hidden_states):
        lowered = [low(weight) for weight in weights]
        parameters = tuple(lowered[:4]) + tuple(split_vectors(lowered[4]))

        def scan_step(running, row_data):
            result, loss_row = jax.checkpoint(row_forward)(parameters, row_data[0], row_data[1], row_data[2])
            return (running + loss_row, result)
        loss_total, results = lax.scan(scan_step, jnp.zeros((), jnp.float32), (hidden_states, segments, targets))
        return (loss_total, results)
    loss_total, back_fn, results = jax.vjp(total_loss, masters, states, has_aux=True)
    gradients, states_grad = back_fn(jnp.ones((), loss_total.dtype))
    squares = sum((jnp.sum(gradient * gradient) for gradient in gradients))
    grad_norm = jnp.sqrt(squares)
    clip_value = clip_level()
    factor = clip_value / jnp.maximum(grad_norm, clip_value)
    step_rates = learn_rates()
    firsts = (mixing_first, output_first, expand_first, shrink_first, vectors_first)
    seconds = (mixing_second, output_second, expand_second, shrink_second, vectors_second)
    fresh = [adamw(masters[index], firsts[index], seconds[index], gradients[index] * factor, step_rates[index]) for index in range(5)]
    return (results.astype(jnp.bfloat16), states_grad.astype(jnp.bfloat16), grad_norm, fresh[0][0], fresh[1][0], fresh[2][0], fresh[3][0], fresh[4][0], fresh[0][1], fresh[1][1], fresh[2][1], fresh[3][1], fresh[4][1], fresh[0][2], fresh[1][2], fresh[2][2], fresh[3][2], fresh[4][2])
```

```python
from functools import partial
import math

import jax
import jax.numpy as jnp
from jax import lax
from jax.experimental import pallas as pl
from jax.experimental.pallas import tpu as pltpu
from jax.sharding import PartitionSpec as P

D = 768
HEADS = 12
HD = 64
FF = 3072
LEN = 1024
NDOC = 8
STEP = 10


NEGATIVE = -1e30
NORM_EPS = 1e-05
BETA_ONE = 0.9
BETA_TWO = 0.999
ADAM_EPS = 1e-08
WEIGHT_DECAY = 0.01


def layer_norm(values, norm_gain, norm_shift):
    center = values - jnp.mean(values, axis=-1, keepdims=True)
    spread = jnp.mean(center * center, axis=-1, keepdims=True)
    return center * lax.rsqrt(spread + NORM_EPS) * norm_gain + norm_shift


def gelu_tanh(values):
    return jax.nn.gelu(values, approximate=True)


def split_vectors(packed):
    return jnp.split(packed, [D, 2 * D, 3 * D, 4 * D, 5 * D, 6 * D, 7 * D, 7 * D + FF])


def adamw(master, first, second, gradient, rate):
    first_new = BETA_ONE * first + (1.0 - BETA_ONE) * gradient
    second_new = BETA_TWO * second + (1.0 - BETA_TWO) * gradient * gradient
    first_hat = first_new / (1.0 - BETA_ONE**STEP)
    second_hat = second_new / (1.0 - BETA_TWO**STEP)
    updated = master - rate * (
        first_hat / (jnp.sqrt(second_hat) + ADAM_EPS) + WEIGHT_DECAY * master
    )
    return (updated, first_new, second_new)


def learn_rates():
    return (
        1.0 / math.sqrt(2 * D),
        1.0 / math.sqrt(max(1, 2 * D * NDOC // LEN)),
        1.0 / math.sqrt(D),
        1.0 / math.sqrt(FF),
        0.3,
    )


def clip_level():
    return 0.5 * math.sqrt(4 * D * D + 2 * D * FF + 8 * D + FF)


def visible(query_pos, key_pos, query_seg, key_seg):
    return (key_pos[None, :] <= query_pos[:, None]) & (key_seg[None, :] == query_seg[:, None])


def attend_rows(query_pos, key_pos, packed_args):
    queries, keys_all, values_all, query_seg, key_seg = packed_args
    scores = jnp.einsum("qhd,khd->hqk", queries, keys_all, preferred_element_type=jnp.float32)
    scores = jnp.where(visible(query_pos, key_pos, query_seg, key_seg)[None], scores, NEGATIVE)
    top_score = jnp.max(scores, axis=-1, keepdims=True)
    exponent = jnp.exp(scores - top_score)
    totals = jnp.sum(exponent, axis=-1, keepdims=True)
    probability = (exponent / totals).astype(jnp.bfloat16)
    attended = jnp.einsum(
        "hqk,khd->qhd", probability, values_all, preferred_element_type=jnp.float32
    )
    return (attended, (top_score + jnp.log(totals))[..., 0])


def attend_back(query_pos, key_pos, packed_args):
    queries, keys_all, values_all, upstream, log_totals, query_seg, key_seg = packed_args
    scores = jnp.einsum("qhd,khd->hqk", queries, keys_all, preferred_element_type=jnp.float32)
    scores = jnp.where(visible(query_pos, key_pos, query_seg, key_seg)[None], scores, NEGATIVE)
    probability = jnp.exp(scores - log_totals[..., None])
    prob_low = probability.astype(jnp.bfloat16)
    prob_grad = jnp.einsum("qhd,khd->hqk", upstream, values_all, preferred_element_type=jnp.float32)
    value_part = jnp.einsum("hqk,qhd->khd", prob_low, upstream, preferred_element_type=jnp.float32)
    score_grad = probability * (
        prob_grad - jnp.sum(probability * prob_grad, axis=-1, keepdims=True)
    )
    score_low = score_grad.astype(jnp.bfloat16)
    query_part = jnp.einsum("hqk,khd->qhd", score_low, keys_all, preferred_element_type=jnp.float32)
    key_part = jnp.einsum("hqk,qhd->khd", score_low, queries, preferred_element_type=jnp.float32)
    key_count = keys_all.shape[0]
    return (
        query_part,
        jnp.concatenate(
            [key_part.reshape(key_count, -1), value_part.reshape(key_count, -1)], axis=1
        ),
    )


def body(
    inputs,
    segments,
    teacher,
    mixing_weight,
    output_weight,
    expand_weight,
    shrink_weight,
    vectors,
    mixing_first,
    output_first,
    expand_first,
    shrink_first,
    vectors_first,
    mixing_second,
    output_second,
    expand_second,
    shrink_second,
    vectors_second,
):
    bfloat = jnp.bfloat16
    floats = jnp.float32
    seq_count, local_len, features = inputs.shape
    row_count = seq_count * local_len
    scale = 1.0 / math.sqrt(HD)
    mixing_low, output_low, expand_low, shrink_low, vectors_low = (
        lax.all_gather(mixing_weight.astype(bfloat), "dp", axis=0, tiled=True),
        lax.all_gather(output_weight.astype(bfloat), "dp", axis=0, tiled=True),
        lax.all_gather(expand_weight.astype(bfloat), "dp", axis=0, tiled=True),
        lax.all_gather(shrink_weight.astype(bfloat), "dp", axis=0, tiled=True),
        lax.all_gather(vectors.astype(bfloat), "dp", axis=0, tiled=True),
    )
    (
        gain_one,
        shift_one,
        bias_query,
        bias_value,
        bias_output,
        gain_two,
        shift_two,
        bias_expand,
        bias_shrink,
    ) = split_vectors(vectors_low.astype(floats))
    states = inputs.astype(floats).reshape(row_count, features)
    normed = layer_norm(states, gain_one, shift_one)
    normed_low = normed.astype(bfloat)
    projected = jnp.dot(normed_low, mixing_low, preferred_element_type=floats)
    query_low = ((projected[:, :features] + bias_query) * scale).astype(bfloat)
    key_low = projected[:, features : 2 * features].astype(bfloat)
    value_low = (projected[:, 2 * features :] + bias_value).astype(bfloat)
    key_all, value_all = (
        lax.all_gather(key_low.reshape(seq_count, local_len, features), "seq", axis=1, tiled=True),
        lax.all_gather(
            value_low.reshape(seq_count, local_len, features), "seq", axis=1, tiled=True
        ),
    )
    segment_all = lax.all_gather(segments, "seq", axis=1, tiled=True)
    full_len = key_all.shape[1]
    query_pos = lax.axis_index("seq") * local_len + jnp.arange(local_len, dtype=jnp.int32)
    key_pos = jnp.arange(full_len, dtype=jnp.int32)
    query_heads = query_low.reshape(seq_count, local_len, HEADS, HD)
    key_heads = key_all.reshape(seq_count, full_len, HEADS, HD)
    value_heads = value_all.reshape(seq_count, full_len, HEADS, HD)
    attended, log_totals = lax.map(
        partial(attend_rows, query_pos, key_pos),
        (query_heads, key_heads, value_heads, segments, segment_all),
    )
    attended_low = attended.reshape(row_count, features).astype(bfloat)
    middle = states + jnp.dot(attended_low, output_low, preferred_element_type=floats) + bias_output
    normed_two = layer_norm(middle, gain_two, shift_two)
    normed_two_low = normed_two.astype(bfloat)
    hidden = jnp.dot(normed_two_low, expand_low, preferred_element_type=floats) + bias_expand
    active, gelu_back = jax.vjp(gelu_tanh, hidden)
    active_low = active.astype(bfloat)
    result = middle + jnp.dot(active_low, shrink_low, preferred_element_type=floats) + bias_shrink
    block_output = result.astype(bfloat).reshape(seq_count, local_len, features)
    target_prob = jax.nn.softmax(teacher.astype(floats).reshape(row_count, features), axis=-1)
    result_grad = features * (jax.nn.softmax(result, axis=-1) - target_prob)
    result_low = result_grad.astype(bfloat)
    grad_shrink = jnp.dot(active_low.T, result_low, preferred_element_type=floats)
    grad_bias_shrink = jnp.sum(result_grad, axis=0)
    active_grad = jnp.dot(result_low, shrink_low.T, preferred_element_type=floats)
    active_round = lax.optimization_barrier(active_grad.astype(bfloat)).astype(floats)
    hidden_low = gelu_back(active_round)[0].astype(bfloat)
    grad_bias_expand = jnp.sum(hidden_low.astype(floats), axis=0)
    grad_expand = jnp.dot(normed_two_low.T, hidden_low, preferred_element_type=floats)
    normed_two_grad = jnp.dot(hidden_low, expand_low.T, preferred_element_type=floats)
    norm_two_back = jax.vjp(layer_norm, middle, gain_two, shift_two)[1]
    middle_part, grad_gain_two, grad_shift_two = norm_two_back(normed_two_grad)
    middle_grad = result_grad + middle_part
    middle_low = middle_grad.astype(bfloat)
    grad_bias_output = jnp.sum(middle_grad, axis=0)
    grad_output = jnp.dot(attended_low.T, middle_low, preferred_element_type=floats)
    attended_grad = jnp.dot(middle_low, output_low.T, preferred_element_type=floats).astype(bfloat)
    upstream_heads = attended_grad.reshape(seq_count, local_len, HEADS, HD)
    query_grad, kv_terms = lax.map(
        partial(attend_back, query_pos, key_pos),
        (query_heads, key_heads, value_heads, upstream_heads, log_totals, segments, segment_all),
    )
    kv_sums = (
        lax.psum_scatter(kv_terms.astype(jnp.bfloat16), "seq", scatter_dimension=1, tiled=True)
        .astype(jnp.float32)
        .reshape(row_count, 2 * features)
    )
    key_grad_low = kv_sums[:, :features].astype(bfloat)
    value_grad_low = kv_sums[:, features:].astype(bfloat)
    query_grad_low = query_grad.reshape(row_count, features).astype(bfloat)
    query_scaled = query_grad_low.astype(floats) * scale
    grad_bias_query = jnp.sum(query_scaled, axis=0)
    grad_bias_value = jnp.sum(value_grad_low.astype(floats), axis=0)
    projected_grad = jnp.concatenate(
        [query_scaled.astype(bfloat), key_grad_low, value_grad_low], axis=1
    )
    grad_mixing = jnp.dot(normed_low.T, projected_grad, preferred_element_type=floats)
    normed_grad = jnp.dot(projected_grad, mixing_low.T, preferred_element_type=floats)
    norm_one_back = jax.vjp(layer_norm, states, gain_one, shift_one)[1]
    states_part, grad_gain_one, grad_shift_one = norm_one_back(normed_grad)
    input_grad = (middle_grad + states_part).astype(bfloat).reshape(seq_count, local_len, features)
    grad_vectors = jnp.concatenate(
        [
            grad_gain_one,
            grad_shift_one,
            grad_bias_query,
            grad_bias_value,
            grad_bias_output,
            grad_gain_two,
            grad_shift_two,
            grad_bias_expand,
            grad_bias_shrink,
        ]
    )
    vector_rows = grad_vectors.reshape(lax.axis_size("dp"), -1)
    mixing_part, output_part, expand_part, shrink_part, vector_part = (
        lax.psum_scatter(
            grad_mixing.astype(jnp.bfloat16), "dp", scatter_dimension=0, tiled=True
        ).astype(jnp.float32),
        lax.psum_scatter(
            grad_output.astype(jnp.bfloat16), "dp", scatter_dimension=0, tiled=True
        ).astype(jnp.float32),
        lax.psum_scatter(
            grad_expand.astype(jnp.bfloat16), "dp", scatter_dimension=0, tiled=True
        ).astype(jnp.float32),
        lax.psum_scatter(
            grad_shrink.astype(jnp.bfloat16), "dp", scatter_dimension=0, tiled=True
        ).astype(jnp.float32),
        lax.psum_scatter(
            vector_rows.astype(jnp.bfloat16), "dp", scatter_dimension=0, tiled=True
        ).astype(jnp.float32),
    )
    mixing_sum, output_sum, expand_sum, shrink_sum, vector_sum = (
        lax.psum(mixing_part.astype(jnp.bfloat16), "seq").astype(jnp.float32),
        lax.psum(output_part.astype(jnp.bfloat16), "seq").astype(jnp.float32),
        lax.psum(expand_part.astype(jnp.bfloat16), "seq").astype(jnp.float32),
        lax.psum(shrink_part.astype(jnp.bfloat16), "seq").astype(jnp.float32),
        lax.psum(vector_part.astype(jnp.bfloat16), "seq").astype(jnp.float32),
    )
    vector_sum = vector_sum.reshape(-1)
    squares = (
        jnp.sum(mixing_sum * mixing_sum)
        + jnp.sum(output_sum * output_sum)
        + jnp.sum(expand_sum * expand_sum)
        + jnp.sum(shrink_sum * shrink_sum)
        + jnp.sum(vector_sum * vector_sum)
    )
    grad_norm = jnp.sqrt(lax.psum(squares, "dp"))
    clip_value = clip_level()
    factor = clip_value / jnp.maximum(grad_norm, clip_value)
    step_rates = learn_rates()
    mixing_new = adamw(
        mixing_weight, mixing_first, mixing_second, mixing_sum * factor, step_rates[0]
    )
    output_new = adamw(
        output_weight, output_first, output_second, output_sum * factor, step_rates[1]
    )
    expand_new = adamw(
        expand_weight, expand_first, expand_second, expand_sum * factor, step_rates[2]
    )
    shrink_new = adamw(
        shrink_weight, shrink_first, shrink_second, shrink_sum * factor, step_rates[3]
    )
    vectors_new = adamw(vectors, vectors_first, vectors_second, vector_sum * factor, step_rates[4])
    return (
        block_output,
        input_grad,
        grad_norm,
        mixing_new[0],
        output_new[0],
        expand_new[0],
        shrink_new[0],
        vectors_new[0],
        mixing_new[1],
        output_new[1],
        expand_new[1],
        shrink_new[1],
        vectors_new[1],
        mixing_new[2],
        output_new[2],
        expand_new[2],
        shrink_new[2],
        vectors_new[2],
    )

MESH = pl.DeviceIdType.MESH
BF = jnp.bfloat16
F32 = jnp.float32
BLK = 256
NN = ((1,), (0,))
NT = ((1,), (1,))
TN = ((0,), (0,))
VMEM_BYTES = 60 * 2**20
VROWS = 16


def dot(left, right, dims):
    return lax.dot_general(left, right, (dims, ((), ())), preferred_element_type=F32)


class Place:
    def __init__(self, count):
        self.count = count
        self.dp = lax.axis_index("dp")
        self.seq = lax.axis_index("seq")
        odd = self.dp % 2
        self.pos = (1 - odd) * (self.dp // 2) + odd * (count - 1 - self.dp // 2)
        self.core = self.seq % 2
        self.step = 1 - 2 * self.core
        self.next = (self.at(self.pos + self.step + count), self.seq)
        self.mate = (self.dp, self.seq + 1 - 2 * self.core)
        self.across = (self.dp, self.seq + 2 - 4 * (self.seq // 2))

    def at(self, pos):
        pos = pos % self.count
        upper = pos // (self.count // 2)
        return (1 - upper) * (2 * pos) + upper * (2 * (self.count - 1 - pos) + 1)

    def behind(self, steps):
        return self.at(self.pos - steps * self.step + 2 * self.count)

    def seq_peer(self, offset):
        return (self.dp, (self.seq + offset) % 4)

    def dp_peer(self, offset):
        return ((self.dp + offset) % self.count, self.seq)

    def greet(self):
        barrier = pltpu.get_barrier_semaphore()
        peers = [self.seq_peer(k) for k in range(1, 4)]
        peers += [self.dp_peer(k) for k in range(1, self.count)]
        for peer in peers:
            pl.semaphore_signal(barrier, inc=1, device_id=peer, device_id_type=MESH)
        return lambda: pl.semaphore_wait(barrier, len(peers))


def remote(src, dst, send, recv, device):
    copy = pltpu.make_async_remote_copy(
        src_ref=src,
        dst_ref=dst,
        send_sem=send,
        recv_sem=recv,
        device_id=device,
        device_id_type=MESH,
    )
    copy.start()
    return copy


def local(src, dst, sem):
    copy = pltpu.make_async_copy(src, dst, sem)
    copy.start()
    return copy


def gather_kernel(count, *refs):
    weights, vec_ref, inputs, teacher, seg_ref = refs[0:4], refs[4], refs[5], refs[6], refs[7]
    full, vec_all, rows, targets, segs = refs[8:12], refs[12], refs[13], refs[14], refs[15]
    stage, vec_stage = refs[16:20], refs[20]
    (own_sem, ring_s, ring_r, mate_s, mate_r, row_s, row_r, row_l, vec_s, vec_r, vec_l) = refs[21:]
    place = Place(count)
    ready = place.greet()
    for part, shard in zip(stage, weights):
        part[...] = shard[...].astype(BF).reshape(part.shape)
    vec_stage[...] = jnp.concatenate(
        [vec_ref[...].astype(BF).astype(F32), jnp.zeros((VROWS - vec_ref.shape[0], 128), F32)],
        axis=0,
    )
    ready()
    waits = []
    flows = []
    me = pl.ds(pl.multiple_of(place.seq * BLK, BLK), BLK)
    for k in range(1, 4):
        peer = place.seq_peer(k)
        row = peer[1]
        waits.append(remote(inputs.at[row], rows.at[me], row_s.at[k, 0], row_r.at[k, 0], peer))
        waits.append(remote(seg_ref.at[row], segs.at[place.seq], row_s.at[k, 1], row_r.at[k, 1], peer))
        waits.append(remote(teacher.at[row], targets.at[me], row_s.at[k, 2], row_r.at[k, 2], peer))
    waits.append(local(inputs.at[place.seq], rows.at[me], row_l.at[0]))
    waits.append(local(seg_ref.at[place.seq], segs.at[place.seq], row_l.at[1]))
    waits.append(local(teacher.at[place.seq], targets.at[me], row_l.at[2]))
    for k in range(1, count):
        waits.append(
            remote(vec_stage, vec_all.at[place.dp], vec_s.at[k], vec_r.at[k], place.dp_peer(k))
        )
    waits.append(local(vec_stage, vec_all.at[place.dp], vec_l))
    current = []
    for w in range(4):
        waits.append(local(stage[w], full[w].at[place.dp], own_sem.at[w]))
        current.append(
            remote(
                stage[w].at[place.core],
                full[w].at[place.dp, place.core],
                ring_s.at[w, 0],
                ring_r.at[w, 0],
                place.next,
            )
        )
    for t in range(1, count):
        owner = place.behind(t)
        for w in range(4):
            current[w].wait_recv()
            block = full[w].at[owner, place.core]
            flows.append(current[w])
            if t < count - 1:
                current[w] = remote(block, block, ring_s.at[w, t], ring_r.at[w, t], place.next)
            waits.append(remote(block, block, mate_s.at[w, t], mate_r.at[w, t], place.mate))
    for copy in flows:
        copy.wait_send()
    for copy in waits:
        copy.wait()


def gather_all(count, weights, vectors, inputs, teacher, segments):
    shards = [w.shape for w in weights]
    halves = [(2, r // 2, c) for r, c in shards]
    any_spec = pl.BlockSpec(memory_space=pl.ANY)
    vmem = pl.BlockSpec(memory_space=pltpu.VMEM)
    dma = pltpu.SemaphoreType.DMA
    rows, local_len, features = inputs.shape
    out_shape = [jax.ShapeDtypeStruct((count,) + h, BF) for h in halves]
    out_shape.append(jax.ShapeDtypeStruct((count, VROWS, 128), F32))
    out_shape += [jax.ShapeDtypeStruct((rows * local_len, features), BF)] * 2
    out_shape.append(jax.ShapeDtypeStruct((rows, 8, local_len), jnp.int32))
    return pl.pallas_call(
        partial(gather_kernel, count),
        out_shape=out_shape,
        in_specs=[vmem] * 5 + [any_spec] * 3,
        out_specs=[any_spec] * len(out_shape),
        scratch_shapes=[pltpu.VMEM(h, BF) for h in halves]
        + [pltpu.VMEM((VROWS, 128), F32)]
        + [
            dma((4,)),
            dma((4, count)),
            dma((4, count)),
            dma((4, count)),
            dma((4, count)),
            dma((4, 3)),
            dma((4, 3)),
            dma((3,)),
            dma((count,)),
            dma((count,)),
            dma,
        ],
        compiler_params=pltpu.CompilerParams(
            collective_id=1, has_side_effects=True, vmem_limit_bytes=VMEM_BYTES
        ),
    )(*weights, vectors.reshape(-1, 128), inputs, teacher, segments)


def scatter_kernel(count, *refs):
    grads, vec_ref, outs_ref, back_ref = refs[0:4], refs[4], refs[5], refs[6]
    sums, vec_sum, norm_ref, out_rows, back_rows = refs[7:11], refs[11], refs[12], refs[13], refs[14]
    mate_buf, ring_buf, first, cross_mine, cross = (
        refs[15:19],
        refs[19:23],
        refs[23:27],
        refs[27:31],
        refs[31:35],
    )
    vec_buf, vec_mine, vec_seq, sq_mine, sq_buf = refs[35:40]
    (
        mate_s, mate_r, ring_s, ring_r, cross_s, cross_r, tot_s, tot_r,
        row_s, row_r, row_l, vec_s, vec_r, vecq_s, vecq_r, sq_s, sq_r,
    ) = refs[40:]
    place = Place(count)
    place.greet()()
    waits = []
    order = (3, 2, 1, 0)
    mates = {}
    for w in order:
        mates[w] = remote(
            grads[w].at[:, 1 - place.core], mate_buf[w], mate_s.at[w], mate_r.at[w], place.mate
        )
    for k in range(1, count):
        waits.append(
            remote(
                vec_ref.at[place.dp_peer(k)[0]],
                vec_buf.at[place.dp],
                vec_s.at[k],
                vec_r.at[k],
                place.dp_peer(k),
            )
        )
    vec_buf[place.dp] = vec_ref[place.dp]
    mine = pl.ds(pl.multiple_of(place.seq * BLK, BLK), BLK)
    for k in range(1, 4):
        peer = place.seq_peer(k)
        theirs = pl.ds(pl.multiple_of(peer[1] * BLK, BLK), BLK)
        waits.append(
            remote(outs_ref.at[theirs], out_rows.at[place.seq], row_s.at[k, 0], row_r.at[k, 0], peer)
        )
        waits.append(
            remote(back_ref.at[theirs], back_rows.at[place.seq], row_s.at[k, 1], row_r.at[k, 1], peer)
        )
    waits.append(local(outs_ref.at[mine], out_rows.at[place.seq], row_l.at[0]))
    waits.append(local(back_ref.at[mine], back_rows.at[place.seq], row_l.at[1]))
    flows = []
    current = {}

    def term(w, owner):
        return grads[w][owner, place.core].astype(F32) + mate_buf[w][owner].astype(F32)

    for w in order:
        mates[w].wait_recv()
        first[w][...] = term(w, place.behind(1)).astype(BF)
        current[w] = remote(first[w], ring_buf[w].at[0], ring_s.at[w, 0], ring_r.at[w, 0], place.next)
    for t in range(1, count):
        for w in order:
            current[w].wait_recv()
            flows.append(current[w])
            slot = ring_buf[w].at[t - 1]
            total = (slot[...].astype(F32) + term(w, place.behind(t + 1))).astype(BF)
            if t < count - 1:
                slot[...] = total
                current[w] = remote(
                    slot, ring_buf[w].at[t], ring_s.at[w, t], ring_r.at[w, t], place.next
                )
            else:
                cross_mine[w][...] = total
                current[w] = remote(
                    cross_mine[w], cross[w], cross_s.at[w], cross_r.at[w], place.across
                )
    totals = []
    for w in order:
        current[w].wait_recv()
        flows.append(current[w])
        sums[w][place.core] = (cross_mine[w][...].astype(F32) + cross[w][...].astype(F32)).astype(BF)
        block = sums[w].at[place.core]
        totals.append(remote(block, block, tot_s.at[w], tot_r.at[w], place.mate))
    for copy in waits[: count - 1]:
        copy.wait_recv()
    vec_mine[...] = jnp.sum(vec_buf[...], axis=0)
    vec_seq[place.seq] = vec_mine[...]
    seqs = []
    for k in range(1, 4):
        seqs.append(
            remote(vec_mine, vec_seq.at[place.seq], vecq_s.at[k], vecq_r.at[k], place.seq_peer(k))
        )
    for copy in seqs:
        copy.wait_recv()
    vec_total = jnp.sum(vec_seq[...], axis=0)
    vec_sum[...] = vec_total
    squares = jnp.sum(vec_total * vec_total, axis=0, keepdims=True)
    for copy in totals:
        copy.wait_recv()
    for w in range(4):
        for half in range(2):
            value = sums[w][half].astype(F32)
            part = jnp.sum(value * value, axis=0, keepdims=True)
            for lane in range(part.shape[1] // 128):
                squares = squares + part[:, lane * 128 : (lane + 1) * 128]
    sq_mine[...] = jnp.broadcast_to(squares, (8, 128))
    sq_buf[place.dp] = sq_mine[...]
    sqs = []
    for k in range(1, count):
        sqs.append(remote(sq_mine, sq_buf.at[place.dp], sq_s.at[k], sq_r.at[k], place.dp_peer(k)))
    for copy in sqs:
        copy.wait_recv()
    total = jnp.sum(jnp.sum(sq_buf[...], axis=0), axis=1, keepdims=True)
    norm_ref[...] = jnp.broadcast_to(jnp.sqrt(total), (8, 128))
    for copy in waits[: count - 1] + flows + seqs + totals + sqs + list(mates.values()):
        copy.wait_send()
    for copy in waits[count - 1 :]:
        copy.wait()


def scatter_all(count, grads, vector_rows, block_output, input_grad, rows):
    halves = [g.shape[2:] for g in grads]
    any_spec = pl.BlockSpec(memory_space=pl.ANY)
    vmem = pl.BlockSpec(memory_space=pltpu.VMEM)
    dma = pltpu.SemaphoreType.DMA
    length, features = block_output.shape
    row_shape = jax.ShapeDtypeStruct((rows, length // rows, features), BF)
    out_shape = [jax.ShapeDtypeStruct((2,) + h, BF) for h in halves]
    out_shape += [
        jax.ShapeDtypeStruct((VROWS, 128), F32),
        jax.ShapeDtypeStruct((8, 128), F32),
        row_shape,
        row_shape,
    ]
    buffers = [pltpu.VMEM((count,) + h, BF) for h in halves]
    buffers += [pltpu.VMEM((count - 1,) + h, BF) for h in halves]
    buffers += [pltpu.VMEM(h, BF) for h in halves] * 3
    buffers += [
        pltpu.VMEM((count, VROWS, 128), F32),
        pltpu.VMEM((VROWS, 128), F32),
        pltpu.VMEM((4, VROWS, 128), F32),
        pltpu.VMEM((8, 128), F32),
        pltpu.VMEM((count, 8, 128), F32),
    ]
    sems = [(4,), (4,), (4, count), (4, count), (4,), (4,), (4,), (4,), (4, 2), (4, 2), (2,)]
    sems += [(count,), (count,), (4,), (4,), (count,), (count,)]
    return pl.pallas_call(
        partial(scatter_kernel, count),
        out_shape=out_shape,
        in_specs=[vmem] * 5 + [any_spec] * 2,
        out_specs=[vmem] * 6 + [any_spec] * 2,
        scratch_shapes=buffers + [dma(s) for s in sems],
        compiler_params=pltpu.CompilerParams(
            collective_id=2, has_side_effects=True, vmem_limit_bytes=VMEM_BYTES
        ),
    )(*grads, vector_rows, block_output, input_grad)


def attend_kernel(qkv, segr, segc, out, lse, scores):
    length = qkv.shape[0]
    lane = lax.broadcasted_iota(jnp.int32, (1, 128), 1)

    def pair(hp, _):
        cq = pl.ds(pl.multiple_of(hp * 128, 128), 128)
        ck = pl.ds(pl.multiple_of(D + hp * 128, 128), 128)
        cv = pl.ds(pl.multiple_of(2 * D + hp * 128, 128), 128)
        vt = qkv[:, cv].T
        for i in range(length // BLK):
            rq = slice(i * BLK, (i + 1) * BLK)
            qb = qkv[rq, cq]
            sq = segr[0:1, rq]
            outs = []
            for hd in range(2):
                qm = jnp.where((lane < 64) if hd == 0 else (lane >= 64), qb, jnp.zeros_like(qb))
                top = None
                for j in range(i + 1):
                    rk = slice(j * BLK, (j + 1) * BLK)
                    s = jnp.where(
                        seen(segc[rk, :], sq, i == j), dot(qkv[rk, ck], qm, NT), NEGATIVE
                    )
                    scores[hd, rk, :] = s
                    best = jnp.max(s, axis=0, keepdims=True)
                    top = best if top is None else jnp.maximum(top, best)
                total = acc = None
                for j in range(i + 1):
                    rk = slice(j * BLK, (j + 1) * BLK)
                    p = jnp.exp(scores[hd, rk, :] - top)
                    part = jnp.sum(p, axis=0, keepdims=True)
                    total = part if total is None else total + part
                    term = dot(vt[hd * 64 : (hd + 1) * 64, rk], p.astype(BF), NN)
                    acc = term if acc is None else acc + term
                outs.append(acc * (1.0 / total))
                lse[pl.ds(hp * 2 + hd, 1), rq] = top + jnp.log(total)
            out[rq, cq] = jnp.concatenate(outs, axis=0).T.astype(BF)
        return 0

    lax.fori_loop(0, D // 128, pair, 0)


def seen(sk, sq, diagonal):
    vis = jnp.concatenate([sk] * (BLK // 128), axis=1) == sq
    if diagonal:
        vis = vis & (
            lax.broadcasted_iota(jnp.int32, (BLK, BLK), 0)
            <= lax.broadcasted_iota(jnp.int32, (BLK, BLK), 1)
        )
    return vis


def attend_back_kernel(qkv, segr, segc, out, upstream, lse, dqkv, dk_sum, dv_sum):
    length = qkv.shape[0]
    lane = lax.broadcasted_iota(jnp.int32, (1, 128), 1)

    def pair(hp, _):
        cq = pl.ds(pl.multiple_of(hp * 128, 128), 128)
        ck = pl.ds(pl.multiple_of(D + hp * 128, 128), 128)
        cv = pl.ds(pl.multiple_of(2 * D + hp * 128, 128), 128)
        kt = qkv[:, ck].T
        for i in range(length // BLK):
            rq = slice(i * BLK, (i + 1) * BLK)
            qb = qkv[rq, cq]
            db = upstream[rq, cq]
            prod = (db.astype(F32) * out[rq, cq].astype(F32)).T
            sq = segr[0:1, rq]
            dqs = []
            for hd in range(2):
                half = (lane < 64) if hd == 0 else (lane >= 64)
                qm = jnp.where(half, qb, jnp.zeros_like(qb))
                dm = jnp.where(half, db, jnp.zeros_like(db))
                delta = jnp.sum(prod[hd * 64 : (hd + 1) * 64, :], axis=0, keepdims=True)
                ls = lse[pl.ds(hp * 2 + hd, 1), rq]
                dq = None
                for j in range(i + 1):
                    rk = slice(j * BLK, (j + 1) * BLK)
                    s = jnp.where(
                        seen(segc[rk, :], sq, i == j), dot(qkv[rk, ck], qm, NT), NEGATIVE
                    )
                    p = jnp.exp(s - ls)
                    ds = (p * (dot(qkv[rk, cv], dm, NT) - delta)).astype(BF)
                    pv = dot(p.astype(BF), dm, NN)
                    pk = dot(ds, qm, NN)
                    if i == j and hd == 0:
                        dv_sum[rk, :] = pv
                        dk_sum[rk, :] = pk
                    else:
                        dv_sum[rk, :] += pv
                        dk_sum[rk, :] += pk
                    term = dot(kt[hd * 64 : (hd + 1) * 64, rk], ds, NN)
                    dq = term if dq is None else dq + term
                dqs.append(dq)
            low = jnp.concatenate(dqs, axis=0).T.astype(BF).astype(F32)
            dqkv[rq, cq] = (low * (1.0 / math.sqrt(HD))).astype(BF)
        dqkv[:, ck] = dk_sum[...].astype(BF)
        dqkv[:, cv] = dv_sum[...].astype(BF)
        return 0

    lax.fori_loop(0, D // 128, pair, 0)


def attend(qkv, segr, segc):
    vmem = pl.BlockSpec(memory_space=pltpu.VMEM)
    length = qkv.shape[0]
    return pl.pallas_call(
        attend_kernel,
        out_shape=[
            jax.ShapeDtypeStruct((length, D), BF),
            jax.ShapeDtypeStruct((HEADS, length), F32),
        ],
        in_specs=[vmem] * 3,
        out_specs=[vmem] * 2,
        scratch_shapes=[pltpu.VMEM((2, length, BLK), F32)],
        compiler_params=pltpu.CompilerParams(vmem_limit_bytes=VMEM_BYTES),
    )(qkv, segr, segc)


def attend_grad(qkv, segr, segc, out, upstream, lse):
    vmem = pl.BlockSpec(memory_space=pltpu.VMEM)
    length = qkv.shape[0]
    return pl.pallas_call(
        attend_back_kernel,
        out_shape=jax.ShapeDtypeStruct((length, 3 * D), BF),
        in_specs=[vmem] * 6,
        out_specs=vmem,
        scratch_shapes=[pltpu.VMEM((length, 128), F32)] * 2,
        compiler_params=pltpu.CompilerParams(vmem_limit_bytes=VMEM_BYTES),
    )(qkv, segr, segc, out, upstream, lse)


def row_body(
    inputs,
    segments,
    teacher,
    mixing_weight,
    output_weight,
    expand_weight,
    shrink_weight,
    vectors,
    mixing_first,
    output_first,
    expand_first,
    shrink_first,
    vectors_first,
    mixing_second,
    output_second,
    expand_second,
    shrink_second,
    vectors_second,
):
    count = lax.axis_size("dp")
    rows, local_len, features = inputs.shape
    masters = (mixing_weight, output_weight, expand_weight, shrink_weight)
    wide = jnp.broadcast_to(segments[:, None, :], (rows, 8, local_len))
    gathered = gather_all(count, masters, vectors, inputs, teacher, wide)
    mixing_low, output_low, expand_low, shrink_low = (
        g.reshape(count * m.shape[0], m.shape[1]) for g, m in zip(gathered[:4], masters)
    )
    per = vectors.shape[0] // 128
    (
        gain_one,
        shift_one,
        bias_query,
        bias_value,
        bias_output,
        gain_two,
        shift_two,
        bias_expand,
        bias_shrink,
    ) = split_vectors(gathered[4][:, :per].reshape(-1))
    states = gathered[5].astype(F32)
    targets = gathered[6].astype(F32)
    segs = gathered[7][:, 0, :].reshape(1, -1)
    length = segs.shape[1]
    segc = jnp.broadcast_to(segs.reshape(-1, 1), (length, 128))
    scale = 1.0 / math.sqrt(HD)
    normed_low = layer_norm(states, gain_one, shift_one).astype(BF)
    projected = jnp.dot(normed_low, mixing_low, preferred_element_type=F32)
    zero = jnp.zeros_like(bias_query)
    qkv = (
        (projected + jnp.concatenate([bias_query, zero, bias_value]))
        * jnp.concatenate([zero + scale, zero + 1.0, zero + 1.0])
    ).astype(BF)
    attended_low, lse = attend(qkv, segs, segc)
    middle = states + jnp.dot(attended_low, output_low, preferred_element_type=F32) + bias_output
    normed_two_low = layer_norm(middle, gain_two, shift_two).astype(BF)
    hidden = jnp.dot(normed_two_low, expand_low, preferred_element_type=F32) + bias_expand
    active, gelu_back = jax.vjp(gelu_tanh, hidden)
    active_low = active.astype(BF)
    result = middle + jnp.dot(active_low, shrink_low, preferred_element_type=F32) + bias_shrink
    target_prob = jax.nn.softmax(targets, axis=-1)
    result_grad = features * (jax.nn.softmax(result, axis=-1) - target_prob)
    result_low = result_grad.astype(BF)
    grad_shrink = jnp.dot(active_low.T, result_low, preferred_element_type=F32)
    grad_bias_shrink = jnp.sum(result_grad, axis=0)
    active_grad = jnp.dot(result_low, shrink_low.T, preferred_element_type=F32)
    active_round = lax.optimization_barrier(active_grad.astype(BF)).astype(F32)
    hidden_low = gelu_back(active_round)[0].astype(BF)
    grad_bias_expand = jnp.sum(hidden_low.astype(F32), axis=0)
    grad_expand = jnp.dot(normed_two_low.T, hidden_low, preferred_element_type=F32)
    normed_two_grad = jnp.dot(hidden_low, expand_low.T, preferred_element_type=F32)
    norm_two_back = jax.vjp(layer_norm, middle, gain_two, shift_two)[1]
    middle_part, grad_gain_two, grad_shift_two = norm_two_back(normed_two_grad)
    middle_grad = result_grad + middle_part
    middle_low = middle_grad.astype(BF)
    grad_bias_output = jnp.sum(middle_grad, axis=0)
    grad_output = jnp.dot(attended_low.T, middle_low, preferred_element_type=F32)
    upstream = jnp.dot(middle_low, output_low.T, preferred_element_type=F32).astype(BF)
    dqkv = attend_grad(qkv, segs, segc, attended_low, upstream, lse)
    grad_bias_query = jnp.sum(dqkv[:, :features].astype(F32), axis=0)
    grad_bias_value = jnp.sum(dqkv[:, 2 * features :].astype(F32), axis=0)
    grad_mixing = jnp.dot(normed_low.T, dqkv, preferred_element_type=F32)
    normed_grad = jnp.dot(dqkv, mixing_low.T, preferred_element_type=F32)
    norm_one_back = jax.vjp(layer_norm, states, gain_one, shift_one)[1]
    states_part, grad_gain_one, grad_shift_one = norm_one_back(normed_grad)
    input_grad = (middle_grad + states_part).astype(BF)
    grad_vectors = jnp.concatenate(
        [
            grad_gain_one,
            grad_shift_one,
            grad_bias_query,
            grad_bias_value,
            grad_bias_output,
            grad_gain_two,
            grad_shift_two,
            grad_bias_expand,
            grad_bias_shrink,
        ]
    )
    vector_rows = jnp.pad(grad_vectors.reshape(count, per, 128), ((0, 0), (0, VROWS - per), (0, 0)))
    grads = [
        g.astype(BF).reshape(count, 2, m.shape[0] // 2, m.shape[1])
        for g, m in zip((grad_mixing, grad_output, grad_expand, grad_shrink), masters)
    ]
    scattered = scatter_all(count, grads, vector_rows, result.astype(BF), input_grad, rows)
    sums = [s.reshape(m.shape).astype(F32) for s, m in zip(scattered[:4], masters)]
    sums.append(scattered[4][:per].reshape(-1))
    grad_norm = scattered[5][0, 0]
    clip_value = clip_level()
    factor = clip_value / jnp.maximum(grad_norm, clip_value)
    firsts = (mixing_first, output_first, expand_first, shrink_first, vectors_first)
    seconds = (mixing_second, output_second, expand_second, shrink_second, vectors_second)
    fresh = [
        adamw(master, first, second, total * factor, rate)
        for master, first, second, total, rate in zip(
            masters + (vectors,), firsts, seconds, sums, learn_rates()
        )
    ]
    return (
        scattered[6],
        scattered[7],
        grad_norm,
        *(f[0] for f in fresh),
        *(f[1] for f in fresh),
        *(f[2] for f in fresh),
    )


def whole_rows(mesh):
    return mesh.shape["seq"] == 4 and mesh.shape["dp"] == 8


def solution(mesh):
    in_specs = (
        P("dp", "seq", None),
        P("dp", "seq"),
        P("dp", "seq", None),
        P("dp", None),
        P("dp", None),
        P("dp", None),
        P("dp", None),
        P("dp"),
        P("dp", None),
        P("dp", None),
        P("dp", None),
        P("dp", None),
        P("dp"),
        P("dp", None),
        P("dp", None),
        P("dp", None),
        P("dp", None),
        P("dp"),
    )
    out_specs = (
        P("dp", "seq", None),
        P("dp", "seq", None),
        P(),
        P("dp", None),
        P("dp", None),
        P("dp", None),
        P("dp", None),
        P("dp"),
        P("dp", None),
        P("dp", None),
        P("dp", None),
        P("dp", None),
        P("dp"),
        P("dp", None),
        P("dp", None),
        P("dp", None),
        P("dp", None),
        P("dp"),
    )
    chosen = row_body if whole_rows(mesh) else body
    return jax.shard_map(chosen, mesh=mesh, in_specs=in_specs, out_specs=out_specs, check_vma=False)
```

```python
from functools import partial
import math

import jax
import jax.numpy as jnp
from jax import lax
from jax.experimental import pallas as pl
from jax.experimental.pallas import tpu as pltpu
from jax.sharding import PartitionSpec as P

D = 768
HEADS = 12
HD = 64
FF = 3072
LEN = 1024
NDOC = 8
STEP = 10


NEGATIVE = -1e30
NORM_EPS = 1e-05
BETA_ONE = 0.9
BETA_TWO = 0.999
ADAM_EPS = 1e-08
WEIGHT_DECAY = 0.01


def layer_norm(values, norm_gain, norm_shift):
    center = values - jnp.mean(values, axis=-1, keepdims=True)
    spread = jnp.mean(center * center, axis=-1, keepdims=True)
    return center * lax.rsqrt(spread + NORM_EPS) * norm_gain + norm_shift


def gelu_tanh(values):
    return jax.nn.gelu(values, approximate=True)


def split_vectors(packed):
    return jnp.split(packed, [D, 2 * D, 3 * D, 4 * D, 5 * D, 6 * D, 7 * D, 7 * D + FF])


def adamw(master, first, second, gradient, rate):
    first_new = BETA_ONE * first + (1.0 - BETA_ONE) * gradient
    second_new = BETA_TWO * second + (1.0 - BETA_TWO) * gradient * gradient
    first_hat = first_new / (1.0 - BETA_ONE**STEP)
    second_hat = second_new / (1.0 - BETA_TWO**STEP)
    updated = master - rate * (
        first_hat / (jnp.sqrt(second_hat) + ADAM_EPS) + WEIGHT_DECAY * master
    )
    return (updated, first_new, second_new)


def learn_rates():
    return (
        1.0 / math.sqrt(2 * D),
        1.0 / math.sqrt(max(1, 2 * D * NDOC // LEN)),
        1.0 / math.sqrt(D),
        1.0 / math.sqrt(FF),
        0.3,
    )


def clip_level():
    return 0.5 * math.sqrt(4 * D * D + 2 * D * FF + 8 * D + FF)


def visible(query_pos, key_pos, query_seg, key_seg):
    return (key_pos[None, :] <= query_pos[:, None]) & (key_seg[None, :] == query_seg[:, None])


def attend_rows(query_pos, key_pos, packed_args):
    queries, keys_all, values_all, query_seg, key_seg = packed_args
    scores = jnp.einsum("qhd,khd->hqk", queries, keys_all, preferred_element_type=jnp.float32)
    scores = jnp.where(visible(query_pos, key_pos, query_seg, key_seg)[None], scores, NEGATIVE)
    top_score = jnp.max(scores, axis=-1, keepdims=True)
    exponent = jnp.exp(scores - top_score)
    totals = jnp.sum(exponent, axis=-1, keepdims=True)
    probability = (exponent / totals).astype(jnp.bfloat16)
    attended = jnp.einsum(
        "hqk,khd->qhd", probability, values_all, preferred_element_type=jnp.float32
    )
    return (attended, (top_score + jnp.log(totals))[..., 0])


def attend_back(query_pos, key_pos, packed_args):
    queries, keys_all, values_all, upstream, log_totals, query_seg, key_seg = packed_args
    scores = jnp.einsum("qhd,khd->hqk", queries, keys_all, preferred_element_type=jnp.float32)
    scores = jnp.where(visible(query_pos, key_pos, query_seg, key_seg)[None], scores, NEGATIVE)
    probability = jnp.exp(scores - log_totals[..., None])
    prob_low = probability.astype(jnp.bfloat16)
    prob_grad = jnp.einsum("qhd,khd->hqk", upstream, values_all, preferred_element_type=jnp.float32)
    value_part = jnp.einsum("hqk,qhd->khd", prob_low, upstream, preferred_element_type=jnp.float32)
    score_grad = probability * (
        prob_grad - jnp.sum(probability * prob_grad, axis=-1, keepdims=True)
    )
    score_low = score_grad.astype(jnp.bfloat16)
    query_part = jnp.einsum("hqk,khd->qhd", score_low, keys_all, preferred_element_type=jnp.float32)
    key_part = jnp.einsum("hqk,qhd->khd", score_low, queries, preferred_element_type=jnp.float32)
    key_count = keys_all.shape[0]
    return (
        query_part,
        jnp.concatenate(
            [key_part.reshape(key_count, -1), value_part.reshape(key_count, -1)], axis=1
        ),
    )


def body(
    inputs,
    segments,
    teacher,
    mixing_weight,
    output_weight,
    expand_weight,
    shrink_weight,
    vectors,
    mixing_first,
    output_first,
    expand_first,
    shrink_first,
    vectors_first,
    mixing_second,
    output_second,
    expand_second,
    shrink_second,
    vectors_second,
):
    bfloat = jnp.bfloat16
    floats = jnp.float32
    seq_count, local_len, features = inputs.shape
    row_count = seq_count * local_len
    scale = 1.0 / math.sqrt(HD)
    mixing_low, output_low, expand_low, shrink_low, vectors_low = (
        lax.all_gather(mixing_weight.astype(bfloat), "dp", axis=0, tiled=True),
        lax.all_gather(output_weight.astype(bfloat), "dp", axis=0, tiled=True),
        lax.all_gather(expand_weight.astype(bfloat), "dp", axis=0, tiled=True),
        lax.all_gather(shrink_weight.astype(bfloat), "dp", axis=0, tiled=True),
        lax.all_gather(vectors.astype(bfloat), "dp", axis=0, tiled=True),
    )
    (
        gain_one,
        shift_one,
        bias_query,
        bias_value,
        bias_output,
        gain_two,
        shift_two,
        bias_expand,
        bias_shrink,
    ) = split_vectors(vectors_low.astype(floats))
    states = inputs.astype(floats).reshape(row_count, features)
    normed = layer_norm(states, gain_one, shift_one)
    normed_low = normed.astype(bfloat)
    projected = jnp.dot(normed_low, mixing_low, preferred_element_type=floats)
    query_low = ((projected[:, :features] + bias_query) * scale).astype(bfloat)
    key_low = projected[:, features : 2 * features].astype(bfloat)
    value_low = (projected[:, 2 * features :] + bias_value).astype(bfloat)
    key_all, value_all = (
        lax.all_gather(key_low.reshape(seq_count, local_len, features), "seq", axis=1, tiled=True),
        lax.all_gather(
            value_low.reshape(seq_count, local_len, features), "seq", axis=1, tiled=True
        ),
    )
    segment_all = lax.all_gather(segments, "seq", axis=1, tiled=True)
    full_len = key_all.shape[1]
    query_pos = lax.axis_index("seq") * local_len + jnp.arange(local_len, dtype=jnp.int32)
    key_pos = jnp.arange(full_len, dtype=jnp.int32)
    query_heads = query_low.reshape(seq_count, local_len, HEADS, HD)
    key_heads = key_all.reshape(seq_count, full_len, HEADS, HD)
    value_heads = value_all.reshape(seq_count, full_len, HEADS, HD)
    attended, log_totals = lax.map(
        partial(attend_rows, query_pos, key_pos),
        (query_heads, key_heads, value_heads, segments, segment_all),
    )
    attended_low = attended.reshape(row_count, features).astype(bfloat)
    middle = states + jnp.dot(attended_low, output_low, preferred_element_type=floats) + bias_output
    normed_two = layer_norm(middle, gain_two, shift_two)
    normed_two_low = normed_two.astype(bfloat)
    hidden = jnp.dot(normed_two_low, expand_low, preferred_element_type=floats) + bias_expand
    active, gelu_back = jax.vjp(gelu_tanh, hidden)
    active_low = active.astype(bfloat)
    result = middle + jnp.dot(active_low, shrink_low, preferred_element_type=floats) + bias_shrink
    block_output = result.astype(bfloat).reshape(seq_count, local_len, features)
    target_prob = jax.nn.softmax(teacher.astype(floats).reshape(row_count, features), axis=-1)
    result_grad = features * (jax.nn.softmax(result, axis=-1) - target_prob)
    result_low = result_grad.astype(bfloat)
    grad_shrink = jnp.dot(active_low.T, result_low, preferred_element_type=floats)
    grad_bias_shrink = jnp.sum(result_grad, axis=0)
    active_grad = jnp.dot(result_low, shrink_low.T, preferred_element_type=floats)
    active_round = lax.optimization_barrier(active_grad.astype(bfloat)).astype(floats)
    hidden_low = gelu_back(active_round)[0].astype(bfloat)
    grad_bias_expand = jnp.sum(hidden_low.astype(floats), axis=0)
    grad_expand = jnp.dot(normed_two_low.T, hidden_low, preferred_element_type=floats)
    normed_two_grad = jnp.dot(hidden_low, expand_low.T, preferred_element_type=floats)
    norm_two_back = jax.vjp(layer_norm, middle, gain_two, shift_two)[1]
    middle_part, grad_gain_two, grad_shift_two = norm_two_back(normed_two_grad)
    middle_grad = result_grad + middle_part
    middle_low = middle_grad.astype(bfloat)
    grad_bias_output = jnp.sum(middle_grad, axis=0)
    grad_output = jnp.dot(attended_low.T, middle_low, preferred_element_type=floats)
    attended_grad = jnp.dot(middle_low, output_low.T, preferred_element_type=floats).astype(bfloat)
    upstream_heads = attended_grad.reshape(seq_count, local_len, HEADS, HD)
    query_grad, kv_terms = lax.map(
        partial(attend_back, query_pos, key_pos),
        (query_heads, key_heads, value_heads, upstream_heads, log_totals, segments, segment_all),
    )
    kv_sums = (
        lax.psum_scatter(kv_terms.astype(jnp.bfloat16), "seq", scatter_dimension=1, tiled=True)
        .astype(jnp.float32)
        .reshape(row_count, 2 * features)
    )
    key_grad_low = kv_sums[:, :features].astype(bfloat)
    value_grad_low = kv_sums[:, features:].astype(bfloat)
    query_grad_low = query_grad.reshape(row_count, features).astype(bfloat)
    query_scaled = query_grad_low.astype(floats) * scale
    grad_bias_query = jnp.sum(query_scaled, axis=0)
    grad_bias_value = jnp.sum(value_grad_low.astype(floats), axis=0)
    projected_grad = jnp.concatenate(
        [query_scaled.astype(bfloat), key_grad_low, value_grad_low], axis=1
    )
    grad_mixing = jnp.dot(normed_low.T, projected_grad, preferred_element_type=floats)
    normed_grad = jnp.dot(projected_grad, mixing_low.T, preferred_element_type=floats)
    norm_one_back = jax.vjp(layer_norm, states, gain_one, shift_one)[1]
    states_part, grad_gain_one, grad_shift_one = norm_one_back(normed_grad)
    input_grad = (middle_grad + states_part).astype(bfloat).reshape(seq_count, local_len, features)
    grad_vectors = jnp.concatenate(
        [
            grad_gain_one,
            grad_shift_one,
            grad_bias_query,
            grad_bias_value,
            grad_bias_output,
            grad_gain_two,
            grad_shift_two,
            grad_bias_expand,
            grad_bias_shrink,
        ]
    )
    vector_rows = grad_vectors.reshape(lax.axis_size("dp"), -1)
    mixing_part, output_part, expand_part, shrink_part, vector_part = (
        lax.psum_scatter(
            grad_mixing.astype(jnp.bfloat16), "dp", scatter_dimension=0, tiled=True
        ).astype(jnp.float32),
        lax.psum_scatter(
            grad_output.astype(jnp.bfloat16), "dp", scatter_dimension=0, tiled=True
        ).astype(jnp.float32),
        lax.psum_scatter(
            grad_expand.astype(jnp.bfloat16), "dp", scatter_dimension=0, tiled=True
        ).astype(jnp.float32),
        lax.psum_scatter(
            grad_shrink.astype(jnp.bfloat16), "dp", scatter_dimension=0, tiled=True
        ).astype(jnp.float32),
        lax.psum_scatter(
            vector_rows.astype(jnp.bfloat16), "dp", scatter_dimension=0, tiled=True
        ).astype(jnp.float32),
    )
    mixing_sum, output_sum, expand_sum, shrink_sum, vector_sum = (
        lax.psum(mixing_part.astype(jnp.bfloat16), "seq").astype(jnp.float32),
        lax.psum(output_part.astype(jnp.bfloat16), "seq").astype(jnp.float32),
        lax.psum(expand_part.astype(jnp.bfloat16), "seq").astype(jnp.float32),
        lax.psum(shrink_part.astype(jnp.bfloat16), "seq").astype(jnp.float32),
        lax.psum(vector_part.astype(jnp.bfloat16), "seq").astype(jnp.float32),
    )
    vector_sum = vector_sum.reshape(-1)
    squares = (
        jnp.sum(mixing_sum * mixing_sum)
        + jnp.sum(output_sum * output_sum)
        + jnp.sum(expand_sum * expand_sum)
        + jnp.sum(shrink_sum * shrink_sum)
        + jnp.sum(vector_sum * vector_sum)
    )
    grad_norm = jnp.sqrt(lax.psum(squares, "dp"))
    clip_value = clip_level()
    factor = clip_value / jnp.maximum(grad_norm, clip_value)
    step_rates = learn_rates()
    mixing_new = adamw(
        mixing_weight, mixing_first, mixing_second, mixing_sum * factor, step_rates[0]
    )
    output_new = adamw(
        output_weight, output_first, output_second, output_sum * factor, step_rates[1]
    )
    expand_new = adamw(
        expand_weight, expand_first, expand_second, expand_sum * factor, step_rates[2]
    )
    shrink_new = adamw(
        shrink_weight, shrink_first, shrink_second, shrink_sum * factor, step_rates[3]
    )
    vectors_new = adamw(vectors, vectors_first, vectors_second, vector_sum * factor, step_rates[4])
    return (
        block_output,
        input_grad,
        grad_norm,
        mixing_new[0],
        output_new[0],
        expand_new[0],
        shrink_new[0],
        vectors_new[0],
        mixing_new[1],
        output_new[1],
        expand_new[1],
        shrink_new[1],
        vectors_new[1],
        mixing_new[2],
        output_new[2],
        expand_new[2],
        shrink_new[2],
        vectors_new[2],
    )

MESH = pl.DeviceIdType.MESH
BF = jnp.bfloat16
F32 = jnp.float32
BLK = 256
NN = ((1,), (0,))
NT = ((1,), (1,))
TN = ((0,), (0,))
VMEM_BYTES = 64 * 2**20 - 2**17
VROWS = 16
MIX, OUT, EXP, SHR = 0, 1, 2, 3
SUBS = (2, 1, 2, 2)


def dot(left, right, dims):
    return lax.dot_general(left, right, (dims, ((), ())), preferred_element_type=F32)


class Place:
    def __init__(self, count):
        self.count = count
        self.dp = lax.axis_index("dp")
        self.seq = lax.axis_index("seq")
        odd = self.dp % 2
        self.pos = (1 - odd) * (self.dp // 2) + odd * (count - 1 - self.dp // 2)
        self.core = self.seq % 2
        self.step = 1 - 2 * self.core
        self.next = (self.at(self.pos + self.step + count), self.seq)
        self.prev = (self.at(self.pos - self.step + count), self.seq)
        self.mate = (self.dp, self.seq + 1 - 2 * self.core)
        self.across = (self.dp, self.seq + 2 - 4 * (self.seq // 2))

    def at(self, pos):
        pos = pos % self.count
        upper = pos // (self.count // 2)
        return (1 - upper) * (2 * pos) + upper * (2 * (self.count - 1 - pos) + 1)

    def behind(self, steps):
        return self.at(self.pos - steps * self.step + 2 * self.count)

    def seq_peer(self, offset):
        return (self.dp, (self.seq + offset) % 4)

    def dp_peer(self, offset):
        return ((self.dp + offset) % self.count, self.seq)

    def greet(self):
        barrier = pltpu.get_barrier_semaphore()
        peers = [self.seq_peer(k) for k in range(1, 4)]
        peers += [self.dp_peer(k) for k in range(1, self.count)]
        for peer in peers:
            pl.semaphore_signal(barrier, inc=1, device_id=peer, device_id_type=MESH)
        return lambda: pl.semaphore_wait(barrier, len(peers))


def describe(src, dst, send, recv, device):
    return pltpu.make_async_remote_copy(
        src_ref=src,
        dst_ref=dst,
        send_sem=send,
        recv_sem=recv,
        device_id=device,
        device_id_type=MESH,
    )


def remote(src, dst, send, recv, device):
    copy = describe(src, dst, send, recv, device)
    copy.start()
    return copy


def local(src, dst, sem):
    copy = pltpu.make_async_copy(src, dst, sem)
    copy.start()
    return copy


def span(start, size, unit):
    return pl.ds(start if isinstance(start, int) else pl.multiple_of(start, unit), size)


def sub_block(ref, w, sub):
    rows, columns = ref.shape
    if w == SHR:
        return ref.at[span(sub * (rows // 2), rows // 2, 16)]
    size = columns // SUBS[w]
    return ref.at[:, span(sub * size, size, 128)]


class Gather:
    def __init__(self, place, full, sems):
        self.place, self.full = place, full
        self.ring_s, self.ring_r, self.mate_s, self.mate_r = sems

    def block(self, w, owner, core, sub):
        return sub_block(self.full[w].at[owner, core], w, sub)

    def ring(self, w, sub, t):
        block = self.block(w, self.place.behind(t), self.place.core, sub)
        return describe(
            block, block, self.ring_s.at[w, sub, t], self.ring_r.at[w, sub, t], self.place.next
        )

    def pair(self, w, sub, t):
        block = self.block(w, self.place.behind(t), self.place.core, sub)
        return describe(
            block, block, self.mate_s.at[w, sub, t], self.mate_r.at[w, sub, t], self.place.mate
        )

    def start(self, w):
        for sub in range(SUBS[w]):
            self.ring(w, sub, 0).start()

    def tick(self, w, sub, t):
        self.ring(w, sub, t - 1).wait_recv()
        if isinstance(t, int):
            if t < self.place.count - 1:
                self.ring(w, sub, t).start()
        else:
            pl.when(t < self.place.count - 1)(lambda: self.ring(w, sub, t).start())
        self.pair(w, sub, t).start()

    def arrived(self, w):
        def step(t, _):
            for sub in range(SUBS[w]):
                self.pair(w, sub, t).wait_recv()
            return 0

        lax.fori_loop(1, self.place.count, step, 0)

    def drain(self, w):
        def step(t, _):
            for sub in range(SUBS[w]):
                self.ring(w, sub, t).wait_send()
                self.pair(w, sub, t + 1).wait_send()
            return 0

        lax.fori_loop(0, self.place.count - 1, step, 0)


class Scatter:
    def __init__(self, place, grads, mates, slots, cross, sums, sems):
        self.place, self.grads, self.mates, self.slots = place, grads, mates, slots
        self.cross_mine, self.cross_in = cross
        self.sums = sums
        (
            self.mate_s,
            self.mate_r,
            self.ring_s,
            self.ring_r,
            self.cross_s,
            self.cross_r,
            self.total_s,
            self.total_r,
        ) = sems

    def own(self, w, owner, core, sub):
        return sub_block(self.grads[w].at[owner, core], w, sub)

    def mate(self, w, owner, sub):
        return sub_block(self.mates(w, owner), w, sub)

    def slot(self, w, t, sub):
        return sub_block(self.slots(w, t), w, sub)

    def pair(self, w, sub, owner):
        return describe(
            self.own(w, owner, 1 - self.place.core, sub),
            self.mate(w, owner, sub),
            self.mate_s.at[w, sub, owner],
            self.mate_r.at[w, sub, owner],
            self.place.mate,
        )

    def ring(self, w, sub, t):
        src = self.own(w, self.place.behind(1), self.place.core, sub) if (
            isinstance(t, int) and t == 0
        ) else self.slot(w, t - 1, sub)
        return describe(
            src, self.slot(w, t, sub), self.ring_s.at[w, sub, t], self.ring_r.at[w, sub, t], self.place.next
        )

    def over(self, w, sub):
        return describe(
            sub_block(self.cross_mine[w], w, sub),
            sub_block(self.cross_in[w], w, sub),
            self.cross_s.at[w, sub],
            self.cross_r.at[w, sub],
            self.place.across,
        )

    def total(self, w, sub):
        block = sub_block(self.sums[w].at[self.place.core], w, sub)
        return describe(
            block, block, self.total_s.at[w, sub], self.total_r.at[w, sub], self.place.mate
        )

    def hand(self, w, sub):
        for owner in range(self.place.count):
            self.pair(w, sub, owner).start()

    def term(self, w, owner, sub):
        return self.own(w, owner, self.place.core, sub)[...].astype(F32) + self.mate(w, owner, sub)[
            ...
        ].astype(F32)

    def start(self, w, sub):
        for owner in range(self.place.count):
            self.pair(w, sub, owner).wait_recv()
        owner = self.place.behind(1)
        self.own(w, owner, self.place.core, sub)[...] = self.term(w, owner, sub).astype(BF)
        self.ring(w, sub, 0).start()

    def tick(self, w, sub, t):
        count = self.place.count
        if isinstance(t, int):
            self.ring(w, sub, t - 1).wait_recv()
        else:
            slot = self.slot(w, t - 1, sub)
            describe(
                slot, slot, self.ring_s.at[w, sub, t - 1], self.ring_r.at[w, sub, t - 1], self.place.next
            ).wait_recv()
        slot = self.slot(w, t - 1, sub)
        total = (slot[...].astype(F32) + self.term(w, self.place.behind(t + 1), sub)).astype(BF)

        def pass_on():
            slot[...] = total
            self.ring(w, sub, t).start()

        def finish():
            sub_block(self.cross_mine[w], w, sub)[...] = total
            self.over(w, sub).start()

        if isinstance(t, int):
            (pass_on if t < count - 1 else finish)()
        else:
            pl.when(t < count - 1)(pass_on)
            pl.when(t == count - 1)(finish)

    def crossed(self, w, sub):
        self.over(w, sub).wait_recv()
        value = sub_block(self.cross_mine[w], w, sub)[...].astype(F32)
        value = value + sub_block(self.cross_in[w], w, sub)[...].astype(F32)
        sub_block(self.sums[w].at[self.place.core], w, sub)[...] = value.astype(BF)
        self.total(w, sub).start()

    def arrived(self, w, sub):
        self.total(w, sub).wait_recv()

    def drain(self, w):
        for sub in range(SUBS[w]):
            for owner in range(self.place.count):
                self.pair(w, sub, owner).wait_send()
            for t in range(self.place.count - 1):
                self.ring(w, sub, t).wait_send()
            self.over(w, sub).wait_send()
            self.total(w, sub).wait_send()


def seen(sk, sq, diagonal):
    vis = jnp.concatenate([sk] * (BLK // 128), axis=1) == sq
    if diagonal:
        vis = vis & (
            lax.broadcasted_iota(jnp.int32, (BLK, BLK), 0)
            <= lax.broadcasted_iota(jnp.int32, (BLK, BLK), 1)
        )
    return vis


def columns_of(hp):
    return [span(part * D + hp * 128, 128, 128) for part in range(3)]


def attend_pair(hp, qkv, segr, segc, out, lse, scores, tick):
    lane = lax.broadcasted_iota(jnp.int32, (1, 128), 1)
    cq, ck, cv = columns_of(hp)
    vt = qkv[:, cv].T
    for i in range(qkv.shape[0] // BLK):
        tick(i)
        rq = slice(i * BLK, (i + 1) * BLK)
        qb = qkv[rq, cq]
        sq = segr[0:1, rq]
        outs = []
        for hd in range(2):
            kept = slice(hd * BLK, (hd + 1) * BLK)
            qm = jnp.where((lane < 64) if hd == 0 else (lane >= 64), qb, jnp.zeros_like(qb))
            top = None
            for j in range(i + 1):
                rk = slice(j * BLK, (j + 1) * BLK)
                s = jnp.where(seen(segc[rk, :], sq, i == j), dot(qkv[rk, ck], qm, NT), NEGATIVE)
                scores[rk, kept] = s
                best = jnp.max(s, axis=0, keepdims=True)
                top = best if top is None else jnp.maximum(top, best)
            total = acc = None
            for j in range(i + 1):
                rk = slice(j * BLK, (j + 1) * BLK)
                p = jnp.exp(scores[rk, kept] - top)
                part = jnp.sum(p, axis=0, keepdims=True)
                total = part if total is None else total + part
                term = dot(vt[hd * 64 : (hd + 1) * 64, rk], p.astype(BF), NN)
                acc = term if acc is None else acc + term
            outs.append(acc * (1.0 / total))
            lse[pl.ds(hp * 2 + hd, 1), rq] = top + jnp.log(total)
        out[rq, cq] = jnp.concatenate(outs, axis=0).T.astype(BF)


def attend_back_pair(hp, qkv, segr, segc, out, upstream, lse, sums, tick):
    lane = lax.broadcasted_iota(jnp.int32, (1, 128), 1)
    cq, ck, cv = columns_of(hp)
    in_v, in_k = slice(0, 128), slice(128, 256)
    kt = qkv[:, ck].T
    for i in range(qkv.shape[0] // BLK):
        tick(i)
        rq = slice(i * BLK, (i + 1) * BLK)
        qb = qkv[rq, cq]
        db = upstream[rq, cq]
        prod = (db.astype(F32) * out[rq, cq].astype(F32)).T
        sq = segr[0:1, rq]
        dqs = []
        for hd in range(2):
            half = (lane < 64) if hd == 0 else (lane >= 64)
            qm = jnp.where(half, qb, jnp.zeros_like(qb))
            dm = jnp.where(half, db, jnp.zeros_like(db))
            delta = jnp.sum(prod[hd * 64 : (hd + 1) * 64, :], axis=0, keepdims=True)
            ls = lse[pl.ds(hp * 2 + hd, 1), rq]
            dq = None
            for j in range(i + 1):
                rk = slice(j * BLK, (j + 1) * BLK)
                s = jnp.where(seen(segc[rk, :], sq, i == j), dot(qkv[rk, ck], qm, NT), NEGATIVE)
                p = jnp.exp(s - ls)
                ds = (p * (dot(qkv[rk, cv], dm, NT) - delta)).astype(BF)
                pv = dot(p.astype(BF), dm, NN)
                pk = dot(ds, qm, NN)
                if i == j and hd == 0:
                    sums[rk, in_v] = pv
                    sums[rk, in_k] = pk
                else:
                    sums[rk, in_v] += pv
                    sums[rk, in_k] += pk
                term = dot(kt[hd * 64 : (hd + 1) * 64, rk], ds, NN)
                dq = term if dq is None else dq + term
            dqs.append(dq)
        low = jnp.concatenate(dqs, axis=0).T.astype(BF).astype(F32)
        qkv[rq, cq] = (low * (1.0 / math.sqrt(HD))).astype(BF)
    qkv[:, ck] = sums[:, in_k].astype(BF)
    qkv[:, cv] = sums[:, in_v].astype(BF)


def normalised(values):
    center = values - jnp.mean(values, axis=-1, keepdims=True)
    inverse = lax.rsqrt(jnp.mean(center * center, axis=-1, keepdims=True) + NORM_EPS)
    return center * inverse, inverse


def norm_grad(values, gain, upstream):
    hat, inverse = normalised(values)
    scaled = upstream * gain
    first = jnp.mean(scaled, axis=-1, keepdims=True)
    second = jnp.mean(scaled * hat, axis=-1, keepdims=True)
    return (
        inverse * (scaled - first - hat * second),
        jnp.sum(upstream * hat, axis=0, keepdims=True),
        jnp.sum(upstream, axis=0, keepdims=True),
    )


def gelu_both(u):
    slope = math.sqrt(2.0 / math.pi)
    square = u * u
    th = jnp.tanh(slope * u * (1.0 + 0.044715 * square))
    half = 0.5 * (1.0 + th)
    return u * half, half + 0.5 * u * (1.0 - th * th) * (slope * (1.0 + 3.0 * 0.044715 * square))


def softmax(values):
    e = jnp.exp(values - jnp.max(values, axis=-1, keepdims=True))
    return e * (1.0 / jnp.sum(e, axis=-1, keepdims=True))


def whole(ref):
    return ref[...].reshape(-1, ref.shape[-1])


VEC_PLACES = (("g1", D), ("b1", D), ("bq", D), ("bv", D), ("bo", D), ("g2", D), ("b2", D), ("bf1", FF), ("bf2", D))
VEC_ROW = {name: row for row, (name, _) in enumerate(VEC_PLACES)}
VEC_SIZE = dict(VEC_PLACES)


def block_kernel(count, *refs):
    inputs, teacher, segments, masters, vec_ref = refs[0], refs[1], refs[2], refs[3:7], refs[7]
    sums, vec_sum, norm_ref, out_rows, back_rows = refs[8:12], refs[12], refs[13], refs[14], refs[15]
    (
        full0, full1, full2, full3, x, h1, qkv, att, x1, h2, act, slope, dy, low, sent, mixing_grad,
        shr_mate, shr_slot, cm0, cm1, cm2, cm3, ci0, ci1, ci2, ci3, lse, segs, seg_stage, segr, segc,
        vec_stage, vec_all, vec, gvec, vec_out, vec_buf, vec_mine, vec_seq, sq_mine, sq_buf,
        load_sem, g_ring_s, g_ring_r, g_mate_s, g_mate_r,
        s_mate_s, s_mate_r, s_ring_s, s_ring_r, s_cross_s, s_cross_r, s_total_s, s_total_r,
        row_s, row_r, row_l, vec_s, vec_r, vecq_s, vecq_r, sq_s, sq_r, free,
    ) = refs[16:]
    full = (full0, full1, full2, full3)
    place = Place(count)
    ready = place.greet()
    length = x.shape[0]
    blocks = length // BLK
    last = count - 1
    scale = 1.0 / math.sqrt(HD)

    def rows(i):
        return span(i * BLK, BLK, BLK)

    loads = []
    pieces = []
    used = [0, 0]
    for w in (MIX, OUT, EXP, SHR):
        master = masters[w]
        height, width = master.shape
        for column in range(0, width, D):
            which = 0 if used[0] + height <= length else 1
            buffer = (dy, x1)[which]
            where = buffer.at[pl.ds(used[which], height)]
            used[which] += height
            source = master.at[:, pl.ds(column, D)]
            loads.append(local(source, where, load_sem.at[len(loads)]))
            pieces.append((w, column, where))
    seg_stage[...] = jnp.broadcast_to(segments[...][:, None, :], seg_stage.shape)
    vec_stage[...] = jnp.concatenate(
        [vec_ref[...].astype(BF).astype(F32), jnp.zeros((VROWS - vec_ref.shape[0], 128), F32)],
        axis=0,
    )
    ready()

    me = rows(place.seq)
    row_in, teach_in, vec_in = [], [], []
    row_in.append(local(inputs.at[place.seq], x.at[me], row_l.at[0]))
    teach_in.append(local(teacher.at[place.seq], low.at[me], row_l.at[1]))
    segs[place.seq] = seg_stage[place.seq]
    for k in range(1, 4):
        peer = place.seq_peer(k)
        row_in.append(
            remote(inputs.at[peer[1]], x.at[me], row_s.at[k, 0], row_r.at[k, 0], peer)
        )
        row_in.append(
            remote(seg_stage.at[peer[1]], segs.at[place.seq], row_s.at[k, 1], row_r.at[k, 1], peer)
        )
    for k in range(1, count):
        vec_in.append(
            remote(vec_stage, vec_all.at[place.dp], vec_s.at[k], vec_r.at[k], place.dp_peer(k))
        )
    vec_all[place.dp] = vec_stage[...]

    gather = Gather(place, full, (g_ring_s, g_ring_r, g_mate_s, g_mate_r))
    done = 0
    for w in (MIX, OUT, EXP, SHR):
        for load, (owner, column, where) in zip(loads, pieces):
            if owner == w:
                load.wait()
                full[w][place.dp, :, :, pl.ds(column, D)] = (
                    where[...].astype(BF).reshape(full[w].shape[1:3] + (D,))
                )
        if w in (MIX, OUT):
            gather.start(w)
    for k in range(1, 4):
        peer = place.seq_peer(k)
        teach_in.append(
            remote(teacher.at[peer[1]], low.at[me], row_s.at[k, 2], row_r.at[k, 2], peer)
        )
    for t in range(1, count):
        gather.tick(MIX, 0, t)
        gather.tick(OUT, 0, t)
        gather.tick(MIX, 1, t)
        if t == last - 1:
            gather.start(EXP)

    for copy in vec_in:
        copy.wait_recv()
    per = vec_ref.shape[0]
    flat = 0
    for name, size in VEC_PLACES:
        parts = []
        for r in range(flat, flat + size // 128):
            parts.append(vec_all[r // per, r % per : r % per + 1, :])
        vec[VEC_ROW[name] : VEC_ROW[name] + 1, 0:size] = jnp.concatenate(parts, axis=1)
        flat += size // 128

    def of(name):
        return vec[VEC_ROW[name] : VEC_ROW[name] + 1, 0 : VEC_SIZE[name]]

    def add_grad(name, term):
        gvec[VEC_ROW[name] : VEC_ROW[name] + 1, 0 : VEC_SIZE[name]] += term

    gvec[...] = jnp.zeros_like(gvec)
    for copy in row_in:
        copy.wait() if copy is row_in[0] else copy.wait_recv()

    segr[...] = jnp.concatenate([segs[s, 0:1, :] for s in range(4)], axis=1).astype(F32)
    for s in range(4):
        segc[s * BLK : (s + 1) * BLK, :] = jnp.concatenate([segs[s].astype(F32)] * 16, axis=0).T

    def first_norm(i, _):
        hat, _ = normalised(x[rows(i), :].astype(F32))
        h1[rows(i), :] = (hat * of("g1") + of("b1")).astype(BF)
        return 0

    lax.fori_loop(0, blocks, first_norm, 0)
    gather.arrived(MIX)
    gather.arrived(OUT)

    def project(i, _):
        value = dot(h1[rows(i), :], whole(full[MIX]), NN)
        qkv[rows(i), 0:D] = ((value[:, 0:D] + of("bq")) * scale).astype(BF)
        qkv[rows(i), D : 2 * D] = value[:, D : 2 * D].astype(BF)
        qkv[rows(i), 2 * D :] = (value[:, 2 * D :] + of("bv")).astype(BF)
        gather.tick(EXP, 0, i + 1)
        gather.tick(EXP, 1, i + 1)
        return 0

    lax.fori_loop(0, blocks, project, 0)

    def forward_pair(hp, _):
        def tick(i):
            k = hp * blocks + i
            ahead = 2 * (last - blocks)

            def expand():
                gather.tick(EXP, k % 2, blocks + 1 + k // 2)

            def shrink():
                gather.tick(SHR, (k - ahead) % 2, 1 + (k - ahead) // 2)

            pl.when(k < ahead)(expand)
            pl.when(k == ahead - 1)(lambda: gather.start(SHR))
            pl.when(jnp.logical_and(k >= ahead, k < ahead + 2 * last))(shrink)

        attend_pair(hp, qkv, segr, segc, att, lse, dy, tick)
        return 0

    lax.fori_loop(0, D // 128, forward_pair, 0)

    def middle(i, _):
        value = x[rows(i), :].astype(F32) + dot(att[rows(i), :], whole(full[OUT]), NN) + of("bo")
        x1[rows(i), :] = value
        hat, _ = normalised(value)
        h2[rows(i), :] = (hat * of("g2") + of("b2")).astype(BF)
        return 0

    lax.fori_loop(0, blocks, middle, 0)
    gather.arrived(EXP)

    def expand(i, _):
        for n in range(FF // D):
            c = slice(n * D, (n + 1) * D)
            weight = full[EXP][:, :, :, c].reshape(D, D)
            u = dot(h2[rows(i), :], weight, NN) + vec[VEC_ROW["bf1"] : VEC_ROW["bf1"] + 1, c]
            a, s = gelu_both(u)
            act[rows(i), c] = a.astype(BF)
            slope[rows(i), c] = s.astype(BF)
        return 0

    lax.fori_loop(0, blocks, expand, 0)
    gather.arrived(SHR)
    for copy in teach_in:
        copy.wait() if copy is teach_in[0] else copy.wait_recv()

    def shrink(i, _):
        value = x1[rows(i), :] + dot(act[rows(i), :], whole(full[SHR]), NN) + of("bf2")
        sent[rows(i), :] = value.astype(BF)
        grad = D * (softmax(value) - softmax(low[rows(i), :].astype(F32)))
        dy[rows(i), :] = grad
        low[rows(i), :] = grad.astype(BF)
        add_grad("bf2", jnp.sum(grad, axis=0, keepdims=True))
        return 0

    lax.fori_loop(0, blocks, shrink, 0)
    for w in (MIX, OUT, EXP, SHR):
        gather.drain(w)
    out_copies = [local(sent.at[me], out_rows.at[place.seq], row_l.at[2])]
    for k in range(1, 4):
        peer = place.seq_peer(k)
        out_copies.append(
            remote(sent.at[rows(peer[1])], out_rows.at[place.seq], row_s.at[k, 3], row_r.at[k, 3], peer)
        )

    half = full[MIX].shape[2]

    def mates(w, owner):
        if w == SHR:
            return shr_mate.at[owner]
        where = span(owner * half, half, 16)
        if w == EXP:
            return act.at[where]
        return slope.at[where, pl.ds(0, 3 * D)] if w == MIX else slope.at[where, pl.ds(3 * D, D)]

    def slots(w, t):
        if w == SHR:
            return shr_slot.at[t]
        where = span((count + t) * half, half, 16)
        if w == EXP:
            return act.at[where]
        return slope.at[where, pl.ds(0, 3 * D)] if w == MIX else slope.at[where, pl.ds(3 * D, D)]

    grads = (mixing_grad, full1, full2, full3)
    scatter = Scatter(
        place,
        grads,
        mates,
        slots,
        ((cm0, cm1, cm2, cm3), (ci0, ci1, ci2, ci3)),
        sums,
        (s_mate_s, s_mate_r, s_ring_s, s_ring_r, s_cross_s, s_cross_r, s_total_s, s_total_r),
    )

    def offer(which):
        pl.semaphore_signal(free.at[which], inc=1, device_id=place.prev, device_id_type=MESH)
        pl.semaphore_signal(free.at[which + 1], inc=1, device_id=place.mate, device_id_type=MESH)

    def accept(which):
        pl.semaphore_wait(free.at[which], 1)

    def expand_back(i, _):
        for n in range(FF // D):
            c = slice(n * D, (n + 1) * D)
            weight = full[SHR][2 * n : 2 * n + 2].reshape(D, D)
            da = dot(low[rows(i), :], weight, NT).astype(BF).astype(F32)
            du = (da * slope[rows(i), c].astype(F32)).astype(BF)
            slope[rows(i), c] = du
            gvec[VEC_ROW["bf1"] : VEC_ROW["bf1"] + 1, c] += jnp.sum(
                du.astype(F32), axis=0, keepdims=True
            )
        return 0

    lax.fori_loop(0, blocks, expand_back, 0)

    def shrink_grad(n, _):
        value = dot(act[:, span(n * D, D, 128)], low[...], TN).astype(BF)
        full3[pl.ds(2 * n, 2)] = value.reshape((2,) + full3.shape[1:])
        return 0

    lax.fori_loop(0, FF // D, shrink_grad, 0)
    offer(0)
    scatter.hand(SHR, 0)
    scatter.hand(SHR, 1)

    def middle_back(i, _):
        upstream = dot(slope[rows(i), :], whole(full[EXP]), NT)
        part, gain, shift = norm_grad(x1[rows(i), :], of("g2"), upstream)
        value = dy[rows(i), :] + part
        dy[rows(i), :] = value
        low[rows(i), :] = value.astype(BF)
        add_grad("g2", gain)
        add_grad("b2", shift)
        add_grad("bo", jnp.sum(value, axis=0, keepdims=True))

        def begin():
            scatter.start(SHR, 0)
            scatter.start(SHR, 1)

        def go_on():
            scatter.tick(SHR, 0, i)
            scatter.tick(SHR, 1, i)

        pl.when(i == 0)(begin)
        pl.when(i > 0)(go_on)
        return 0

    lax.fori_loop(0, blocks, middle_back, 0)

    def expand_grad(n, _):
        c = span(n * D, D, 128)
        value = dot(h2[...], slope[:, c], TN).astype(BF)
        full2[:, :, :, c] = value.reshape(full2.shape[:3] + (D,))
        pl.when(n < last - blocks + 1)(lambda: scatter.tick(SHR, 0, n + blocks))
        pl.when(n < last - blocks + 1)(lambda: scatter.tick(SHR, 1, n + blocks))
        return 0

    lax.fori_loop(0, FF // D, expand_grad, 0)
    offer(2)
    accept(1)
    scatter.hand(EXP, 0)
    scatter.hand(EXP, 1)

    def upstream_rows(i, _):
        h2[rows(i), :] = dot(low[rows(i), :], whole(full[OUT]), NT).astype(BF)
        return 0

    lax.fori_loop(0, blocks, upstream_rows, 0)
    accept(0)
    scatter.start(EXP, 0)
    scatter.start(EXP, 1)
    full1[...] = dot(att[...], low[...], TN).astype(BF).reshape(full1.shape)
    accept(3)
    scatter.hand(OUT, 0)
    accept(2)
    scatter.start(OUT, 0)

    def backward_pair(hp, _):
        def tick(i):
            k = hp * blocks + i

            def expand():
                scatter.tick(EXP, k % 2, 1 + k // 2)

            def output():
                scatter.tick(OUT, 0, 1 + k - 2 * last)

            pl.when(k < 2 * last)(expand)
            pl.when(jnp.logical_and(k >= 2 * last, k < 3 * last))(output)

        attend_back_pair(hp, qkv, segr, segc, att, h2, lse, x1, tick)
        return 0

    lax.fori_loop(0, D // 128, backward_pair, 0)

    for w in range(2):
        c = slice(w * (3 * D // 2), (w + 1) * (3 * D // 2))
        mixing_grad[:, :, :, c] = (
            dot(h1[...], qkv[:, c], TN).astype(BF).reshape(mixing_grad.shape[:3] + (3 * D // 2,))
        )
        scatter.hand(MIX, w)
    for copy in out_copies:
        copy.wait_send() if copy is not out_copies[0] else copy.wait()

    scatter.start(MIX, 0)

    def input_back(i, _):
        d = qkv[rows(i), :]
        part, gain, shift = norm_grad(
            x[rows(i), :].astype(F32), of("g1"), dot(d, whole(full[MIX]), NT)
        )
        sent[rows(i), :] = (dy[rows(i), :] + part).astype(BF)
        add_grad("g1", gain)
        add_grad("b1", shift)
        add_grad("bq", jnp.sum(d[:, 0:D].astype(F32), axis=0, keepdims=True))
        add_grad("bv", jnp.sum(d[:, 2 * D :].astype(F32), axis=0, keepdims=True))
        pl.when(i == 0)(lambda: scatter.start(MIX, 1))
        pl.when(i > 0)(lambda: scatter.tick(MIX, 0, i))
        pl.when(i > 0)(lambda: scatter.tick(MIX, 1, i))
        return 0

    lax.fori_loop(0, blocks, input_back, 0)
    back_copies = [local(sent.at[me], back_rows.at[place.seq], row_l.at[3])]
    for k in range(1, 4):
        peer = place.seq_peer(k)
        back_copies.append(
            remote(sent.at[rows(peer[1])], back_rows.at[place.seq], row_s.at[k, 4], row_r.at[k, 4], peer)
        )
    flat = 0
    vec_out[...] = jnp.zeros_like(vec_out)
    for name, size in VEC_PLACES:
        for n in range(size // 128):
            r = flat + n
            vec_out[r // per, r % per : r % per + 1, :] = gvec[
                VEC_ROW[name] : VEC_ROW[name] + 1, n * 128 : (n + 1) * 128
            ]
        flat += size // 128
    vec_copies = []
    for k in range(1, count):
        peer = place.dp_peer(k)
        vec_copies.append(
            remote(vec_out.at[peer[0]], vec_buf.at[place.dp], vecq_s.at[k], vecq_r.at[k], peer)
        )
    vec_buf[place.dp] = vec_out[place.dp]
    for t in range(blocks, count):
        scatter.tick(MIX, 0, t)
        scatter.tick(MIX, 1, t)
    for copy in vec_copies:
        copy.wait_recv()
    vec_mine[...] = jnp.sum(vec_buf[...], axis=0)
    vec_seq[place.seq] = vec_mine[...]
    seq_copies = []
    for k in range(1, 4):
        seq_copies.append(
            remote(vec_mine, vec_seq.at[place.seq], row_s.at[k, 5], row_r.at[k, 5], place.seq_peer(k))
        )
    for w in (SHR, EXP, OUT, MIX):
        for sub in range(SUBS[w]):
            scatter.crossed(w, sub)
    for copy in seq_copies:
        copy.wait_recv()
    vec_total = jnp.sum(vec_seq[...], axis=0)
    vec_sum[...] = vec_total
    squares = jnp.sum(vec_total * vec_total, axis=0, keepdims=True)
    for w in (SHR, EXP, OUT, MIX):
        for sub in range(SUBS[w]):
            scatter.arrived(w, sub)
        for core in range(2):
            value = sums[w][core].astype(F32)
            part = jnp.sum(value * value, axis=0, keepdims=True)
            for n in range(part.shape[1] // 128):
                squares = squares + part[:, n * 128 : (n + 1) * 128]
    sq_mine[...] = jnp.broadcast_to(squares, sq_mine.shape)
    sq_buf[place.dp] = sq_mine[...]
    sq_copies = []
    for k in range(1, count):
        sq_copies.append(remote(sq_mine, sq_buf.at[place.dp], sq_s.at[k], sq_r.at[k], place.dp_peer(k)))
    for copy in sq_copies:
        copy.wait_recv()
    total = jnp.sum(jnp.sum(sq_buf[...], axis=0), axis=1, keepdims=True)
    norm_ref[...] = jnp.broadcast_to(jnp.sqrt(total), norm_ref.shape)
    for w in (MIX, OUT, EXP, SHR):
        scatter.drain(w)
    for copy in row_in[1:] + teach_in[1:] + vec_in + vec_copies + seq_copies + sq_copies:
        copy.wait_send()
    for copy in out_copies[1:]:
        copy.wait_recv()
    for copy in back_copies:
        copy.wait()


def block_call(count, inputs, teacher, segments, masters, vectors):
    rows, local_len, features = inputs.shape
    length = rows * local_len
    halves = [(2, m.shape[0] // 2, m.shape[1]) for m in masters]
    any_spec = pl.BlockSpec(memory_space=pl.ANY)
    vmem = pl.BlockSpec(memory_space=pltpu.VMEM)
    row_shape = jax.ShapeDtypeStruct(inputs.shape, BF)
    out_shape = [jax.ShapeDtypeStruct(h, BF) for h in halves]
    out_shape += [
        jax.ShapeDtypeStruct((VROWS, 128), F32),
        jax.ShapeDtypeStruct((8, 128), F32),
        row_shape,
        row_shape,
    ]

    def low(*shape):
        return pltpu.VMEM(shape, BF)

    def wide(*shape):
        return pltpu.VMEM(shape, F32)

    def dma(*shape):
        return pltpu.SemaphoreType.DMA(shape)

    shrink_half = halves[SHR][1:]
    buffers = [low(count, *h) for h in halves]
    buffers += [
        low(length, D),
        low(length, D),
        low(length, 3 * D),
        low(length, D),
        wide(length, D),
        low(length, D),
        low(length, FF),
        low(length, FF),
        wide(length, D),
        low(length, D),
        low(length, D),
        low(count, *halves[MIX]),
        low(count, *shrink_half),
        low(count - 1, *shrink_half),
    ]
    buffers += [low(*h[1:]) for h in halves] * 2
    buffers += [
        wide(16, length),
        pltpu.VMEM((rows, 8, local_len), jnp.int32),
        pltpu.VMEM((rows, 8, local_len), jnp.int32),
        wide(1, length),
        wide(length, 128),
        wide(VROWS, 128),
        wide(count, VROWS, 128),
        wide(16, FF),
        wide(16, FF),
        wide(count, VROWS, 128),
        wide(count, VROWS, 128),
        wide(VROWS, 128),
        wide(4, VROWS, 128),
        wide(8, 128),
        wide(count, 8, 128),
    ]
    sems = [dma(16)] + [dma(4, 2, count)] * 4
    sems += [dma(4, 2, count)] * 4 + [dma(4, 2)] * 4
    sems += [dma(4, 6), dma(4, 6), dma(4), dma(count), dma(count), dma(count), dma(count), dma(count), dma(count)]
    sems.append(pltpu.SemaphoreType.REGULAR((4,)))
    return pl.pallas_call(
        partial(block_kernel, count),
        out_shape=out_shape,
        in_specs=[any_spec] * 2 + [vmem] + [any_spec] * 4 + [vmem],
        out_specs=[vmem] * 6 + [any_spec] * 2,
        scratch_shapes=buffers + sems,
        compiler_params=pltpu.CompilerParams(
            collective_id=1, has_side_effects=True, vmem_limit_bytes=VMEM_BYTES
        ),
    )(inputs, teacher, segments, *masters, vectors.reshape(-1, 128))


def row_body(
    inputs,
    segments,
    teacher,
    mixing_weight,
    output_weight,
    expand_weight,
    shrink_weight,
    vectors,
    mixing_first,
    output_first,
    expand_first,
    shrink_first,
    vectors_first,
    mixing_second,
    output_second,
    expand_second,
    shrink_second,
    vectors_second,
):
    masters = (mixing_weight, output_weight, expand_weight, shrink_weight)
    results = block_call(lax.axis_size("dp"), inputs, teacher, segments, masters, vectors)
    per = vectors.shape[0] // 128
    sums = [s.reshape(m.shape).astype(F32) for s, m in zip(results[:4], masters)]
    sums.append(results[4][:per].reshape(-1))
    grad_norm = results[5][0, 0]
    clip_value = clip_level()
    factor = clip_value / jnp.maximum(grad_norm, clip_value)
    firsts = (mixing_first, output_first, expand_first, shrink_first, vectors_first)
    seconds = (mixing_second, output_second, expand_second, shrink_second, vectors_second)
    fresh = [
        adamw(master, first, second, total * factor, rate)
        for master, first, second, total, rate in zip(
            masters + (vectors,), firsts, seconds, sums, learn_rates()
        )
    ]
    return (
        results[6],
        results[7],
        grad_norm,
        *(f[0] for f in fresh),
        *(f[1] for f in fresh),
        *(f[2] for f in fresh),
    )


def whole_rows(mesh):
    return mesh.shape["seq"] == 4 and mesh.shape["dp"] == 8


def solution(mesh):
    in_specs = (
        P("dp", "seq", None),
        P("dp", "seq"),
        P("dp", "seq", None),
        P("dp", None),
        P("dp", None),
        P("dp", None),
        P("dp", None),
        P("dp"),
        P("dp", None),
        P("dp", None),
        P("dp", None),
        P("dp", None),
        P("dp"),
        P("dp", None),
        P("dp", None),
        P("dp", None),
        P("dp", None),
        P("dp"),
    )
    out_specs = (
        P("dp", "seq", None),
        P("dp", "seq", None),
        P(),
        P("dp", None),
        P("dp", None),
        P("dp", None),
        P("dp", None),
        P("dp"),
        P("dp", None),
        P("dp", None),
        P("dp", None),
        P("dp", None),
        P("dp"),
        P("dp", None),
        P("dp", None),
        P("dp", None),
        P("dp", None),
        P("dp"),
    )
    chosen = row_body if whole_rows(mesh) else body
    return jax.shard_map(chosen, mesh=mesh, in_specs=in_specs, out_specs=out_specs, check_vma=False)
```

```python
from functools import partial
import math

import jax
import jax.numpy as jnp
from jax import lax
from jax.experimental import pallas as pl
from jax.experimental.pallas import tpu as pltpu
from jax.sharding import PartitionSpec as P

D = 768
HEADS = 12
HD = 64
FF = 3072
LEN = 1024
NDOC = 8
STEP = 10


NEGATIVE = -1e30
NORM_EPS = 1e-05
BETA_ONE = 0.9
BETA_TWO = 0.999
ADAM_EPS = 1e-08
WEIGHT_DECAY = 0.01


def layer_norm(values, norm_gain, norm_shift):
    center = values - jnp.mean(values, axis=-1, keepdims=True)
    spread = jnp.mean(center * center, axis=-1, keepdims=True)
    return center * lax.rsqrt(spread + NORM_EPS) * norm_gain + norm_shift


def gelu_tanh(values):
    return jax.nn.gelu(values, approximate=True)


def split_vectors(packed):
    return jnp.split(packed, [D, 2 * D, 3 * D, 4 * D, 5 * D, 6 * D, 7 * D, 7 * D + FF])


def adamw(master, first, second, gradient, rate):
    first_new = BETA_ONE * first + (1.0 - BETA_ONE) * gradient
    second_new = BETA_TWO * second + (1.0 - BETA_TWO) * gradient * gradient
    first_hat = first_new / (1.0 - BETA_ONE**STEP)
    second_hat = second_new / (1.0 - BETA_TWO**STEP)
    updated = master - rate * (
        first_hat / (jnp.sqrt(second_hat) + ADAM_EPS) + WEIGHT_DECAY * master
    )
    return (updated, first_new, second_new)


def learn_rates():
    return (
        1.0 / math.sqrt(2 * D),
        1.0 / math.sqrt(max(1, 2 * D * NDOC // LEN)),
        1.0 / math.sqrt(D),
        1.0 / math.sqrt(FF),
        0.3,
    )


def clip_level():
    return 0.5 * math.sqrt(4 * D * D + 2 * D * FF + 8 * D + FF)


def visible(query_pos, key_pos, query_seg, key_seg):
    return (key_pos[None, :] <= query_pos[:, None]) & (key_seg[None, :] == query_seg[:, None])


def attend_rows(query_pos, key_pos, packed_args):
    queries, keys_all, values_all, query_seg, key_seg = packed_args
    scores = jnp.einsum("qhd,khd->hqk", queries, keys_all, preferred_element_type=jnp.float32)
    scores = jnp.where(visible(query_pos, key_pos, query_seg, key_seg)[None], scores, NEGATIVE)
    top_score = jnp.max(scores, axis=-1, keepdims=True)
    exponent = jnp.exp(scores - top_score)
    totals = jnp.sum(exponent, axis=-1, keepdims=True)
    probability = (exponent / totals).astype(jnp.bfloat16)
    attended = jnp.einsum(
        "hqk,khd->qhd", probability, values_all, preferred_element_type=jnp.float32
    )
    return (attended, (top_score + jnp.log(totals))[..., 0])


def attend_back(query_pos, key_pos, packed_args):
    queries, keys_all, values_all, upstream, log_totals, query_seg, key_seg = packed_args
    scores = jnp.einsum("qhd,khd->hqk", queries, keys_all, preferred_element_type=jnp.float32)
    scores = jnp.where(visible(query_pos, key_pos, query_seg, key_seg)[None], scores, NEGATIVE)
    probability = jnp.exp(scores - log_totals[..., None])
    prob_low = probability.astype(jnp.bfloat16)
    prob_grad = jnp.einsum("qhd,khd->hqk", upstream, values_all, preferred_element_type=jnp.float32)
    value_part = jnp.einsum("hqk,qhd->khd", prob_low, upstream, preferred_element_type=jnp.float32)
    score_grad = probability * (
        prob_grad - jnp.sum(probability * prob_grad, axis=-1, keepdims=True)
    )
    score_low = score_grad.astype(jnp.bfloat16)
    query_part = jnp.einsum("hqk,khd->qhd", score_low, keys_all, preferred_element_type=jnp.float32)
    key_part = jnp.einsum("hqk,qhd->khd", score_low, queries, preferred_element_type=jnp.float32)
    key_count = keys_all.shape[0]
    return (
        query_part,
        jnp.concatenate(
            [key_part.reshape(key_count, -1), value_part.reshape(key_count, -1)], axis=1
        ),
    )


def body(
    inputs,
    segments,
    teacher,
    mixing_weight,
    output_weight,
    expand_weight,
    shrink_weight,
    vectors,
    mixing_first,
    output_first,
    expand_first,
    shrink_first,
    vectors_first,
    mixing_second,
    output_second,
    expand_second,
    shrink_second,
    vectors_second,
):
    bfloat = jnp.bfloat16
    floats = jnp.float32
    seq_count, local_len, features = inputs.shape
    row_count = seq_count * local_len
    scale = 1.0 / math.sqrt(HD)
    mixing_low, output_low, expand_low, shrink_low, vectors_low = (
        lax.all_gather(mixing_weight.astype(bfloat), "dp", axis=0, tiled=True),
        lax.all_gather(output_weight.astype(bfloat), "dp", axis=0, tiled=True),
        lax.all_gather(expand_weight.astype(bfloat), "dp", axis=0, tiled=True),
        lax.all_gather(shrink_weight.astype(bfloat), "dp", axis=0, tiled=True),
        lax.all_gather(vectors.astype(bfloat), "dp", axis=0, tiled=True),
    )
    (
        gain_one,
        shift_one,
        bias_query,
        bias_value,
        bias_output,
        gain_two,
        shift_two,
        bias_expand,
        bias_shrink,
    ) = split_vectors(vectors_low.astype(floats))
    states = inputs.astype(floats).reshape(row_count, features)
    normed = layer_norm(states, gain_one, shift_one)
    normed_low = normed.astype(bfloat)
    projected = jnp.dot(normed_low, mixing_low, preferred_element_type=floats)
    query_low = ((projected[:, :features] + bias_query) * scale).astype(bfloat)
    key_low = projected[:, features : 2 * features].astype(bfloat)
    value_low = (projected[:, 2 * features :] + bias_value).astype(bfloat)
    key_all, value_all = (
        lax.all_gather(key_low.reshape(seq_count, local_len, features), "seq", axis=1, tiled=True),
        lax.all_gather(
            value_low.reshape(seq_count, local_len, features), "seq", axis=1, tiled=True
        ),
    )
    segment_all = lax.all_gather(segments, "seq", axis=1, tiled=True)
    full_len = key_all.shape[1]
    query_pos = lax.axis_index("seq") * local_len + jnp.arange(local_len, dtype=jnp.int32)
    key_pos = jnp.arange(full_len, dtype=jnp.int32)
    query_heads = query_low.reshape(seq_count, local_len, HEADS, HD)
    key_heads = key_all.reshape(seq_count, full_len, HEADS, HD)
    value_heads = value_all.reshape(seq_count, full_len, HEADS, HD)
    attended, log_totals = lax.map(
        partial(attend_rows, query_pos, key_pos),
        (query_heads, key_heads, value_heads, segments, segment_all),
    )
    attended_low = attended.reshape(row_count, features).astype(bfloat)
    middle = states + jnp.dot(attended_low, output_low, preferred_element_type=floats) + bias_output
    normed_two = layer_norm(middle, gain_two, shift_two)
    normed_two_low = normed_two.astype(bfloat)
    hidden = jnp.dot(normed_two_low, expand_low, preferred_element_type=floats) + bias_expand
    active, gelu_back = jax.vjp(gelu_tanh, hidden)
    active_low = active.astype(bfloat)
    result = middle + jnp.dot(active_low, shrink_low, preferred_element_type=floats) + bias_shrink
    block_output = result.astype(bfloat).reshape(seq_count, local_len, features)
    target_prob = jax.nn.softmax(teacher.astype(floats).reshape(row_count, features), axis=-1)
    result_grad = features * (jax.nn.softmax(result, axis=-1) - target_prob)
    result_low = result_grad.astype(bfloat)
    grad_shrink = jnp.dot(active_low.T, result_low, preferred_element_type=floats)
    grad_bias_shrink = jnp.sum(result_grad, axis=0)
    active_grad = jnp.dot(result_low, shrink_low.T, preferred_element_type=floats)
    active_round = lax.optimization_barrier(active_grad.astype(bfloat)).astype(floats)
    hidden_low = gelu_back(active_round)[0].astype(bfloat)
    grad_bias_expand = jnp.sum(hidden_low.astype(floats), axis=0)
    grad_expand = jnp.dot(normed_two_low.T, hidden_low, preferred_element_type=floats)
    normed_two_grad = jnp.dot(hidden_low, expand_low.T, preferred_element_type=floats)
    norm_two_back = jax.vjp(layer_norm, middle, gain_two, shift_two)[1]
    middle_part, grad_gain_two, grad_shift_two = norm_two_back(normed_two_grad)
    middle_grad = result_grad + middle_part
    middle_low = middle_grad.astype(bfloat)
    grad_bias_output = jnp.sum(middle_grad, axis=0)
    grad_output = jnp.dot(attended_low.T, middle_low, preferred_element_type=floats)
    attended_grad = jnp.dot(middle_low, output_low.T, preferred_element_type=floats).astype(bfloat)
    upstream_heads = attended_grad.reshape(seq_count, local_len, HEADS, HD)
    query_grad, kv_terms = lax.map(
        partial(attend_back, query_pos, key_pos),
        (query_heads, key_heads, value_heads, upstream_heads, log_totals, segments, segment_all),
    )
    kv_sums = (
        lax.psum_scatter(kv_terms.astype(jnp.bfloat16), "seq", scatter_dimension=1, tiled=True)
        .astype(jnp.float32)
        .reshape(row_count, 2 * features)
    )
    key_grad_low = kv_sums[:, :features].astype(bfloat)
    value_grad_low = kv_sums[:, features:].astype(bfloat)
    query_grad_low = query_grad.reshape(row_count, features).astype(bfloat)
    query_scaled = query_grad_low.astype(floats) * scale
    grad_bias_query = jnp.sum(query_scaled, axis=0)
    grad_bias_value = jnp.sum(value_grad_low.astype(floats), axis=0)
    projected_grad = jnp.concatenate(
        [query_scaled.astype(bfloat), key_grad_low, value_grad_low], axis=1
    )
    grad_mixing = jnp.dot(normed_low.T, projected_grad, preferred_element_type=floats)
    normed_grad = jnp.dot(projected_grad, mixing_low.T, preferred_element_type=floats)
    norm_one_back = jax.vjp(layer_norm, states, gain_one, shift_one)[1]
    states_part, grad_gain_one, grad_shift_one = norm_one_back(normed_grad)
    input_grad = (middle_grad + states_part).astype(bfloat).reshape(seq_count, local_len, features)
    grad_vectors = jnp.concatenate(
        [
            grad_gain_one,
            grad_shift_one,
            grad_bias_query,
            grad_bias_value,
            grad_bias_output,
            grad_gain_two,
            grad_shift_two,
            grad_bias_expand,
            grad_bias_shrink,
        ]
    )
    vector_rows = grad_vectors.reshape(lax.axis_size("dp"), -1)
    mixing_part, output_part, expand_part, shrink_part, vector_part = (
        lax.psum_scatter(
            grad_mixing.astype(jnp.bfloat16), "dp", scatter_dimension=0, tiled=True
        ).astype(jnp.float32),
        lax.psum_scatter(
            grad_output.astype(jnp.bfloat16), "dp", scatter_dimension=0, tiled=True
        ).astype(jnp.float32),
        lax.psum_scatter(
            grad_expand.astype(jnp.bfloat16), "dp", scatter_dimension=0, tiled=True
        ).astype(jnp.float32),
        lax.psum_scatter(
            grad_shrink.astype(jnp.bfloat16), "dp", scatter_dimension=0, tiled=True
        ).astype(jnp.float32),
        lax.psum_scatter(
            vector_rows.astype(jnp.bfloat16), "dp", scatter_dimension=0, tiled=True
        ).astype(jnp.float32),
    )
    mixing_sum, output_sum, expand_sum, shrink_sum, vector_sum = (
        lax.psum(mixing_part.astype(jnp.bfloat16), "seq").astype(jnp.float32),
        lax.psum(output_part.astype(jnp.bfloat16), "seq").astype(jnp.float32),
        lax.psum(expand_part.astype(jnp.bfloat16), "seq").astype(jnp.float32),
        lax.psum(shrink_part.astype(jnp.bfloat16), "seq").astype(jnp.float32),
        lax.psum(vector_part.astype(jnp.bfloat16), "seq").astype(jnp.float32),
    )
    vector_sum = vector_sum.reshape(-1)
    squares = (
        jnp.sum(mixing_sum * mixing_sum)
        + jnp.sum(output_sum * output_sum)
        + jnp.sum(expand_sum * expand_sum)
        + jnp.sum(shrink_sum * shrink_sum)
        + jnp.sum(vector_sum * vector_sum)
    )
    grad_norm = jnp.sqrt(lax.psum(squares, "dp"))
    clip_value = clip_level()
    factor = clip_value / jnp.maximum(grad_norm, clip_value)
    step_rates = learn_rates()
    mixing_new = adamw(
        mixing_weight, mixing_first, mixing_second, mixing_sum * factor, step_rates[0]
    )
    output_new = adamw(
        output_weight, output_first, output_second, output_sum * factor, step_rates[1]
    )
    expand_new = adamw(
        expand_weight, expand_first, expand_second, expand_sum * factor, step_rates[2]
    )
    shrink_new = adamw(
        shrink_weight, shrink_first, shrink_second, shrink_sum * factor, step_rates[3]
    )
    vectors_new = adamw(vectors, vectors_first, vectors_second, vector_sum * factor, step_rates[4])
    return (
        block_output,
        input_grad,
        grad_norm,
        mixing_new[0],
        output_new[0],
        expand_new[0],
        shrink_new[0],
        vectors_new[0],
        mixing_new[1],
        output_new[1],
        expand_new[1],
        shrink_new[1],
        vectors_new[1],
        mixing_new[2],
        output_new[2],
        expand_new[2],
        shrink_new[2],
        vectors_new[2],
    )

MESH = pl.DeviceIdType.MESH
BF = jnp.bfloat16
F32 = jnp.float32
BLK = 256
NN = ((1,), (0,))
NT = ((1,), (1,))
TN = ((0,), (0,))
VMEM_BYTES = 64 * 2**20 - 2**17
VROWS = 16
MIX, OUT, EXP, SHR = 0, 1, 2, 3
HALF = D // 2
MARKS = {(0, 0): 0, (1, 0): 1, (2, 0): 2, (3, 0): 3}
SUBS = (2, 1, 2, 2)


def dot(left, right, dims):
    return lax.dot_general(left, right, (dims, ((), ())), preferred_element_type=F32)


class Place:
    def __init__(self, count):
        self.count = count
        self.hops = (count // 2, count - 1 - count // 2)
        self.dp = lax.axis_index("dp")
        self.seq = lax.axis_index("seq")
        odd = self.dp % 2
        self.pos = (1 - odd) * (self.dp // 2) + odd * (count - 1 - self.dp // 2)
        self.core = self.seq % 2
        self.x = self.seq // 2
        self.step = 1 - 2 * self.core
        self.sides = ((self.ahead(1), self.seq), (self.behind(1), self.seq))
        self.mate = self.kin(1)
        self.across = self.kin(2)

    def at(self, pos):
        pos = pos % self.count
        upper = pos // (self.count // 2)
        return (1 - upper) * (2 * pos) + upper * (2 * (self.count - 1 - pos) + 1)

    def ahead(self, steps):
        return self.at(self.pos + steps * self.step + self.count)

    def behind(self, steps):
        return self.at(self.pos - steps * self.step + self.count)

    def kin(self, which):
        core = self.core + (1 - 2 * self.core) * (which % 2)
        return (self.dp, 2 * (self.x + (1 - 2 * self.x) * (which // 2)) + core)

    def dp_peer(self, offset):
        return ((self.dp + offset) % self.count, self.seq)

    def greet(self):
        barrier = pltpu.get_barrier_semaphore()
        peers = [self.kin(k) for k in range(1, 4)]
        peers += [self.dp_peer(k) for k in range(1, self.count)]
        for peer in peers:
            pl.semaphore_signal(barrier, inc=1, device_id=peer, device_id_type=MESH)
        return lambda: pl.semaphore_wait(barrier, len(peers))


def describe(src, dst, send, recv, device):
    return pltpu.make_async_remote_copy(
        src_ref=src,
        dst_ref=dst,
        send_sem=send,
        recv_sem=recv,
        device_id=device,
        device_id_type=MESH,
    )


def remote(src, dst, send, recv, device):
    copy = describe(src, dst, send, recv, device)
    copy.start()
    return copy


def local(src, dst, sem):
    copy = pltpu.make_async_copy(src, dst, sem)
    copy.start()
    return copy


def span(start, size, unit):
    return pl.ds(start if isinstance(start, int) else pl.multiple_of(start, unit), size)


def spread(ticks, trips, marks):
    places = trips * marks

    def at(trip, mark):
        for n in range(trips):
            here = [
                tick
                for k, tick in enumerate(ticks)
                if k * places // max(len(ticks), 1) == n * marks + mark and tick is not None
            ]

            def run(here=here):
                for tick in here:
                    tick()

            if here:
                pl.when(trip == n)(run)

    return at


class Group:
    def __init__(self, send, recv, of_all_sent, of_all_received, device):
        self.send, self.recv, self.device = send, recv, device
        self.bytes = (of_all_sent, of_all_received)

    def start(self, src, dst, device):
        describe(src, dst, self.send, self.recv, device).start()

    def all(self, which):
        return describe(self.bytes[which], self.bytes[which], self.send, self.recv, self.device)

    def wait_recv(self):
        self.all(1).wait_recv()

    def wait_send(self):
        self.all(0).wait_send()


class Gather:
    def __init__(self, place, full, sems):
        self.place, self.full = place, full
        self.ring_s, self.ring_r, self.mate_s, self.mate_r, self.cross_s, self.cross_r = sems

    def lanes(self, w):
        return (0, 1) if w == MIX else (0,) if w == OUT else (self.place.x, 2)

    def part(self, ref, w, sub):
        rows, columns = ref.shape[-2:]
        lead = (slice(None),) * (len(ref.shape) - 2)
        last = isinstance(sub, int) and sub == 2
        if w == SHR:
            unit = rows // 6
            return ref.at[lead + (span(sub * unit, 4 * unit if last else unit, 16),)]
        unit = columns // (2, 1, 3)[w]
        return ref.at[lead + (slice(None), span(sub * unit, unit, 128))]

    def cut(self, w, owner, core, sub):
        return self.part(self.full[w].at[owner, core], w, sub)

    def block(self, w, sub, way, t):
        owner = self.place.ahead(t) if way else self.place.behind(t)
        return self.cut(w, owner, self.place.core, sub)

    def copy(self, block, send, recv, device):
        return describe(block, block, send, recv, device)

    def ring(self, w, lane, way, t):
        index = (w, lane, t + way * self.place.hops[0])
        block = self.block(w, self.lanes(w)[lane], way, t)
        return self.copy(block, self.ring_s.at[w], self.ring_r.at[index], self.place.sides[way])

    def pair(self, w, sub, way, t):
        block = self.block(w, sub, way, t)
        return self.copy(block, self.mate_s.at[w], self.mate_r.at[w], self.place.mate)

    def over(self, w, way, t):
        recv = self.cross_r.at[w - EXP, t - 1 + way * self.place.hops[0]]
        block = self.block(w, self.place.x, way, t)
        return self.copy(block, self.cross_s.at[w - EXP], recv, self.place.across)

    def start(self, w):
        for lane in range(len(self.lanes(w))):
            for way in range(2):
                self.ring(w, lane, way, 0).start()

    def tick(self, w, lane, way, t):
        self.ring(w, lane, way, t - 1).wait_recv()
        if t < self.place.hops[way]:
            self.ring(w, lane, way, t).start()
        self.pair(w, self.lanes(w)[lane], way, t).start()
        if w >= EXP and lane == 0:
            self.over(w, way, t).start()

    def relay(self, w, way, t):
        self.over(w, way, t).wait_recv()
        self.pair(w, 1 - self.place.x, way, t).start()

    def others(self, w):
        return self.full[w].at[pl.ds(0, self.place.count - 1), self.place.core]

    def arrived(self, w):
        block = self.others(w)
        self.copy(block, self.mate_s.at[w], self.mate_r.at[w], self.place.mate).wait_recv()

    def drain(self, w):
        block = self.others(w)
        self.copy(block, self.mate_s.at[w], self.mate_r.at[w], self.place.mate).wait_send()
        if w >= EXP:
            for lane in range(2):
                part = self.part(block, w, self.lanes(w)[lane])
                self.copy(part, self.ring_s.at[w], self.mate_r.at[w], self.place.mate).wait_send()
            part = self.part(block, w, 0)
            self.copy(part, self.cross_s.at[w - EXP], self.mate_r.at[w], self.place.across).wait_send()
        else:
            self.copy(block, self.ring_s.at[w], self.mate_r.at[w], self.place.mate).wait_send()


class Scatter:
    def __init__(self, place, grads, mates, slots, cross, sums, sems):
        self.place, self.grads, self.mates, self.slots = place, grads, mates, slots
        self.cross_mine, self.cross_in = cross
        self.sums = sums
        (
            self.mate_s,
            self.mate_r,
            self.ring_s,
            self.ring_r,
            self.cross_s,
            self.cross_r,
            self.total_s,
            self.total_r,
        ) = sems

    def cut(self, ref, w, sub):
        rows, columns = ref.shape[-2:]
        lead = (slice(None),) * (len(ref.shape) - 2)
        if w == SHR:
            return ref.at[lead + (span(sub * (rows // 2), rows // 2, 16),)]
        size = columns // SUBS[w]
        return ref.at[lead + (slice(None), span(sub * size, size, 128))]

    def owner(self, way, distance):
        return self.place.behind(distance) if way else self.place.ahead(distance)

    def own(self, w, owner, core, sub):
        return self.cut(self.grads[w].at[owner, core], w, sub)

    def slot(self, w, way, t, sub):
        return self.cut(self.slots(w, t + way * self.place.hops[0]), w, sub)

    def pair(self, w, sub, owner):
        return describe(
            self.own(w, owner, 1 - self.place.core, sub),
            self.cut(self.mates(w, owner), w, sub),
            self.mate_s.at[w, sub],
            self.mate_r.at[w, sub],
            self.place.mate,
        )

    def pairs(self, w, sub):
        block = self.cut(self.grads[w].at[:, self.place.core], w, sub)
        return describe(
            block, block, self.mate_s.at[w, sub], self.mate_r.at[w, sub], self.place.mate
        )

    def ring(self, w, sub, way, t):
        if t == 0:
            owner = self.owner(way, self.place.hops[way])
            src = self.own(w, owner, self.place.core, sub)
        else:
            src = self.slot(w, way, t - 1, sub)
        index = (w, sub, t + way * self.place.hops[0])
        return describe(
            src,
            self.slot(w, way, t, sub),
            self.ring_s.at[w, sub],
            self.ring_r.at[index],
            self.place.sides[way],
        )

    def over(self, w, sub):
        return describe(
            self.cut(self.cross_mine[w], w, sub),
            self.cut(self.cross_in[w], w, sub),
            self.cross_s.at[w, sub],
            self.cross_r.at[w, sub],
            self.place.across,
        )

    def total(self, w, sub):
        block = self.cut(self.sums[w].at[self.place.core], w, sub)
        return describe(
            block, block, self.total_s.at[w, sub], self.total_r.at[w, sub], self.place.mate
        )

    def hand(self, w, sub):
        for owner in range(self.place.count):
            self.pair(w, sub, owner).start()

    def term(self, w, sub, way, distance):
        owner = self.owner(way, distance)
        mine = self.own(w, owner, self.place.core, sub)[...].astype(F32)
        return mine + self.cut(self.mates(w, owner), w, sub)[...].astype(F32)

    def start(self, w, sub):
        self.pairs(w, sub).wait_recv()
        for way, hops in enumerate(self.place.hops):
            term = self.term(w, sub, way, hops)
            self.own(w, self.owner(way, hops), self.place.core, sub)[...] = term.astype(BF)
            self.ring(w, sub, way, 0).start()

    def tick(self, w, sub, way, t):
        self.ring(w, sub, way, t - 1).wait_recv()
        slot = self.slot(w, way, t - 1, sub)
        term = self.term(w, sub, way, self.place.hops[way] - t)
        slot[...] = (slot[...].astype(F32) + term).astype(BF)
        self.ring(w, sub, way, t).start()

    def finish(self, w, sub):
        total = self.term(w, sub, 0, 0)
        for way, hops in enumerate(self.place.hops):
            self.ring(w, sub, way, hops - 1).wait_recv()
            total = total + self.slot(w, way, hops - 1, sub)[...].astype(F32)
        self.cut(self.cross_mine[w], w, sub)[...] = total.astype(BF)
        self.over(w, sub).start()

    def crossed(self, w, sub):
        self.over(w, sub).wait_recv()
        value = self.cut(self.cross_mine[w], w, sub)[...].astype(F32)
        value = value + self.cut(self.cross_in[w], w, sub)[...].astype(F32)
        self.cut(self.sums[w].at[self.place.core], w, sub)[...] = value.astype(BF)
        self.total(w, sub).start()

    def arrived(self, w, sub):
        self.total(w, sub).wait_recv()

    def drain(self, w):
        for sub in range(SUBS[w]):
            self.pairs(w, sub).wait_send()
            sent = self.cut(self.grads[w].at[pl.ds(0, self.place.count - 1), self.place.core], w, sub)
            describe(
                sent, sent, self.ring_s.at[w, sub], self.mate_r.at[w, sub], self.place.mate
            ).wait_send()
            self.over(w, sub).wait_send()
            self.total(w, sub).wait_send()

    def ticks(self, w, t, subs):
        return [
            partial(self.tick, w, sub, way, t)
            for sub in subs
            for way, hops in enumerate(self.place.hops)
            if t < hops
        ]


def seen(sk, sq, diagonal):
    vis = jnp.concatenate([sk] * (BLK // 128), axis=1) == sq
    if diagonal:
        vis = vis & (
            lax.broadcasted_iota(jnp.int32, (BLK, BLK), 0)
            <= lax.broadcasted_iota(jnp.int32, (BLK, BLK), 1)
        )
    return vis


def columns_of(hp):
    first = (hp // 3) * (3 * HALF) + (hp % 3) * 128
    return [span(first + part * HALF, 128, 128) for part in range(3)]


def attend_pair(hp, qkv, segr, segc, out, lse, scores, tick):
    lane = lax.broadcasted_iota(jnp.int32, (1, 128), 1)
    cq, ck, cv = columns_of(hp)
    vt = qkv[:, cv].T
    for i in range(qkv.shape[0] // BLK):
        rq = slice(i * BLK, (i + 1) * BLK)
        qb = qkv[rq, cq]
        sq = segr[0:1, rq]
        outs = []
        for hd in range(2):
            tick(i, hd)
            kept = slice(hd * BLK, (hd + 1) * BLK)
            qm = jnp.where((lane < 64) if hd == 0 else (lane >= 64), qb, jnp.zeros_like(qb))
            top = None
            for j in range(i + 1):
                rk = slice(j * BLK, (j + 1) * BLK)
                s = jnp.where(seen(segc[rk, :], sq, i == j), dot(qkv[rk, ck], qm, NT), NEGATIVE)
                scores[rk, kept] = s
                best = jnp.max(s, axis=0, keepdims=True)
                top = best if top is None else jnp.maximum(top, best)
            total = acc = None
            for j in range(i + 1):
                rk = slice(j * BLK, (j + 1) * BLK)
                p = jnp.exp(scores[rk, kept] - top)
                part = jnp.sum(p, axis=0, keepdims=True)
                total = part if total is None else total + part
                term = dot(vt[hd * 64 : (hd + 1) * 64, rk], p.astype(BF), NN)
                acc = term if acc is None else acc + term
            outs.append(acc * (1.0 / total))
            lse[pl.ds(hp * 2 + hd, 1), rq] = top + jnp.log(total)
        out[rq, span(hp * 128, 128, 128)] = jnp.concatenate(outs, axis=0).T.astype(BF)


def attend_back_pair(hp, qkv, segr, segc, out, upstream, lse, sums, tick):
    lane = lax.broadcasted_iota(jnp.int32, (1, 128), 1)
    cq, ck, cv = columns_of(hp)
    co = span(hp * 128, 128, 128)
    in_v, in_k = slice(0, 128), slice(128, 256)
    kt = qkv[:, ck].T
    for i in range(qkv.shape[0] // BLK):
        rq = slice(i * BLK, (i + 1) * BLK)
        qb = qkv[rq, cq]
        db = upstream[rq, co]
        prod = (db.astype(F32) * out[rq, co].astype(F32)).T
        sq = segr[0:1, rq]
        dqs = []
        for hd in range(2):
            tick(i, hd)
            half = (lane < 64) if hd == 0 else (lane >= 64)
            qm = jnp.where(half, qb, jnp.zeros_like(qb))
            dm = jnp.where(half, db, jnp.zeros_like(db))
            delta = jnp.sum(prod[hd * 64 : (hd + 1) * 64, :], axis=0, keepdims=True)
            ls = lse[pl.ds(hp * 2 + hd, 1), rq]
            dq = None
            for j in range(i + 1):
                rk = slice(j * BLK, (j + 1) * BLK)
                s = jnp.where(seen(segc[rk, :], sq, i == j), dot(qkv[rk, ck], qm, NT), NEGATIVE)
                p = jnp.exp(s - ls)
                ds = (p * (dot(qkv[rk, cv], dm, NT) - delta)).astype(BF)
                pv = dot(p.astype(BF), dm, NN)
                pk = dot(ds, qm, NN)
                if i == j and hd == 0:
                    sums[rk, in_v] = pv
                    sums[rk, in_k] = pk
                else:
                    sums[rk, in_v] += pv
                    sums[rk, in_k] += pk
                term = dot(kt[hd * 64 : (hd + 1) * 64, rk], ds, NN)
                dq = term if dq is None else dq + term
            dqs.append(dq)
        low = jnp.concatenate(dqs, axis=0).T.astype(BF).astype(F32)
        qkv[rq, cq] = (low * (1.0 / math.sqrt(HD))).astype(BF)
    qkv[:, ck] = sums[:, in_k].astype(BF)
    qkv[:, cv] = sums[:, in_v].astype(BF)


def normalised(values):
    center = values - jnp.mean(values, axis=-1, keepdims=True)
    inverse = lax.rsqrt(jnp.mean(center * center, axis=-1, keepdims=True) + NORM_EPS)
    return center * inverse, inverse


def norm_grad(values, gain, upstream):
    hat, inverse = normalised(values)
    scaled = upstream * gain
    first = jnp.mean(scaled, axis=-1, keepdims=True)
    second = jnp.mean(scaled * hat, axis=-1, keepdims=True)
    return (
        inverse * (scaled - first - hat * second),
        jnp.sum(upstream * hat, axis=0, keepdims=True),
        jnp.sum(upstream, axis=0, keepdims=True),
    )


def gelu_both(u):
    slope = math.sqrt(2.0 / math.pi)
    square = u * u
    th = jnp.tanh(slope * u * (1.0 + 0.044715 * square))
    half = 0.5 * (1.0 + th)
    return u * half, half + 0.5 * u * (1.0 - th * th) * (slope * (1.0 + 3.0 * 0.044715 * square))


def softmax(values):
    e = jnp.exp(values - jnp.max(values, axis=-1, keepdims=True))
    return e * (1.0 / jnp.sum(e, axis=-1, keepdims=True))


def whole(ref):
    return ref[...].reshape(-1, ref.shape[-1])


VEC_PLACES = (("g1", D), ("b1", D), ("bq", D), ("bv", D), ("bo", D), ("g2", D), ("b2", D), ("bf1", FF), ("bf2", D))
VEC_ROW = {name: row for row, (name, _) in enumerate(VEC_PLACES)}
VEC_SIZE = dict(VEC_PLACES)


def block_kernel(count, *refs):
    inputs, teacher, segments, masters, vec_ref = refs[0], refs[1], refs[2], refs[3:7], refs[7]
    sums, vec_sum, norm_ref, out_rows, back_rows = refs[8:12], refs[12], refs[13], refs[14], refs[15]
    (
        full0, full1, full2, full3, x, h1, qkv, att, x1, h2, act, slope, dy, low, sent, mixing_grad,
        shr_mate, shr_slot, cm0, cm1, cm2, cm3, ci0, ci1, ci2, ci3, lse, segs, seg_stage, segr, segc,
        vec_stage, vec_all, vec, gvec, vec_out, vec_buf, vec_mine, vec_seq, sq_mine, sq_buf,
        load_sem, g_ring_s, g_ring_r, g_mate_s, g_mate_r, g_cross_s, g_cross_r,
        s_mate_s, s_mate_r, s_ring_s, s_ring_r, s_cross_s, s_cross_r, s_total_s, s_total_r,
        row_s, row_r, row_l, vec_s, vec_r, free,
    ) = refs[16:]
    full = (full0, full1, full2, full3)
    place = Place(count)
    ready = place.greet()
    length = x.shape[0]
    blocks = length // BLK
    pairs = D // 128
    scale = 1.0 / math.sqrt(HD)

    def rows(i):
        return span(i * BLK, BLK, BLK)

    loads, pieces, used = [], [], [0, 0]
    for w in (MIX, OUT, EXP, SHR):
        height, width = masters[w].shape
        for column in range(0, width, D):
            which = 0 if used[0] + height <= length else 1
            where = (dy, x1)[which].at[pl.ds(used[which], height)]
            used[which] += height
            source = masters[w].at[:, pl.ds(column, D)]
            loads.append(local(source, where, load_sem.at[len(loads)]))
            pieces.append((w, column, where))

    def stage(w):
        for load, (owner, column, where) in zip(loads, pieces):
            if owner == w:
                load.wait()
                piece = where[...].astype(BF).reshape(full[w].shape[1:3] + (D,))
                if w == MIX:
                    for part in range(2):
                        c = slice(part * HALF, (part + 1) * HALF)
                        there = pl.ds(part * 3 * HALF + column // 2, HALF)
                        full[w][place.dp, :, :, there] = piece[:, :, c]
                else:
                    full[w][place.dp, :, :, pl.ds(column, D)] = piece

    gather = Gather(place, full, (g_ring_s, g_ring_r, g_mate_s, g_mate_r, g_cross_s, g_cross_r))
    stage(MIX)
    ready()
    gather.start(MIX)

    me = rows(place.seq)
    three, seven = pl.ds(0, 3), pl.ds(0, count - 1)
    most = pl.ds(0, 3 * BLK)

    def group(n, sent, received):
        return Group(row_s.at[n], row_r.at[n], sent, received, place.mate)

    row_in = group(0, inputs.at[three], x.at[most])
    seg_in = group(1, seg_stage.at[three], segs.at[three])
    teach_in = group(2, teacher.at[three], low.at[most])
    out_go = group(3, out_rows.at[three], out_rows.at[three])
    back_go = group(4, back_rows.at[three], back_rows.at[three])
    seq_go = group(5, vec_seq.at[three], vec_seq.at[three])
    vec_in = Group(vec_s.at[0], vec_r.at[0], vec_all.at[seven], vec_all.at[seven], place.mate)
    vec_go = Group(vec_s.at[1], vec_r.at[1], vec_buf.at[seven], vec_buf.at[seven], place.mate)
    sq_go = Group(vec_s.at[2], vec_r.at[2], sq_buf.at[seven], sq_buf.at[seven], place.mate)
    for k in (2, 3, 1):
        peer = place.kin(k)
        row_in.start(inputs.at[peer[1]], x.at[me], peer)
    row_local = local(inputs.at[place.seq], x.at[me], row_l.at[0])
    seg_stage[...] = jnp.broadcast_to(segments[...][:, None, :], seg_stage.shape)
    vec_stage[...] = jnp.concatenate(
        [vec_ref[...].astype(BF).astype(F32), jnp.zeros((VROWS - vec_ref.shape[0], 128), F32)],
        axis=0,
    )
    for k in range(1, count):
        vec_in.start(vec_stage, vec_all.at[place.dp], place.dp_peer(k))
    for k in (2, 3, 1):
        peer = place.kin(k)
        seg_in.start(seg_stage.at[peer[1]], segs.at[place.seq], peer)
    for k in (2, 3, 1):
        peer = place.kin(k)
        teach_in.start(teacher.at[peer[1]], low.at[me], peer)
    segs[place.seq] = seg_stage[place.seq]
    vec_all[place.dp] = vec_stage[...]
    teach_local = local(teacher.at[place.seq], low.at[me], row_l.at[1])
    for w in (OUT, EXP, SHR):
        stage(w)

    def ring_steps(w, t):
        return [
            partial(gather.tick, w, lane, way, t)
            for lane in range(len(gather.lanes(w)))
            for way in range(2)
            if t <= place.hops[way]
        ]

    def relays(w, t):
        return [partial(gather.relay, w, way, t) for way in range(2) if 1 <= t <= place.hops[way]]

    far = place.hops[0]
    for t in range(1, far + 1):
        for step in ring_steps(MIX, t):
            step()
        if t == far - 1:
            gather.start(OUT)
            gather.start(EXP)

    vec_in.wait_recv()
    per = vec_ref.shape[0]
    flat = 0
    for name, size in VEC_PLACES:
        parts = []
        for r in range(flat, flat + size // 128):
            parts.append(vec_all[r // per, r % per : r % per + 1, :])
        vec[VEC_ROW[name] : VEC_ROW[name] + 1, 0:size] = jnp.concatenate(parts, axis=1)
        flat += size // 128

    def of(name):
        return vec[VEC_ROW[name] : VEC_ROW[name] + 1, 0 : VEC_SIZE[name]]

    def add_grad(name, term, start=0):
        gvec[VEC_ROW[name] : VEC_ROW[name] + 1, start : start + term.shape[1]] += term

    gvec[...] = jnp.zeros_like(gvec)
    row_local.wait()
    row_in.wait_recv()
    seg_in.wait_recv()

    segr[...] = jnp.concatenate([segs[s, 0:1, :] for s in range(4)], axis=1).astype(F32)
    for s in range(4):
        segc[s * BLK : (s + 1) * BLK, :] = jnp.concatenate([segs[s].astype(F32)] * 16, axis=0).T

    def first_norm(i, _):
        hat, _ = normalised(x[rows(i), :].astype(F32))
        h1[rows(i), :] = (hat * of("g1") + of("b1")).astype(BF)
        return 0

    lax.fori_loop(0, blocks, first_norm, 0)
    gather.arrived(MIX)

    steps = []
    for t in range(1, far + 1):
        steps += ring_steps(OUT, t) + ring_steps(EXP, t)
        if t == far - 1:
            steps.append(partial(gather.start, SHR))
    steps += ring_steps(SHR, 1) + relays(EXP, 1) + relays(EXP, 2)
    steps += ring_steps(SHR, 2) + relays(EXP, 3) + relays(EXP, 4)
    before_expand = len(steps)
    for t in range(3, far + 1):
        steps += ring_steps(SHR, t)
    for t in range(1, far + 1):
        steps += relays(SHR, t)
    after_expand = len(steps) - before_expand

    def take(trips, marks, most=None):
        most = trips * marks if most is None else most
        taken, steps[:] = steps[:most], steps[most:]
        return spread(taken, trips, marks)

    in_project = take(blocks, 2)

    def project(i, _):
        in_project(i, 0)
        value = dot(h1[rows(i), :], whole(full[MIX]), NN)
        for part in range(2):
            c = slice(part * HALF, (part + 1) * HALF)
            q, k, v = (
                slice(part * 3 * HALF + n * HALF, part * 3 * HALF + (n + 1) * HALF) for n in range(3)
            )
            qkv[rows(i), q] = ((value[:, q] + of("bq")[:, c]) * scale).astype(BF)
            qkv[rows(i), k] = value[:, k].astype(BF)
            qkv[rows(i), v] = (value[:, v] + of("bv")[:, c]).astype(BF)
        in_project(i, 1)
        return 0

    lax.fori_loop(0, blocks, project, 0)
    in_forward = take(pairs, len(MARKS))

    def forward_pair(hp, _):
        def tick(i, hd):
            if (i, hd) in MARKS:
                in_forward(hp, MARKS[i, hd])

        attend_pair(hp, qkv, segr, segc, att, lse, dy, tick)
        return 0

    lax.fori_loop(0, pairs, forward_pair, 0)
    in_middle = take(blocks, 1, len(steps) - after_expand)

    def middle(i, _):
        value = x[rows(i), :].astype(F32) + dot(att[rows(i), :], whole(full[OUT]), NN) + of("bo")
        x1[rows(i), :] = value
        hat, _ = normalised(value)
        h2[rows(i), :] = (hat * of("g2") + of("b2")).astype(BF)
        in_middle(i, 0)
        return 0

    gather.arrived(OUT)
    lax.fori_loop(0, blocks, middle, 0)
    gather.arrived(EXP)
    in_expand = take(blocks, 2, len(steps))

    def expand(i, _):
        for n in range(FF // D):
            c = slice(n * D, (n + 1) * D)
            weight = full[EXP][:, :, :, c].reshape(D, D)
            u = dot(h2[rows(i), :], weight, NN) + vec[VEC_ROW["bf1"] : VEC_ROW["bf1"] + 1, c]
            a, s = gelu_both(u)
            act[rows(i), c] = a.astype(BF)
            slope[rows(i), c] = s.astype(BF)
            if n % 2:
                in_expand(i, n // 2)
        return 0

    lax.fori_loop(0, blocks, expand, 0)
    gather.arrived(SHR)
    teach_local.wait()
    teach_in.wait_recv()

    def shrink(i, _):
        value = x1[rows(i), :] + dot(act[rows(i), :], whole(full[SHR]), NN) + of("bf2")
        sent[rows(i), :] = value.astype(BF)
        grad = D * (softmax(value) - softmax(low[rows(i), :].astype(F32)))
        dy[rows(i), :] = grad
        low[rows(i), :] = grad.astype(BF)
        add_grad("bf2", jnp.sum(grad, axis=0, keepdims=True))
        return 0

    lax.fori_loop(0, blocks, shrink, 0)
    for w in (MIX, OUT, EXP, SHR):
        gather.drain(w)

    def send_rows(rows_out, copies, k):
        peer = place.kin(k)
        copies.start(sent.at[rows(peer[1])], rows_out.at[place.seq], peer)

    out_local = local(sent.at[me], out_rows.at[place.seq], row_l.at[2])
    for k in (2, 3, 1):
        send_rows(out_rows, out_go, k)

    half = full[MIX].shape[2]

    def part_of(buffer, w, where):
        if w == EXP:
            return act.at[where]
        return slope.at[where, pl.ds(0, 3 * D)] if w == MIX else slope.at[where, pl.ds(3 * D, D)]

    def mates(w, owner):
        if w == SHR:
            return shr_mate.at[owner]
        return part_of(act, w, span(owner * half, half, 16))

    def slots(w, t):
        if w == SHR:
            return shr_slot.at[t]
        return part_of(act, w, span((count + t) * half, half, 16))

    scatter = Scatter(
        place,
        (mixing_grad, full1, full2, full3),
        mates,
        slots,
        ((cm0, cm1, cm2, cm3), (ci0, ci1, ci2, ci3)),
        sums,
        (s_mate_s, s_mate_r, s_ring_s, s_ring_r, s_cross_s, s_cross_r, s_total_s, s_total_r),
    )

    def offer(which):
        for n, peer in enumerate((place.mate,) + place.sides):
            pl.semaphore_signal(
                free.at[3 * which + n], inc=1, device_id=peer, device_id_type=MESH
            )

    def accept(which, which_sides):
        for n in range(1, 3) if which_sides else range(1):
            pl.semaphore_wait(free.at[3 * which + n], 1)

    def expand_back(i, _):
        for n in range(FF // D):
            c = slice(n * D, (n + 1) * D)
            weight = full[SHR][2 * n : 2 * n + 2].reshape(D, D)
            da = dot(low[rows(i), :], weight, NT).astype(BF).astype(F32)
            du = (da * slope[rows(i), c].astype(F32)).astype(BF)
            slope[rows(i), c] = du
            gvec[VEC_ROW["bf1"] : VEC_ROW["bf1"] + 1, c] += jnp.sum(
                du.astype(F32), axis=0, keepdims=True
            )
        return 0

    lax.fori_loop(0, blocks, expand_back, 0)

    def shrink_grad(n, _):
        value = dot(act[:, span(n * D, D, 128)], low[...], TN).astype(BF)
        full3[pl.ds(2 * n, 2)] = value.reshape((2,) + full3.shape[1:])
        for owner in range(2):
            for sub in range(2):
                scatter.pair(SHR, sub, 2 * n + owner).start()
        return 0

    lax.fori_loop(0, FF // D, shrink_grad, 0)
    offer(0)
    for sub in range(2):
        scatter.start(SHR, sub)
    steps = [None] + scatter.ticks(SHR, 1, (0, 1)) + scatter.ticks(SHR, 2, (0, 1))
    in_middle_back = take(blocks, 1)

    def middle_back(i, _):
        in_middle_back(i, 0)
        upstream = dot(slope[rows(i), :], whole(full[EXP]), NT)
        part, gain, shift = norm_grad(x1[rows(i), :], of("g2"), upstream)
        value = dy[rows(i), :] + part
        dy[rows(i), :] = value
        low[rows(i), :] = value.astype(BF)
        add_grad("g2", gain)
        add_grad("b2", shift)
        add_grad("bo", jnp.sum(value, axis=0, keepdims=True))
        return 0

    lax.fori_loop(0, blocks, middle_back, 0)
    accept(0, False)
    in_expand_grad = take(FF // D, 1, len(steps))

    def expand_grad(n, _):
        in_expand_grad(n, 0)
        c = span(n * D, D, 128)
        value = dot(h2[...], slope[:, c], TN).astype(BF)
        full2[:, :, :, c] = value.reshape(full2.shape[:3] + (D,))
        pl.when(n == FF // D // 2 - 1)(lambda: scatter.hand(EXP, 0))
        return 0

    lax.fori_loop(0, FF // D, expand_grad, 0)
    scatter.hand(EXP, 1)
    offer(1)
    accept(0, True)
    steps = [partial(scatter.start, EXP, 0), None, None, partial(scatter.start, EXP, 1)]
    in_upstream = take(blocks, 1)

    def upstream_rows(i, _):
        in_upstream(i, 0)
        h2[rows(i), :] = dot(low[rows(i), :], whole(full[OUT]), NT).astype(BF)
        return 0

    lax.fori_loop(0, blocks, upstream_rows, 0)
    full1[...] = dot(att[...], low[...], TN).astype(BF).reshape(full1.shape)
    accept(1, False)
    scatter.hand(OUT, 0)
    accept(1, True)
    steps = scatter.ticks(SHR, 3, (0, 1)) + [partial(scatter.start, OUT, 0)]
    steps += scatter.ticks(EXP, 1, (0, 1))
    steps += [partial(scatter.finish, SHR, 0), partial(scatter.finish, SHR, 1)]
    steps += scatter.ticks(OUT, 1, (0,)) + scatter.ticks(EXP, 2, (0, 1))

    def mixing_part(part):
        c = slice(part * 3 * HALF, (part + 1) * 3 * HALF)
        value = dot(h1[...], qkv[:, c], TN).astype(BF)
        mixing_grad[:, :, :, c] = value.reshape(mixing_grad.shape[:3] + (3 * HALF,))
        scatter.hand(MIX, part)

    for part in range(2):
        in_backward = take(pairs // 2, len(MARKS), len(steps))

        def backward_pair(hp, _):
            def tick(i, hd):
                if (i, hd) in MARKS:
                    in_backward(hp, MARKS[i, hd])

            attend_back_pair(part * (pairs // 2) + hp, qkv, segr, segc, att, h2, lse, x1, tick)
            return 0

        lax.fori_loop(0, pairs // 2, backward_pair, 0)
        mixing_part(part)
        steps = scatter.ticks(OUT, 2, (0,)) + [partial(scatter.start, MIX, 0)]
        steps += scatter.ticks(EXP, 3, (0, 1)) + scatter.ticks(OUT, 3, (0,))
        steps += scatter.ticks(MIX, 1, (0,))
        steps += [partial(scatter.finish, EXP, 0), partial(scatter.finish, EXP, 1)]
        steps += [partial(scatter.finish, OUT, 0)] + scatter.ticks(MIX, 2, (0,))
        steps += [partial(scatter.crossed, SHR, 0), partial(scatter.crossed, SHR, 1)]
        steps += scatter.ticks(MIX, 3, (0,)) + [None, partial(scatter.finish, MIX, 0)]
    scatter.start(MIX, 1)
    out_local.wait()
    out_go.wait_send()
    steps = [None] + scatter.ticks(MIX, 1, (1,)) + scatter.ticks(MIX, 2, (1,))
    in_input_back = take(blocks, 1)

    def input_back(j, _):
        in_input_back(j, 0)
        core = place.core + (1 - 2 * place.core) * (j % 2)
        i = 2 * (place.x + (1 - 2 * place.x) * (1 - j // 2)) + core
        d = qkv[rows(i), :]
        part, gain, shift = norm_grad(
            x[rows(i), :].astype(F32), of("g1"), dot(d, whole(full[MIX]), NT)
        )
        sent[rows(i), :] = (dy[rows(i), :] + part).astype(BF)
        add_grad("g1", gain)
        add_grad("b1", shift)
        for half_of in range(2):
            first = half_of * 3 * HALF
            for name, start in (("bq", first), ("bv", first + 2 * HALF)):
                term = d[:, start : start + HALF].astype(F32)
                add_grad(name, jnp.sum(term, axis=0, keepdims=True), half_of * HALF)
        for n, k in ((0, 2), (1, 3), (3, 1)):
            pl.when(j == n)(lambda k=k: send_rows(back_rows, back_go, k))
        return 0

    lax.fori_loop(0, blocks, input_back, 0)
    back_local = local(sent.at[me], back_rows.at[place.seq], row_l.at[3])
    flat = 0
    vec_out[...] = jnp.zeros_like(vec_out)
    for name, size in VEC_PLACES:
        for n in range(size // 128):
            r = flat + n
            vec_out[r // per, r % per : r % per + 1, :] = gvec[
                VEC_ROW[name] : VEC_ROW[name] + 1, n * 128 : (n + 1) * 128
            ]
        flat += size // 128
    for k in range(1, count):
        peer = place.dp_peer(k)
        vec_go.start(vec_out.at[peer[0]], vec_buf.at[place.dp], peer)
    vec_buf[place.dp] = vec_out[place.dp]
    for step in steps:
        step()
    for step in scatter.ticks(MIX, 3, (1,)):
        step()
    for w, sub in ((EXP, 0), (EXP, 1), (OUT, 0), (MIX, 0)):
        scatter.crossed(w, sub)
    vec_go.wait_recv()
    vec_mine[...] = jnp.sum(vec_buf[...], axis=0)
    vec_seq[place.seq] = vec_mine[...]
    for k in (2, 3, 1):
        seq_go.start(vec_mine, vec_seq.at[place.seq], place.kin(k))

    def squares_of(w, part, total):
        c = slice(None) if part is None else slice(part * 3 * HALF, (part + 1) * 3 * HALF)
        for core in range(2):
            value = sums[w][core, :, c].astype(F32)
            term = jnp.sum(value * value, axis=0, keepdims=True)
            for n in range(term.shape[1] // 128):
                total = total + term[:, n * 128 : (n + 1) * 128]
        return total

    squares = jnp.zeros((1, 128), F32)
    for w in (SHR, EXP, OUT):
        for sub in range(SUBS[w]):
            scatter.arrived(w, sub)
        squares = squares_of(w, None, squares)
    scatter.arrived(MIX, 0)
    squares = squares_of(MIX, 0, squares)
    scatter.finish(MIX, 1)
    seq_go.wait_recv()
    vec_total = jnp.sum(vec_seq[...], axis=0)
    vec_sum[...] = vec_total
    squares = squares + jnp.sum(vec_total * vec_total, axis=0, keepdims=True)
    scatter.crossed(MIX, 1)
    scatter.arrived(MIX, 1)
    squares = squares_of(MIX, 1, squares)
    sq_mine[...] = jnp.broadcast_to(squares, sq_mine.shape)
    sq_buf[place.dp] = sq_mine[...]
    for k in range(1, count):
        sq_go.start(sq_mine, sq_buf.at[place.dp], place.dp_peer(k))
    for w in (MIX, OUT, EXP, SHR):
        scatter.drain(w)
    for copies in (row_in, seg_in, teach_in, vec_in, vec_go, seq_go, back_go, sq_go):
        copies.wait_send()
    back_local.wait()
    out_go.wait_recv()
    back_go.wait_recv()
    sq_go.wait_recv()
    total = jnp.sum(jnp.sum(sq_buf[...], axis=0), axis=1, keepdims=True)
    norm_ref[...] = jnp.broadcast_to(jnp.sqrt(total), norm_ref.shape)


def block_call(count, inputs, teacher, segments, masters, vectors):
    rows, local_len, features = inputs.shape
    length = rows * local_len
    halves = [(2, m.shape[0] // 2, m.shape[1]) for m in masters]
    any_spec = pl.BlockSpec(memory_space=pl.ANY)
    vmem = pl.BlockSpec(memory_space=pltpu.VMEM)
    row_shape = jax.ShapeDtypeStruct(inputs.shape, BF)
    out_shape = [jax.ShapeDtypeStruct(h, BF) for h in halves]
    out_shape += [
        jax.ShapeDtypeStruct((VROWS, 128), F32),
        jax.ShapeDtypeStruct((8, 128), F32),
        row_shape,
        row_shape,
    ]

    def low(*shape):
        return pltpu.VMEM(shape, BF)

    def wide(*shape):
        return pltpu.VMEM(shape, F32)

    def dma(*shape):
        return pltpu.SemaphoreType.DMA(shape)

    shrink_half = halves[SHR][1:]
    buffers = [low(count, *h) for h in halves]
    buffers += [
        low(length, D),
        low(length, D),
        low(length, 3 * D),
        low(length, D),
        wide(length, D),
        low(length, D),
        low(length, FF),
        low(length, FF),
        wide(length, D),
        low(length, D),
        low(length, D),
        low(count, *halves[MIX]),
        low(count, *shrink_half),
        low(count - 1, *shrink_half),
    ]
    buffers += [low(*h[1:]) for h in halves] * 2
    buffers += [
        wide(16, length),
        pltpu.VMEM((rows, 8, local_len), jnp.int32),
        pltpu.VMEM((rows, 8, local_len), jnp.int32),
        wide(1, length),
        wide(length, 128),
        wide(VROWS, 128),
        wide(count, VROWS, 128),
        wide(16, FF),
        wide(16, FF),
        wide(count, VROWS, 128),
        wide(count, VROWS, 128),
        wide(VROWS, 128),
        wide(4, VROWS, 128),
        wide(8, 128),
        wide(count, 8, 128),
    ]
    hops = count - 1
    sems = [dma(9), dma(4), dma(4, 2, hops), dma(4), dma(4), dma(2), dma(2, hops)]
    sems += [dma(4, 2), dma(4, 2), dma(4, 2), dma(4, 2, hops)] + [dma(4, 2)] * 4
    sems += [dma(6), dma(6), dma(4), dma(3), dma(3)]
    sems.append(pltpu.SemaphoreType.REGULAR((6,)))
    return pl.pallas_call(
        partial(block_kernel, count),
        out_shape=out_shape,
        in_specs=[any_spec] * 2 + [vmem] + [any_spec] * 4 + [vmem],
        out_specs=[vmem] * 6 + [any_spec] * 2,
        scratch_shapes=buffers + sems,
        compiler_params=pltpu.CompilerParams(
            collective_id=1, has_side_effects=True, vmem_limit_bytes=VMEM_BYTES
        ),
    )(inputs, teacher, segments, *masters, vectors.reshape(-1, 128))


def update_kernel(steps, norm_ref, *refs):
    sums, masters, firsts, seconds = refs[0:5], refs[5:10], refs[10:15], refs[15:20]
    out_from, back_from = refs[20:22]
    updated, first_out, second_out = refs[22:27], refs[27:32], refs[32:37]
    out_to, back_to, norm_out, held, sem = refs[37:42]
    step = pl.program_id(0)
    norm = norm_ref[0:1, 0:1]
    factor = clip_level() / jnp.maximum(norm, clip_level())
    takes = [
        pltpu.make_async_copy(rows, held.at[n], sem.at[n])
        for n, rows in enumerate((out_from, back_from))
    ]
    gives = [
        pltpu.make_async_copy(held.at[n], rows, sem.at[2 + n])
        for n, rows in enumerate((out_to, back_to))
    ]

    @pl.when(step == 0)
    def _():
        for copy in takes:
            copy.start()
        norm_out[...] = norm

    @pl.when(step == steps // 2)
    def _():
        for take, give in zip(takes, gives):
            take.wait()
            give.start()

    def apply(n, gradient):
        results = adamw(
            masters[n][...], firsts[n][...], seconds[n][...], gradient * factor, learn_rates()[n]
        )
        updated[n][...], first_out[n][...], second_out[n][...] = results

    for w in range(4):
        gradient = sums[w][...].astype(F32)
        if w == MIX:
            order = (0, 3, 1, 4, 2, 5)
            gradient = jnp.concatenate(
                [gradient[:, n * HALF : (n + 1) * HALF] for n in order], axis=1
            )
        apply(w, gradient)

    @pl.when(step == 0)
    def _():
        apply(4, sums[4][0 : masters[4].shape[0], :])

    @pl.when(step == steps - 1)
    def _():
        for copy in gives:
            copy.wait()


def update_call(results, masters, firsts, seconds):
    half = results[MIX].shape[1]
    parts = half // 16
    steps = 2 * parts

    def fixed(shape):
        return pl.BlockSpec(shape, lambda i: (0,) * len(shape))

    any_spec = pl.BlockSpec(memory_space=pl.ANY)
    sum_specs, state_specs, states = [], [], []
    for total in results[:4]:
        rows, columns = total.shape[1] // parts, total.shape[2]
        sum_specs.append(pl.BlockSpec((None, rows, columns), lambda i: (i // parts, i % parts, 0)))
        state_specs.append(pl.BlockSpec((rows, columns), lambda i: (i, 0)))
    packed = (masters[4].shape[0] // 128, 128)
    state_specs.append(fixed(packed))
    sum_specs.append(fixed(results[4].shape))
    for group in (masters, firsts, seconds):
        states += list(group[:4]) + [group[4].reshape(packed)]
    out_shape = [jax.ShapeDtypeStruct(state.shape, F32) for state in states]
    out_shape += [jax.ShapeDtypeStruct(results[6].shape, BF)] * 2
    out_shape.append(jax.ShapeDtypeStruct((1, 1), F32))
    return pl.pallas_call(
        partial(update_kernel, steps),
        grid=(steps,),
        out_shape=out_shape,
        in_specs=[fixed(results[5].shape)] + sum_specs + state_specs * 3 + [any_spec] * 2,
        out_specs=state_specs * 3 + [any_spec] * 2 + [fixed((1, 1))],
        scratch_shapes=[
            pltpu.VMEM((2,) + results[6].shape, BF),
            pltpu.SemaphoreType.DMA((4,)),
        ],
        compiler_params=pltpu.CompilerParams(vmem_limit_bytes=VMEM_BYTES),
    )(results[5], *results[:5], *states, *results[6:8])


def row_body(
    inputs,
    segments,
    teacher,
    mixing_weight,
    output_weight,
    expand_weight,
    shrink_weight,
    vectors,
    mixing_first,
    output_first,
    expand_first,
    shrink_first,
    vectors_first,
    mixing_second,
    output_second,
    expand_second,
    shrink_second,
    vectors_second,
):
    masters = (mixing_weight, output_weight, expand_weight, shrink_weight, vectors)
    firsts = (mixing_first, output_first, expand_first, shrink_first, vectors_first)
    seconds = (mixing_second, output_second, expand_second, shrink_second, vectors_second)
    results = block_call(lax.axis_size("dp"), inputs, teacher, segments, masters[:4], vectors)
    fresh = update_call(results, masters, firsts, seconds)
    states = [
        state.reshape(vectors.shape) if n % 5 == 4 else state for n, state in enumerate(fresh[:15])
    ]
    return (fresh[15], fresh[16], fresh[17].reshape(()), *states)


def whole_rows(mesh):
    return mesh.shape["seq"] == 4 and mesh.shape["dp"] == 8


def solution(mesh):
    in_specs = (
        P("dp", "seq", None),
        P("dp", "seq"),
        P("dp", "seq", None),
        P("dp", None),
        P("dp", None),
        P("dp", None),
        P("dp", None),
        P("dp"),
        P("dp", None),
        P("dp", None),
        P("dp", None),
        P("dp", None),
        P("dp"),
        P("dp", None),
        P("dp", None),
        P("dp", None),
        P("dp", None),
        P("dp"),
    )
    out_specs = (
        P("dp", "seq", None),
        P("dp", "seq", None),
        P(),
        P("dp", None),
        P("dp", None),
        P("dp", None),
        P("dp", None),
        P("dp"),
        P("dp", None),
        P("dp", None),
        P("dp", None),
        P("dp", None),
        P("dp"),
        P("dp", None),
        P("dp", None),
        P("dp", None),
        P("dp", None),
        P("dp"),
    )
    chosen = row_body if whole_rows(mesh) else body
    return jax.shard_map(chosen, mesh=mesh, in_specs=in_specs, out_specs=out_specs, check_vma=False)
```

```python
from functools import partial
import math

import jax
import jax.numpy as jnp
from jax import lax
from jax.experimental import pallas as pl
from jax.experimental.pallas import tpu as pltpu
from jax.sharding import PartitionSpec as P

D = 768
HEADS = 12
HD = 64
FF = 3072
LEN = 1024
NDOC = 8
STEP = 10


NEGATIVE = -1e30
NORM_EPS = 1e-05
BETA_ONE = 0.9
BETA_TWO = 0.999
ADAM_EPS = 1e-08
WEIGHT_DECAY = 0.01


def layer_norm(values, norm_gain, norm_shift):
    center = values - jnp.mean(values, axis=-1, keepdims=True)
    spread = jnp.mean(center * center, axis=-1, keepdims=True)
    return center * lax.rsqrt(spread + NORM_EPS) * norm_gain + norm_shift


def gelu_tanh(values):
    return jax.nn.gelu(values, approximate=True)


def split_vectors(packed):
    return jnp.split(packed, [D, 2 * D, 3 * D, 4 * D, 5 * D, 6 * D, 7 * D, 7 * D + FF])


def adamw(master, first, second, gradient, rate):
    first_new = BETA_ONE * first + (1.0 - BETA_ONE) * gradient
    second_new = BETA_TWO * second + (1.0 - BETA_TWO) * gradient * gradient
    first_hat = first_new / (1.0 - BETA_ONE**STEP)
    second_hat = second_new / (1.0 - BETA_TWO**STEP)
    updated = master - rate * (
        first_hat / (jnp.sqrt(second_hat) + ADAM_EPS) + WEIGHT_DECAY * master
    )
    return (updated, first_new, second_new)


def learn_rates():
    return (
        1.0 / math.sqrt(2 * D),
        1.0 / math.sqrt(max(1, 2 * D * NDOC // LEN)),
        1.0 / math.sqrt(D),
        1.0 / math.sqrt(FF),
        0.3,
    )


def clip_level():
    return 0.5 * math.sqrt(4 * D * D + 2 * D * FF + 8 * D + FF)


def visible(query_pos, key_pos, query_seg, key_seg):
    return (key_pos[None, :] <= query_pos[:, None]) & (key_seg[None, :] == query_seg[:, None])


def attend_rows(query_pos, key_pos, packed_args):
    queries, keys_all, values_all, query_seg, key_seg = packed_args
    scores = jnp.einsum("qhd,khd->hqk", queries, keys_all, preferred_element_type=jnp.float32)
    scores = jnp.where(visible(query_pos, key_pos, query_seg, key_seg)[None], scores, NEGATIVE)
    top_score = jnp.max(scores, axis=-1, keepdims=True)
    exponent = jnp.exp(scores - top_score)
    totals = jnp.sum(exponent, axis=-1, keepdims=True)
    probability = (exponent / totals).astype(jnp.bfloat16)
    attended = jnp.einsum(
        "hqk,khd->qhd", probability, values_all, preferred_element_type=jnp.float32
    )
    return (attended, (top_score + jnp.log(totals))[..., 0])


def attend_back(query_pos, key_pos, packed_args):
    queries, keys_all, values_all, upstream, log_totals, query_seg, key_seg = packed_args
    scores = jnp.einsum("qhd,khd->hqk", queries, keys_all, preferred_element_type=jnp.float32)
    scores = jnp.where(visible(query_pos, key_pos, query_seg, key_seg)[None], scores, NEGATIVE)
    probability = jnp.exp(scores - log_totals[..., None])
    prob_low = probability.astype(jnp.bfloat16)
    prob_grad = jnp.einsum("qhd,khd->hqk", upstream, values_all, preferred_element_type=jnp.float32)
    value_part = jnp.einsum("hqk,qhd->khd", prob_low, upstream, preferred_element_type=jnp.float32)
    score_grad = probability * (
        prob_grad - jnp.sum(probability * prob_grad, axis=-1, keepdims=True)
    )
    score_low = score_grad.astype(jnp.bfloat16)
    query_part = jnp.einsum("hqk,khd->qhd", score_low, keys_all, preferred_element_type=jnp.float32)
    key_part = jnp.einsum("hqk,qhd->khd", score_low, queries, preferred_element_type=jnp.float32)
    key_count = keys_all.shape[0]
    return (
        query_part,
        jnp.concatenate(
            [key_part.reshape(key_count, -1), value_part.reshape(key_count, -1)], axis=1
        ),
    )


def body(
    inputs,
    segments,
    teacher,
    mixing_weight,
    output_weight,
    expand_weight,
    shrink_weight,
    vectors,
    mixing_first,
    output_first,
    expand_first,
    shrink_first,
    vectors_first,
    mixing_second,
    output_second,
    expand_second,
    shrink_second,
    vectors_second,
):
    bfloat = jnp.bfloat16
    floats = jnp.float32
    seq_count, local_len, features = inputs.shape
    row_count = seq_count * local_len
    scale = 1.0 / math.sqrt(HD)
    mixing_low, output_low, expand_low, shrink_low, vectors_low = (
        lax.all_gather(mixing_weight.astype(bfloat), "dp", axis=0, tiled=True),
        lax.all_gather(output_weight.astype(bfloat), "dp", axis=0, tiled=True),
        lax.all_gather(expand_weight.astype(bfloat), "dp", axis=0, tiled=True),
        lax.all_gather(shrink_weight.astype(bfloat), "dp", axis=0, tiled=True),
        lax.all_gather(vectors.astype(bfloat), "dp", axis=0, tiled=True),
    )
    (
        gain_one,
        shift_one,
        bias_query,
        bias_value,
        bias_output,
        gain_two,
        shift_two,
        bias_expand,
        bias_shrink,
    ) = split_vectors(vectors_low.astype(floats))
    states = inputs.astype(floats).reshape(row_count, features)
    normed = layer_norm(states, gain_one, shift_one)
    normed_low = normed.astype(bfloat)
    projected = jnp.dot(normed_low, mixing_low, preferred_element_type=floats)
    query_low = ((projected[:, :features] + bias_query) * scale).astype(bfloat)
    key_low = projected[:, features : 2 * features].astype(bfloat)
    value_low = (projected[:, 2 * features :] + bias_value).astype(bfloat)
    key_all, value_all = (
        lax.all_gather(key_low.reshape(seq_count, local_len, features), "seq", axis=1, tiled=True),
        lax.all_gather(
            value_low.reshape(seq_count, local_len, features), "seq", axis=1, tiled=True
        ),
    )
    segment_all = lax.all_gather(segments, "seq", axis=1, tiled=True)
    full_len = key_all.shape[1]
    query_pos = lax.axis_index("seq") * local_len + jnp.arange(local_len, dtype=jnp.int32)
    key_pos = jnp.arange(full_len, dtype=jnp.int32)
    query_heads = query_low.reshape(seq_count, local_len, HEADS, HD)
    key_heads = key_all.reshape(seq_count, full_len, HEADS, HD)
    value_heads = value_all.reshape(seq_count, full_len, HEADS, HD)
    attended, log_totals = lax.map(
        partial(attend_rows, query_pos, key_pos),
        (query_heads, key_heads, value_heads, segments, segment_all),
    )
    attended_low = attended.reshape(row_count, features).astype(bfloat)
    middle = states + jnp.dot(attended_low, output_low, preferred_element_type=floats) + bias_output
    normed_two = layer_norm(middle, gain_two, shift_two)
    normed_two_low = normed_two.astype(bfloat)
    hidden = jnp.dot(normed_two_low, expand_low, preferred_element_type=floats) + bias_expand
    active, gelu_back = jax.vjp(gelu_tanh, hidden)
    active_low = active.astype(bfloat)
    result = middle + jnp.dot(active_low, shrink_low, preferred_element_type=floats) + bias_shrink
    block_output = result.astype(bfloat).reshape(seq_count, local_len, features)
    target_prob = jax.nn.softmax(teacher.astype(floats).reshape(row_count, features), axis=-1)
    result_grad = features * (jax.nn.softmax(result, axis=-1) - target_prob)
    result_low = result_grad.astype(bfloat)
    grad_shrink = jnp.dot(active_low.T, result_low, preferred_element_type=floats)
    grad_bias_shrink = jnp.sum(result_grad, axis=0)
    active_grad = jnp.dot(result_low, shrink_low.T, preferred_element_type=floats)
    active_round = lax.optimization_barrier(active_grad.astype(bfloat)).astype(floats)
    hidden_low = gelu_back(active_round)[0].astype(bfloat)
    grad_bias_expand = jnp.sum(hidden_low.astype(floats), axis=0)
    grad_expand = jnp.dot(normed_two_low.T, hidden_low, preferred_element_type=floats)
    normed_two_grad = jnp.dot(hidden_low, expand_low.T, preferred_element_type=floats)
    norm_two_back = jax.vjp(layer_norm, middle, gain_two, shift_two)[1]
    middle_part, grad_gain_two, grad_shift_two = norm_two_back(normed_two_grad)
    middle_grad = result_grad + middle_part
    middle_low = middle_grad.astype(bfloat)
    grad_bias_output = jnp.sum(middle_grad, axis=0)
    grad_output = jnp.dot(attended_low.T, middle_low, preferred_element_type=floats)
    attended_grad = jnp.dot(middle_low, output_low.T, preferred_element_type=floats).astype(bfloat)
    upstream_heads = attended_grad.reshape(seq_count, local_len, HEADS, HD)
    query_grad, kv_terms = lax.map(
        partial(attend_back, query_pos, key_pos),
        (query_heads, key_heads, value_heads, upstream_heads, log_totals, segments, segment_all),
    )
    kv_sums = (
        lax.psum_scatter(kv_terms.astype(jnp.bfloat16), "seq", scatter_dimension=1, tiled=True)
        .astype(jnp.float32)
        .reshape(row_count, 2 * features)
    )
    key_grad_low = kv_sums[:, :features].astype(bfloat)
    value_grad_low = kv_sums[:, features:].astype(bfloat)
    query_grad_low = query_grad.reshape(row_count, features).astype(bfloat)
    query_scaled = query_grad_low.astype(floats) * scale
    grad_bias_query = jnp.sum(query_scaled, axis=0)
    grad_bias_value = jnp.sum(value_grad_low.astype(floats), axis=0)
    projected_grad = jnp.concatenate(
        [query_scaled.astype(bfloat), key_grad_low, value_grad_low], axis=1
    )
    grad_mixing = jnp.dot(normed_low.T, projected_grad, preferred_element_type=floats)
    normed_grad = jnp.dot(projected_grad, mixing_low.T, preferred_element_type=floats)
    norm_one_back = jax.vjp(layer_norm, states, gain_one, shift_one)[1]
    states_part, grad_gain_one, grad_shift_one = norm_one_back(normed_grad)
    input_grad = (middle_grad + states_part).astype(bfloat).reshape(seq_count, local_len, features)
    grad_vectors = jnp.concatenate(
        [
            grad_gain_one,
            grad_shift_one,
            grad_bias_query,
            grad_bias_value,
            grad_bias_output,
            grad_gain_two,
            grad_shift_two,
            grad_bias_expand,
            grad_bias_shrink,
        ]
    )
    vector_rows = grad_vectors.reshape(lax.axis_size("dp"), -1)
    mixing_part, output_part, expand_part, shrink_part, vector_part = (
        lax.psum_scatter(
            grad_mixing.astype(jnp.bfloat16), "dp", scatter_dimension=0, tiled=True
        ).astype(jnp.float32),
        lax.psum_scatter(
            grad_output.astype(jnp.bfloat16), "dp", scatter_dimension=0, tiled=True
        ).astype(jnp.float32),
        lax.psum_scatter(
            grad_expand.astype(jnp.bfloat16), "dp", scatter_dimension=0, tiled=True
        ).astype(jnp.float32),
        lax.psum_scatter(
            grad_shrink.astype(jnp.bfloat16), "dp", scatter_dimension=0, tiled=True
        ).astype(jnp.float32),
        lax.psum_scatter(
            vector_rows.astype(jnp.bfloat16), "dp", scatter_dimension=0, tiled=True
        ).astype(jnp.float32),
    )
    mixing_sum, output_sum, expand_sum, shrink_sum, vector_sum = (
        lax.psum(mixing_part.astype(jnp.bfloat16), "seq").astype(jnp.float32),
        lax.psum(output_part.astype(jnp.bfloat16), "seq").astype(jnp.float32),
        lax.psum(expand_part.astype(jnp.bfloat16), "seq").astype(jnp.float32),
        lax.psum(shrink_part.astype(jnp.bfloat16), "seq").astype(jnp.float32),
        lax.psum(vector_part.astype(jnp.bfloat16), "seq").astype(jnp.float32),
    )
    vector_sum = vector_sum.reshape(-1)
    squares = (
        jnp.sum(mixing_sum * mixing_sum)
        + jnp.sum(output_sum * output_sum)
        + jnp.sum(expand_sum * expand_sum)
        + jnp.sum(shrink_sum * shrink_sum)
        + jnp.sum(vector_sum * vector_sum)
    )
    grad_norm = jnp.sqrt(lax.psum(squares, "dp"))
    clip_value = clip_level()
    factor = clip_value / jnp.maximum(grad_norm, clip_value)
    step_rates = learn_rates()
    mixing_new = adamw(
        mixing_weight, mixing_first, mixing_second, mixing_sum * factor, step_rates[0]
    )
    output_new = adamw(
        output_weight, output_first, output_second, output_sum * factor, step_rates[1]
    )
    expand_new = adamw(
        expand_weight, expand_first, expand_second, expand_sum * factor, step_rates[2]
    )
    shrink_new = adamw(
        shrink_weight, shrink_first, shrink_second, shrink_sum * factor, step_rates[3]
    )
    vectors_new = adamw(vectors, vectors_first, vectors_second, vector_sum * factor, step_rates[4])
    return (
        block_output,
        input_grad,
        grad_norm,
        mixing_new[0],
        output_new[0],
        expand_new[0],
        shrink_new[0],
        vectors_new[0],
        mixing_new[1],
        output_new[1],
        expand_new[1],
        shrink_new[1],
        vectors_new[1],
        mixing_new[2],
        output_new[2],
        expand_new[2],
        shrink_new[2],
        vectors_new[2],
    )

MESH = pl.DeviceIdType.MESH
BF = jnp.bfloat16
F32 = jnp.float32
BLK = 256
NN = ((1,), (0,))
NT = ((1,), (1,))
TN = ((0,), (0,))
VMEM_BYTES = 64 * 2**20 - 2**17
VROWS = 16
MIX, OUT, EXP, SHR = 0, 1, 2, 3
HALF = D // 2
PAIRS = D // 128
EXPAND_TILE = D
SUBS = (4, 1, 2, 2)
LANES = (0, 4, 5, 7)


def dot(left, right, dims):
    return lax.dot_general(left, right, (dims, ((), ())), preferred_element_type=F32)


class Place:
    def __init__(self, count):
        self.count = count
        self.hops = (count // 2, count - 1 - count // 2)
        self.dp = lax.axis_index("dp")
        self.seq = lax.axis_index("seq")
        odd = self.dp % 2
        self.pos = (1 - odd) * (self.dp // 2) + odd * (count - 1 - self.dp // 2)
        self.core = self.seq % 2
        self.x = self.seq // 2
        self.step = 1 - 2 * self.core
        self.sides = ((self.ahead(1), self.seq), (self.behind(1), self.seq))
        self.mate = self.kin(1)
        self.across = self.kin(2)

    def at(self, pos):
        pos = pos % self.count
        upper = pos // (self.count // 2)
        return (1 - upper) * (2 * pos) + upper * (2 * (self.count - 1 - pos) + 1)

    def ahead(self, steps):
        return self.at(self.pos + steps * self.step + self.count)

    def behind(self, steps):
        return self.at(self.pos - steps * self.step + self.count)

    def kin(self, which):
        core = self.core + (1 - 2 * self.core) * (which % 2)
        return (self.dp, 2 * (self.x + (1 - 2 * self.x) * (which // 2)) + core)

    def dp_peer(self, offset):
        return ((self.dp + offset) % self.count, self.seq)

    def greet(self):
        barrier = pltpu.get_barrier_semaphore()
        peers = [self.kin(k) for k in range(1, 4)]
        peers += [self.dp_peer(k) for k in range(1, self.count)]
        for peer in peers:
            pl.semaphore_signal(barrier, inc=1, device_id=peer, device_id_type=MESH)
        return lambda: pl.semaphore_wait(barrier, len(peers))


def describe(src, dst, send, recv, device):
    return pltpu.make_async_remote_copy(
        src_ref=src,
        dst_ref=dst,
        send_sem=send,
        recv_sem=recv,
        device_id=device,
        device_id_type=MESH,
    )


def remote(src, dst, send, recv, device):
    copy = describe(src, dst, send, recv, device)
    copy.start()
    return copy


def local(src, dst, sem):
    copy = pltpu.make_async_copy(src, dst, sem)
    copy.start()
    return copy


def span(start, size, unit):
    return pl.ds(start if isinstance(start, int) else pl.multiple_of(start, unit), size)


def spread(ticks, marks):
    def at(trip, mark, first=0, past=None):
        for n in range(first, len(ticks) // marks if past is None else past):
            here = ticks[n * marks + mark]
            if here:

                def run(here=here):
                    for tick in here:
                        tick()

                pl.when(trip == n)(run)

    return at


class Group:
    def __init__(self, send, recv, of_all_sent, of_all_received, device):
        self.send, self.recv, self.device = send, recv, device
        self.bytes = (of_all_sent, of_all_received)

    def start(self, src, dst, device):
        describe(src, dst, self.send, self.recv, device).start()

    def all(self, which):
        return describe(self.bytes[which], self.bytes[which], self.send, self.recv, self.device)

    def wait_recv(self):
        self.all(1).wait_recv()

    def wait_send(self):
        self.all(0).wait_send()


class Gather:
    def __init__(self, place, full, sems):
        self.place, self.full = place, full
        self.ring_s, self.ring_r, self.mate_s, self.mate_r, self.cross_s, self.cross_r = sems

    def lanes(self, w):
        return ((0, 1), (0,), (self.place.x, 2), (self.place.x, 2, 3))[w]

    def part(self, ref, w, sub):
        rows, columns = ref.shape[-2:]
        lead = (slice(None),) * (len(ref.shape) - 2)
        if w == SHR:
            unit = rows // 6
            if isinstance(sub, int) and sub >= 2:
                return ref.at[lead + (pl.ds((2 * sub - 2) * unit, 2 * unit),)]
            return ref.at[lead + (span(sub * unit, unit, 16),)]
        unit = columns // (2, 1, 3)[w]
        return ref.at[lead + (slice(None), span(sub * unit, unit, 128))]

    def cut(self, w, owner, core, sub):
        return self.part(self.full[w].at[owner, core], w, sub)

    def block(self, w, sub, way, t):
        owner = self.place.ahead(t) if way else self.place.behind(t)
        return self.cut(w, owner, self.place.core, sub)

    def copy(self, block, send, recv, device):
        return describe(block, block, send, recv, device)

    def ring(self, w, lane, way, t):
        index = ((0, 2, 3, 5)[w] + lane, t + way * self.place.hops[0])
        block = self.block(w, self.lanes(w)[lane], way, t)
        return self.copy(block, self.ring_s.at[w], self.ring_r.at[index], self.place.sides[way])

    def pair(self, w, sub, way, t):
        block = self.block(w, sub, way, t)
        return self.copy(block, self.mate_s.at[w], self.mate_r.at[w], self.place.mate)

    def over(self, w, way, t):
        recv = self.cross_r.at[w - EXP, t - 1 + way * self.place.hops[0]]
        block = self.block(w, self.place.x, way, t)
        return self.copy(block, self.cross_s.at[w - EXP], recv, self.place.across)

    def start(self, w):
        for lane in range(len(self.lanes(w))):
            for way in range(2):
                self.ring(w, lane, way, 0).start()

    def tick(self, w, lane, way, t):
        self.ring(w, lane, way, t - 1).wait_recv()
        if t < self.place.hops[way]:
            self.ring(w, lane, way, t).start()
        self.pair(w, self.lanes(w)[lane], way, t).start()
        if w >= EXP and lane == 0:
            self.over(w, way, t).start()

    def relay(self, w, way, t):
        self.over(w, way, t).wait_recv()
        self.pair(w, 1 - self.place.x, way, t).start()

    def others(self, w):
        return self.full[w].at[pl.ds(0, self.place.count - 1), self.place.core]

    def arrived(self, w):
        block = self.others(w)
        self.copy(block, self.mate_s.at[w], self.mate_r.at[w], self.place.mate).wait_recv()

    def drain(self, w):
        block = self.others(w)
        self.copy(block, self.mate_s.at[w], self.mate_r.at[w], self.place.mate).wait_send()
        if w >= EXP:
            for lane in range(len(self.lanes(w))):
                part = self.part(block, w, self.lanes(w)[lane])
                self.copy(part, self.ring_s.at[w], self.mate_r.at[w], self.place.mate).wait_send()
            part = self.part(block, w, 0)
            self.copy(part, self.cross_s.at[w - EXP], self.mate_r.at[w], self.place.across).wait_send()
        else:
            self.copy(block, self.ring_s.at[w], self.mate_r.at[w], self.place.mate).wait_send()


class Scatter:
    def __init__(self, place, grads, mates, slots, sums, sems):
        self.place, self.grads, self.mates, self.slots = place, grads, mates, slots
        self.sums = sums
        (
            self.mate_s,
            self.mate_r,
            self.ring_s,
            self.ring_r,
            self.cross_s,
            self.cross_r,
            self.total_s,
            self.total_r,
        ) = sems

    def cut(self, ref, w, sub):
        rows, columns = ref.shape[-2:]
        lead = (slice(None),) * (len(ref.shape) - 2)
        if w == SHR:
            return ref.at[lead + (span(sub * (rows // 2), rows // 2, 16),)]
        if w == MIX:
            rows = self.sums[w].shape[1]
            there = pl.ds((sub - 1) * (rows // 3), rows // 3) if sub else pl.ds(0, rows)
            return ref.at[lead + (there, pl.ds(HALF if sub else 0, HALF))]
        size = columns // SUBS[w]
        return ref.at[lead + (slice(None), span(sub * size, size, 128))]

    def owner(self, way, distance):
        return self.place.behind(distance) if way else self.place.ahead(distance)

    def own(self, w, owner, core, sub):
        return self.cut(self.grads[w].at[owner, core], w, sub)

    def slot(self, w, way, t, sub):
        return self.cut(self.slots(w, t + way * self.place.hops[0]), w, sub)

    def pair(self, w, sub, owner):
        return describe(
            self.own(w, owner, 1 - self.place.core, sub),
            self.cut(self.mates(w, owner), w, sub),
            self.mate_s.at[LANES[w] + sub],
            self.mate_r.at[LANES[w] + sub],
            self.place.mate,
        )

    def pairs(self, w, sub):
        block = self.cut(self.grads[w].at[:, self.place.core], w, sub)
        return describe(
            block, block, self.mate_s.at[LANES[w] + sub], self.mate_r.at[LANES[w] + sub], self.place.mate
        )

    def ring(self, w, sub, way, t):
        if t == 0:
            owner = self.owner(way, self.place.hops[way])
            src = self.own(w, owner, self.place.core, sub)
        else:
            src = self.slot(w, way, t - 1, sub)
        index = (LANES[w] + sub, t + way * self.place.hops[0])
        return describe(
            src,
            self.slot(w, way, t, sub),
            self.ring_s.at[LANES[w] + sub],
            self.ring_r.at[index],
            self.place.sides[way],
        )

    def over(self, w, sub):
        return describe(
            self.own(w, self.place.dp, self.place.core, sub),
            self.cut(self.sums[w].at[self.place.core], w, sub),
            self.cross_s.at[LANES[w] + sub],
            self.cross_r.at[LANES[w] + sub],
            self.place.across,
        )

    def total(self, w, sub):
        block = self.cut(self.sums[w].at[self.place.core], w, sub)
        return describe(
            block, block, self.total_s.at[LANES[w] + sub], self.total_r.at[LANES[w] + sub], self.place.mate
        )

    def hand(self, w, sub):
        for owner in range(self.place.count):
            self.pair(w, sub, owner).start()

    def term(self, w, sub, way, distance):
        owner = self.owner(way, distance)
        mine = self.own(w, owner, self.place.core, sub)[...].astype(F32)
        return mine + self.cut(self.mates(w, owner), w, sub)[...].astype(F32)

    def start(self, w, sub):
        self.pairs(w, sub).wait_recv()
        for way, hops in enumerate(self.place.hops):
            term = self.term(w, sub, way, hops)
            self.own(w, self.owner(way, hops), self.place.core, sub)[...] = term.astype(BF)
            self.ring(w, sub, way, 0).start()

    def tick(self, w, sub, way, t):
        self.ring(w, sub, way, t - 1).wait_recv()
        slot = self.slot(w, way, t - 1, sub)
        term = self.term(w, sub, way, self.place.hops[way] - t)
        slot[...] = (slot[...].astype(F32) + term).astype(BF)
        self.ring(w, sub, way, t).start()

    def finish(self, w, sub):
        total = self.term(w, sub, 0, 0)
        for way, hops in enumerate(self.place.hops):
            self.ring(w, sub, way, hops - 1).wait_recv()
            total = total + self.slot(w, way, hops - 1, sub)[...].astype(F32)
        self.own(w, self.place.dp, self.place.core, sub)[...] = total.astype(BF)
        self.over(w, sub).start()

    def crossed(self, w, sub):
        self.over(w, sub).wait_recv()
        value = self.own(w, self.place.dp, self.place.core, sub)[...].astype(F32)
        there = self.cut(self.sums[w].at[self.place.core], w, sub)
        there[...] = (value + there[...].astype(F32)).astype(BF)
        self.total(w, sub).start()

    def arrived(self, w, sub):
        self.total(w, sub).wait_recv()

    def drain(self, w):
        for sub in range(SUBS[w]):
            self.pairs(w, sub).wait_send()
            sent = self.cut(self.grads[w].at[pl.ds(0, self.place.count - 1), self.place.core], w, sub)
            describe(
                sent, sent, self.ring_s.at[LANES[w] + sub], self.mate_r.at[LANES[w] + sub], self.place.mate
            ).wait_send()
            self.over(w, sub).wait_send()
            self.total(w, sub).wait_send()

    def ticks(self, w, t, subs):
        return [
            partial(self.tick, w, sub, way, t)
            for sub in subs
            for way, hops in enumerate(self.place.hops)
            if t < hops
        ]


def half_lanes(hd):
    lane = lax.broadcasted_iota(jnp.int32, (1, 128), 1)
    return (lane < 64) if hd == 0 else (lane >= 64)


def document_lanes(documents):
    lane = lax.broadcasted_iota(jnp.int32, documents.shape, 1) % 64
    same = jnp.logical_and(documents == lane.astype(F32), lane < 8)
    return jnp.where(same, 1.0, 0.0).astype(BF)


def marked_keys(keys, marked):
    hidden = ((1.0 - marked.astype(F32)) * NEGATIVE).astype(BF)
    return [jnp.where(half_lanes(hd), keys, hidden) for hd in range(2)]


def columns_of(hp):
    first = (hp // 3) * (3 * HALF) + (hp % 3) * 128
    return [span(first + part * HALF, 128, 128) for part in range(3)]


def attend_pair(hp, qkv, marked, causal, out, lse, scores, tick):
    cq, ck, cv = columns_of(hp)
    vt = qkv[:, cv].T
    ones = jnp.ones((8, vt.shape[1]), BF)
    keys = marked_keys(qkv[:, ck], marked[...])
    values = [jnp.concatenate([vt[hd * 64 : (hd + 1) * 64, :], ones], axis=0) for hd in range(2)]
    def rows_of(n):
        return slice(n * BLK, (n + 1) * BLK)

    def score(i, hd):
        kept = rows_of(hd)
        query = jnp.where(half_lanes(hd), qkv[rows_of(i), cq], marked[rows_of(i), :])
        top = None
        for j in range(i + 1):
            s = dot(keys[hd][rows_of(j), :], query, NT)
            if i == j:
                s = s + causal[...]
            scores[rows_of(j), kept] = s
            best = jnp.max(s, axis=0, keepdims=True)
            top = best if top is None else jnp.maximum(top, best)
        return top

    def weigh(i, hd, top):
        parts = [
            jnp.exp(scores[rows_of(j), rows_of(hd)] - top).astype(BF) for j in range(i + 1)
        ]
        return i, hd, top, parts

    outs = []

    def collect(i, hd, top, parts):
        acc = None
        for j, p in enumerate(parts):
            term = dot(values[hd][:, rows_of(j)], p, NN)
            acc = term if acc is None else acc + term
        total = acc[64:65, :]
        lse[pl.ds(hp * 2 + hd, 1), rows_of(i)] = top + jnp.log(total)
        outs.append(acc[0:64, :] * (1.0 / total))
        if hd == 1:
            out[rows_of(i), span(hp * 128, 128, 128)] = (
                jnp.concatenate(outs, axis=0).T.astype(BF)
            )
            outs[:] = []

    chains = [(i, hd) for i in range(qkv.shape[0] // BLK) for hd in range(2)]
    tick(0)
    top = score(*chains[0])
    behind = None
    for n, (i, hd) in enumerate(chains):
        after = None
        if n + 1 < len(chains):
            if hd == 1:
                tick(i + 1)
            after = score(*chains[n + 1])
        if behind is not None:
            collect(*behind)
        behind = weigh(i, hd, top)
        top = after
    collect(*behind)


def attend_back_pair(hp, qkv, marked, causal, out, upstream, lse, sums, tick):
    cq, ck, cv = columns_of(hp)
    co = span(hp * 128, 128, 128)
    in_v, in_k = slice(0, 128), slice(128, 256)
    kt = qkv[:, ck].T
    keys = marked_keys(qkv[:, ck], marked[...])
    def rows_of(n):
        return slice(n * BLK, (n + 1) * BLK)

    def operands(i):
        qb = qkv[rows_of(i), cq]
        db = upstream[rows_of(i), co]
        none = jnp.zeros_like(qb)
        prod = (db.astype(F32) * out[rows_of(i), co].astype(F32)).T
        queries = [jnp.where(half_lanes(hd), qb, marked[rows_of(i), :]) for hd in range(2)]
        grads = [jnp.where(half_lanes(hd), db, none) for hd in range(2)]
        return (
            queries,
            grads,
            [jnp.sum(prod[hd * 64 : (hd + 1) * 64, :], axis=0, keepdims=True) for hd in range(2)],
            [lse[pl.ds(hp * 2 + hd, 1), rows_of(i)] for hd in range(2)],
            jnp.concatenate([jnp.where(half_lanes(hd), qb, none) for hd in range(2)], axis=0),
            jnp.concatenate(grads, axis=0),
        )

    def products(n, ops):
        i, j = blocks[n]
        kept = slice((1 + n % 2) * BLK, (2 + n % 2) * BLK)
        for hd in range(2):
            s = dot(keys[hd][rows_of(j), :], ops[0][hd], NT)
            sums[rows_of(hd), kept] = s + causal[...] if i == j else s
            sums[rows_of(2 + hd), kept] = dot(qkv[rows_of(j), cv], ops[1][hd], NT)

    blocks = [(i, j) for i in range(qkv.shape[0] // BLK) for j in range(i + 1)]
    tick(0)
    ops = operands(0)
    products(0, ops)
    dqs = [None, None]

    def gather_block(i, j, now, ps, dss):
        for hd in range(2):
            term = dot(kt[hd * 64 : (hd + 1) * 64, rows_of(j)], dss[hd], NN)
            dqs[hd] = term if dqs[hd] is None else dqs[hd] + term
        pv = dot(jnp.concatenate(ps, axis=1), now[5], NN)
        pk = dot(jnp.concatenate(dss, axis=1), now[4], NN)
        if i == j:
            sums[rows_of(j), in_v] = pv
            sums[rows_of(j), in_k] = pk
            low = jnp.concatenate(dqs, axis=0).T.astype(BF).astype(F32)
            qkv[rows_of(i), cq] = (low * (1.0 / math.sqrt(HD))).astype(BF)
            dqs[:] = [None, None]
        else:
            sums[rows_of(j), in_v] += pv
            sums[rows_of(j), in_k] += pk

    behind = None
    for n, (i, j) in enumerate(blocks):
        now = ops
        kept = slice((1 + n % 2) * BLK, (2 + n % 2) * BLK)
        if n + 1 < len(blocks):
            if blocks[n + 1][1] == 0:
                tick(i + 1)
                ops = operands(i + 1)
            products(n + 1, ops)
        if behind is not None:
            gather_block(*behind)
        ps, dss = [], []
        for hd in range(2):
            p = jnp.exp(sums[rows_of(hd), kept] - now[3][hd])
            ps.append(p.astype(BF))
            dss.append((p * (sums[rows_of(2 + hd), kept] - now[2][hd])).astype(BF))
        behind = (i, j, now, ps, dss)
    gather_block(*behind)
    qkv[:, ck] = sums[:, in_k].astype(BF)
    qkv[:, cv] = sums[:, in_v].astype(BF)


def normalised(values):
    center = values - jnp.mean(values, axis=-1, keepdims=True)
    inverse = lax.rsqrt(jnp.mean(center * center, axis=-1, keepdims=True) + NORM_EPS)
    return center * inverse, inverse


def norm_grad(values, gain, upstream):
    hat, inverse = normalised(values)
    scaled = upstream * gain
    first = jnp.mean(scaled, axis=-1, keepdims=True)
    second = jnp.mean(scaled * hat, axis=-1, keepdims=True)
    return (
        inverse * (scaled - first - hat * second),
        jnp.sum(upstream * hat, axis=0, keepdims=True),
        jnp.sum(upstream, axis=0, keepdims=True),
    )


def gelu_both(u):
    inner = math.sqrt(2.0 / math.pi)
    cubic = inner * 0.044715
    square = u * u
    half = 0.5 + 0.5 * jnp.tanh(u * (inner + cubic * square))
    value = u * half
    return value, half + value * (1.0 - half) * (2.0 * inner + 6.0 * cubic * square)


def softmax(values):
    e = jnp.exp(values - jnp.max(values, axis=-1, keepdims=True))
    return e * (1.0 / jnp.sum(e, axis=-1, keepdims=True))


def whole(ref):
    return ref[...].reshape(-1, ref.shape[-1])


VEC_PLACES = (("g1", D), ("b1", D), ("bq", D), ("bv", D), ("bo", D), ("g2", D), ("b2", D), ("bf1", FF), ("bf2", D))
VEC_ROW = {name: row for row, (name, _) in enumerate(VEC_PLACES)}
VEC_SIZE = dict(VEC_PLACES)


def block_kernel(count, *refs):
    inputs, teacher, segments, masters, vec_ref = refs[0], refs[1], refs[2], refs[3:7], refs[7]
    sums, vec_sum, norm_ref, out_rows, back_rows = refs[8:12], refs[12], refs[13], refs[14], refs[15]
    (
        full0, full1, full2, full3, x, h1, qkv, att, x1, h2, act, slope, dy, low, sent, shrink_grads,
        shr_mate, shr_slot, lse, segs, seg_stage, marked, causal,
        vec_stage, vec_all, vec, gvec, vec_out, vec_buf, vec_mine, vec_seq, sq_mine, sq_buf,
        load_sem, g_ring_s, g_ring_r, g_mate_s, g_mate_r, g_cross_s, g_cross_r,
        s_mate_s, s_mate_r, s_ring_s, s_ring_r, s_cross_s, s_cross_r, s_total_s, s_total_r,
        row_s, row_r, row_l, vec_s, vec_r, free,
    ) = refs[16:]
    full = (full0, full1, full2, full3)
    place = Place(count)
    ready = place.greet()
    length = x.shape[0]
    blocks = length // BLK
    scale = 1.0 / math.sqrt(HD)

    def rows(i):
        return span(i * BLK, BLK, BLK)

    loads, pieces, used = [], [], [0, 0]
    for w in (MIX, OUT, EXP, SHR):
        height, width = masters[w].shape
        for column in range(0, width, D):
            which = 0 if used[0] + height <= length else 1
            where = (dy, x1)[which].at[pl.ds(used[which], height)]
            used[which] += height
            source = masters[w].at[:, pl.ds(column, D)]
            loads.append(local(source, where, load_sem.at[len(loads)]))
            pieces.append((w, column, where))

    def stage(w):
        for load, (owner, column, where) in zip(loads, pieces):
            if owner == w:
                load.wait()
                piece = where[...].astype(BF).reshape(full[w].shape[1:3] + (D,))
                if w == MIX:
                    for part in range(2):
                        c = slice(part * HALF, (part + 1) * HALF)
                        there = pl.ds(part * 3 * HALF + column // 2, HALF)
                        full[w][place.dp, :, :, there] = piece[:, :, c]
                else:
                    full[w][place.dp, :, :, pl.ds(column, D)] = piece

    gather = Gather(place, full, (g_ring_s, g_ring_r, g_mate_s, g_mate_r, g_cross_s, g_cross_r))
    stage(MIX)
    ready()
    gather.start(MIX)

    me = rows(place.seq)
    three, seven = pl.ds(0, 3), pl.ds(0, count - 1)
    most = pl.ds(0, 3 * BLK)

    def group(n, sent, received):
        return Group(row_s.at[n], row_r.at[n], sent, received, place.mate)

    row_in = group(0, inputs.at[three], x.at[most])
    seg_in = group(1, seg_stage.at[three], segs.at[three])
    teach_in = group(2, teacher.at[three], low.at[most])
    out_go = group(3, out_rows.at[three], out_rows.at[three])
    back_go = group(4, back_rows.at[three], back_rows.at[three])
    seq_go = group(5, vec_seq.at[three], vec_seq.at[three])
    vec_in = Group(vec_s.at[0], vec_r.at[0], vec_all.at[seven], vec_all.at[seven], place.mate)
    vec_go = Group(vec_s.at[1], vec_r.at[1], vec_buf.at[seven], vec_buf.at[seven], place.mate)
    sq_go = Group(vec_s.at[2], vec_r.at[2], sq_buf.at[seven], sq_buf.at[seven], place.mate)
    for k in (2, 3, 1):
        peer = place.kin(k)
        row_in.start(inputs.at[peer[1]], x.at[me], peer)
    row_local = local(inputs.at[place.seq], x.at[me], row_l.at[0])
    seg_stage[...] = jnp.broadcast_to(segments[...][:, None, :], seg_stage.shape)
    vec_stage[...] = jnp.concatenate(
        [vec_ref[...].astype(BF).astype(F32), jnp.zeros((VROWS - vec_ref.shape[0], 128), F32)],
        axis=0,
    )
    for k in range(1, count):
        vec_in.start(vec_stage, vec_all.at[place.dp], place.dp_peer(k))
    for k in (2, 3, 1):
        peer = place.kin(k)
        seg_in.start(seg_stage.at[peer[1]], segs.at[place.seq], peer)
    for k in (2, 3, 1):
        peer = place.kin(k)
        teach_in.start(teacher.at[peer[1]], low.at[me], peer)
    segs[place.seq] = seg_stage[place.seq]
    vec_all[place.dp] = vec_stage[...]
    teach_local = local(teacher.at[place.seq], low.at[me], row_l.at[1])
    for w in (OUT, EXP, SHR):
        stage(w)

    def ring_steps(w, t):
        return [
            partial(gather.tick, w, lane, way, t)
            for lane in range(len(gather.lanes(w)))
            for way in range(2)
            if t <= place.hops[way]
        ]

    def relays(w, t):
        return [partial(gather.relay, w, way, t) for way in range(2) if 1 <= t <= place.hops[way]]

    far = place.hops[0]
    for t in range(1, far + 1):
        for step in ring_steps(MIX, t):
            step()
        if t == far - 2:
            gather.start(OUT)
        if t == far - 1:
            gather.start(EXP)
    for step in ring_steps(OUT, 1):
        step()

    vec_in.wait_recv()
    per = vec_ref.shape[0]
    flat = 0
    for name, size in VEC_PLACES:
        parts = []
        for r in range(flat, flat + size // 128):
            parts.append(vec_all[r // per, r % per : r % per + 1, :])
        vec[VEC_ROW[name] : VEC_ROW[name] + 1, 0:size] = jnp.concatenate(parts, axis=1)
        flat += size // 128

    def of(name):
        return vec[VEC_ROW[name] : VEC_ROW[name] + 1, 0 : VEC_SIZE[name]]

    def add_grad(name, term, start=0):
        gvec[VEC_ROW[name] : VEC_ROW[name] + 1, start : start + term.shape[1]] += term

    gvec[...] = jnp.zeros_like(gvec)
    row_local.wait()
    row_in.wait_recv()
    seg_in.wait_recv()

    for s in range(4):
        documents = jnp.concatenate([segs[s].astype(F32)] * 16, axis=0).T
        marked[s * BLK : (s + 1) * BLK, :] = document_lanes(documents)
    earlier = lax.broadcasted_iota(jnp.int32, (BLK, BLK), 0) <= lax.broadcasted_iota(
        jnp.int32, (BLK, BLK), 1
    )
    causal[...] = jnp.where(earlier, 0.0, NEGATIVE)

    def first_norm(i, _):
        hat, _ = normalised(x[rows(i), :].astype(F32))
        h1[rows(i), :] = (hat * of("g1") + of("b1")).astype(BF)
        return 0

    lax.fori_loop(0, blocks, first_norm, 0)
    gather.arrived(MIX)

    def lane(w, number, t):
        return [partial(gather.tick, w, number, way, t) for way in range(2) if t <= place.hops[way]]

    in_project = spread(
        [[], [], lane(EXP, 0, 1), [], [], lane(EXP, 1, 1), [], lane(OUT, 0, 2)],
        2,
    )
    in_forward = spread(
        [
            [],
            lane(EXP, 0, 2),
            lane(EXP, 1, 2) + lane(OUT, 0, 3),
            [],
            lane(EXP, 0, 3) + lane(OUT, 0, 4),
            lane(EXP, 1, 3) + [partial(gather.start, SHR)],
        ],
        1,
    )
    in_middle = spread([[], lane(EXP, 0, 4), [], lane(EXP, 1, 4)], 1)
    before_expand = relays(EXP, 1) + relays(EXP, 2) + lane(SHR, 0, 1) + relays(EXP, 3)
    before_expand += lane(SHR, 1, 1) + relays(EXP, 4)
    in_expand = spread(
        [
            lane(SHR, 2, 1), lane(SHR, 0, 2),
            [], lane(SHR, 1, 2),
            lane(SHR, 2, 2), lane(SHR, 0, 3),
            lane(SHR, 1, 3), [],
        ],
        2,
    )
    after_expand = lane(SHR, 2, 3) + lane(SHR, 0, 4) + lane(SHR, 1, 4) + lane(SHR, 2, 4)
    for t in range(1, far + 1):
        after_expand += relays(SHR, t)

    def project(i, _):
        in_project(i, 0)
        value = dot(h1[rows(i), :], whole(full[MIX]), NN)
        for part in range(2):
            c = slice(part * HALF, (part + 1) * HALF)
            q, k, v = (
                slice(part * 3 * HALF + n * HALF, part * 3 * HALF + (n + 1) * HALF) for n in range(3)
            )
            qkv[rows(i), q] = ((value[:, q] + of("bq")[:, c]) * scale).astype(BF)
            qkv[rows(i), k] = value[:, k].astype(BF)
            qkv[rows(i), v] = (value[:, v] + of("bv")[:, c]).astype(BF)
        in_project(i, 1)
        return 0

    lax.fori_loop(0, blocks, project, 0)
    def forward_pair(hp, _):
        attend_pair(
            hp,
            qkv,
            marked,
            causal,
            att,
            lse,
            dy,
            lambda i: in_forward(hp, 0) if i == 0 else None,
        )
        return 0

    lax.fori_loop(0, PAIRS, forward_pair, 0)
    def middle(i, _):
        in_middle(i, 0)
        value = x[rows(i), :].astype(F32) + dot(att[rows(i), :], whole(full[OUT]), NN) + of("bo")
        x1[rows(i), :] = value
        hat, _ = normalised(value)
        h2[rows(i), :] = (hat * of("g2") + of("b2")).astype(BF)
        return 0

    gather.arrived(OUT)
    lax.fori_loop(0, blocks, middle, 0)
    teach_local.wait()
    teach_in.wait_recv()

    def target(i, _):
        dy[rows(i), :] = softmax(low[rows(i), :].astype(F32))
        return 0

    for tick in before_expand[:6]:
        tick()
    lax.fori_loop(0, blocks, target, 0)
    for tick in before_expand[6:]:
        tick()
    gather.arrived(EXP)

    def expand(i, _):
        for n in range(FF // EXPAND_TILE):
            if n % 2 == 0:
                in_expand(i, n // 2)
            c = slice(n * EXPAND_TILE, (n + 1) * EXPAND_TILE)
            weight = full[EXP][:, :, :, c].reshape(D, EXPAND_TILE)
            u = dot(h2[rows(i), :], weight, NN) + vec[VEC_ROW["bf1"] : VEC_ROW["bf1"] + 1, c]
            a, s = gelu_both(u)
            act[rows(i), c] = a.astype(BF)
            slope[rows(i), c] = s.astype(BF)
        return 0

    lax.fori_loop(0, blocks, expand, 0)
    for tick in after_expand:
        tick()
    gather.arrived(SHR)

    def shrink(i, _):
        value = x1[rows(i), :] + dot(act[rows(i), :], whole(full[SHR]), NN) + of("bf2")
        sent[rows(i), :] = value.astype(BF)
        grad = D * (softmax(value) - dy[rows(i), :])
        dy[rows(i), :] = grad
        low[rows(i), :] = grad.astype(BF)
        add_grad("bf2", jnp.sum(grad, axis=0, keepdims=True))
        return 0

    lax.fori_loop(0, blocks, shrink, 0)
    for w in (MIX, OUT, EXP, SHR):
        gather.drain(w)

    def send_rows(rows_out, copies, k, first=0, size=BLK):
        peer = place.kin(k)
        source = sent.at[span(peer[1] * BLK + first, size, 128)]
        copies.start(source, rows_out.at[place.seq, pl.ds(first, size)], peer)

    out_local = local(sent.at[me], out_rows.at[place.seq], row_l.at[2])
    for k in (2, 3, 1):
        send_rows(out_rows, out_go, k)

    half, some = full[MIX].shape[2], count // 2

    def part_of(buffer, w, where):
        if w == EXP:
            return act.at[where]
        return slope.at[where, pl.ds(3 * D, D)]

    def third(group, n):
        return slope.at[span(n * 3 * half, 3 * half, 16), span(group * D, D, 128)]

    def mates(w, owner):
        if w == SHR:
            return shr_mate.at[owner]
        if w == MIX:
            return third(owner // (count // 2), owner % (count // 2))
        return part_of(act, w, span(owner * half, half, 16))

    def slots(w, t):
        if w == SHR:
            return shr_slot.at[t]
        if w == MIX:
            return third(2, t)
        return part_of(act, w, span((count + t) * half, half, 16))

    scatter = Scatter(
        place,
        (full3, full1, full2, shrink_grads),
        mates,
        slots,
        sums,
        (s_mate_s, s_mate_r, s_ring_s, s_ring_r, s_cross_s, s_cross_r, s_total_s, s_total_r),
    )

    def offer(which):
        for n, peer in enumerate((place.mate,) + place.sides):
            pl.semaphore_signal(
                free.at[3 * which + n], inc=1, device_id=peer, device_id_type=MESH
            )

    def accept(which, which_sides):
        for n in range(1, 3) if which_sides else range(1):
            pl.semaphore_wait(free.at[3 * which + n], 1)

    def shrink_grad(n, _):
        value = dot(act[:, span(n * D, D, 128)], low[...], TN).astype(BF)
        shrink_grads[pl.ds(2 * n, 2)] = value.reshape((2,) + shrink_grads.shape[1:])
        for owner in range(2):
            for sub in range(2):
                scatter.pair(SHR, sub, 2 * n + owner).start()
        return 0

    lax.fori_loop(0, FF // D, shrink_grad, 0)
    offer(0)
    for sub in range(2):
        scatter.start(SHR, sub)

    def hop(w, t, sub):
        return scatter.ticks(w, t, (sub,))

    def end(w, sub):
        return [partial(scatter.finish, w, sub)]

    in_middle_back = spread([hop(SHR, 1, 0), [], hop(SHR, 1, 1), []], 1)
    in_expand_grad = spread([hop(SHR, 2, 0), [], hop(SHR, 2, 1), []], 1)
    in_upstream = spread(
        [[partial(scatter.start, EXP, 0)] + hop(SHR, 3, 0), [], [partial(scatter.start, EXP, 1)], []],
        1,
    )
    in_backward = spread(
        [
            hop(SHR, 3, 1), [], [], [partial(scatter.start, OUT, 0)],
            hop(EXP, 1, 0), [], [], [],
            hop(EXP, 1, 1) + end(SHR, 0), [], [], hop(EXP, 2, 0) + hop(OUT, 1, 0) + end(SHR, 1),
            hop(EXP, 2, 1), [], [], [partial(scatter.start, MIX, 0)] + hop(OUT, 2, 0),
            hop(EXP, 3, 0), [], [], hop(EXP, 3, 1) + hop(OUT, 3, 0),
            hop(MIX, 1, 0), [], [], end(EXP, 0),
        ],
        4,
    )

    def expand_back(i, _):
        for n in range(FF // D):
            c = slice(n * D, (n + 1) * D)
            weight = full[SHR][2 * n : 2 * n + 2].reshape(D, D)
            da = dot(low[rows(i), :], weight, NT).astype(BF).astype(F32)
            du = (da * slope[rows(i), c].astype(F32)).astype(BF)
            slope[rows(i), c] = du
            gvec[VEC_ROW["bf1"] : VEC_ROW["bf1"] + 1, c] += jnp.sum(
                du.astype(F32), axis=0, keepdims=True
            )
        return 0

    lax.fori_loop(0, blocks, expand_back, 0)


    def middle_back(i, _):
        in_middle_back(i, 0)
        upstream = dot(slope[rows(i), :], whole(full[EXP]), NT)
        part, gain, shift = norm_grad(x1[rows(i), :], of("g2"), upstream)
        value = dy[rows(i), :] + part
        dy[rows(i), :] = value
        low[rows(i), :] = value.astype(BF)
        add_grad("g2", gain)
        add_grad("b2", shift)
        add_grad("bo", jnp.sum(value, axis=0, keepdims=True))
        return 0

    lax.fori_loop(0, blocks, middle_back, 0)
    accept(0, False)

    def expand_grad(n, _):
        in_expand_grad(n, 0)
        c = span(n * D, D, 128)
        for owners in range(2):
            value = dot(h2[:, owners * HALF : (owners + 1) * HALF], slope[:, c], TN).astype(BF)
            full2[owners * some : (owners + 1) * some, :, :, c] = value.reshape(
                (some,) + full2.shape[1:3] + (D,)
            )
        pl.when(n == FF // D // 2 - 1)(lambda: scatter.hand(EXP, 0))
        return 0

    lax.fori_loop(0, FF // D, expand_grad, 0)
    scatter.hand(EXP, 1)
    offer(1)
    accept(0, True)

    def upstream_rows(i, _):
        in_upstream(i, 0)
        h2[rows(i), :] = dot(low[rows(i), :], whole(full[OUT]), NT).astype(BF)
        return 0

    lax.fori_loop(0, blocks, upstream_rows, 0)
    for owners in range(2):
        value = dot(att[:, owners * HALF : (owners + 1) * HALF], low[...], TN).astype(BF)
        full1[owners * some : (owners + 1) * some] = value.reshape((some,) + full1.shape[1:])
    accept(1, False)
    scatter.hand(OUT, 0)
    accept(1, True)
    def backward_part(part, _):
        def backward_pair(hp, _):
            def tick(i):
                for n in range(2):
                    first = n * (PAIRS // 2)
                    pl.when(part == n)(
                        lambda first=first: in_backward(hp + first, i, first, first + PAIRS // 2)
                    )

            number = part * (PAIRS // 2) + hp
            attend_back_pair(
                number, qkv, marked, causal, att, h2, lse, x1, tick
            )
            return 0

        lax.fori_loop(0, PAIRS // 2, backward_pair, 0)
        c = span(part * 3 * HALF, 3 * HALF, 128)
        for owners in range(2):
            mine = slice(owners * HALF, (owners + 1) * HALF)
            value = dot(h1[:, mine], qkv[:, c], TN).astype(BF)
            for n in range(3):
                there = span(part * HALF, HALF, 128)
                full3[owners * some : (owners + 1) * some, :, n * half : (n + 1) * half, there] = (
                    value[:, n * HALF : (n + 1) * HALF].reshape(some, 2, half, HALF)
                )
        pl.when(part == 0)(lambda: scatter.hand(MIX, 0))
        pl.when(part == 1)(lambda: [scatter.hand(MIX, sub) for sub in range(1, 4)] and None)
        return 0

    lax.fori_loop(0, 2, backward_part, 0)
    for sub in range(1, 4):
        scatter.start(MIX, sub)
    for tick in hop(MIX, 2, 0) + end(EXP, 1) + end(OUT, 0):
        tick()
    out_local.wait()
    out_go.wait_send()
    in_input_back = spread([[], [], hop(MIX, 1, 1), hop(MIX, 1, 2) + hop(MIX, 1, 3)], 1)
    late = BLK // 2

    def input_back(j, _):
        in_input_back(j, 0)
        core = place.core + (1 - 2 * place.core) * (j % 2)
        i = 2 * (place.x + (1 - 2 * place.x) * (1 - j // 2)) + core
        d = qkv[rows(i), :]
        part, gain, shift = norm_grad(
            x[rows(i), :].astype(F32), of("g1"), dot(d, whole(full[MIX]), NT)
        )
        sent[rows(i), :] = (dy[rows(i), :] + part).astype(BF)
        add_grad("g1", gain)
        add_grad("b1", shift)
        for half_of in range(2):
            first = half_of * 3 * HALF
            for name, start in (("bq", first), ("bv", first + 2 * HALF)):
                term = d[:, start : start + HALF].astype(F32)
                add_grad(name, jnp.sum(term, axis=0, keepdims=True), half_of * HALF)
        pl.when(j == 0)(lambda: send_rows(back_rows, back_go, 2))
        pl.when(j == 1)(lambda: send_rows(back_rows, back_go, 3, 0, late))
        pl.when(j == 3)(lambda: send_rows(back_rows, back_go, 1))
        return 0

    lax.fori_loop(0, blocks, input_back, 0)
    back_local = local(sent.at[me], back_rows.at[place.seq], row_l.at[3])
    flat = 0
    vec_out[...] = jnp.zeros_like(vec_out)
    for name, size in VEC_PLACES:
        for n in range(size // 128):
            r = flat + n
            vec_out[r // per, r % per : r % per + 1, :] = gvec[
                VEC_ROW[name] : VEC_ROW[name] + 1, n * 128 : (n + 1) * 128
            ]
        flat += size // 128
    for k in range(1, count):
        peer = place.dp_peer(k)
        vec_go.start(vec_out.at[peer[0]], vec_buf.at[place.dp], peer)
    vec_buf[place.dp] = vec_out[place.dp]
    for tick in hop(MIX, 3, 0) + hop(MIX, 2, 1) + hop(MIX, 2, 2) + hop(MIX, 2, 3):
        tick()
    for w, sub in ((SHR, 0), (SHR, 1), (EXP, 0)):
        scatter.crossed(w, sub)
    for tick in hop(MIX, 3, 1) + hop(MIX, 3, 2) + hop(MIX, 3, 3) + end(MIX, 0):
        tick()
    vec_go.wait_recv()
    vec_mine[...] = jnp.sum(vec_buf[...], axis=0)
    vec_seq[place.seq] = vec_mine[...]
    for k in (2, 3, 1):
        seq_go.start(vec_mine, vec_seq.at[place.seq], place.kin(k))
    for sub in range(1, 4):
        scatter.finish(MIX, sub)
    send_rows(back_rows, back_go, 3, late, BLK - late)
    for w, sub in ((EXP, 1), (OUT, 0), (MIX, 0)):
        scatter.crossed(w, sub)

    def squares_of(w, part, total):
        c = slice(None) if part is None else slice(part * HALF, (part + 1) * HALF)
        for core in range(2):
            value = sums[w][core, :, c].astype(F32)
            term = jnp.sum(value * value, axis=0, keepdims=True)
            for n in range(term.shape[1] // 128):
                total = total + term[:, n * 128 : (n + 1) * 128]
        return total

    squares = jnp.zeros((1, 128), F32)
    for w in (SHR, EXP, OUT):
        for sub in range(SUBS[w]):
            scatter.arrived(w, sub)
        squares = squares_of(w, None, squares)
    scatter.arrived(MIX, 0)
    squares = squares_of(MIX, 0, squares)
    seq_go.wait_recv()
    vec_total = jnp.sum(vec_seq[...], axis=0)
    vec_sum[...] = vec_total
    squares = squares + jnp.sum(vec_total * vec_total, axis=0, keepdims=True)
    for sub in range(1, 4):
        scatter.crossed(MIX, sub)
    for sub in range(1, 4):
        scatter.arrived(MIX, sub)
    squares = squares_of(MIX, 1, squares)
    sq_mine[...] = jnp.broadcast_to(squares, sq_mine.shape)
    sq_buf[place.dp] = sq_mine[...]
    for k in range(1, count):
        sq_go.start(sq_mine, sq_buf.at[place.dp], place.dp_peer(k))
    for w in (MIX, OUT, EXP, SHR):
        scatter.drain(w)
    for copies in (row_in, seg_in, teach_in, vec_in, vec_go, seq_go, back_go, sq_go):
        copies.wait_send()
    back_local.wait()
    out_go.wait_recv()
    back_go.wait_recv()
    sq_go.wait_recv()
    total = jnp.sum(jnp.sum(sq_buf[...], axis=0), axis=1, keepdims=True)
    norm_ref[...] = jnp.broadcast_to(jnp.sqrt(total), norm_ref.shape)


def block_call(count, inputs, teacher, segments, masters, vectors):
    rows, local_len, features = inputs.shape
    length = rows * local_len
    halves = [(2, m.shape[0] // 2, m.shape[1]) for m in masters]
    any_spec = pl.BlockSpec(memory_space=pl.ANY)
    vmem = pl.BlockSpec(memory_space=pltpu.VMEM)
    row_shape = jax.ShapeDtypeStruct(inputs.shape, BF)
    folded = [(2, 3 * halves[MIX][1], D)] + halves[1:]
    out_shape = [jax.ShapeDtypeStruct(h, BF) for h in folded]
    out_shape += [
        jax.ShapeDtypeStruct((VROWS, 128), F32),
        jax.ShapeDtypeStruct((8, 128), F32),
        row_shape,
        row_shape,
    ]

    def low(*shape):
        return pltpu.VMEM(shape, BF)

    def wide(*shape):
        return pltpu.VMEM(shape, F32)

    def dma(*shape):
        return pltpu.SemaphoreType.DMA(shape)

    shrink_half = halves[SHR][1:]
    buffers = [low(count, *h) for h in halves]
    buffers += [
        low(length, D),
        low(length, D),
        low(length, 3 * D),
        low(length, D),
        wide(length, D),
        low(length, D),
        low(length, FF),
        low(length, FF),
        wide(length, D),
        low(length, D),
        low(length, D),
        low(count, *halves[SHR]),
        low(count, *shrink_half),
        low(count - 1, *shrink_half),
    ]
    buffers += [
        wide(16, length),
        pltpu.VMEM((rows, 8, local_len), jnp.int32),
        pltpu.VMEM((rows, 8, local_len), jnp.int32),
        low(length, 128),
        wide(BLK, BLK),
        wide(VROWS, 128),
        wide(count, VROWS, 128),
        wide(16, FF),
        wide(16, FF),
        wide(count, VROWS, 128),
        wide(count, VROWS, 128),
        wide(VROWS, 128),
        wide(4, VROWS, 128),
        wide(8, 128),
        wide(count, 8, 128),
    ]
    hops = count - 1
    sems = [dma(9), dma(4), dma(8, hops), dma(4), dma(4), dma(2), dma(2, hops)]
    sems += [dma(9), dma(9), dma(9), dma(9, hops)] + [dma(9)] * 4
    sems += [dma(6), dma(6), dma(4), dma(3), dma(3)]
    sems.append(pltpu.SemaphoreType.REGULAR((6,)))
    return pl.pallas_call(
        partial(block_kernel, count),
        out_shape=out_shape,
        in_specs=[any_spec] * 2 + [vmem] + [any_spec] * 4 + [vmem],
        out_specs=[vmem] * 6 + [any_spec] * 2,
        scratch_shapes=buffers + sems,
        compiler_params=pltpu.CompilerParams(
            collective_id=1, has_side_effects=True, vmem_limit_bytes=VMEM_BYTES
        ),
    )(inputs, teacher, segments, *masters, vectors.reshape(-1, 128))


def update_kernel(steps, norm_ref, *refs):
    sums, masters, firsts, seconds = refs[0:5], refs[5:10], refs[10:15], refs[15:20]
    out_from, back_from = refs[20:22]
    updated, first_out, second_out = refs[22:27], refs[27:32], refs[32:37]
    out_to, back_to, norm_out, held, sem = refs[37:42]
    step = pl.program_id(0)
    norm = norm_ref[0:1, 0:1]
    factor = clip_level() / jnp.maximum(norm, clip_level())
    takes = [
        pltpu.make_async_copy(rows, held.at[n], sem.at[n])
        for n, rows in enumerate((out_from, back_from))
    ]
    gives = [
        pltpu.make_async_copy(held.at[n], rows, sem.at[2 + n])
        for n, rows in enumerate((out_to, back_to))
    ]

    @pl.when(step == 0)
    def _():
        for copy in takes:
            copy.start()
        norm_out[...] = norm

    @pl.when(step == steps // 2)
    def _():
        for take, give in zip(takes, gives):
            take.wait()
            give.start()

    def apply(n, gradient):
        results = adamw(
            masters[n][...], firsts[n][...], seconds[n][...], gradient * factor, learn_rates()[n]
        )
        updated[n][...], first_out[n][...], second_out[n][...] = results

    for w in range(4):
        gradient = sums[w][...].astype(F32)
        if w == MIX:
            gradient = jnp.concatenate([gradient[n] for n in range(3)], axis=1)
        apply(w, gradient)

    @pl.when(step == 0)
    def _():
        apply(4, sums[4][0 : masters[4].shape[0], :])

    @pl.when(step == steps - 1)
    def _():
        for copy in gives:
            copy.wait()


def update_call(results, masters, firsts, seconds):
    half = results[OUT].shape[1]
    parts = half // 16
    steps = 2 * parts
    mixed = results[MIX].reshape(2, 3, half, D)

    def fixed(shape):
        return pl.BlockSpec(shape, lambda i: (0,) * len(shape))

    any_spec = pl.BlockSpec(memory_space=pl.ANY)
    sum_specs, state_specs, states = [], [], []
    for master in masters[:4]:
        rows, columns = master.shape[0] // steps, master.shape[1]
        sum_specs.append(pl.BlockSpec((None, rows, columns), lambda i: (i // parts, i % parts, 0)))
        state_specs.append(pl.BlockSpec((rows, columns), lambda i: (i, 0)))
    sum_specs[MIX] = pl.BlockSpec((None, 3, 16, D), lambda i: (i // parts, 0, i % parts, 0))
    packed = (masters[4].shape[0] // 128, 128)
    state_specs.append(fixed(packed))
    sum_specs.append(fixed(results[4].shape))
    for group in (masters, firsts, seconds):
        states += list(group[:4]) + [group[4].reshape(packed)]
    out_shape = [jax.ShapeDtypeStruct(state.shape, F32) for state in states]
    out_shape += [jax.ShapeDtypeStruct(results[6].shape, BF)] * 2
    out_shape.append(jax.ShapeDtypeStruct((1, 1), F32))
    return pl.pallas_call(
        partial(update_kernel, steps),
        grid=(steps,),
        out_shape=out_shape,
        in_specs=[fixed(results[5].shape)] + sum_specs + state_specs * 3 + [any_spec] * 2,
        out_specs=state_specs * 3 + [any_spec] * 2 + [fixed((1, 1))],
        scratch_shapes=[
            pltpu.VMEM((2,) + results[6].shape, BF),
            pltpu.SemaphoreType.DMA((4,)),
        ],
        compiler_params=pltpu.CompilerParams(vmem_limit_bytes=VMEM_BYTES),
    )(results[5], mixed, *results[1:5], *states, *results[6:8])


def row_body(
    inputs,
    segments,
    teacher,
    mixing_weight,
    output_weight,
    expand_weight,
    shrink_weight,
    vectors,
    mixing_first,
    output_first,
    expand_first,
    shrink_first,
    vectors_first,
    mixing_second,
    output_second,
    expand_second,
    shrink_second,
    vectors_second,
):
    masters = (mixing_weight, output_weight, expand_weight, shrink_weight, vectors)
    firsts = (mixing_first, output_first, expand_first, shrink_first, vectors_first)
    seconds = (mixing_second, output_second, expand_second, shrink_second, vectors_second)
    results = block_call(lax.axis_size("dp"), inputs, teacher, segments, masters[:4], vectors)
    fresh = update_call(results, masters, firsts, seconds)
    states = [
        state.reshape(vectors.shape) if n % 5 == 4 else state for n, state in enumerate(fresh[:15])
    ]
    return (fresh[15], fresh[16], fresh[17].reshape(()), *states)


def whole_rows(mesh):
    return mesh.shape["seq"] == 4 and mesh.shape["dp"] == 8


def solution(mesh):
    in_specs = (
        P("dp", "seq", None),
        P("dp", "seq"),
        P("dp", "seq", None),
        P("dp", None),
        P("dp", None),
        P("dp", None),
        P("dp", None),
        P("dp"),
        P("dp", None),
        P("dp", None),
        P("dp", None),
        P("dp", None),
        P("dp"),
        P("dp", None),
        P("dp", None),
        P("dp", None),
        P("dp", None),
        P("dp"),
    )
    out_specs = (
        P("dp", "seq", None),
        P("dp", "seq", None),
        P(),
        P("dp", None),
        P("dp", None),
        P("dp", None),
        P("dp", None),
        P("dp"),
        P("dp", None),
        P("dp", None),
        P("dp", None),
        P("dp", None),
        P("dp"),
        P("dp", None),
        P("dp", None),
        P("dp", None),
        P("dp", None),
        P("dp"),
    )
    chosen = row_body if whole_rows(mesh) else body
    return jax.shard_map(chosen, mesh=mesh, in_specs=in_specs, out_specs=out_specs, check_vma=False)
```

```python
from functools import partial
import math

import jax
import jax.numpy as jnp
from jax import lax
from jax.experimental import pallas as pl
from jax.experimental.pallas import tpu as pltpu
from jax.sharding import PartitionSpec as P

D = 768
HEADS = 12
HD = 64
FF = 3072
LEN = 1024
NDOC = 8
STEP = 10


NEGATIVE = -1e30
NORM_EPS = 1e-05
BETA_ONE = 0.9
BETA_TWO = 0.999
ADAM_EPS = 1e-08
WEIGHT_DECAY = 0.01


def layer_norm(values, norm_gain, norm_shift):
    center = values - jnp.mean(values, axis=-1, keepdims=True)
    spread = jnp.mean(center * center, axis=-1, keepdims=True)
    return center * lax.rsqrt(spread + NORM_EPS) * norm_gain + norm_shift


def gelu_tanh(values):
    return jax.nn.gelu(values, approximate=True)


def split_vectors(packed):
    return jnp.split(packed, [D, 2 * D, 3 * D, 4 * D, 5 * D, 6 * D, 7 * D, 7 * D + FF])


def adamw(master, first, second, gradient, rate):
    first_new = BETA_ONE * first + (1.0 - BETA_ONE) * gradient
    second_new = BETA_TWO * second + (1.0 - BETA_TWO) * gradient * gradient
    first_hat = first_new / (1.0 - BETA_ONE**STEP)
    second_hat = second_new / (1.0 - BETA_TWO**STEP)
    updated = master - rate * (
        first_hat / (jnp.sqrt(second_hat) + ADAM_EPS) + WEIGHT_DECAY * master
    )
    return (updated, first_new, second_new)


def learn_rates():
    return (
        1.0 / math.sqrt(2 * D),
        1.0 / math.sqrt(max(1, 2 * D * NDOC // LEN)),
        1.0 / math.sqrt(D),
        1.0 / math.sqrt(FF),
        0.3,
    )


def clip_level():
    return 0.5 * math.sqrt(4 * D * D + 2 * D * FF + 8 * D + FF)


def visible(query_pos, key_pos, query_seg, key_seg):
    return (key_pos[None, :] <= query_pos[:, None]) & (key_seg[None, :] == query_seg[:, None])


def attend_rows(query_pos, key_pos, packed_args):
    queries, keys_all, values_all, query_seg, key_seg = packed_args
    scores = jnp.einsum("qhd,khd->hqk", queries, keys_all, preferred_element_type=jnp.float32)
    scores = jnp.where(visible(query_pos, key_pos, query_seg, key_seg)[None], scores, NEGATIVE)
    top_score = jnp.max(scores, axis=-1, keepdims=True)
    exponent = jnp.exp(scores - top_score)
    totals = jnp.sum(exponent, axis=-1, keepdims=True)
    probability = (exponent / totals).astype(jnp.bfloat16)
    attended = jnp.einsum(
        "hqk,khd->qhd", probability, values_all, preferred_element_type=jnp.float32
    )
    return (attended, (top_score + jnp.log(totals))[..., 0])


def attend_back(query_pos, key_pos, packed_args):
    queries, keys_all, values_all, upstream, log_totals, query_seg, key_seg = packed_args
    scores = jnp.einsum("qhd,khd->hqk", queries, keys_all, preferred_element_type=jnp.float32)
    scores = jnp.where(visible(query_pos, key_pos, query_seg, key_seg)[None], scores, NEGATIVE)
    probability = jnp.exp(scores - log_totals[..., None])
    prob_low = probability.astype(jnp.bfloat16)
    prob_grad = jnp.einsum("qhd,khd->hqk", upstream, values_all, preferred_element_type=jnp.float32)
    value_part = jnp.einsum("hqk,qhd->khd", prob_low, upstream, preferred_element_type=jnp.float32)
    score_grad = probability * (
        prob_grad - jnp.sum(probability * prob_grad, axis=-1, keepdims=True)
    )
    score_low = score_grad.astype(jnp.bfloat16)
    query_part = jnp.einsum("hqk,khd->qhd", score_low, keys_all, preferred_element_type=jnp.float32)
    key_part = jnp.einsum("hqk,qhd->khd", score_low, queries, preferred_element_type=jnp.float32)
    key_count = keys_all.shape[0]
    return (
        query_part,
        jnp.concatenate(
            [key_part.reshape(key_count, -1), value_part.reshape(key_count, -1)], axis=1
        ),
    )


def body(
    inputs,
    segments,
    teacher,
    mixing_weight,
    output_weight,
    expand_weight,
    shrink_weight,
    vectors,
    mixing_first,
    output_first,
    expand_first,
    shrink_first,
    vectors_first,
    mixing_second,
    output_second,
    expand_second,
    shrink_second,
    vectors_second,
):
    bfloat = jnp.bfloat16
    floats = jnp.float32
    seq_count, local_len, features = inputs.shape
    row_count = seq_count * local_len
    scale = 1.0 / math.sqrt(HD)
    mixing_low, output_low, expand_low, shrink_low, vectors_low = (
        lax.all_gather(mixing_weight.astype(bfloat), "dp", axis=0, tiled=True),
        lax.all_gather(output_weight.astype(bfloat), "dp", axis=0, tiled=True),
        lax.all_gather(expand_weight.astype(bfloat), "dp", axis=0, tiled=True),
        lax.all_gather(shrink_weight.astype(bfloat), "dp", axis=0, tiled=True),
        lax.all_gather(vectors.astype(bfloat), "dp", axis=0, tiled=True),
    )
    (
        gain_one,
        shift_one,
        bias_query,
        bias_value,
        bias_output,
        gain_two,
        shift_two,
        bias_expand,
        bias_shrink,
    ) = split_vectors(vectors_low.astype(floats))
    states = inputs.astype(floats).reshape(row_count, features)
    normed = layer_norm(states, gain_one, shift_one)
    normed_low = normed.astype(bfloat)
    projected = jnp.dot(normed_low, mixing_low, preferred_element_type=floats)
    query_low = ((projected[:, :features] + bias_query) * scale).astype(bfloat)
    key_low = projected[:, features : 2 * features].astype(bfloat)
    value_low = (projected[:, 2 * features :] + bias_value).astype(bfloat)
    key_all, value_all = (
        lax.all_gather(key_low.reshape(seq_count, local_len, features), "seq", axis=1, tiled=True),
        lax.all_gather(
            value_low.reshape(seq_count, local_len, features), "seq", axis=1, tiled=True
        ),
    )
    segment_all = lax.all_gather(segments, "seq", axis=1, tiled=True)
    full_len = key_all.shape[1]
    query_pos = lax.axis_index("seq") * local_len + jnp.arange(local_len, dtype=jnp.int32)
    key_pos = jnp.arange(full_len, dtype=jnp.int32)
    query_heads = query_low.reshape(seq_count, local_len, HEADS, HD)
    key_heads = key_all.reshape(seq_count, full_len, HEADS, HD)
    value_heads = value_all.reshape(seq_count, full_len, HEADS, HD)
    attended, log_totals = lax.map(
        partial(attend_rows, query_pos, key_pos),
        (query_heads, key_heads, value_heads, segments, segment_all),
    )
    attended_low = attended.reshape(row_count, features).astype(bfloat)
    middle = states + jnp.dot(attended_low, output_low, preferred_element_type=floats) + bias_output
    normed_two = layer_norm(middle, gain_two, shift_two)
    normed_two_low = normed_two.astype(bfloat)
    hidden = jnp.dot(normed_two_low, expand_low, preferred_element_type=floats) + bias_expand
    active, gelu_back = jax.vjp(gelu_tanh, hidden)
    active_low = active.astype(bfloat)
    result = middle + jnp.dot(active_low, shrink_low, preferred_element_type=floats) + bias_shrink
    block_output = result.astype(bfloat).reshape(seq_count, local_len, features)
    target_prob = jax.nn.softmax(teacher.astype(floats).reshape(row_count, features), axis=-1)
    result_grad = features * (jax.nn.softmax(result, axis=-1) - target_prob)
    result_low = result_grad.astype(bfloat)
    grad_shrink = jnp.dot(active_low.T, result_low, preferred_element_type=floats)
    grad_bias_shrink = jnp.sum(result_grad, axis=0)
    active_grad = jnp.dot(result_low, shrink_low.T, preferred_element_type=floats)
    active_round = lax.optimization_barrier(active_grad.astype(bfloat)).astype(floats)
    hidden_low = gelu_back(active_round)[0].astype(bfloat)
    grad_bias_expand = jnp.sum(hidden_low.astype(floats), axis=0)
    grad_expand = jnp.dot(normed_two_low.T, hidden_low, preferred_element_type=floats)
    normed_two_grad = jnp.dot(hidden_low, expand_low.T, preferred_element_type=floats)
    norm_two_back = jax.vjp(layer_norm, middle, gain_two, shift_two)[1]
    middle_part, grad_gain_two, grad_shift_two = norm_two_back(normed_two_grad)
    middle_grad = result_grad + middle_part
    middle_low = middle_grad.astype(bfloat)
    grad_bias_output = jnp.sum(middle_grad, axis=0)
    grad_output = jnp.dot(attended_low.T, middle_low, preferred_element_type=floats)
    attended_grad = jnp.dot(middle_low, output_low.T, preferred_element_type=floats).astype(bfloat)
    upstream_heads = attended_grad.reshape(seq_count, local_len, HEADS, HD)
    query_grad, kv_terms = lax.map(
        partial(attend_back, query_pos, key_pos),
        (query_heads, key_heads, value_heads, upstream_heads, log_totals, segments, segment_all),
    )
    kv_sums = (
        lax.psum_scatter(kv_terms.astype(jnp.bfloat16), "seq", scatter_dimension=1, tiled=True)
        .astype(jnp.float32)
        .reshape(row_count, 2 * features)
    )
    key_grad_low = kv_sums[:, :features].astype(bfloat)
    value_grad_low = kv_sums[:, features:].astype(bfloat)
    query_grad_low = query_grad.reshape(row_count, features).astype(bfloat)
    query_scaled = query_grad_low.astype(floats) * scale
    grad_bias_query = jnp.sum(query_scaled, axis=0)
    grad_bias_value = jnp.sum(value_grad_low.astype(floats), axis=0)
    projected_grad = jnp.concatenate(
        [query_scaled.astype(bfloat), key_grad_low, value_grad_low], axis=1
    )
    grad_mixing = jnp.dot(normed_low.T, projected_grad, preferred_element_type=floats)
    normed_grad = jnp.dot(projected_grad, mixing_low.T, preferred_element_type=floats)
    norm_one_back = jax.vjp(layer_norm, states, gain_one, shift_one)[1]
    states_part, grad_gain_one, grad_shift_one = norm_one_back(normed_grad)
    input_grad = (middle_grad + states_part).astype(bfloat).reshape(seq_count, local_len, features)
    grad_vectors = jnp.concatenate(
        [
            grad_gain_one,
            grad_shift_one,
            grad_bias_query,
            grad_bias_value,
            grad_bias_output,
            grad_gain_two,
            grad_shift_two,
            grad_bias_expand,
            grad_bias_shrink,
        ]
    )
    vector_rows = grad_vectors.reshape(lax.axis_size("dp"), -1)
    mixing_part, output_part, expand_part, shrink_part, vector_part = (
        lax.psum_scatter(
            grad_mixing.astype(jnp.bfloat16), "dp", scatter_dimension=0, tiled=True
        ).astype(jnp.float32),
        lax.psum_scatter(
            grad_output.astype(jnp.bfloat16), "dp", scatter_dimension=0, tiled=True
        ).astype(jnp.float32),
        lax.psum_scatter(
            grad_expand.astype(jnp.bfloat16), "dp", scatter_dimension=0, tiled=True
        ).astype(jnp.float32),
        lax.psum_scatter(
            grad_shrink.astype(jnp.bfloat16), "dp", scatter_dimension=0, tiled=True
        ).astype(jnp.float32),
        lax.psum_scatter(
            vector_rows.astype(jnp.bfloat16), "dp", scatter_dimension=0, tiled=True
        ).astype(jnp.float32),
    )
    mixing_sum, output_sum, expand_sum, shrink_sum, vector_sum = (
        lax.psum(mixing_part.astype(jnp.bfloat16), "seq").astype(jnp.float32),
        lax.psum(output_part.astype(jnp.bfloat16), "seq").astype(jnp.float32),
        lax.psum(expand_part.astype(jnp.bfloat16), "seq").astype(jnp.float32),
        lax.psum(shrink_part.astype(jnp.bfloat16), "seq").astype(jnp.float32),
        lax.psum(vector_part.astype(jnp.bfloat16), "seq").astype(jnp.float32),
    )
    vector_sum = vector_sum.reshape(-1)
    squares = (
        jnp.sum(mixing_sum * mixing_sum)
        + jnp.sum(output_sum * output_sum)
        + jnp.sum(expand_sum * expand_sum)
        + jnp.sum(shrink_sum * shrink_sum)
        + jnp.sum(vector_sum * vector_sum)
    )
    grad_norm = jnp.sqrt(lax.psum(squares, "dp"))
    clip_value = clip_level()
    factor = clip_value / jnp.maximum(grad_norm, clip_value)
    step_rates = learn_rates()
    mixing_new = adamw(
        mixing_weight, mixing_first, mixing_second, mixing_sum * factor, step_rates[0]
    )
    output_new = adamw(
        output_weight, output_first, output_second, output_sum * factor, step_rates[1]
    )
    expand_new = adamw(
        expand_weight, expand_first, expand_second, expand_sum * factor, step_rates[2]
    )
    shrink_new = adamw(
        shrink_weight, shrink_first, shrink_second, shrink_sum * factor, step_rates[3]
    )
    vectors_new = adamw(vectors, vectors_first, vectors_second, vector_sum * factor, step_rates[4])
    return (
        block_output,
        input_grad,
        grad_norm,
        mixing_new[0],
        output_new[0],
        expand_new[0],
        shrink_new[0],
        vectors_new[0],
        mixing_new[1],
        output_new[1],
        expand_new[1],
        shrink_new[1],
        vectors_new[1],
        mixing_new[2],
        output_new[2],
        expand_new[2],
        shrink_new[2],
        vectors_new[2],
    )

MESH = pl.DeviceIdType.MESH
BF = jnp.bfloat16
F32 = jnp.float32
BLK = 256
NN = ((1,), (0,))
NT = ((1,), (1,))
TN = ((0,), (0,))
VMEM_BYTES = 64 * 2**20 - 2**17
VROWS = 16
MIX, OUT, EXP, SHR = 0, 1, 2, 3
HALF = D // 2
PAIRS = D // 128
EXPAND_TILE = D
SUBS = (4, 1, 2, 2)
LANES = (0, 4, 5, 7)


def dot(left, right, dims):
    return lax.dot_general(left, right, (dims, ((), ())), preferred_element_type=F32)


class Place:
    def __init__(self, count):
        self.count = count
        self.hops = (count // 2, count - 1 - count // 2)
        self.dp = lax.axis_index("dp")
        self.seq = lax.axis_index("seq")
        odd = self.dp % 2
        self.pos = (1 - odd) * (self.dp // 2) + odd * (count - 1 - self.dp // 2)
        self.core = self.seq % 2
        self.x = self.seq // 2
        self.step = 1 - 2 * self.core
        self.sides = ((self.ahead(1), self.seq), (self.behind(1), self.seq))
        self.mate = self.kin(1)
        self.across = self.kin(2)

    def at(self, pos):
        pos = pos % self.count
        upper = pos // (self.count // 2)
        return (1 - upper) * (2 * pos) + upper * (2 * (self.count - 1 - pos) + 1)

    def ahead(self, steps):
        return self.at(self.pos + steps * self.step + self.count)

    def behind(self, steps):
        return self.at(self.pos - steps * self.step + self.count)

    def kin(self, which):
        core = self.core + (1 - 2 * self.core) * (which % 2)
        return (self.dp, 2 * (self.x + (1 - 2 * self.x) * (which // 2)) + core)

    def dp_peer(self, offset):
        return ((self.dp + offset) % self.count, self.seq)

    def greet(self):
        barrier = pltpu.get_barrier_semaphore()
        peers = [self.kin(k) for k in range(1, 4)]
        peers += [self.dp_peer(k) for k in range(1, self.count)]
        for peer in peers:
            pl.semaphore_signal(barrier, inc=1, device_id=peer, device_id_type=MESH)
        return lambda: pl.semaphore_wait(barrier, len(peers))


def describe(src, dst, send, recv, device):
    return pltpu.make_async_remote_copy(
        src_ref=src,
        dst_ref=dst,
        send_sem=send,
        recv_sem=recv,
        device_id=device,
        device_id_type=MESH,
    )


def remote(src, dst, send, recv, device):
    copy = describe(src, dst, send, recv, device)
    copy.start()
    return copy


def local(src, dst, sem):
    copy = pltpu.make_async_copy(src, dst, sem)
    copy.start()
    return copy


def span(start, size, unit):
    return pl.ds(start if isinstance(start, int) else pl.multiple_of(start, unit), size)


def spread(ticks, marks):
    def at(trip, mark, first=0, past=None):
        for n in range(first, len(ticks) // marks if past is None else past):
            here = ticks[n * marks + mark]
            if here:

                def run(here=here):
                    for tick in here:
                        tick()

                pl.when(trip == n)(run)

    return at


class Group:
    def __init__(self, send, recv, of_all_sent, of_all_received, device):
        self.send, self.recv, self.device = send, recv, device
        self.bytes = (of_all_sent, of_all_received)

    def start(self, src, dst, device):
        describe(src, dst, self.send, self.recv, device).start()

    def all(self, which):
        return describe(self.bytes[which], self.bytes[which], self.send, self.recv, self.device)

    def wait_recv(self):
        self.all(1).wait_recv()

    def wait_send(self):
        self.all(0).wait_send()


class Gather:
    def __init__(self, place, full, sems):
        self.place, self.full = place, full
        self.ring_s, self.ring_r, self.mate_s, self.mate_r, self.cross_s, self.cross_r = sems

    def lanes(self, w):
        return ((0, 1, 2), (0,), (self.place.x, 2, 3), (self.place.x, 2, 3))[w]

    def part(self, ref, w, sub):
        rows, columns = ref.shape[-2:]
        lead = (slice(None),) * (len(ref.shape) - 2)
        if w == SHR:
            unit = rows // 6
            if isinstance(sub, int) and sub >= 2:
                return ref.at[lead + (pl.ds((2 * sub - 2) * unit, 2 * unit),)]
            return ref.at[lead + (span(sub * unit, unit, 16),)]
        unit = columns // (3, 1, 4)[w]
        return ref.at[lead + (slice(None), span(sub * unit, unit, 128))]

    def cut(self, w, owner, core, sub):
        return self.part(self.full[w].at[owner, core], w, sub)

    def block(self, w, sub, way, t):
        owner = self.place.ahead(t) if way else self.place.behind(t)
        return self.cut(w, owner, self.place.core, sub)

    def copy(self, block, send, recv, device):
        return describe(block, block, send, recv, device)

    def ring(self, w, lane, way, t):
        index = ((0, 3, 4, 7)[w] + lane, t + way * self.place.hops[0])
        block = self.block(w, self.lanes(w)[lane], way, t)
        return self.copy(block, self.ring_s.at[w], self.ring_r.at[index], self.place.sides[way])

    def pair(self, w, sub, way, t):
        block = self.block(w, sub, way, t)
        return self.copy(block, self.mate_s.at[w], self.mate_r.at[w], self.place.mate)

    def over(self, w, way, t):
        recv = self.cross_r.at[w - EXP, t - 1 + way * self.place.hops[0]]
        block = self.block(w, self.place.x, way, t)
        return self.copy(block, self.cross_s.at[w - EXP], recv, self.place.across)

    def start(self, w):
        for lane in range(len(self.lanes(w))):
            for way in range(2):
                self.ring(w, lane, way, 0).start()

    def tick(self, w, lane, way, t):
        self.ring(w, lane, way, t - 1).wait_recv()
        if t < self.place.hops[way]:
            self.ring(w, lane, way, t).start()
        self.pair(w, self.lanes(w)[lane], way, t).start()
        if w >= EXP and lane == 0:
            self.over(w, way, t).start()

    def relay(self, w, way, t):
        self.over(w, way, t).wait_recv()
        self.pair(w, 1 - self.place.x, way, t).start()

    def others(self, w):
        return self.full[w].at[pl.ds(0, self.place.count - 1), self.place.core]

    def arrived(self, w):
        block = self.others(w)
        self.copy(block, self.mate_s.at[w], self.mate_r.at[w], self.place.mate).wait_recv()

    def drain(self, w):
        block = self.others(w)
        self.copy(block, self.mate_s.at[w], self.mate_r.at[w], self.place.mate).wait_send()
        if w >= EXP:
            for lane in range(len(self.lanes(w))):
                part = self.part(block, w, self.lanes(w)[lane])
                self.copy(part, self.ring_s.at[w], self.mate_r.at[w], self.place.mate).wait_send()
            part = self.part(block, w, 0)
            self.copy(part, self.cross_s.at[w - EXP], self.mate_r.at[w], self.place.across).wait_send()
        else:
            self.copy(block, self.ring_s.at[w], self.mate_r.at[w], self.place.mate).wait_send()


class Scatter:
    def __init__(self, place, grads, mates, slots, sums, sems):
        self.place, self.grads, self.mates, self.slots = place, grads, mates, slots
        self.sums = sums
        (
            self.mate_s,
            self.mate_r,
            self.ring_s,
            self.ring_r,
            self.cross_s,
            self.cross_r,
            self.total_s,
            self.total_r,
        ) = sems

    def cut(self, ref, w, sub):
        rows, columns = ref.shape[-2:]
        lead = (slice(None),) * (len(ref.shape) - 2)
        if w == SHR:
            return ref.at[lead + (span(sub * (rows // 2), rows // 2, 16),)]
        if w == MIX:
            rows = self.sums[w].shape[1]
            there = pl.ds((sub - 1) * (rows // 3), rows // 3) if sub else pl.ds(0, rows)
            return ref.at[lead + (there, pl.ds(HALF if sub else 0, HALF))]
        size = columns // SUBS[w]
        return ref.at[lead + (slice(None), span(sub * size, size, 128))]

    def owner(self, way, distance):
        return self.place.behind(distance) if way else self.place.ahead(distance)

    def own(self, w, owner, core, sub):
        return self.cut(self.grads[w].at[owner, core], w, sub)

    def slot(self, w, way, t, sub):
        return self.cut(self.slots(w, t + way * self.place.hops[0]), w, sub)

    def pair(self, w, sub, owner):
        return describe(
            self.own(w, owner, 1 - self.place.core, sub),
            self.cut(self.mates(w, owner), w, sub),
            self.mate_s.at[LANES[w] + sub],
            self.mate_r.at[LANES[w] + sub],
            self.place.mate,
        )

    def pairs(self, w, sub):
        block = self.cut(self.grads[w].at[:, self.place.core], w, sub)
        return describe(
            block, block, self.mate_s.at[LANES[w] + sub], self.mate_r.at[LANES[w] + sub], self.place.mate
        )

    def ring(self, w, sub, way, t):
        if t == 0:
            owner = self.owner(way, self.place.hops[way])
            src = self.own(w, owner, self.place.core, sub)
        else:
            src = self.slot(w, way, t - 1, sub)
        index = (LANES[w] + sub, t + way * self.place.hops[0])
        return describe(
            src,
            self.slot(w, way, t, sub),
            self.ring_s.at[LANES[w] + sub],
            self.ring_r.at[index],
            self.place.sides[way],
        )

    def over(self, w, sub):
        return describe(
            self.own(w, self.place.dp, self.place.core, sub),
            self.cut(self.sums[w].at[self.place.core], w, sub),
            self.cross_s.at[LANES[w] + sub],
            self.cross_r.at[LANES[w] + sub],
            self.place.across,
        )

    def total(self, w, sub):
        block = self.cut(self.sums[w].at[self.place.core], w, sub)
        return describe(
            block, block, self.total_s.at[LANES[w] + sub], self.total_r.at[LANES[w] + sub], self.place.mate
        )

    def hand(self, w, sub):
        for owner in range(self.place.count):
            self.pair(w, sub, owner).start()

    def term(self, w, sub, way, distance):
        owner = self.owner(way, distance)
        mine = self.own(w, owner, self.place.core, sub)[...].astype(F32)
        return mine + self.cut(self.mates(w, owner), w, sub)[...].astype(F32)

    def start(self, w, sub):
        self.pairs(w, sub).wait_recv()
        for way, hops in enumerate(self.place.hops):
            term = self.term(w, sub, way, hops)
            self.own(w, self.owner(way, hops), self.place.core, sub)[...] = term.astype(BF)
            self.ring(w, sub, way, 0).start()

    def tick(self, w, sub, way, t):
        self.ring(w, sub, way, t - 1).wait_recv()
        slot = self.slot(w, way, t - 1, sub)
        term = self.term(w, sub, way, self.place.hops[way] - t)
        slot[...] = (slot[...].astype(F32) + term).astype(BF)
        self.ring(w, sub, way, t).start()

    def finish(self, w, sub):
        total = self.term(w, sub, 0, 0)
        for way, hops in enumerate(self.place.hops):
            self.ring(w, sub, way, hops - 1).wait_recv()
            total = total + self.slot(w, way, hops - 1, sub)[...].astype(F32)
        self.own(w, self.place.dp, self.place.core, sub)[...] = total.astype(BF)
        self.over(w, sub).start()

    def crossed(self, w, sub):
        self.over(w, sub).wait_recv()
        value = self.own(w, self.place.dp, self.place.core, sub)[...].astype(F32)
        there = self.cut(self.sums[w].at[self.place.core], w, sub)
        there[...] = (value + there[...].astype(F32)).astype(BF)
        self.total(w, sub).start()

    def arrived(self, w, sub):
        self.total(w, sub).wait_recv()

    def drain(self, w):
        for sub in range(SUBS[w]):
            self.pairs(w, sub).wait_send()
            sent = self.cut(self.grads[w].at[pl.ds(0, self.place.count - 1), self.place.core], w, sub)
            describe(
                sent, sent, self.ring_s.at[LANES[w] + sub], self.mate_r.at[LANES[w] + sub], self.place.mate
            ).wait_send()
            self.over(w, sub).wait_send()
            self.total(w, sub).wait_send()

    def ticks(self, w, t, subs):
        return [
            partial(self.tick, w, sub, way, t)
            for sub in subs
            for way, hops in enumerate(self.place.hops)
            if t < hops
        ]


def half_lanes(hd):
    lane = lax.broadcasted_iota(jnp.int32, (1, 128), 1)
    return (lane < 64) if hd == 0 else (lane >= 64)


def document_lanes(documents):
    lane = lax.broadcasted_iota(jnp.int32, documents.shape, 1) % 64
    same = jnp.logical_and(documents == lane.astype(F32), lane < 8)
    return jnp.where(same, 1.0, 0.0).astype(BF)


def marked_keys(keys, marked):
    hidden = ((1.0 - marked.astype(F32)) * NEGATIVE).astype(BF)
    return [jnp.where(half_lanes(hd), keys, hidden) for hd in range(2)]


def columns_of(hp):
    first = (hp // 3) * (3 * HALF) + (hp % 3) * 128
    return [span(first + part * HALF, 128, 128) for part in range(3)]


def attend_pair(hp, qkv, marked, causal, out, lse, scores, tick):
    cq, ck, cv = columns_of(hp)
    vt = qkv[:, cv].T
    ones = jnp.ones((8, vt.shape[1]), BF)
    keys = marked_keys(qkv[:, ck], marked[...])
    values = [jnp.concatenate([vt[hd * 64 : (hd + 1) * 64, :], ones], axis=0) for hd in range(2)]
    def rows_of(n):
        return slice(n * BLK, (n + 1) * BLK)

    def score(i, hd):
        kept = rows_of(hd)
        query = jnp.where(half_lanes(hd), qkv[rows_of(i), cq], marked[rows_of(i), :])
        top = None
        for j in range(i + 1):
            s = dot(keys[hd][rows_of(j), :], query, NT)
            if i == j:
                s = s + causal[...]
            scores[rows_of(j), kept] = s
            best = jnp.max(s, axis=0, keepdims=True)
            top = best if top is None else jnp.maximum(top, best)
        return top

    def weigh(i, hd, top):
        parts = [
            jnp.exp(scores[rows_of(j), rows_of(hd)] - top).astype(BF) for j in range(i + 1)
        ]
        return i, hd, top, parts

    outs = []

    def collect(i, hd, top, parts):
        acc = None
        for j, p in enumerate(parts):
            term = dot(values[hd][:, rows_of(j)], p, NN)
            acc = term if acc is None else acc + term
        total = acc[64:65, :]
        lse[pl.ds(hp * 2 + hd, 1), rows_of(i)] = top + jnp.log(total)
        outs.append(acc[0:64, :] * (1.0 / total))
        if hd == 1:
            out[rows_of(i), span(hp * 128, 128, 128)] = (
                jnp.concatenate(outs, axis=0).T.astype(BF)
            )
            outs[:] = []

    chains = [(i, hd) for i in range(qkv.shape[0] // BLK) for hd in range(2)]
    tick(0)
    top = score(*chains[0])
    behind = None
    for n, (i, hd) in enumerate(chains):
        after = None
        if n + 1 < len(chains):
            if hd == 1:
                tick(i + 1)
            after = score(*chains[n + 1])
        if behind is not None:
            collect(*behind)
        behind = weigh(i, hd, top)
        top = after
    collect(*behind)


def attend_back_pair(hp, qkv, marked, causal, out, upstream, lse, sums, tick):
    cq, ck, cv = columns_of(hp)
    co = span(hp * 128, 128, 128)
    in_v, in_k = slice(0, 128), slice(128, 256)
    kt = qkv[:, ck].T
    keys = marked_keys(qkv[:, ck], marked[...])
    def rows_of(n):
        return slice(n * BLK, (n + 1) * BLK)

    def operands(i):
        qb = qkv[rows_of(i), cq]
        db = upstream[rows_of(i), co]
        none = jnp.zeros_like(qb)
        prod = (db.astype(F32) * out[rows_of(i), co].astype(F32)).T
        queries = [jnp.where(half_lanes(hd), qb, marked[rows_of(i), :]) for hd in range(2)]
        grads = [jnp.where(half_lanes(hd), db, none) for hd in range(2)]
        return (
            queries,
            grads,
            [jnp.sum(prod[hd * 64 : (hd + 1) * 64, :], axis=0, keepdims=True) for hd in range(2)],
            [lse[pl.ds(hp * 2 + hd, 1), rows_of(i)] for hd in range(2)],
            jnp.concatenate([jnp.where(half_lanes(hd), qb, none) for hd in range(2)], axis=0),
            jnp.concatenate(grads, axis=0),
        )

    def products(n, ops):
        i, j = blocks[n]
        kept = slice((1 + n % 2) * BLK, (2 + n % 2) * BLK)
        for hd in range(2):
            s = dot(keys[hd][rows_of(j), :], ops[0][hd], NT)
            sums[rows_of(hd), kept] = s + causal[...] if i == j else s
            sums[rows_of(2 + hd), kept] = dot(qkv[rows_of(j), cv], ops[1][hd], NT)

    blocks = [(i, j) for i in range(qkv.shape[0] // BLK) for j in range(i + 1)]
    tick(0)
    ops = operands(0)
    products(0, ops)
    dqs = [None, None]

    def gather_block(i, j, now, ps, dss):
        for hd in range(2):
            term = dot(kt[hd * 64 : (hd + 1) * 64, rows_of(j)], dss[hd], NN)
            dqs[hd] = term if dqs[hd] is None else dqs[hd] + term
        pv = dot(jnp.concatenate(ps, axis=1), now[5], NN)
        pk = dot(jnp.concatenate(dss, axis=1), now[4], NN)
        if i == j:
            sums[rows_of(j), in_v] = pv
            sums[rows_of(j), in_k] = pk
            low = jnp.concatenate(dqs, axis=0).T.astype(BF).astype(F32)
            qkv[rows_of(i), cq] = (low * (1.0 / math.sqrt(HD))).astype(BF)
            dqs[:] = [None, None]
        else:
            sums[rows_of(j), in_v] += pv
            sums[rows_of(j), in_k] += pk

    behind = None
    for n, (i, j) in enumerate(blocks):
        now = ops
        kept = slice((1 + n % 2) * BLK, (2 + n % 2) * BLK)
        if n + 1 < len(blocks):
            if blocks[n + 1][1] == 0:
                tick(i + 1)
                ops = operands(i + 1)
            products(n + 1, ops)
        if behind is not None:
            gather_block(*behind)
        ps, dss = [], []
        for hd in range(2):
            p = jnp.exp(sums[rows_of(hd), kept] - now[3][hd])
            ps.append(p.astype(BF))
            dss.append((p * (sums[rows_of(2 + hd), kept] - now[2][hd])).astype(BF))
        behind = (i, j, now, ps, dss)
    gather_block(*behind)
    qkv[:, ck] = sums[:, in_k].astype(BF)
    qkv[:, cv] = sums[:, in_v].astype(BF)


def normalised(values):
    center = values - jnp.mean(values, axis=-1, keepdims=True)
    inverse = lax.rsqrt(jnp.mean(center * center, axis=-1, keepdims=True) + NORM_EPS)
    return center * inverse, inverse


def norm_grad(values, gain, upstream):
    hat, inverse = normalised(values)
    scaled = upstream * gain
    first = jnp.mean(scaled, axis=-1, keepdims=True)
    second = jnp.mean(scaled * hat, axis=-1, keepdims=True)
    return (
        inverse * (scaled - first - hat * second),
        jnp.sum(upstream * hat, axis=0, keepdims=True),
        jnp.sum(upstream, axis=0, keepdims=True),
    )


def gelu_both(u):
    inner = math.sqrt(2.0 / math.pi)
    cubic = inner * 0.044715
    square = u * u
    half = 0.5 + 0.5 * jnp.tanh(u * (inner + cubic * square))
    value = u * half
    return value, half + value * (1.0 - half) * (2.0 * inner + 6.0 * cubic * square)


def softmax(values):
    e = jnp.exp(values - jnp.max(values, axis=-1, keepdims=True))
    return e * (1.0 / jnp.sum(e, axis=-1, keepdims=True))


def whole(ref):
    return ref[...].reshape(-1, ref.shape[-1])


VEC_PLACES = (("g1", D), ("b1", D), ("bq", D), ("bv", D), ("bo", D), ("g2", D), ("b2", D), ("bf1", FF), ("bf2", D))
VEC_ROW = {name: row for row, (name, _) in enumerate(VEC_PLACES)}
VEC_SIZE = dict(VEC_PLACES)


def block_kernel(count, *refs):
    inputs, teacher, segments, masters, vec_ref = refs[0], refs[1], refs[2], refs[3:7], refs[7]
    sums_out, vec_sum, norm_ref, out_rows, back_rows = refs[8:12], *refs[12:16]
    (
        full0, full1, full2, full3, x, h1, qkv, att, x1, h2, act, slope, dy, low, sent, shrink_grads,
        shr_mate, shr_slot, lse, segs, seg_stage, marked, causal,
        sums0, sums1, sums2, sums3, vec_stage, vec_all, vec, gvec, vec_out, vec_buf, vec_mine, vec_seq, sq_mine, sq_buf,
        load_sem, g_ring_s, g_ring_r, g_mate_s, g_mate_r, g_cross_s, g_cross_r,
        s_mate_s, s_mate_r, s_ring_s, s_ring_r, s_cross_s, s_cross_r, s_total_s, s_total_r,
        row_s, row_r, row_l, vec_s, vec_r, free,
    ) = refs[16:]
    full = (full0, full1, full2, full3)
    sums = (sums0, sums1, sums2, sums3)
    place = Place(count)
    ready = place.greet()
    length = x.shape[0]
    blocks = length // BLK
    scale = 1.0 / math.sqrt(HD)

    def rows(i):
        return span(i * BLK, BLK, BLK)

    loads, pieces, used = [], [], [0, 0]
    for w in (MIX, OUT, EXP, SHR):
        height, width = masters[w].shape
        for column in range(0, width, D):
            which = 0 if used[0] + height <= length else 1
            where = (dy, x1)[which].at[pl.ds(used[which], height)]
            used[which] += height
            source = masters[w].at[:, pl.ds(column, D)]
            loads.append(local(source, where, load_sem.at[len(loads)]))
            pieces.append((w, column, where))

    def stage(w):
        for load, (owner, column, where) in zip(loads, pieces):
            if owner == w:
                load.wait()
                piece = where[...].astype(BF).reshape(full[w].shape[1:3] + (D,))
                if w == MIX:
                    for part in range(2):
                        c = slice(part * HALF, (part + 1) * HALF)
                        there = pl.ds(part * 3 * HALF + column // 2, HALF)
                        full[w][place.dp, :, :, there] = piece[:, :, c]
                else:
                    full[w][place.dp, :, :, pl.ds(column, D)] = piece

    gather = Gather(place, full, (g_ring_s, g_ring_r, g_mate_s, g_mate_r, g_cross_s, g_cross_r))
    stage(MIX)
    ready()
    gather.start(MIX)

    me = rows(place.seq)
    three, seven = pl.ds(0, 3), pl.ds(0, count - 1)
    most = pl.ds(0, 3 * BLK)

    def group(n, sent, received):
        return Group(row_s.at[n], row_r.at[n], sent, received, place.mate)

    row_in = group(0, inputs.at[three], x.at[most])
    seg_in = group(1, seg_stage.at[three], segs.at[three])
    teach_in = group(2, teacher.at[three], low.at[most])
    out_go = group(3, out_rows.at[three], out_rows.at[three])
    back_go = group(4, back_rows.at[three], back_rows.at[three])
    seq_go = group(5, vec_seq.at[three], vec_seq.at[three])
    vec_in = Group(vec_s.at[0], vec_r.at[0], vec_all.at[seven], vec_all.at[seven], place.mate)
    vec_go = Group(vec_s.at[1], vec_r.at[1], vec_buf.at[seven], vec_buf.at[seven], place.mate)
    sq_go = Group(vec_s.at[2], vec_r.at[2], sq_buf.at[seven], sq_buf.at[seven], place.mate)
    for k in (2, 3, 1):
        peer = place.kin(k)
        row_in.start(inputs.at[peer[1]], x.at[me], peer)
    row_local = local(inputs.at[place.seq], x.at[me], row_l.at[0])
    seg_stage[...] = jnp.broadcast_to(segments[...][:, None, :], seg_stage.shape)
    vec_stage[...] = jnp.concatenate(
        [vec_ref[...].astype(BF).astype(F32), jnp.zeros((VROWS - vec_ref.shape[0], 128), F32)],
        axis=0,
    )
    for k in range(1, count):
        vec_in.start(vec_stage, vec_all.at[place.dp], place.dp_peer(k))
    for k in (2, 3, 1):
        peer = place.kin(k)
        seg_in.start(seg_stage.at[peer[1]], segs.at[place.seq], peer)

    def send_teacher(k, part=0, parts=1):
        size = BLK // parts
        there = low.at[span(place.seq * BLK + part * size, size, 16)]
        peer = place.kin(k)
        teach_in.start(teacher.at[peer[1], pl.ds(part * size, size)], there, peer)

    for k in (2, 1):
        send_teacher(k)
    segs[place.seq] = seg_stage[place.seq]
    vec_all[place.dp] = vec_stage[...]
    teach_local = local(teacher.at[place.seq], low.at[me], row_l.at[1])
    for w in (OUT, EXP, SHR):
        stage(w)

    def ring_steps(w, t):
        return [
            partial(gather.tick, w, lane, way, t)
            for lane in range(len(gather.lanes(w)))
            for way in range(2)
            if t <= place.hops[way]
        ]

    def relays(w, t):
        return [partial(gather.relay, w, way, t) for way in range(2) if 1 <= t <= place.hops[way]]

    far = place.hops[0]
    for t in range(1, far + 1):
        for step in ring_steps(MIX, t):
            step()
        if t == far - 2:
            gather.start(OUT)
        if t == far - 1:
            gather.start(EXP)
    for step in ring_steps(OUT, 1):
        step()

    vec_in.wait_recv()
    per = vec_ref.shape[0]
    flat = 0
    for name, size in VEC_PLACES:
        parts = []
        for r in range(flat, flat + size // 128):
            parts.append(vec_all[r // per, r % per : r % per + 1, :])
        vec[VEC_ROW[name] : VEC_ROW[name] + 1, 0:size] = jnp.concatenate(parts, axis=1)
        flat += size // 128

    def of(name):
        return vec[VEC_ROW[name] : VEC_ROW[name] + 1, 0 : VEC_SIZE[name]]

    def add_grad(name, term, start=0):
        gvec[VEC_ROW[name] : VEC_ROW[name] + 1, start : start + term.shape[1]] += term

    gvec[...] = jnp.zeros_like(gvec)
    row_local.wait()
    row_in.wait_recv()
    seg_in.wait_recv()

    for s in range(4):
        documents = jnp.concatenate([segs[s].astype(F32)] * 16, axis=0).T
        marked[s * BLK : (s + 1) * BLK, :] = document_lanes(documents)
    earlier = lax.broadcasted_iota(jnp.int32, (BLK, BLK), 0) <= lax.broadcasted_iota(
        jnp.int32, (BLK, BLK), 1
    )
    causal[...] = jnp.where(earlier, 0.0, NEGATIVE)

    def first_norm(i, _):
        hat, _ = normalised(x[rows(i), :].astype(F32))
        h1[rows(i), :] = (hat * of("g1") + of("b1")).astype(BF)
        return 0

    lax.fori_loop(0, blocks, first_norm, 0)
    gather.arrived(MIX)

    def lane(w, number, t):
        return [partial(gather.tick, w, number, way, t) for way in range(2) if t <= place.hops[way]]

    def piece(n):
        return [partial(send_teacher, 3, n, 4)]

    in_project = spread(
        [[], [], lane(EXP, 0, 1), lane(EXP, 1, 1), piece(0), lane(EXP, 2, 1), [], lane(OUT, 0, 2)],
        2,
    )
    in_forward = spread(
        [
            [],
            lane(EXP, 0, 2) + piece(1),
            lane(EXP, 1, 2) + lane(EXP, 2, 2),
            lane(OUT, 0, 3),
            lane(EXP, 0, 3) + lane(OUT, 0, 4) + piece(2),
            lane(EXP, 1, 3) + lane(EXP, 2, 3) + [partial(gather.start, SHR)],
        ],
        1,
    )
    in_middle = spread([[], lane(EXP, 0, 4) + piece(3), lane(EXP, 1, 4), lane(EXP, 2, 4)], 1)
    before_expand = relays(EXP, 1) + relays(EXP, 2) + lane(SHR, 0, 1) + relays(EXP, 3)
    before_expand += lane(SHR, 1, 1) + relays(EXP, 4)
    in_expand = spread(
        [
            lane(SHR, 2, 1), lane(SHR, 0, 2),
            [], lane(SHR, 1, 2),
            lane(SHR, 2, 2) + lane(SHR, 0, 3), [],
            lane(SHR, 1, 3), lane(SHR, 0, 4) + lane(SHR, 2, 3),
        ],
        2,
    )
    after_expand = lane(SHR, 1, 4) + lane(SHR, 2, 4)
    for t in range(1, far + 1):
        after_expand += relays(SHR, t)

    def project(i, _):
        in_project(i, 0)
        value = dot(h1[rows(i), :], whole(full[MIX]), NN)
        for part in range(2):
            c = slice(part * HALF, (part + 1) * HALF)
            q, k, v = (
                slice(part * 3 * HALF + n * HALF, part * 3 * HALF + (n + 1) * HALF) for n in range(3)
            )
            qkv[rows(i), q] = ((value[:, q] + of("bq")[:, c]) * scale).astype(BF)
            qkv[rows(i), k] = value[:, k].astype(BF)
            qkv[rows(i), v] = (value[:, v] + of("bv")[:, c]).astype(BF)
        in_project(i, 1)
        return 0

    lax.fori_loop(0, blocks, project, 0)
    def forward_pair(hp, _):
        attend_pair(
            hp,
            qkv,
            marked,
            causal,
            att,
            lse,
            dy,
            lambda i: in_forward(hp, 0) if i == 0 else None,
        )
        return 0

    lax.fori_loop(0, PAIRS, forward_pair, 0)
    def middle(i, _):
        in_middle(i, 0)
        value = x[rows(i), :].astype(F32) + dot(att[rows(i), :], whole(full[OUT]), NN) + of("bo")
        x1[rows(i), :] = value
        hat, _ = normalised(value)
        h2[rows(i), :] = (hat * of("g2") + of("b2")).astype(BF)
        return 0

    gather.arrived(OUT)
    lax.fori_loop(0, blocks, middle, 0)

    def target(i, _):
        dy[rows(i), :] = softmax(low[rows(i), :].astype(F32))
        return 0

    for tick in before_expand:
        tick()
    teach_local.wait()
    teach_in.wait_recv()
    lax.fori_loop(0, blocks, target, 0)
    gather.arrived(EXP)

    def expand(i, _):
        for n in range(FF // EXPAND_TILE):
            if n % 2 == 0:
                in_expand(i, n // 2)
            c = slice(n * EXPAND_TILE, (n + 1) * EXPAND_TILE)
            weight = full[EXP][:, :, :, c].reshape(D, EXPAND_TILE)
            u = dot(h2[rows(i), :], weight, NN) + vec[VEC_ROW["bf1"] : VEC_ROW["bf1"] + 1, c]
            a, s = gelu_both(u)
            act[rows(i), c] = a.astype(BF)
            slope[rows(i), c] = s.astype(BF)
        return 0

    lax.fori_loop(0, blocks, expand, 0)
    for tick in after_expand:
        tick()
    gather.arrived(SHR)

    def shrink(i, _):
        value = x1[rows(i), :] + dot(act[rows(i), :], whole(full[SHR]), NN) + of("bf2")
        sent[rows(i), :] = value.astype(BF)
        grad = D * (softmax(value) - dy[rows(i), :])
        dy[rows(i), :] = grad
        low[rows(i), :] = grad.astype(BF)
        add_grad("bf2", jnp.sum(grad, axis=0, keepdims=True))
        return 0

    lax.fori_loop(0, blocks, shrink, 0)
    for w in (MIX, OUT, EXP, SHR):
        gather.drain(w)

    def send_rows(rows_out, copies, k, first=0, size=BLK):
        peer = place.kin(k)
        source = sent.at[span(peer[1] * BLK + first, size, 128)]
        copies.start(source, rows_out.at[place.seq, pl.ds(first, size)], peer)

    out_local = local(sent.at[me], out_rows.at[place.seq], row_l.at[2])
    for k in (2, 3, 1):
        send_rows(out_rows, out_go, k)

    half, some = full[MIX].shape[2], count // 2

    def part_of(buffer, w, where):
        if w == EXP:
            return act.at[where]
        return slope.at[where, pl.ds(3 * D, D)]

    def third(group, n):
        return slope.at[span(n * 3 * half, 3 * half, 16), span(group * D, D, 128)]

    def mates(w, owner):
        if w == SHR:
            return shr_mate.at[owner]
        if w == MIX:
            return third(owner // (count // 2), owner % (count // 2))
        return part_of(act, w, span(owner * half, half, 16))

    def slots(w, t):
        if w == SHR:
            return shr_slot.at[t]
        if w == MIX:
            return third(2, t)
        return part_of(act, w, span((count + t) * half, half, 16))

    scatter = Scatter(
        place,
        (full3, full1, full2, shrink_grads),
        mates,
        slots,
        sums,
        (s_mate_s, s_mate_r, s_ring_s, s_ring_r, s_cross_s, s_cross_r, s_total_s, s_total_r),
    )

    def offer(which):
        for n, peer in enumerate((place.mate,) + place.sides):
            pl.semaphore_signal(
                free.at[3 * which + n], inc=1, device_id=peer, device_id_type=MESH
            )

    def accept(which, which_sides):
        for n in range(1, 3) if which_sides else range(1):
            pl.semaphore_wait(free.at[3 * which + n], 1)

    def shrink_grad(n, _):
        value = dot(act[:, span(n * D, D, 128)], low[...], TN).astype(BF)
        shrink_grads[pl.ds(2 * n, 2)] = value.reshape((2,) + shrink_grads.shape[1:])
        for owner in range(2):
            for sub in range(2):
                scatter.pair(SHR, sub, 2 * n + owner).start()
        return 0

    lax.fori_loop(0, FF // D, shrink_grad, 0)
    offer(0)

    def hop(w, t, sub):
        return scatter.ticks(w, t, (sub,))

    def end(w, sub):
        return [partial(scatter.finish, w, sub)]

    in_middle_back = spread([hop(SHR, 1, 0), [], hop(SHR, 1, 1), []], 1)
    in_expand_grad = spread([hop(SHR, 2, 0), [], hop(SHR, 2, 1), []], 1)
    in_upstream = spread(
        [[partial(scatter.start, EXP, 0)] + hop(SHR, 3, 0), [], [], []],
        1,
    )
    in_backward = spread(
        [
            hop(SHR, 3, 1), [], [], [partial(scatter.start, OUT, 0)],
            hop(EXP, 1, 0) + end(SHR, 0), [], [], [],
            hop(EXP, 1, 1) + hop(OUT, 1, 0), [], [], hop(EXP, 2, 0) + end(SHR, 1),
            hop(OUT, 2, 0) + hop(EXP, 2, 1), [], [], hop(EXP, 3, 0) + [partial(scatter.start, MIX, 0)],
            [], [], [], hop(OUT, 3, 0) + hop(EXP, 3, 1),
            end(EXP, 0), [], [], hop(MIX, 1, 0) + end(OUT, 0) + end(EXP, 1),
        ],
        4,
    )

    in_expand_back = spread([[], [partial(scatter.start, SHR, sub) for sub in range(2)], [], []], 1)

    def expand_back(i, _):
        in_expand_back(i, 0)
        for n in range(FF // D):
            c = slice(n * D, (n + 1) * D)
            weight = full[SHR][2 * n : 2 * n + 2].reshape(D, D)
            da = dot(low[rows(i), :], weight, NT).astype(BF).astype(F32)
            du = (da * slope[rows(i), c].astype(F32)).astype(BF)
            slope[rows(i), c] = du
            gvec[VEC_ROW["bf1"] : VEC_ROW["bf1"] + 1, c] += jnp.sum(
                du.astype(F32), axis=0, keepdims=True
            )
        return 0

    lax.fori_loop(0, blocks, expand_back, 0)


    def middle_back(i, _):
        in_middle_back(i, 0)
        upstream = dot(slope[rows(i), :], whole(full[EXP]), NT)
        part, gain, shift = norm_grad(x1[rows(i), :], of("g2"), upstream)
        value = dy[rows(i), :] + part
        dy[rows(i), :] = value
        low[rows(i), :] = value.astype(BF)
        add_grad("g2", gain)
        add_grad("b2", shift)
        add_grad("bo", jnp.sum(value, axis=0, keepdims=True))
        return 0

    lax.fori_loop(0, blocks, middle_back, 0)
    accept(0, False)

    def expand_grad(n, _):
        in_expand_grad(n, 0)
        c = span(n * D, D, 128)
        for owners in range(2):
            value = dot(h2[:, owners * HALF : (owners + 1) * HALF], slope[:, c], TN).astype(BF)
            full2[owners * some : (owners + 1) * some, :, :, c] = value.reshape(
                (some,) + full2.shape[1:3] + (D,)
            )
        pl.when(n == FF // D // 2 - 1)(lambda: scatter.hand(EXP, 0))
        return 0

    lax.fori_loop(0, FF // D, expand_grad, 0)
    scatter.hand(EXP, 1)
    offer(1)
    accept(0, True)

    def upstream_rows(i, _):
        in_upstream(i, 0)
        h2[rows(i), :] = dot(low[rows(i), :], whole(full[OUT]), NT).astype(BF)
        return 0

    lax.fori_loop(0, blocks, upstream_rows, 0)
    for owners in range(2):
        if owners:
            scatter.start(EXP, 1)
        value = dot(att[:, owners * HALF : (owners + 1) * HALF], low[...], TN).astype(BF)
        full1[owners * some : (owners + 1) * some] = value.reshape((some,) + full1.shape[1:])
    accept(1, False)
    scatter.hand(OUT, 0)
    accept(1, True)
    def backward_part(part, _):
        def backward_pair(hp, _):
            def tick(i):
                for n in range(2):
                    first = n * (PAIRS // 2)
                    pl.when(part == n)(
                        lambda first=first: in_backward(hp + first, i, first, first + PAIRS // 2)
                    )

            number = part * (PAIRS // 2) + hp
            attend_back_pair(
                number, qkv, marked, causal, att, h2, lse, x1, tick
            )
            return 0

        lax.fori_loop(0, PAIRS // 2, backward_pair, 0)
        c = span(part * 3 * HALF, 3 * HALF, 128)
        for owners in range(2):
            mine = slice(owners * HALF, (owners + 1) * HALF)
            value = dot(h1[:, mine], qkv[:, c], TN).astype(BF)
            for n in range(3):
                there = span(part * HALF, HALF, 128)
                full3[owners * some : (owners + 1) * some, :, n * half : (n + 1) * half, there] = (
                    value[:, n * HALF : (n + 1) * HALF].reshape(some, 2, half, HALF)
                )
            for number in range(2):

                def hand(number=number, owners=owners):
                    for sub in ((0,), (1, 2, 3))[number]:
                        for owner in range(owners * some, (owners + 1) * some):
                            scatter.pair(MIX, sub, owner).start()

                pl.when(part == number)(hand)
        return 0

    lax.fori_loop(0, 2, backward_part, 0)
    for tick in hop(MIX, 2, 0):
        tick()
    out_local.wait()
    out_go.wait_send()
    in_input_back = spread(
        [
            [],
            [partial(scatter.start, MIX, sub) for sub in range(1, 4)],
            hop(MIX, 3, 0),
            hop(MIX, 1, 1),
        ],
        1,
    )
    late = BLK // 2

    def input_back(j, _):
        in_input_back(j, 0)
        core = place.core + (1 - 2 * place.core) * (j % 2)
        i = 2 * (place.x + (1 - 2 * place.x) * (1 - j // 2)) + core
        d = qkv[rows(i), :]
        part, gain, shift = norm_grad(
            x[rows(i), :].astype(F32), of("g1"), dot(d, whole(full[MIX]), NT)
        )
        sent[rows(i), :] = (dy[rows(i), :] + part).astype(BF)
        add_grad("g1", gain)
        add_grad("b1", shift)
        for half_of in range(2):
            first = half_of * 3 * HALF
            for name, start in (("bq", first), ("bv", first + 2 * HALF)):
                term = d[:, start : start + HALF].astype(F32)
                add_grad(name, jnp.sum(term, axis=0, keepdims=True), half_of * HALF)
        pl.when(j == 0)(lambda: send_rows(back_rows, back_go, 2))
        pl.when(j == 1)(lambda: send_rows(back_rows, back_go, 3, 0, late) if late else None)
        pl.when(j == 3)(lambda: send_rows(back_rows, back_go, 1))
        return 0

    lax.fori_loop(0, blocks, input_back, 0)
    back_local = local(sent.at[me], back_rows.at[place.seq], row_l.at[3])
    flat = 0
    vec_out[...] = jnp.zeros_like(vec_out)
    for name, size in VEC_PLACES:
        for n in range(size // 128):
            r = flat + n
            vec_out[r // per, r % per : r % per + 1, :] = gvec[
                VEC_ROW[name] : VEC_ROW[name] + 1, n * 128 : (n + 1) * 128
            ]
        flat += size // 128
    for k in range(1, count):
        peer = place.dp_peer(k)
        vec_go.start(vec_out.at[peer[0]], vec_buf.at[place.dp], peer)
    vec_buf[place.dp] = vec_out[place.dp]
    for tick in hop(MIX, 1, 2) + hop(MIX, 1, 3) + end(MIX, 0) + hop(MIX, 2, 1) + hop(MIX, 2, 2) + hop(MIX, 2, 3):
        tick()
    for w, sub in ((SHR, 0), (SHR, 1), (EXP, 0)):
        scatter.crossed(w, sub)
    for tick in hop(MIX, 3, 1) + hop(MIX, 3, 2) + hop(MIX, 3, 3):
        tick()
    vec_go.wait_recv()
    vec_mine[...] = jnp.sum(vec_buf[...], axis=0)
    vec_seq[place.seq] = vec_mine[...]
    for k in (2, 3, 1):
        seq_go.start(vec_mine, vec_seq.at[place.seq], place.kin(k))
    for sub in range(1, 4):
        scatter.finish(MIX, sub)
    send_rows(back_rows, back_go, 3, late, BLK - late)
    for w, sub in ((EXP, 1), (OUT, 0), (MIX, 0)):
        scatter.crossed(w, sub)

    def squares_of(w, part, total):
        c = slice(None) if part is None else slice(part * HALF, (part + 1) * HALF)
        for core in range(2):
            value = sums[w][core, :, c].astype(F32)
            term = jnp.sum(value * value, axis=0, keepdims=True)
            for n in range(term.shape[1] // 128):
                total = total + term[:, n * 128 : (n + 1) * 128]
        return total

    squares = jnp.zeros((1, 128), F32)
    for w in (SHR, EXP, OUT):
        for sub in range(SUBS[w]):
            scatter.arrived(w, sub)
        squares = squares_of(w, None, squares)
    scatter.arrived(MIX, 0)
    squares = squares_of(MIX, 0, squares)
    seq_go.wait_recv()
    vec_total = jnp.sum(vec_seq[...], axis=0)
    vec_sum[...] = vec_total
    squares = squares + jnp.sum(vec_total * vec_total, axis=0, keepdims=True)
    for sub in range(1, 4):
        scatter.crossed(MIX, sub)
    for sub in range(1, 4):
        scatter.arrived(MIX, sub)
    squares = squares_of(MIX, 1, squares)
    sq_mine[...] = jnp.broadcast_to(squares, sq_mine.shape)
    sq_buf[place.dp] = sq_mine[...]
    for k in range(1, count):
        sq_go.start(sq_mine, sq_buf.at[place.dp], place.dp_peer(k))
    saved = [local(sums[w], sums_out[w], load_sem.at[w]) for w in range(4)]
    for w in (MIX, OUT, EXP, SHR):
        scatter.drain(w)
    for copies in (row_in, seg_in, teach_in, vec_in, vec_go, seq_go, back_go, sq_go):
        copies.wait_send()
    for copy in saved + [back_local]:
        copy.wait()
    out_go.wait_recv()
    back_go.wait_recv()
    sq_go.wait_recv()
    total = jnp.sum(jnp.sum(sq_buf[...], axis=0), axis=1, keepdims=True)
    norm_ref[...] = jnp.broadcast_to(jnp.sqrt(total), norm_ref.shape)


def block_call(count, inputs, teacher, segments, masters, vectors):
    rows, local_len, features = inputs.shape
    length = rows * local_len
    halves = [(2, m.shape[0] // 2, m.shape[1]) for m in masters]
    any_spec = pl.BlockSpec(memory_space=pl.ANY)
    vmem = pl.BlockSpec(memory_space=pltpu.VMEM)
    row_shape = jax.ShapeDtypeStruct(inputs.shape, BF)
    folded = [(2, 3 * halves[MIX][1], D)] + halves[1:]
    out_shape = [jax.ShapeDtypeStruct(h, BF) for h in folded]
    out_shape += [
        jax.ShapeDtypeStruct((VROWS, 128), F32),
        jax.ShapeDtypeStruct((8, 128), F32),
        row_shape,
        row_shape,
    ]

    def low(*shape):
        return pltpu.VMEM(shape, BF)

    def wide(*shape):
        return pltpu.VMEM(shape, F32)

    def dma(*shape):
        return pltpu.SemaphoreType.DMA(shape)

    shrink_half = halves[SHR][1:]
    buffers = [low(count, *h) for h in halves]
    buffers += [
        low(length, D),
        low(length, D),
        low(length, 3 * D),
        low(length, D),
        wide(length, D),
        low(length, D),
        low(length, FF),
        low(length, FF),
        wide(length, D),
        low(length, D),
        low(length, D),
        low(count, *halves[SHR]),
        low(count, *shrink_half),
        low(count - 1, *shrink_half),
    ]
    buffers += [
        wide(16, length),
        pltpu.VMEM((rows, 8, local_len), jnp.int32),
        pltpu.VMEM((rows, 8, local_len), jnp.int32),
        low(length, 128),
        wide(BLK, BLK),
        *(low(*shape) for shape in folded),
        wide(VROWS, 128),
        wide(count, VROWS, 128),
        wide(16, FF),
        wide(16, FF),
        wide(count, VROWS, 128),
        wide(count, VROWS, 128),
        wide(VROWS, 128),
        wide(4, VROWS, 128),
        wide(8, 128),
        wide(count, 8, 128),
    ]
    hops = count - 1
    sems = [dma(9), dma(4), dma(10, hops), dma(4), dma(4), dma(2), dma(2, hops)]
    sems += [dma(9), dma(9), dma(9), dma(9, hops)] + [dma(9)] * 4
    sems += [dma(6), dma(6), dma(4), dma(3), dma(3)]
    sems.append(pltpu.SemaphoreType.REGULAR((6,)))
    return pl.pallas_call(
        partial(block_kernel, count),
        out_shape=out_shape,
        in_specs=[any_spec] * 2 + [vmem] + [any_spec] * 4 + [vmem],
        out_specs=[any_spec] * 4 + [vmem] * 2 + [any_spec] * 2,
        scratch_shapes=buffers + sems,
        compiler_params=pltpu.CompilerParams(
            collective_id=1, has_side_effects=True, vmem_limit_bytes=VMEM_BYTES
        ),
    )(inputs, teacher, segments, *masters, vectors.reshape(-1, 128))


def update_kernel(steps, norm_ref, *refs):
    sums, masters, firsts, seconds = refs[0:5], refs[5:10], refs[10:15], refs[15:20]
    out_from, back_from = refs[20:22]
    updated, first_out, second_out = refs[22:27], refs[27:32], refs[32:37]
    out_to, back_to, norm_out, held, sem = refs[37:42]
    step = pl.program_id(0)
    norm = norm_ref[0:1, 0:1]
    factor = clip_level() / jnp.maximum(norm, clip_level())
    takes = [
        pltpu.make_async_copy(rows, held.at[n], sem.at[n])
        for n, rows in enumerate((out_from, back_from))
    ]
    gives = [
        pltpu.make_async_copy(held.at[n], rows, sem.at[2 + n])
        for n, rows in enumerate((out_to, back_to))
    ]

    @pl.when(step == 0)
    def _():
        for copy in takes:
            copy.start()
        norm_out[...] = norm

    @pl.when(step == steps // 2)
    def _():
        for take, give in zip(takes, gives):
            take.wait()
            give.start()

    def apply(n, gradient):
        rate = learn_rates()[n]
        clipped = gradient * factor
        first = BETA_ONE * firsts[n][...] + (1.0 - BETA_ONE) * clipped
        second = BETA_TWO * seconds[n][...] + (1.0 - BETA_TWO) * (clipped * clipped)
        scale = jnp.sqrt(second * (1.0 / (1.0 - BETA_TWO**STEP))) + ADAM_EPS
        change = first * (rate / (1.0 - BETA_ONE**STEP)) / scale
        updated[n][...] = masters[n][...] * (1.0 - rate * WEIGHT_DECAY) - change
        first_out[n][...] = first
        second_out[n][...] = second

    for w in range(4):
        gradient = sums[w][...].astype(F32)
        if w == MIX:
            gradient = jnp.concatenate([gradient[n] for n in range(3)], axis=1)
        apply(w, gradient)

    @pl.when(step == 0)
    def _():
        apply(4, sums[4][0 : masters[4].shape[0], :])

    @pl.when(step == steps - 1)
    def _():
        for copy in gives:
            copy.wait()


def update_call(results, masters, firsts, seconds):
    half = results[OUT].shape[1]
    parts = 1
    steps = 2 * parts
    mixed = results[MIX].reshape(2, 3, half, D)

    def fixed(shape):
        return pl.BlockSpec(shape, lambda i: (0,) * len(shape))

    any_spec = pl.BlockSpec(memory_space=pl.ANY)
    sum_specs, state_specs, states = [], [], []
    for master in masters[:4]:
        rows, columns = master.shape[0] // steps, master.shape[1]
        sum_specs.append(pl.BlockSpec((None, rows, columns), lambda i: (i // parts, i % parts, 0)))
        state_specs.append(pl.BlockSpec((rows, columns), lambda i: (i, 0)))
    sum_specs[MIX] = pl.BlockSpec(
        (None, 3, half // parts, D), lambda i: (i // parts, 0, i % parts, 0)
    )
    packed = (masters[4].shape[0] // 128, 128)
    state_specs.append(fixed(packed))
    sum_specs.append(fixed(results[4].shape))
    for group in (masters, firsts, seconds):
        states += list(group[:4]) + [group[4].reshape(packed)]
    out_shape = [jax.ShapeDtypeStruct(state.shape, F32) for state in states]
    out_shape += [jax.ShapeDtypeStruct(results[6].shape, BF)] * 2
    out_shape.append(jax.ShapeDtypeStruct((1, 1), F32))
    return pl.pallas_call(
        partial(update_kernel, steps),
        grid=(steps,),
        out_shape=out_shape,
        in_specs=[fixed(results[5].shape)] + sum_specs + state_specs * 3 + [any_spec] * 2,
        out_specs=state_specs * 3 + [any_spec] * 2 + [fixed((1, 1))],
        scratch_shapes=[
            pltpu.VMEM((2,) + results[6].shape, BF),
            pltpu.SemaphoreType.DMA((4,)),
        ],
        compiler_params=pltpu.CompilerParams(vmem_limit_bytes=VMEM_BYTES),
    )(results[5], mixed, *results[1:5], *states, *results[6:8])


def row_body(
    inputs,
    segments,
    teacher,
    mixing_weight,
    output_weight,
    expand_weight,
    shrink_weight,
    vectors,
    mixing_first,
    output_first,
    expand_first,
    shrink_first,
    vectors_first,
    mixing_second,
    output_second,
    expand_second,
    shrink_second,
    vectors_second,
):
    masters = (mixing_weight, output_weight, expand_weight, shrink_weight, vectors)
    firsts = (mixing_first, output_first, expand_first, shrink_first, vectors_first)
    seconds = (mixing_second, output_second, expand_second, shrink_second, vectors_second)
    results = block_call(lax.axis_size("dp"), inputs, teacher, segments, masters[:4], vectors)
    fresh = update_call(results, masters, firsts, seconds)
    states = [
        state.reshape(vectors.shape) if n % 5 == 4 else state for n, state in enumerate(fresh[:15])
    ]
    return (fresh[15], fresh[16], fresh[17].reshape(()), *states)


def whole_rows(mesh):
    return mesh.shape["seq"] == 4 and mesh.shape["dp"] == 8


def solution(mesh):
    in_specs = (
        P("dp", "seq", None),
        P("dp", "seq"),
        P("dp", "seq", None),
        P("dp", None),
        P("dp", None),
        P("dp", None),
        P("dp", None),
        P("dp"),
        P("dp", None),
        P("dp", None),
        P("dp", None),
        P("dp", None),
        P("dp"),
        P("dp", None),
        P("dp", None),
        P("dp", None),
        P("dp", None),
        P("dp"),
    )
    out_specs = (
        P("dp", "seq", None),
        P("dp", "seq", None),
        P(),
        P("dp", None),
        P("dp", None),
        P("dp", None),
        P("dp", None),
        P("dp"),
        P("dp", None),
        P("dp", None),
        P("dp", None),
        P("dp", None),
        P("dp"),
        P("dp", None),
        P("dp", None),
        P("dp", None),
        P("dp", None),
        P("dp"),
    )
    chosen = row_body if whole_rows(mesh) else body
    return jax.shard_map(chosen, mesh=mesh, in_specs=in_specs, out_specs=out_specs, check_vma=False)
```

```python
from functools import partial
import math

import jax
import jax.numpy as jnp
from jax import lax
from jax.experimental import pallas as pl
from jax.experimental.pallas import tpu as pltpu
from jax.sharding import PartitionSpec as P

D = 768
HEADS = 12
HD = 64
FF = 3072
LEN = 1024
NDOC = 8
STEP = 10


NEGATIVE = -1e30
NORM_EPS = 1e-05
BETA_ONE = 0.9
BETA_TWO = 0.999
ADAM_EPS = 1e-08
WEIGHT_DECAY = 0.01


def layer_norm(values, norm_gain, norm_shift):
    center = values - jnp.mean(values, axis=-1, keepdims=True)
    spread = jnp.mean(center * center, axis=-1, keepdims=True)
    return center * lax.rsqrt(spread + NORM_EPS) * norm_gain + norm_shift


def gelu_tanh(values):
    return jax.nn.gelu(values, approximate=True)


def split_vectors(packed):
    return jnp.split(packed, [D, 2 * D, 3 * D, 4 * D, 5 * D, 6 * D, 7 * D, 7 * D + FF])


def adamw(master, first, second, gradient, rate):
    first_new = BETA_ONE * first + (1.0 - BETA_ONE) * gradient
    second_new = BETA_TWO * second + (1.0 - BETA_TWO) * gradient * gradient
    first_hat = first_new / (1.0 - BETA_ONE**STEP)
    second_hat = second_new / (1.0 - BETA_TWO**STEP)
    updated = master - rate * (
        first_hat / (jnp.sqrt(second_hat) + ADAM_EPS) + WEIGHT_DECAY * master
    )
    return (updated, first_new, second_new)


def learn_rates():
    return (
        1.0 / math.sqrt(2 * D),
        1.0 / math.sqrt(max(1, 2 * D * NDOC // LEN)),
        1.0 / math.sqrt(D),
        1.0 / math.sqrt(FF),
        0.3,
    )


def clip_level():
    return 0.5 * math.sqrt(4 * D * D + 2 * D * FF + 8 * D + FF)


def visible(query_pos, key_pos, query_seg, key_seg):
    return (key_pos[None, :] <= query_pos[:, None]) & (key_seg[None, :] == query_seg[:, None])


def attend_rows(query_pos, key_pos, packed_args):
    queries, keys_all, values_all, query_seg, key_seg = packed_args
    scores = jnp.einsum("qhd,khd->hqk", queries, keys_all, preferred_element_type=jnp.float32)
    scores = jnp.where(visible(query_pos, key_pos, query_seg, key_seg)[None], scores, NEGATIVE)
    top_score = jnp.max(scores, axis=-1, keepdims=True)
    exponent = jnp.exp(scores - top_score)
    totals = jnp.sum(exponent, axis=-1, keepdims=True)
    probability = (exponent / totals).astype(jnp.bfloat16)
    attended = jnp.einsum(
        "hqk,khd->qhd", probability, values_all, preferred_element_type=jnp.float32
    )
    return (attended, (top_score + jnp.log(totals))[..., 0])


def attend_back(query_pos, key_pos, packed_args):
    queries, keys_all, values_all, upstream, log_totals, query_seg, key_seg = packed_args
    scores = jnp.einsum("qhd,khd->hqk", queries, keys_all, preferred_element_type=jnp.float32)
    scores = jnp.where(visible(query_pos, key_pos, query_seg, key_seg)[None], scores, NEGATIVE)
    probability = jnp.exp(scores - log_totals[..., None])
    prob_low = probability.astype(jnp.bfloat16)
    prob_grad = jnp.einsum("qhd,khd->hqk", upstream, values_all, preferred_element_type=jnp.float32)
    value_part = jnp.einsum("hqk,qhd->khd", prob_low, upstream, preferred_element_type=jnp.float32)
    score_grad = probability * (
        prob_grad - jnp.sum(probability * prob_grad, axis=-1, keepdims=True)
    )
    score_low = score_grad.astype(jnp.bfloat16)
    query_part = jnp.einsum("hqk,khd->qhd", score_low, keys_all, preferred_element_type=jnp.float32)
    key_part = jnp.einsum("hqk,qhd->khd", score_low, queries, preferred_element_type=jnp.float32)
    key_count = keys_all.shape[0]
    return (
        query_part,
        jnp.concatenate(
            [key_part.reshape(key_count, -1), value_part.reshape(key_count, -1)], axis=1
        ),
    )


def body(
    inputs,
    segments,
    teacher,
    mixing_weight,
    output_weight,
    expand_weight,
    shrink_weight,
    vectors,
    mixing_first,
    output_first,
    expand_first,
    shrink_first,
    vectors_first,
    mixing_second,
    output_second,
    expand_second,
    shrink_second,
    vectors_second,
):
    bfloat = jnp.bfloat16
    floats = jnp.float32
    seq_count, local_len, features = inputs.shape
    row_count = seq_count * local_len
    scale = 1.0 / math.sqrt(HD)
    mixing_low, output_low, expand_low, shrink_low, vectors_low = (
        lax.all_gather(mixing_weight.astype(bfloat), "dp", axis=0, tiled=True),
        lax.all_gather(output_weight.astype(bfloat), "dp", axis=0, tiled=True),
        lax.all_gather(expand_weight.astype(bfloat), "dp", axis=0, tiled=True),
        lax.all_gather(shrink_weight.astype(bfloat), "dp", axis=0, tiled=True),
        lax.all_gather(vectors.astype(bfloat), "dp", axis=0, tiled=True),
    )
    (
        gain_one,
        shift_one,
        bias_query,
        bias_value,
        bias_output,
        gain_two,
        shift_two,
        bias_expand,
        bias_shrink,
    ) = split_vectors(vectors_low.astype(floats))
    states = inputs.astype(floats).reshape(row_count, features)
    normed = layer_norm(states, gain_one, shift_one)
    normed_low = normed.astype(bfloat)
    projected = jnp.dot(normed_low, mixing_low, preferred_element_type=floats)
    query_low = ((projected[:, :features] + bias_query) * scale).astype(bfloat)
    key_low = projected[:, features : 2 * features].astype(bfloat)
    value_low = (projected[:, 2 * features :] + bias_value).astype(bfloat)
    key_all, value_all = (
        lax.all_gather(key_low.reshape(seq_count, local_len, features), "seq", axis=1, tiled=True),
        lax.all_gather(
            value_low.reshape(seq_count, local_len, features), "seq", axis=1, tiled=True
        ),
    )
    segment_all = lax.all_gather(segments, "seq", axis=1, tiled=True)
    full_len = key_all.shape[1]
    query_pos = lax.axis_index("seq") * local_len + jnp.arange(local_len, dtype=jnp.int32)
    key_pos = jnp.arange(full_len, dtype=jnp.int32)
    query_heads = query_low.reshape(seq_count, local_len, HEADS, HD)
    key_heads = key_all.reshape(seq_count, full_len, HEADS, HD)
    value_heads = value_all.reshape(seq_count, full_len, HEADS, HD)
    attended, log_totals = lax.map(
        partial(attend_rows, query_pos, key_pos),
        (query_heads, key_heads, value_heads, segments, segment_all),
    )
    attended_low = attended.reshape(row_count, features).astype(bfloat)
    middle = states + jnp.dot(attended_low, output_low, preferred_element_type=floats) + bias_output
    normed_two = layer_norm(middle, gain_two, shift_two)
    normed_two_low = normed_two.astype(bfloat)
    hidden = jnp.dot(normed_two_low, expand_low, preferred_element_type=floats) + bias_expand
    active, gelu_back = jax.vjp(gelu_tanh, hidden)
    active_low = active.astype(bfloat)
    result = middle + jnp.dot(active_low, shrink_low, preferred_element_type=floats) + bias_shrink
    block_output = result.astype(bfloat).reshape(seq_count, local_len, features)
    target_prob = jax.nn.softmax(teacher.astype(floats).reshape(row_count, features), axis=-1)
    result_grad = features * (jax.nn.softmax(result, axis=-1) - target_prob)
    result_low = result_grad.astype(bfloat)
    grad_shrink = jnp.dot(active_low.T, result_low, preferred_element_type=floats)
    grad_bias_shrink = jnp.sum(result_grad, axis=0)
    active_grad = jnp.dot(result_low, shrink_low.T, preferred_element_type=floats)
    active_round = lax.optimization_barrier(active_grad.astype(bfloat)).astype(floats)
    hidden_low = gelu_back(active_round)[0].astype(bfloat)
    grad_bias_expand = jnp.sum(hidden_low.astype(floats), axis=0)
    grad_expand = jnp.dot(normed_two_low.T, hidden_low, preferred_element_type=floats)
    normed_two_grad = jnp.dot(hidden_low, expand_low.T, preferred_element_type=floats)
    norm_two_back = jax.vjp(layer_norm, middle, gain_two, shift_two)[1]
    middle_part, grad_gain_two, grad_shift_two = norm_two_back(normed_two_grad)
    middle_grad = result_grad + middle_part
    middle_low = middle_grad.astype(bfloat)
    grad_bias_output = jnp.sum(middle_grad, axis=0)
    grad_output = jnp.dot(attended_low.T, middle_low, preferred_element_type=floats)
    attended_grad = jnp.dot(middle_low, output_low.T, preferred_element_type=floats).astype(bfloat)
    upstream_heads = attended_grad.reshape(seq_count, local_len, HEADS, HD)
    query_grad, kv_terms = lax.map(
        partial(attend_back, query_pos, key_pos),
        (query_heads, key_heads, value_heads, upstream_heads, log_totals, segments, segment_all),
    )
    kv_sums = (
        lax.psum_scatter(kv_terms.astype(jnp.bfloat16), "seq", scatter_dimension=1, tiled=True)
        .astype(jnp.float32)
        .reshape(row_count, 2 * features)
    )
    key_grad_low = kv_sums[:, :features].astype(bfloat)
    value_grad_low = kv_sums[:, features:].astype(bfloat)
    query_grad_low = query_grad.reshape(row_count, features).astype(bfloat)
    query_scaled = query_grad_low.astype(floats) * scale
    grad_bias_query = jnp.sum(query_scaled, axis=0)
    grad_bias_value = jnp.sum(value_grad_low.astype(floats), axis=0)
    projected_grad = jnp.concatenate(
        [query_scaled.astype(bfloat), key_grad_low, value_grad_low], axis=1
    )
    grad_mixing = jnp.dot(normed_low.T, projected_grad, preferred_element_type=floats)
    normed_grad = jnp.dot(projected_grad, mixing_low.T, preferred_element_type=floats)
    norm_one_back = jax.vjp(layer_norm, states, gain_one, shift_one)[1]
    states_part, grad_gain_one, grad_shift_one = norm_one_back(normed_grad)
    input_grad = (middle_grad + states_part).astype(bfloat).reshape(seq_count, local_len, features)
    grad_vectors = jnp.concatenate(
        [
            grad_gain_one,
            grad_shift_one,
            grad_bias_query,
            grad_bias_value,
            grad_bias_output,
            grad_gain_two,
            grad_shift_two,
            grad_bias_expand,
            grad_bias_shrink,
        ]
    )
    vector_rows = grad_vectors.reshape(lax.axis_size("dp"), -1)
    mixing_part, output_part, expand_part, shrink_part, vector_part = (
        lax.psum_scatter(
            grad_mixing.astype(jnp.bfloat16), "dp", scatter_dimension=0, tiled=True
        ).astype(jnp.float32),
        lax.psum_scatter(
            grad_output.astype(jnp.bfloat16), "dp", scatter_dimension=0, tiled=True
        ).astype(jnp.float32),
        lax.psum_scatter(
            grad_expand.astype(jnp.bfloat16), "dp", scatter_dimension=0, tiled=True
        ).astype(jnp.float32),
        lax.psum_scatter(
            grad_shrink.astype(jnp.bfloat16), "dp", scatter_dimension=0, tiled=True
        ).astype(jnp.float32),
        lax.psum_scatter(
            vector_rows.astype(jnp.bfloat16), "dp", scatter_dimension=0, tiled=True
        ).astype(jnp.float32),
    )
    mixing_sum, output_sum, expand_sum, shrink_sum, vector_sum = (
        lax.psum(mixing_part.astype(jnp.bfloat16), "seq").astype(jnp.float32),
        lax.psum(output_part.astype(jnp.bfloat16), "seq").astype(jnp.float32),
        lax.psum(expand_part.astype(jnp.bfloat16), "seq").astype(jnp.float32),
        lax.psum(shrink_part.astype(jnp.bfloat16), "seq").astype(jnp.float32),
        lax.psum(vector_part.astype(jnp.bfloat16), "seq").astype(jnp.float32),
    )
    vector_sum = vector_sum.reshape(-1)
    squares = (
        jnp.sum(mixing_sum * mixing_sum)
        + jnp.sum(output_sum * output_sum)
        + jnp.sum(expand_sum * expand_sum)
        + jnp.sum(shrink_sum * shrink_sum)
        + jnp.sum(vector_sum * vector_sum)
    )
    grad_norm = jnp.sqrt(lax.psum(squares, "dp"))
    clip_value = clip_level()
    factor = clip_value / jnp.maximum(grad_norm, clip_value)
    step_rates = learn_rates()
    mixing_new = adamw(
        mixing_weight, mixing_first, mixing_second, mixing_sum * factor, step_rates[0]
    )
    output_new = adamw(
        output_weight, output_first, output_second, output_sum * factor, step_rates[1]
    )
    expand_new = adamw(
        expand_weight, expand_first, expand_second, expand_sum * factor, step_rates[2]
    )
    shrink_new = adamw(
        shrink_weight, shrink_first, shrink_second, shrink_sum * factor, step_rates[3]
    )
    vectors_new = adamw(vectors, vectors_first, vectors_second, vector_sum * factor, step_rates[4])
    return (
        block_output,
        input_grad,
        grad_norm,
        mixing_new[0],
        output_new[0],
        expand_new[0],
        shrink_new[0],
        vectors_new[0],
        mixing_new[1],
        output_new[1],
        expand_new[1],
        shrink_new[1],
        vectors_new[1],
        mixing_new[2],
        output_new[2],
        expand_new[2],
        shrink_new[2],
        vectors_new[2],
    )

MESH = pl.DeviceIdType.MESH
BF = jnp.bfloat16
F32 = jnp.float32
BLK = 256
NN = ((1,), (0,))
NT = ((1,), (1,))
TN = ((0,), (0,))
VMEM_BYTES = 64 * 2**20 - 2**17
VROWS = 16
MIX, OUT, EXP, SHR = 0, 1, 2, 3
HALF = D // 2
PAIRS = D // 128
EXPAND_TILE = D
SUBS = (4, 1, 2, 2)
LANES = (0, 4, 5, 7)


def dot(left, right, dims):
    return lax.dot_general(left, right, (dims, ((), ())), preferred_element_type=F32)


class Place:
    def __init__(self, count):
        self.count = count
        self.hops = (count // 2, count - 1 - count // 2)
        self.dp = lax.axis_index("dp")
        self.seq = lax.axis_index("seq")
        odd = self.dp % 2
        self.pos = (1 - odd) * (self.dp // 2) + odd * (count - 1 - self.dp // 2)
        self.core = self.seq % 2
        self.x = self.seq // 2
        self.step = 1 - 2 * self.core
        self.sides = ((self.ahead(1), self.seq), (self.behind(1), self.seq))
        self.mate = self.kin(1)
        self.across = self.kin(2)

    def at(self, pos):
        pos = pos % self.count
        upper = pos // (self.count // 2)
        return (1 - upper) * (2 * pos) + upper * (2 * (self.count - 1 - pos) + 1)

    def ahead(self, steps):
        return self.at(self.pos + steps * self.step + self.count)

    def behind(self, steps):
        return self.at(self.pos - steps * self.step + self.count)

    def kin(self, which):
        core = self.core + (1 - 2 * self.core) * (which % 2)
        return (self.dp, 2 * (self.x + (1 - 2 * self.x) * (which // 2)) + core)

    def dp_peer(self, offset):
        return ((self.dp + offset) % self.count, self.seq)

    def greet(self):
        barrier = pltpu.get_barrier_semaphore()
        peers = [self.kin(k) for k in range(1, 4)]
        peers += [self.dp_peer(k) for k in range(1, self.count)]
        for peer in peers:
            pl.semaphore_signal(barrier, inc=1, device_id=peer, device_id_type=MESH)
        return lambda: pl.semaphore_wait(barrier, len(peers))


def describe(src, dst, send, recv, device):
    return pltpu.make_async_remote_copy(
        src_ref=src,
        dst_ref=dst,
        send_sem=send,
        recv_sem=recv,
        device_id=device,
        device_id_type=MESH,
    )


def remote(src, dst, send, recv, device):
    copy = describe(src, dst, send, recv, device)
    copy.start()
    return copy


def local(src, dst, sem):
    copy = pltpu.make_async_copy(src, dst, sem)
    copy.start()
    return copy


def span(start, size, unit):
    return pl.ds(start if isinstance(start, int) else pl.multiple_of(start, unit), size)


def spread(ticks, marks):
    def at(trip, mark, first=0, past=None):
        for n in range(first, len(ticks) // marks if past is None else past):
            here = ticks[n * marks + mark]
            if here:

                def run(here=here):
                    for tick in here:
                        tick()

                pl.when(trip == n)(run)

    return at


class Group:
    def __init__(self, send, recv, of_all_sent, of_all_received, device):
        self.send, self.recv, self.device = send, recv, device
        self.bytes = (of_all_sent, of_all_received)

    def start(self, src, dst, device):
        describe(src, dst, self.send, self.recv, device).start()

    def all(self, which):
        return describe(self.bytes[which], self.bytes[which], self.send, self.recv, self.device)

    def wait_recv(self):
        self.all(1).wait_recv()

    def wait_send(self):
        self.all(0).wait_send()


class Gather:
    def __init__(self, place, full, sems):
        self.place, self.full = place, full
        self.ring_s, self.ring_r, self.mate_s, self.mate_r, self.cross_s, self.cross_r = sems

    def lanes(self, w):
        return ((0, 1, 2), (0,), (self.place.x, 2, 3), (self.place.x, 2, 3))[w]

    def part(self, ref, w, sub):
        rows, columns = ref.shape[-2:]
        lead = (slice(None),) * (len(ref.shape) - 2)
        if w == SHR:
            unit = rows // 4
            return ref.at[lead + (span(sub * unit, unit, 16),)]
        unit = columns // (3, 1, 4)[w]
        return ref.at[lead + (slice(None), span(sub * unit, unit, 128))]

    def cut(self, w, owner, core, sub):
        return self.part(self.full[w].at[owner, core], w, sub)

    def block(self, w, sub, way, t):
        owner = self.place.ahead(t) if way else self.place.behind(t)
        return self.cut(w, owner, self.place.core, sub)

    def copy(self, block, send, recv, device):
        return describe(block, block, send, recv, device)

    def ring(self, w, lane, way, t):
        index = ((0, 3, 4, 7)[w] + lane, t + way * self.place.hops[0])
        block = self.block(w, self.lanes(w)[lane], way, t)
        return self.copy(block, self.ring_s.at[w], self.ring_r.at[index], self.place.sides[way])

    def pair(self, w, sub, way, t):
        block = self.block(w, sub, way, t)
        return self.copy(block, self.mate_s.at[w], self.mate_r.at[w], self.place.mate)

    def over(self, w, way, t):
        recv = self.cross_r.at[w - EXP, t - 1 + way * self.place.hops[0]]
        block = self.block(w, self.place.x, way, t)
        return self.copy(block, self.cross_s.at[w - EXP], recv, self.place.across)

    def start(self, w):
        for lane in range(len(self.lanes(w))):
            for way in range(2):
                self.ring(w, lane, way, 0).start()

    def tick(self, w, lane, way, t):
        self.ring(w, lane, way, t - 1).wait_recv()
        if t < self.place.hops[way]:
            self.ring(w, lane, way, t).start()
        self.pair(w, self.lanes(w)[lane], way, t).start()
        if w >= EXP and lane == 0:
            self.over(w, way, t).start()

    def relay(self, w, way, t):
        self.over(w, way, t).wait_recv()
        self.pair(w, 1 - self.place.x, way, t).start()

    def others(self, w):
        return self.full[w].at[pl.ds(0, self.place.count - 1), self.place.core]

    def arrived(self, w):
        block = self.others(w)
        self.copy(block, self.mate_s.at[w], self.mate_r.at[w], self.place.mate).wait_recv()

    def drain(self, w):
        block = self.others(w)
        self.copy(block, self.mate_s.at[w], self.mate_r.at[w], self.place.mate).wait_send()
        if w >= EXP:
            for lane in range(len(self.lanes(w))):
                part = self.part(block, w, self.lanes(w)[lane])
                self.copy(part, self.ring_s.at[w], self.mate_r.at[w], self.place.mate).wait_send()
            part = self.part(block, w, 0)
            self.copy(part, self.cross_s.at[w - EXP], self.mate_r.at[w], self.place.across).wait_send()
        else:
            self.copy(block, self.ring_s.at[w], self.mate_r.at[w], self.place.mate).wait_send()


class Scatter:
    def __init__(self, place, grads, mates, slots, sums, sems):
        self.place, self.grads, self.mates, self.slots = place, grads, mates, slots
        self.sums = sums
        (
            self.mate_s,
            self.mate_r,
            self.ring_s,
            self.ring_r,
            self.cross_s,
            self.cross_r,
            self.total_s,
            self.total_r,
        ) = sems

    def cut(self, ref, w, sub):
        rows, columns = ref.shape[-2:]
        lead = (slice(None),) * (len(ref.shape) - 2)
        if w == SHR:
            return ref.at[lead + (span(sub * (rows // 2), rows // 2, 16),)]
        if w == MIX:
            rows = self.sums[w].shape[1]
            there = pl.ds((sub - 1) * (rows // 3), rows // 3) if sub else pl.ds(0, rows)
            return ref.at[lead + (there, pl.ds(HALF if sub else 0, HALF))]
        size = columns // SUBS[w]
        return ref.at[lead + (slice(None), span(sub * size, size, 128))]

    def owner(self, way, distance):
        return self.place.behind(distance) if way else self.place.ahead(distance)

    def own(self, w, owner, core, sub):
        return self.cut(self.grads[w].at[owner, core], w, sub)

    def slot(self, w, way, t, sub):
        return self.cut(self.slots(w, t + way * self.place.hops[0]), w, sub)

    def pair(self, w, sub, owner):
        return describe(
            self.own(w, owner, 1 - self.place.core, sub),
            self.cut(self.mates(w, owner), w, sub),
            self.mate_s.at[LANES[w] + sub],
            self.mate_r.at[LANES[w] + sub],
            self.place.mate,
        )

    def pairs(self, w, sub):
        block = self.cut(self.grads[w].at[:, self.place.core], w, sub)
        return describe(
            block, block, self.mate_s.at[LANES[w] + sub], self.mate_r.at[LANES[w] + sub], self.place.mate
        )

    def ring(self, w, sub, way, t):
        if t == 0:
            owner = self.owner(way, self.place.hops[way])
            src = self.own(w, owner, self.place.core, sub)
        else:
            src = self.slot(w, way, t - 1, sub)
        index = (LANES[w] + sub, t + way * self.place.hops[0])
        return describe(
            src,
            self.slot(w, way, t, sub),
            self.ring_s.at[LANES[w] + sub],
            self.ring_r.at[index],
            self.place.sides[way],
        )

    def over(self, w, sub):
        return describe(
            self.own(w, self.place.dp, self.place.core, sub),
            self.cut(self.sums[w].at[self.place.core], w, sub),
            self.cross_s.at[LANES[w] + sub],
            self.cross_r.at[LANES[w] + sub],
            self.place.across,
        )

    def total(self, w, sub):
        block = self.cut(self.sums[w].at[self.place.core], w, sub)
        return describe(
            block, block, self.total_s.at[LANES[w] + sub], self.total_r.at[LANES[w] + sub], self.place.mate
        )

    def hand(self, w, sub):
        for owner in range(self.place.count):
            self.pair(w, sub, owner).start()

    def term(self, w, sub, way, distance):
        owner = self.owner(way, distance)
        mine = self.own(w, owner, self.place.core, sub)[...].astype(F32)
        return mine + self.cut(self.mates(w, owner), w, sub)[...].astype(F32)

    def start(self, w, sub):
        self.pairs(w, sub).wait_recv()
        for way, hops in enumerate(self.place.hops):
            term = self.term(w, sub, way, hops)
            self.own(w, self.owner(way, hops), self.place.core, sub)[...] = term.astype(BF)
            self.ring(w, sub, way, 0).start()

    def tick(self, w, sub, way, t):
        self.ring(w, sub, way, t - 1).wait_recv()
        slot = self.slot(w, way, t - 1, sub)
        term = self.term(w, sub, way, self.place.hops[way] - t)
        slot[...] = (slot[...].astype(F32) + term).astype(BF)
        self.ring(w, sub, way, t).start()

    def finish(self, w, sub):
        total = self.term(w, sub, 0, 0)
        for way, hops in enumerate(self.place.hops):
            self.ring(w, sub, way, hops - 1).wait_recv()
            total = total + self.slot(w, way, hops - 1, sub)[...].astype(F32)
        self.own(w, self.place.dp, self.place.core, sub)[...] = total.astype(BF)
        self.over(w, sub).start()

    def crossed(self, w, sub):
        self.over(w, sub).wait_recv()
        value = self.own(w, self.place.dp, self.place.core, sub)[...].astype(F32)
        there = self.cut(self.sums[w].at[self.place.core], w, sub)
        there[...] = (value + there[...].astype(F32)).astype(BF)
        self.total(w, sub).start()

    def arrived(self, w, sub):
        self.total(w, sub).wait_recv()

    def drain(self, w):
        for sub in range(SUBS[w]):
            self.pairs(w, sub).wait_send()
            sent = self.cut(self.grads[w].at[pl.ds(0, self.place.count - 1), self.place.core], w, sub)
            describe(
                sent, sent, self.ring_s.at[LANES[w] + sub], self.mate_r.at[LANES[w] + sub], self.place.mate
            ).wait_send()
            self.over(w, sub).wait_send()
            self.total(w, sub).wait_send()

    def ticks(self, w, t, subs):
        return [
            partial(self.tick, w, sub, way, t)
            for sub in subs
            for way, hops in enumerate(self.place.hops)
            if t < hops
        ]


def half_lanes(hd):
    lane = lax.broadcasted_iota(jnp.int32, (1, 128), 1)
    return (lane < 64) if hd == 0 else (lane >= 64)


def document_lanes(documents):
    lane = lax.broadcasted_iota(jnp.int32, documents.shape, 1) % 64
    same = jnp.logical_and(documents == lane.astype(F32), lane < 8)
    return jnp.where(same, 1.0, 0.0).astype(BF)


def marked_keys(keys, marked):
    hidden = ((1.0 - marked.astype(F32)) * NEGATIVE).astype(BF)
    return [jnp.where(half_lanes(hd), keys, hidden) for hd in range(2)]


def columns_of(hp):
    first = (hp // 3) * (3 * HALF) + (hp % 3) * 128
    return [span(first + part * HALF, 128, 128) for part in range(3)]


def attend_pair(hp, qkv, marked, causal, out, lse, scores, tick):
    cq, ck, cv = columns_of(hp)
    vt = qkv[:, cv].T
    ones = jnp.ones((8, vt.shape[1]), BF)
    keys = marked_keys(qkv[:, ck], marked[...])
    values = [jnp.concatenate([vt[hd * 64 : (hd + 1) * 64, :], ones], axis=0) for hd in range(2)]
    def rows_of(n):
        return slice(n * BLK, (n + 1) * BLK)

    def score(i, hd):
        kept = rows_of(hd)
        query = jnp.where(half_lanes(hd), qkv[rows_of(i), cq], marked[rows_of(i), :])
        top = None
        for j in range(i + 1):
            s = dot(keys[hd][rows_of(j), :], query, NT)
            if i == j:
                s = s + causal[...]
            scores[rows_of(j), kept] = s
            best = jnp.max(s, axis=0, keepdims=True)
            top = best if top is None else jnp.maximum(top, best)
        return top

    def weigh(i, hd, top):
        parts = [
            jnp.exp(scores[rows_of(j), rows_of(hd)] - top).astype(BF) for j in range(i + 1)
        ]
        return i, hd, top, parts

    outs = []

    def collect(i, hd, top, parts):
        acc = None
        for j, p in enumerate(parts):
            term = dot(values[hd][:, rows_of(j)], p, NN)
            acc = term if acc is None else acc + term
        total = acc[64:65, :]
        lse[pl.ds(hp * 2 + hd, 1), rows_of(i)] = top + jnp.log(total)
        outs.append(acc[0:64, :] * (1.0 / total))
        if hd == 1:
            out[rows_of(i), span(hp * 128, 128, 128)] = (
                jnp.concatenate(outs, axis=0).T.astype(BF)
            )
            outs[:] = []

    chains = [(i, hd) for i in range(qkv.shape[0] // BLK) for hd in range(2)]
    tick(0)
    top = score(*chains[0])
    behind = None
    for n, (i, hd) in enumerate(chains):
        after = None
        if n + 1 < len(chains):
            if hd == 1:
                tick(i + 1)
            after = score(*chains[n + 1])
        if behind is not None:
            collect(*behind)
        behind = weigh(i, hd, top)
        top = after
    collect(*behind)


def attend_back_pair(hp, qkv, marked, causal, out, upstream, lse, sums, tick):
    cq, ck, cv = columns_of(hp)
    co = span(hp * 128, 128, 128)
    in_v, in_k = slice(0, 128), slice(128, 256)
    kt = qkv[:, ck].T
    keys = marked_keys(qkv[:, ck], marked[...])
    def rows_of(n):
        return slice(n * BLK, (n + 1) * BLK)

    def operands(i):
        qb = qkv[rows_of(i), cq]
        db = upstream[rows_of(i), co]
        none = jnp.zeros_like(qb)
        prod = (db.astype(F32) * out[rows_of(i), co].astype(F32)).T
        queries = [jnp.where(half_lanes(hd), qb, marked[rows_of(i), :]) for hd in range(2)]
        grads = [jnp.where(half_lanes(hd), db, none) for hd in range(2)]
        return (
            queries,
            grads,
            [jnp.sum(prod[hd * 64 : (hd + 1) * 64, :], axis=0, keepdims=True) for hd in range(2)],
            [lse[pl.ds(hp * 2 + hd, 1), rows_of(i)] for hd in range(2)],
            jnp.concatenate([jnp.where(half_lanes(hd), qb, none) for hd in range(2)], axis=0),
            jnp.concatenate(grads, axis=0),
        )

    def products(n, ops):
        i, j = blocks[n]
        kept = slice((1 + n % 2) * BLK, (2 + n % 2) * BLK)
        for hd in range(2):
            s = dot(keys[hd][rows_of(j), :], ops[0][hd], NT)
            sums[rows_of(hd), kept] = s + causal[...] if i == j else s
            sums[rows_of(2 + hd), kept] = dot(qkv[rows_of(j), cv], ops[1][hd], NT)

    blocks = [(i, j) for i in range(qkv.shape[0] // BLK) for j in range(i + 1)]
    tick(0)
    ops = operands(0)
    products(0, ops)
    dqs = [None, None]

    def gather_block(i, j, now, ps, dss):
        for hd in range(2):
            term = dot(kt[hd * 64 : (hd + 1) * 64, rows_of(j)], dss[hd], NN)
            dqs[hd] = term if dqs[hd] is None else dqs[hd] + term
        pv = dot(jnp.concatenate(ps, axis=1), now[5], NN)
        pk = dot(jnp.concatenate(dss, axis=1), now[4], NN)
        if i == j:
            sums[rows_of(j), in_v] = pv
            sums[rows_of(j), in_k] = pk
            low = jnp.concatenate(dqs, axis=0).T.astype(BF).astype(F32)
            qkv[rows_of(i), cq] = (low * (1.0 / math.sqrt(HD))).astype(BF)
            dqs[:] = [None, None]
        else:
            sums[rows_of(j), in_v] += pv
            sums[rows_of(j), in_k] += pk

    behind = None
    for n, (i, j) in enumerate(blocks):
        now = ops
        kept = slice((1 + n % 2) * BLK, (2 + n % 2) * BLK)
        if n + 1 < len(blocks):
            if blocks[n + 1][1] == 0:
                tick(i + 1)
                ops = operands(i + 1)
            products(n + 1, ops)
        if behind is not None:
            gather_block(*behind)
        ps, dss = [], []
        for hd in range(2):
            p = jnp.exp(sums[rows_of(hd), kept] - now[3][hd])
            ps.append(p.astype(BF))
            dss.append((p * (sums[rows_of(2 + hd), kept] - now[2][hd])).astype(BF))
        behind = (i, j, now, ps, dss)
    gather_block(*behind)
    qkv[:, ck] = sums[:, in_k].astype(BF)
    qkv[:, cv] = sums[:, in_v].astype(BF)


def normalised(values):
    center = values - jnp.mean(values, axis=-1, keepdims=True)
    inverse = lax.rsqrt(jnp.mean(center * center, axis=-1, keepdims=True) + NORM_EPS)
    return center * inverse, inverse


def norm_grad(values, gain, upstream):
    hat, inverse = normalised(values)
    scaled = upstream * gain
    first = jnp.mean(scaled, axis=-1, keepdims=True)
    second = jnp.mean(scaled * hat, axis=-1, keepdims=True)
    return (
        inverse * (scaled - first - hat * second),
        jnp.sum(upstream * hat, axis=0, keepdims=True),
        jnp.sum(upstream, axis=0, keepdims=True),
    )


def gelu_both(u):
    inner = math.sqrt(2.0 / math.pi)
    cubic = inner * 0.044715
    square = u * u
    half = 0.5 + 0.5 * jnp.tanh(u * (inner + cubic * square))
    value = u * half
    return value, half + value * (1.0 - half) * (2.0 * inner + 6.0 * cubic * square)


def softmax(values):
    e = jnp.exp(values - jnp.max(values, axis=-1, keepdims=True))
    return e * (1.0 / jnp.sum(e, axis=-1, keepdims=True))


def whole(ref):
    return ref[...].reshape(-1, ref.shape[-1])


VEC_PLACES = (("g1", D), ("b1", D), ("bq", D), ("bv", D), ("bo", D), ("g2", D), ("b2", D), ("bf1", FF), ("bf2", D))
VEC_ROW = {name: row for row, (name, _) in enumerate(VEC_PLACES)}
VEC_SIZE = dict(VEC_PLACES)


def block_kernel(count, *refs):
    inputs, teacher, segments, masters, vec_ref = refs[0], refs[1], refs[2], refs[3:7], refs[7]
    sums_out, vec_sum, norm_ref, out_rows, back_rows = refs[8:12], *refs[12:16]
    (
        full0, full1, full2, full3, x, h1, qkv, att, x1, h2, act, slope, dy, low, sent, shrink_grads,
        shr_mate, shr_slot, lse, segs, seg_stage, marked, causal,
        sums0, sums1, sums2, sums3, vec_stage, vec_all, vec, gvec, vec_out, vec_buf, vec_mine, vec_seq, sq_mine, sq_buf,
        load_sem, g_ring_s, g_ring_r, g_mate_s, g_mate_r, g_cross_s, g_cross_r,
        s_mate_s, s_mate_r, s_ring_s, s_ring_r, s_cross_s, s_cross_r, s_total_s, s_total_r,
        row_s, row_r, row_l, vec_s, vec_r, free,
    ) = refs[16:]
    full = (full0, full1, full2, full3)
    sums = (sums0, sums1, sums2, sums3)
    place = Place(count)
    ready = place.greet()
    length = x.shape[0]
    blocks = length // BLK
    scale = 1.0 / math.sqrt(HD)

    def rows(i):
        return span(i * BLK, BLK, BLK)

    loads, pieces, used = [], [], [0, 0]
    for w in (MIX, OUT, EXP, SHR):
        height, width = masters[w].shape
        for column in range(0, width, D):
            which = 0 if used[0] + height <= length else 1
            where = (dy, x1)[which].at[pl.ds(used[which], height)]
            used[which] += height
            source = masters[w].at[:, pl.ds(column, D)]
            loads.append(local(source, where, load_sem.at[len(loads)]))
            pieces.append((w, column, where))

    def stage(w):
        for load, (owner, column, where) in zip(loads, pieces):
            if owner == w:
                load.wait()
                piece = where[...].astype(BF).reshape(full[w].shape[1:3] + (D,))
                if w == MIX:
                    for part in range(2):
                        c = slice(part * HALF, (part + 1) * HALF)
                        there = pl.ds(part * 3 * HALF + column // 2, HALF)
                        full[w][place.dp, :, :, there] = piece[:, :, c]
                else:
                    full[w][place.dp, :, :, pl.ds(column, D)] = piece

    gather = Gather(place, full, (g_ring_s, g_ring_r, g_mate_s, g_mate_r, g_cross_s, g_cross_r))
    stage(MIX)
    ready()
    gather.start(MIX)

    me = rows(place.seq)
    three, seven = pl.ds(0, 3), pl.ds(0, count - 1)
    most = pl.ds(0, 3 * BLK)

    def group(n, sent, received):
        return Group(row_s.at[n], row_r.at[n], sent, received, place.mate)

    row_in = group(0, inputs.at[three], x.at[most])
    seg_in = group(1, seg_stage.at[three], segs.at[three])
    teach_in = group(2, teacher.at[three], low.at[most])
    out_go = group(3, out_rows.at[three], out_rows.at[three])
    back_go = group(4, back_rows.at[three], back_rows.at[three])
    seq_go = group(5, vec_seq.at[three], vec_seq.at[three])
    vec_in = Group(vec_s.at[0], vec_r.at[0], vec_all.at[seven], vec_all.at[seven], place.mate)
    vec_go = Group(vec_s.at[1], vec_r.at[1], vec_buf.at[seven], vec_buf.at[seven], place.mate)
    sq_go = Group(vec_s.at[2], vec_r.at[2], sq_buf.at[seven], sq_buf.at[seven], place.mate)
    for k in (2, 3, 1):
        peer = place.kin(k)
        row_in.start(inputs.at[peer[1]], x.at[me], peer)
    row_local = local(inputs.at[place.seq], x.at[me], row_l.at[0])
    seg_stage[...] = jnp.broadcast_to(segments[...][:, None, :], seg_stage.shape)
    vec_stage[...] = jnp.concatenate(
        [vec_ref[...].astype(BF).astype(F32), jnp.zeros((VROWS - vec_ref.shape[0], 128), F32)],
        axis=0,
    )
    for k in range(1, count):
        vec_in.start(vec_stage, vec_all.at[place.dp], place.dp_peer(k))
    for k in (2, 3, 1):
        peer = place.kin(k)
        seg_in.start(seg_stage.at[peer[1]], segs.at[place.seq], peer)

    def send_teacher(k, part=0, parts=1):
        size = BLK // parts
        there = low.at[span(place.seq * BLK + part * size, size, 16)]
        peer = place.kin(k)
        teach_in.start(teacher.at[peer[1], pl.ds(part * size, size)], there, peer)

    for k in (2, 1):
        send_teacher(k)
    segs[place.seq] = seg_stage[place.seq]
    vec_all[place.dp] = vec_stage[...]
    teach_local = local(teacher.at[place.seq], low.at[me], row_l.at[1])
    for w in (OUT, EXP, SHR):
        stage(w)

    def ring_steps(w, t):
        return [
            partial(gather.tick, w, lane, way, t)
            for lane in range(len(gather.lanes(w)))
            for way in range(2)
            if t <= place.hops[way]
        ]

    def relays(w, t):
        return [partial(gather.relay, w, way, t) for way in range(2) if 1 <= t <= place.hops[way]]

    far = place.hops[0]
    for t in range(1, far + 1):
        for step in ring_steps(MIX, t):
            step()
        if t == far - 2:
            gather.start(OUT)
        if t == far - 1:
            gather.start(EXP)
    for step in ring_steps(OUT, 1):
        step()

    vec_in.wait_recv()
    per = vec_ref.shape[0]
    flat = 0
    for name, size in VEC_PLACES:
        parts = []
        for r in range(flat, flat + size // 128):
            parts.append(vec_all[r // per, r % per : r % per + 1, :])
        vec[VEC_ROW[name] : VEC_ROW[name] + 1, 0:size] = jnp.concatenate(parts, axis=1)
        flat += size // 128

    def of(name):
        return vec[VEC_ROW[name] : VEC_ROW[name] + 1, 0 : VEC_SIZE[name]]

    def add_grad(name, term, start=0):
        gvec[VEC_ROW[name] : VEC_ROW[name] + 1, start : start + term.shape[1]] += term

    gvec[...] = jnp.zeros_like(gvec)
    row_local.wait()
    row_in.wait_recv()
    seg_in.wait_recv()

    for s in range(4):
        documents = jnp.concatenate([segs[s].astype(F32)] * 16, axis=0).T
        marked[s * BLK : (s + 1) * BLK, :] = document_lanes(documents)
    earlier = lax.broadcasted_iota(jnp.int32, (BLK, BLK), 0) <= lax.broadcasted_iota(
        jnp.int32, (BLK, BLK), 1
    )
    causal[...] = jnp.where(earlier, 0.0, NEGATIVE)

    def first_norm(i, _):
        hat, _ = normalised(x[rows(i), :].astype(F32))
        h1[rows(i), :] = (hat * of("g1") + of("b1")).astype(BF)
        return 0

    lax.fori_loop(0, blocks, first_norm, 0)
    gather.arrived(MIX)

    def lane(w, number, t):
        return [partial(gather.tick, w, number, way, t) for way in range(2) if t <= place.hops[way]]

    def piece(n):
        return [partial(send_teacher, 3, n, 4)]

    in_project = spread(
        [[], [], lane(EXP, 0, 1), lane(EXP, 1, 1), piece(0), lane(EXP, 2, 1), [], lane(OUT, 0, 2)],
        2,
    )
    in_forward = spread(
        [
            [],
            lane(EXP, 0, 2) + piece(1),
            lane(EXP, 1, 2) + lane(EXP, 2, 2),
            lane(OUT, 0, 3),
            lane(EXP, 0, 3) + lane(OUT, 0, 4) + piece(2),
            lane(EXP, 1, 3) + lane(EXP, 2, 3) + [partial(gather.start, SHR)],
        ],
        1,
    )
    in_middle = spread([[], lane(EXP, 0, 4) + piece(3), lane(EXP, 1, 4), lane(EXP, 2, 4)], 1)
    before_expand = relays(EXP, 1) + relays(EXP, 2) + lane(SHR, 0, 1) + relays(EXP, 3)
    before_expand += lane(SHR, 1, 1) + relays(EXP, 4)
    in_expand = spread(
        [
            lane(SHR, 2, 1), lane(SHR, 0, 2),
            lane(SHR, 1, 2), lane(SHR, 2, 2),
            lane(SHR, 0, 3), lane(SHR, 1, 3),
            lane(SHR, 2, 3), lane(SHR, 0, 4),
        ],
        2,
    )
    after_expand = lane(SHR, 1, 4) + lane(SHR, 2, 4)
    for t in range(1, far + 1):
        after_expand += relays(SHR, t)

    def project(i, _):
        in_project(i, 0)
        value = dot(h1[rows(i), :], whole(full[MIX]), NN)
        for part in range(2):
            c = slice(part * HALF, (part + 1) * HALF)
            q, k, v = (
                slice(part * 3 * HALF + n * HALF, part * 3 * HALF + (n + 1) * HALF) for n in range(3)
            )
            qkv[rows(i), q] = ((value[:, q] + of("bq")[:, c]) * scale).astype(BF)
            qkv[rows(i), k] = value[:, k].astype(BF)
            qkv[rows(i), v] = (value[:, v] + of("bv")[:, c]).astype(BF)
        in_project(i, 1)
        return 0

    lax.fori_loop(0, blocks, project, 0)
    def forward_pair(hp, _):
        attend_pair(
            hp,
            qkv,
            marked,
            causal,
            att,
            lse,
            dy,
            lambda i: in_forward(hp, 0) if i == 0 else None,
        )
        return 0

    lax.fori_loop(0, PAIRS, forward_pair, 0)
    def middle(i, _):
        in_middle(i, 0)
        value = x[rows(i), :].astype(F32) + dot(att[rows(i), :], whole(full[OUT]), NN) + of("bo")
        x1[rows(i), :] = value
        hat, _ = normalised(value)
        h2[rows(i), :] = (hat * of("g2") + of("b2")).astype(BF)
        return 0

    gather.arrived(OUT)
    lax.fori_loop(0, blocks, middle, 0)

    def target(i, _):
        dy[rows(i), :] = softmax(low[rows(i), :].astype(F32))
        return 0

    for tick in before_expand:
        tick()
    teach_local.wait()
    teach_in.wait_recv()
    lax.fori_loop(0, blocks, target, 0)
    gather.arrived(EXP)

    def expand(i, _):
        for n in range(FF // EXPAND_TILE):
            if n % 2 == 0:
                in_expand(i, n // 2)
            c = slice(n * EXPAND_TILE, (n + 1) * EXPAND_TILE)
            weight = full[EXP][:, :, :, c].reshape(D, EXPAND_TILE)
            u = dot(h2[rows(i), :], weight, NN) + vec[VEC_ROW["bf1"] : VEC_ROW["bf1"] + 1, c]
            a, s = gelu_both(u)
            act[rows(i), c] = a.astype(BF)
            slope[rows(i), c] = s.astype(BF)
        return 0

    lax.fori_loop(0, blocks, expand, 0)
    for tick in after_expand:
        tick()
    gather.arrived(SHR)

    def shrink(i, _):
        value = x1[rows(i), :] + dot(act[rows(i), :], whole(full[SHR]), NN) + of("bf2")
        sent[rows(i), :] = value.astype(BF)
        grad = D * (softmax(value) - dy[rows(i), :])
        dy[rows(i), :] = grad
        low[rows(i), :] = grad.astype(BF)
        add_grad("bf2", jnp.sum(grad, axis=0, keepdims=True))
        return 0

    lax.fori_loop(0, blocks, shrink, 0)
    for w in (MIX, OUT, EXP, SHR):
        gather.drain(w)

    def send_rows(rows_out, copies, k, first=0, size=BLK):
        peer = place.kin(k)
        source = sent.at[span(peer[1] * BLK + first, size, 128)]
        copies.start(source, rows_out.at[place.seq, pl.ds(first, size)], peer)

    out_local = local(sent.at[me], out_rows.at[place.seq], row_l.at[2])
    for k in (2, 3, 1):
        send_rows(out_rows, out_go, k)

    half, some = full[MIX].shape[2], count // 2

    def part_of(buffer, w, where):
        if w == EXP:
            return act.at[where]
        return slope.at[where, pl.ds(3 * D, D)]

    def third(group, n):
        return slope.at[span(n * 3 * half, 3 * half, 16), span(group * D, D, 128)]

    def mates(w, owner):
        if w == SHR:
            return shr_mate.at[owner]
        if w == MIX:
            return third(owner // (count // 2), owner % (count // 2))
        return part_of(act, w, span(owner * half, half, 16))

    def slots(w, t):
        if w == SHR:
            return shr_slot.at[t]
        if w == MIX:
            return third(2, t)
        return part_of(act, w, span((count + t) * half, half, 16))

    scatter = Scatter(
        place,
        (full3, full1, full2, shrink_grads),
        mates,
        slots,
        sums,
        (s_mate_s, s_mate_r, s_ring_s, s_ring_r, s_cross_s, s_cross_r, s_total_s, s_total_r),
    )

    def offer(which):
        for n, peer in enumerate((place.mate,) + place.sides):
            pl.semaphore_signal(
                free.at[3 * which + n], inc=1, device_id=peer, device_id_type=MESH
            )

    def accept(which, which_sides):
        for n in range(1, 3) if which_sides else range(1):
            pl.semaphore_wait(free.at[3 * which + n], 1)

    def shrink_grad(n, _):
        value = dot(act[:, span(n * D, D, 128)], low[...], TN).astype(BF)
        shrink_grads[pl.ds(2 * n, 2)] = value.reshape((2,) + shrink_grads.shape[1:])
        for owner in range(2):
            for sub in range(2):
                scatter.pair(SHR, sub, 2 * n + owner).start()
        return 0

    lax.fori_loop(0, FF // D, shrink_grad, 0)
    offer(0)

    def hop(w, t, sub):
        return scatter.ticks(w, t, (sub,))

    def end(w, sub):
        return [partial(scatter.finish, w, sub)]

    in_middle_back = spread([hop(SHR, 1, 0), [], hop(SHR, 1, 1), []], 1)
    in_expand_grad = spread([hop(SHR, 2, 0), [], hop(SHR, 2, 1), []], 1)
    in_upstream = spread(
        [[partial(scatter.start, EXP, 0)] + hop(SHR, 3, 0), [], [], []],
        1,
    )
    in_backward = spread(
        [
            hop(SHR, 3, 1), [], [], [],
            [partial(scatter.start, OUT, 0)] + hop(EXP, 1, 0) + end(SHR, 0), [], [], [],
            hop(EXP, 1, 1), [], [], hop(EXP, 2, 0) + hop(OUT, 1, 0) + end(SHR, 1),
            hop(EXP, 2, 1), [], [], hop(OUT, 2, 0) + hop(EXP, 3, 0) + [partial(scatter.start, MIX, 0)],
            [], [], [], hop(EXP, 3, 1) + hop(OUT, 3, 0),
            end(EXP, 0), [], [], hop(MIX, 1, 0) + end(OUT, 0) + end(EXP, 1),
        ],
        4,
    )

    in_expand_back = spread([[], [partial(scatter.start, SHR, sub) for sub in range(2)], [], []], 1)

    def expand_back(i, _):
        in_expand_back(i, 0)
        for n in range(FF // D):
            c = slice(n * D, (n + 1) * D)
            weight = full[SHR][2 * n : 2 * n + 2].reshape(D, D)
            da = dot(low[rows(i), :], weight, NT).astype(BF).astype(F32)
            du = (da * slope[rows(i), c].astype(F32)).astype(BF)
            slope[rows(i), c] = du
            gvec[VEC_ROW["bf1"] : VEC_ROW["bf1"] + 1, c] += jnp.sum(
                du.astype(F32), axis=0, keepdims=True
            )
        return 0

    lax.fori_loop(0, blocks, expand_back, 0)


    def middle_back(i, _):
        in_middle_back(i, 0)
        upstream = dot(slope[rows(i), :], whole(full[EXP]), NT)
        part, gain, shift = norm_grad(x1[rows(i), :], of("g2"), upstream)
        value = dy[rows(i), :] + part
        dy[rows(i), :] = value
        low[rows(i), :] = value.astype(BF)
        add_grad("g2", gain)
        add_grad("b2", shift)
        add_grad("bo", jnp.sum(value, axis=0, keepdims=True))
        return 0

    lax.fori_loop(0, blocks, middle_back, 0)
    accept(0, False)

    def expand_grad(n, _):
        in_expand_grad(n, 0)
        c = span(n * D, D, 128)
        for owners in range(2):
            value = dot(h2[:, owners * HALF : (owners + 1) * HALF], slope[:, c], TN).astype(BF)
            full2[owners * some : (owners + 1) * some, :, :, c] = value.reshape(
                (some,) + full2.shape[1:3] + (D,)
            )
        pl.when(n == FF // D // 2 - 1)(lambda: scatter.hand(EXP, 0))
        return 0

    lax.fori_loop(0, FF // D, expand_grad, 0)
    scatter.hand(EXP, 1)
    offer(1)
    accept(0, True)

    def upstream_rows(i, _):
        in_upstream(i, 0)
        h2[rows(i), :] = dot(low[rows(i), :], whole(full[OUT]), NT).astype(BF)
        return 0

    lax.fori_loop(0, blocks, upstream_rows, 0)
    for owners in range(2):
        if owners:
            scatter.start(EXP, 1)
        value = dot(att[:, owners * HALF : (owners + 1) * HALF], low[...], TN).astype(BF)
        full1[owners * some : (owners + 1) * some] = value.reshape((some,) + full1.shape[1:])
    accept(1, False)
    scatter.hand(OUT, 0)
    accept(1, True)
    def backward_part(part, _):
        def backward_pair(hp, _):
            def tick(i):
                for n in range(2):
                    first = n * (PAIRS // 2)
                    pl.when(part == n)(
                        lambda first=first: in_backward(hp + first, i, first, first + PAIRS // 2)
                    )

            number = part * (PAIRS // 2) + hp
            attend_back_pair(
                number, qkv, marked, causal, att, h2, lse, x1, tick
            )
            return 0

        lax.fori_loop(0, PAIRS // 2, backward_pair, 0)
        c = span(part * 3 * HALF, 3 * HALF, 128)
        for owners in range(2):
            mine = slice(owners * HALF, (owners + 1) * HALF)
            value = dot(h1[:, mine], qkv[:, c], TN).astype(BF)
            for n in range(3):
                there = span(part * HALF, HALF, 128)
                full3[owners * some : (owners + 1) * some, :, n * half : (n + 1) * half, there] = (
                    value[:, n * HALF : (n + 1) * HALF].reshape(some, 2, half, HALF)
                )
            for number in range(2):

                def hand(number=number, owners=owners):
                    for sub in ((0,), (1, 2, 3))[number]:
                        for owner in range(owners * some, (owners + 1) * some):
                            scatter.pair(MIX, sub, owner).start()

                pl.when(part == number)(hand)
        return 0

    lax.fori_loop(0, 2, backward_part, 0)
    for tick in hop(MIX, 2, 0):
        tick()
    out_local.wait()
    out_go.wait_send()
    in_input_back = spread(
        [
            [],
            [partial(scatter.start, MIX, sub) for sub in range(1, 4)],
            hop(MIX, 3, 0),
            hop(MIX, 1, 1),
        ],
        1,
    )
    late = BLK // 2

    def input_back(j, _):
        in_input_back(j, 0)
        core = place.core + (1 - 2 * place.core) * (j % 2)
        i = 2 * (place.x + (1 - 2 * place.x) * (1 - j // 2)) + core
        d = qkv[rows(i), :]
        part, gain, shift = norm_grad(
            x[rows(i), :].astype(F32), of("g1"), dot(d, whole(full[MIX]), NT)
        )
        sent[rows(i), :] = (dy[rows(i), :] + part).astype(BF)
        add_grad("g1", gain)
        add_grad("b1", shift)
        for half_of in range(2):
            first = half_of * 3 * HALF
            for name, start in (("bq", first), ("bv", first + 2 * HALF)):
                term = d[:, start : start + HALF].astype(F32)
                add_grad(name, jnp.sum(term, axis=0, keepdims=True), half_of * HALF)
        pl.when(j == 0)(lambda: send_rows(back_rows, back_go, 2))
        pl.when(j == 1)(lambda: send_rows(back_rows, back_go, 3, 0, late) if late else None)
        pl.when(j == 3)(lambda: send_rows(back_rows, back_go, 1))
        return 0

    lax.fori_loop(0, blocks, input_back, 0)
    back_local = local(sent.at[me], back_rows.at[place.seq], row_l.at[3])
    flat = 0
    vec_out[...] = jnp.zeros_like(vec_out)
    for name, size in VEC_PLACES:
        for n in range(size // 128):
            r = flat + n
            vec_out[r // per, r % per : r % per + 1, :] = gvec[
                VEC_ROW[name] : VEC_ROW[name] + 1, n * 128 : (n + 1) * 128
            ]
        flat += size // 128
    for k in range(1, count):
        peer = place.dp_peer(k)
        vec_go.start(vec_out.at[peer[0]], vec_buf.at[place.dp], peer)
    vec_buf[place.dp] = vec_out[place.dp]
    for tick in hop(MIX, 1, 2) + hop(MIX, 1, 3) + end(MIX, 0) + hop(MIX, 2, 1) + hop(MIX, 2, 2) + hop(MIX, 2, 3):
        tick()
    for w, sub in ((SHR, 0), (SHR, 1), (EXP, 0)):
        scatter.crossed(w, sub)
    for tick in hop(MIX, 3, 1) + hop(MIX, 3, 2) + hop(MIX, 3, 3):
        tick()
    vec_go.wait_recv()
    vec_mine[...] = jnp.sum(vec_buf[...], axis=0)
    vec_seq[place.seq] = vec_mine[...]
    for k in (2, 3, 1):
        seq_go.start(vec_mine, vec_seq.at[place.seq], place.kin(k))
    for sub in range(1, 4):
        scatter.finish(MIX, sub)
    send_rows(back_rows, back_go, 3, late, BLK - late)
    for w, sub in ((EXP, 1), (OUT, 0), (MIX, 0)):
        scatter.crossed(w, sub)

    def squares_of(w, part, total):
        c = slice(None) if part is None else slice(part * HALF, (part + 1) * HALF)
        for core in range(2):
            value = sums[w][core, :, c].astype(F32)
            term = jnp.sum(value * value, axis=0, keepdims=True)
            for n in range(term.shape[1] // 128):
                total = total + term[:, n * 128 : (n + 1) * 128]
        return total

    squares = jnp.zeros((1, 128), F32)
    for w in (SHR, EXP, OUT):
        for sub in range(SUBS[w]):
            scatter.arrived(w, sub)
        squares = squares_of(w, None, squares)
    scatter.arrived(MIX, 0)
    squares = squares_of(MIX, 0, squares)
    seq_go.wait_recv()
    vec_total = jnp.sum(vec_seq[...], axis=0)
    vec_sum[...] = vec_total
    squares = squares + jnp.sum(vec_total * vec_total, axis=0, keepdims=True)
    for sub in range(1, 4):
        scatter.crossed(MIX, sub)
    for sub in range(1, 4):
        scatter.arrived(MIX, sub)
    squares = squares_of(MIX, 1, squares)
    sq_mine[...] = jnp.broadcast_to(squares, sq_mine.shape)
    sq_buf[place.dp] = sq_mine[...]
    for k in range(1, count):
        sq_go.start(sq_mine, sq_buf.at[place.dp], place.dp_peer(k))
    saved = [local(sums[w], sums_out[w], load_sem.at[w]) for w in range(4)]
    for w in (MIX, OUT, EXP, SHR):
        scatter.drain(w)
    for copies in (row_in, seg_in, teach_in, vec_in, vec_go, seq_go, back_go, sq_go):
        copies.wait_send()
    for copy in saved + [back_local]:
        copy.wait()
    out_go.wait_recv()
    back_go.wait_recv()
    sq_go.wait_recv()
    total = jnp.sum(jnp.sum(sq_buf[...], axis=0), axis=1, keepdims=True)
    norm_ref[...] = jnp.broadcast_to(jnp.sqrt(total), norm_ref.shape)


def block_call(count, inputs, teacher, segments, masters, vectors):
    rows, local_len, features = inputs.shape
    length = rows * local_len
    halves = [(2, m.shape[0] // 2, m.shape[1]) for m in masters]
    any_spec = pl.BlockSpec(memory_space=pl.ANY)
    vmem = pl.BlockSpec(memory_space=pltpu.VMEM)
    row_shape = jax.ShapeDtypeStruct(inputs.shape, BF)
    folded = [(2, 3 * halves[MIX][1], D)] + halves[1:]
    out_shape = [jax.ShapeDtypeStruct(h, BF) for h in folded]
    out_shape += [
        jax.ShapeDtypeStruct((VROWS, 128), F32),
        jax.ShapeDtypeStruct((8, 128), F32),
        row_shape,
        row_shape,
    ]

    def low(*shape):
        return pltpu.VMEM(shape, BF)

    def wide(*shape):
        return pltpu.VMEM(shape, F32)

    def dma(*shape):
        return pltpu.SemaphoreType.DMA(shape)

    shrink_half = halves[SHR][1:]
    buffers = [low(count, *h) for h in halves]
    buffers += [
        low(length, D),
        low(length, D),
        low(length, 3 * D),
        low(length, D),
        wide(length, D),
        low(length, D),
        low(length, FF),
        low(length, FF),
        wide(length, D),
        low(length, D),
        low(length, D),
        low(count, *halves[SHR]),
        low(count, *shrink_half),
        low(count - 1, *shrink_half),
    ]
    buffers += [
        wide(16, length),
        pltpu.VMEM((rows, 8, local_len), jnp.int32),
        pltpu.VMEM((rows, 8, local_len), jnp.int32),
        low(length, 128),
        wide(BLK, BLK),
        *(low(*shape) for shape in folded),
        wide(VROWS, 128),
        wide(count, VROWS, 128),
        wide(16, FF),
        wide(16, FF),
        wide(count, VROWS, 128),
        wide(count, VROWS, 128),
        wide(VROWS, 128),
        wide(4, VROWS, 128),
        wide(8, 128),
        wide(count, 8, 128),
    ]
    hops = count - 1
    sems = [dma(9), dma(4), dma(10, hops), dma(4), dma(4), dma(2), dma(2, hops)]
    sems += [dma(9), dma(9), dma(9), dma(9, hops)] + [dma(9)] * 4
    sems += [dma(6), dma(6), dma(4), dma(3), dma(3)]
    sems.append(pltpu.SemaphoreType.REGULAR((6,)))
    return pl.pallas_call(
        partial(block_kernel, count),
        out_shape=out_shape,
        in_specs=[any_spec] * 2 + [vmem] + [any_spec] * 4 + [vmem],
        out_specs=[any_spec] * 4 + [vmem] * 2 + [any_spec] * 2,
        scratch_shapes=buffers + sems,
        compiler_params=pltpu.CompilerParams(
            collective_id=1, has_side_effects=True, vmem_limit_bytes=VMEM_BYTES
        ),
    )(inputs, teacher, segments, *masters, vectors.reshape(-1, 128))


def update_kernel(steps, norm_ref, *refs):
    sums, masters, firsts, seconds = refs[0:5], refs[5:10], refs[10:15], refs[15:20]
    out_from, back_from = refs[20:22]
    updated, first_out, second_out = refs[22:27], refs[27:32], refs[32:37]
    out_to, back_to, norm_out, held, sem = refs[37:42]
    step = pl.program_id(0)
    norm = norm_ref[0:1, 0:1]
    factor = clip_level() / jnp.maximum(norm, clip_level())
    takes = [
        pltpu.make_async_copy(rows, held.at[n], sem.at[n])
        for n, rows in enumerate((out_from, back_from))
    ]
    gives = [
        pltpu.make_async_copy(held.at[n], rows, sem.at[2 + n])
        for n, rows in enumerate((out_to, back_to))
    ]

    @pl.when(step == 0)
    def _():
        for copy in takes:
            copy.start()
        norm_out[...] = norm

    @pl.when(step == steps // 2)
    def _():
        for take, give in zip(takes, gives):
            take.wait()
            give.start()

    def apply(n, gradient):
        rate = learn_rates()[n]
        clipped = gradient * factor
        first = BETA_ONE * firsts[n][...] + (1.0 - BETA_ONE) * clipped
        second = BETA_TWO * seconds[n][...] + (1.0 - BETA_TWO) * (clipped * clipped)
        scale = jnp.sqrt(second * (1.0 / (1.0 - BETA_TWO**STEP))) + ADAM_EPS
        change = first * (rate / (1.0 - BETA_ONE**STEP)) / scale
        updated[n][...] = masters[n][...] * (1.0 - rate * WEIGHT_DECAY) - change
        first_out[n][...] = first
        second_out[n][...] = second

    for w in range(4):
        gradient = sums[w][...].astype(F32)
        if w == MIX:
            gradient = jnp.concatenate([gradient[n] for n in range(3)], axis=1)
        apply(w, gradient)

    @pl.when(step == 0)
    def _():
        apply(4, sums[4][0 : masters[4].shape[0], :])

    @pl.when(step == steps - 1)
    def _():
        for copy in gives:
            copy.wait()


def update_call(results, masters, firsts, seconds):
    half = results[OUT].shape[1]
    parts = 1
    steps = 2 * parts
    mixed = results[MIX].reshape(2, 3, half, D)

    def fixed(shape):
        return pl.BlockSpec(shape, lambda i: (0,) * len(shape))

    any_spec = pl.BlockSpec(memory_space=pl.ANY)
    sum_specs, state_specs, states = [], [], []
    for master in masters[:4]:
        rows, columns = master.shape[0] // steps, master.shape[1]
        sum_specs.append(pl.BlockSpec((None, rows, columns), lambda i: (i // parts, i % parts, 0)))
        state_specs.append(pl.BlockSpec((rows, columns), lambda i: (i, 0)))
    sum_specs[MIX] = pl.BlockSpec(
        (None, 3, half // parts, D), lambda i: (i // parts, 0, i % parts, 0)
    )
    packed = (masters[4].shape[0] // 128, 128)
    state_specs.append(fixed(packed))
    sum_specs.append(fixed(results[4].shape))
    for group in (masters, firsts, seconds):
        states += list(group[:4]) + [group[4].reshape(packed)]
    out_shape = [jax.ShapeDtypeStruct(state.shape, F32) for state in states]
    out_shape += [jax.ShapeDtypeStruct(results[6].shape, BF)] * 2
    out_shape.append(jax.ShapeDtypeStruct((1, 1), F32))
    return pl.pallas_call(
        partial(update_kernel, steps),
        grid=(steps,),
        out_shape=out_shape,
        in_specs=[fixed(results[5].shape)] + sum_specs + state_specs * 3 + [any_spec] * 2,
        out_specs=state_specs * 3 + [any_spec] * 2 + [fixed((1, 1))],
        scratch_shapes=[
            pltpu.VMEM((2,) + results[6].shape, BF),
            pltpu.SemaphoreType.DMA((4,)),
        ],
        compiler_params=pltpu.CompilerParams(vmem_limit_bytes=VMEM_BYTES),
    )(results[5], mixed, *results[1:5], *states, *results[6:8])


def row_body(
    inputs,
    segments,
    teacher,
    mixing_weight,
    output_weight,
    expand_weight,
    shrink_weight,
    vectors,
    mixing_first,
    output_first,
    expand_first,
    shrink_first,
    vectors_first,
    mixing_second,
    output_second,
    expand_second,
    shrink_second,
    vectors_second,
):
    masters = (mixing_weight, output_weight, expand_weight, shrink_weight, vectors)
    firsts = (mixing_first, output_first, expand_first, shrink_first, vectors_first)
    seconds = (mixing_second, output_second, expand_second, shrink_second, vectors_second)
    results = block_call(lax.axis_size("dp"), inputs, teacher, segments, masters[:4], vectors)
    fresh = update_call(results, masters, firsts, seconds)
    states = [
        state.reshape(vectors.shape) if n % 5 == 4 else state for n, state in enumerate(fresh[:15])
    ]
    return (fresh[15], fresh[16], fresh[17].reshape(()), *states)


def whole_rows(mesh):
    return mesh.shape["seq"] == 4 and mesh.shape["dp"] == 8


def solution(mesh):
    in_specs = (
        P("dp", "seq", None),
        P("dp", "seq"),
        P("dp", "seq", None),
        P("dp", None),
        P("dp", None),
        P("dp", None),
        P("dp", None),
        P("dp"),
        P("dp", None),
        P("dp", None),
        P("dp", None),
        P("dp", None),
        P("dp"),
        P("dp", None),
        P("dp", None),
        P("dp", None),
        P("dp", None),
        P("dp"),
    )
    out_specs = (
        P("dp", "seq", None),
        P("dp", "seq", None),
        P(),
        P("dp", None),
        P("dp", None),
        P("dp", None),
        P("dp", None),
        P("dp"),
        P("dp", None),
        P("dp", None),
        P("dp", None),
        P("dp", None),
        P("dp"),
        P("dp", None),
        P("dp", None),
        P("dp", None),
        P("dp", None),
        P("dp"),
    )
    chosen = row_body if whole_rows(mesh) else body
    return jax.shard_map(chosen, mesh=mesh, in_specs=in_specs, out_specs=out_specs, check_vma=False)
```

```python
from functools import partial
import math

import jax
import jax.numpy as jnp
from jax import lax
from jax.experimental import pallas as pl
from jax.experimental.pallas import tpu as pltpu
from jax.sharding import PartitionSpec as P

D = 768
HEADS = 12
HD = 64
FF = 3072
LEN = 1024
NDOC = 8
STEP = 10


NEGATIVE = -1e30
NORM_EPS = 1e-05
BETA_ONE = 0.9
BETA_TWO = 0.999
ADAM_EPS = 1e-08
WEIGHT_DECAY = 0.01


def layer_norm(values, norm_gain, norm_shift):
    center = values - jnp.mean(values, axis=-1, keepdims=True)
    spread = jnp.mean(center * center, axis=-1, keepdims=True)
    return center * lax.rsqrt(spread + NORM_EPS) * norm_gain + norm_shift


def gelu_tanh(values):
    return jax.nn.gelu(values, approximate=True)


def split_vectors(packed):
    return jnp.split(packed, [D, 2 * D, 3 * D, 4 * D, 5 * D, 6 * D, 7 * D, 7 * D + FF])


def adamw(master, first, second, gradient, rate):
    first_new = BETA_ONE * first + (1.0 - BETA_ONE) * gradient
    second_new = BETA_TWO * second + (1.0 - BETA_TWO) * gradient * gradient
    first_hat = first_new / (1.0 - BETA_ONE**STEP)
    second_hat = second_new / (1.0 - BETA_TWO**STEP)
    updated = master - rate * (
        first_hat / (jnp.sqrt(second_hat) + ADAM_EPS) + WEIGHT_DECAY * master
    )
    return (updated, first_new, second_new)


def learn_rates():
    return (
        1.0 / math.sqrt(2 * D),
        1.0 / math.sqrt(max(1, 2 * D * NDOC // LEN)),
        1.0 / math.sqrt(D),
        1.0 / math.sqrt(FF),
        0.3,
    )


def clip_level():
    return 0.5 * math.sqrt(4 * D * D + 2 * D * FF + 8 * D + FF)


def visible(query_pos, key_pos, query_seg, key_seg):
    return (key_pos[None, :] <= query_pos[:, None]) & (key_seg[None, :] == query_seg[:, None])


def attend_rows(query_pos, key_pos, packed_args):
    queries, keys_all, values_all, query_seg, key_seg = packed_args
    scores = jnp.einsum("qhd,khd->hqk", queries, keys_all, preferred_element_type=jnp.float32)
    scores = jnp.where(visible(query_pos, key_pos, query_seg, key_seg)[None], scores, NEGATIVE)
    top_score = jnp.max(scores, axis=-1, keepdims=True)
    exponent = jnp.exp(scores - top_score)
    totals = jnp.sum(exponent, axis=-1, keepdims=True)
    probability = (exponent / totals).astype(jnp.bfloat16)
    attended = jnp.einsum(
        "hqk,khd->qhd", probability, values_all, preferred_element_type=jnp.float32
    )
    return (attended, (top_score + jnp.log(totals))[..., 0])


def attend_back(query_pos, key_pos, packed_args):
    queries, keys_all, values_all, upstream, log_totals, query_seg, key_seg = packed_args
    scores = jnp.einsum("qhd,khd->hqk", queries, keys_all, preferred_element_type=jnp.float32)
    scores = jnp.where(visible(query_pos, key_pos, query_seg, key_seg)[None], scores, NEGATIVE)
    probability = jnp.exp(scores - log_totals[..., None])
    prob_low = probability.astype(jnp.bfloat16)
    prob_grad = jnp.einsum("qhd,khd->hqk", upstream, values_all, preferred_element_type=jnp.float32)
    value_part = jnp.einsum("hqk,qhd->khd", prob_low, upstream, preferred_element_type=jnp.float32)
    score_grad = probability * (
        prob_grad - jnp.sum(probability * prob_grad, axis=-1, keepdims=True)
    )
    score_low = score_grad.astype(jnp.bfloat16)
    query_part = jnp.einsum("hqk,khd->qhd", score_low, keys_all, preferred_element_type=jnp.float32)
    key_part = jnp.einsum("hqk,qhd->khd", score_low, queries, preferred_element_type=jnp.float32)
    key_count = keys_all.shape[0]
    return (
        query_part,
        jnp.concatenate(
            [key_part.reshape(key_count, -1), value_part.reshape(key_count, -1)], axis=1
        ),
    )


def body(
    inputs,
    segments,
    teacher,
    mixing_weight,
    output_weight,
    expand_weight,
    shrink_weight,
    vectors,
    mixing_first,
    output_first,
    expand_first,
    shrink_first,
    vectors_first,
    mixing_second,
    output_second,
    expand_second,
    shrink_second,
    vectors_second,
):
    bfloat = jnp.bfloat16
    floats = jnp.float32
    seq_count, local_len, features = inputs.shape
    row_count = seq_count * local_len
    scale = 1.0 / math.sqrt(HD)
    mixing_low, output_low, expand_low, shrink_low, vectors_low = (
        lax.all_gather(mixing_weight.astype(bfloat), "dp", axis=0, tiled=True),
        lax.all_gather(output_weight.astype(bfloat), "dp", axis=0, tiled=True),
        lax.all_gather(expand_weight.astype(bfloat), "dp", axis=0, tiled=True),
        lax.all_gather(shrink_weight.astype(bfloat), "dp", axis=0, tiled=True),
        lax.all_gather(vectors.astype(bfloat), "dp", axis=0, tiled=True),
    )
    (
        gain_one,
        shift_one,
        bias_query,
        bias_value,
        bias_output,
        gain_two,
        shift_two,
        bias_expand,
        bias_shrink,
    ) = split_vectors(vectors_low.astype(floats))
    states = inputs.astype(floats).reshape(row_count, features)
    normed = layer_norm(states, gain_one, shift_one)
    normed_low = normed.astype(bfloat)
    projected = jnp.dot(normed_low, mixing_low, preferred_element_type=floats)
    query_low = ((projected[:, :features] + bias_query) * scale).astype(bfloat)
    key_low = projected[:, features : 2 * features].astype(bfloat)
    value_low = (projected[:, 2 * features :] + bias_value).astype(bfloat)
    key_all, value_all = (
        lax.all_gather(key_low.reshape(seq_count, local_len, features), "seq", axis=1, tiled=True),
        lax.all_gather(
            value_low.reshape(seq_count, local_len, features), "seq", axis=1, tiled=True
        ),
    )
    segment_all = lax.all_gather(segments, "seq", axis=1, tiled=True)
    full_len = key_all.shape[1]
    query_pos = lax.axis_index("seq") * local_len + jnp.arange(local_len, dtype=jnp.int32)
    key_pos = jnp.arange(full_len, dtype=jnp.int32)
    query_heads = query_low.reshape(seq_count, local_len, HEADS, HD)
    key_heads = key_all.reshape(seq_count, full_len, HEADS, HD)
    value_heads = value_all.reshape(seq_count, full_len, HEADS, HD)
    attended, log_totals = lax.map(
        partial(attend_rows, query_pos, key_pos),
        (query_heads, key_heads, value_heads, segments, segment_all),
    )
    attended_low = attended.reshape(row_count, features).astype(bfloat)
    middle = states + jnp.dot(attended_low, output_low, preferred_element_type=floats) + bias_output
    normed_two = layer_norm(middle, gain_two, shift_two)
    normed_two_low = normed_two.astype(bfloat)
    hidden = jnp.dot(normed_two_low, expand_low, preferred_element_type=floats) + bias_expand
    active, gelu_back = jax.vjp(gelu_tanh, hidden)
    active_low = active.astype(bfloat)
    result = middle + jnp.dot(active_low, shrink_low, preferred_element_type=floats) + bias_shrink
    block_output = result.astype(bfloat).reshape(seq_count, local_len, features)
    target_prob = jax.nn.softmax(teacher.astype(floats).reshape(row_count, features), axis=-1)
    result_grad = features * (jax.nn.softmax(result, axis=-1) - target_prob)
    result_low = result_grad.astype(bfloat)
    grad_shrink = jnp.dot(active_low.T, result_low, preferred_element_type=floats)
    grad_bias_shrink = jnp.sum(result_grad, axis=0)
    active_grad = jnp.dot(result_low, shrink_low.T, preferred_element_type=floats)
    active_round = lax.optimization_barrier(active_grad.astype(bfloat)).astype(floats)
    hidden_low = gelu_back(active_round)[0].astype(bfloat)
    grad_bias_expand = jnp.sum(hidden_low.astype(floats), axis=0)
    grad_expand = jnp.dot(normed_two_low.T, hidden_low, preferred_element_type=floats)
    normed_two_grad = jnp.dot(hidden_low, expand_low.T, preferred_element_type=floats)
    norm_two_back = jax.vjp(layer_norm, middle, gain_two, shift_two)[1]
    middle_part, grad_gain_two, grad_shift_two = norm_two_back(normed_two_grad)
    middle_grad = result_grad + middle_part
    middle_low = middle_grad.astype(bfloat)
    grad_bias_output = jnp.sum(middle_grad, axis=0)
    grad_output = jnp.dot(attended_low.T, middle_low, preferred_element_type=floats)
    attended_grad = jnp.dot(middle_low, output_low.T, preferred_element_type=floats).astype(bfloat)
    upstream_heads = attended_grad.reshape(seq_count, local_len, HEADS, HD)
    query_grad, kv_terms = lax.map(
        partial(attend_back, query_pos, key_pos),
        (query_heads, key_heads, value_heads, upstream_heads, log_totals, segments, segment_all),
    )
    kv_sums = (
        lax.psum_scatter(kv_terms.astype(jnp.bfloat16), "seq", scatter_dimension=1, tiled=True)
        .astype(jnp.float32)
        .reshape(row_count, 2 * features)
    )
    key_grad_low = kv_sums[:, :features].astype(bfloat)
    value_grad_low = kv_sums[:, features:].astype(bfloat)
    query_grad_low = query_grad.reshape(row_count, features).astype(bfloat)
    query_scaled = query_grad_low.astype(floats) * scale
    grad_bias_query = jnp.sum(query_scaled, axis=0)
    grad_bias_value = jnp.sum(value_grad_low.astype(floats), axis=0)
    projected_grad = jnp.concatenate(
        [query_scaled.astype(bfloat), key_grad_low, value_grad_low], axis=1
    )
    grad_mixing = jnp.dot(normed_low.T, projected_grad, preferred_element_type=floats)
    normed_grad = jnp.dot(projected_grad, mixing_low.T, preferred_element_type=floats)
    norm_one_back = jax.vjp(layer_norm, states, gain_one, shift_one)[1]
    states_part, grad_gain_one, grad_shift_one = norm_one_back(normed_grad)
    input_grad = (middle_grad + states_part).astype(bfloat).reshape(seq_count, local_len, features)
    grad_vectors = jnp.concatenate(
        [
            grad_gain_one,
            grad_shift_one,
            grad_bias_query,
            grad_bias_value,
            grad_bias_output,
            grad_gain_two,
            grad_shift_two,
            grad_bias_expand,
            grad_bias_shrink,
        ]
    )
    vector_rows = grad_vectors.reshape(lax.axis_size("dp"), -1)
    mixing_part, output_part, expand_part, shrink_part, vector_part = (
        lax.psum_scatter(
            grad_mixing.astype(jnp.bfloat16), "dp", scatter_dimension=0, tiled=True
        ).astype(jnp.float32),
        lax.psum_scatter(
            grad_output.astype(jnp.bfloat16), "dp", scatter_dimension=0, tiled=True
        ).astype(jnp.float32),
        lax.psum_scatter(
            grad_expand.astype(jnp.bfloat16), "dp", scatter_dimension=0, tiled=True
        ).astype(jnp.float32),
        lax.psum_scatter(
            grad_shrink.astype(jnp.bfloat16), "dp", scatter_dimension=0, tiled=True
        ).astype(jnp.float32),
        lax.psum_scatter(
            vector_rows.astype(jnp.bfloat16), "dp", scatter_dimension=0, tiled=True
        ).astype(jnp.float32),
    )
    mixing_sum, output_sum, expand_sum, shrink_sum, vector_sum = (
        lax.psum(mixing_part.astype(jnp.bfloat16), "seq").astype(jnp.float32),
        lax.psum(output_part.astype(jnp.bfloat16), "seq").astype(jnp.float32),
        lax.psum(expand_part.astype(jnp.bfloat16), "seq").astype(jnp.float32),
        lax.psum(shrink_part.astype(jnp.bfloat16), "seq").astype(jnp.float32),
        lax.psum(vector_part.astype(jnp.bfloat16), "seq").astype(jnp.float32),
    )
    vector_sum = vector_sum.reshape(-1)
    squares = (
        jnp.sum(mixing_sum * mixing_sum)
        + jnp.sum(output_sum * output_sum)
        + jnp.sum(expand_sum * expand_sum)
        + jnp.sum(shrink_sum * shrink_sum)
        + jnp.sum(vector_sum * vector_sum)
    )
    grad_norm = jnp.sqrt(lax.psum(squares, "dp"))
    clip_value = clip_level()
    factor = clip_value / jnp.maximum(grad_norm, clip_value)
    step_rates = learn_rates()
    mixing_new = adamw(
        mixing_weight, mixing_first, mixing_second, mixing_sum * factor, step_rates[0]
    )
    output_new = adamw(
        output_weight, output_first, output_second, output_sum * factor, step_rates[1]
    )
    expand_new = adamw(
        expand_weight, expand_first, expand_second, expand_sum * factor, step_rates[2]
    )
    shrink_new = adamw(
        shrink_weight, shrink_first, shrink_second, shrink_sum * factor, step_rates[3]
    )
    vectors_new = adamw(vectors, vectors_first, vectors_second, vector_sum * factor, step_rates[4])
    return (
        block_output,
        input_grad,
        grad_norm,
        mixing_new[0],
        output_new[0],
        expand_new[0],
        shrink_new[0],
        vectors_new[0],
        mixing_new[1],
        output_new[1],
        expand_new[1],
        shrink_new[1],
        vectors_new[1],
        mixing_new[2],
        output_new[2],
        expand_new[2],
        shrink_new[2],
        vectors_new[2],
    )

MESH = pl.DeviceIdType.MESH
BF = jnp.bfloat16
F32 = jnp.float32
BLK = 256
NN = ((1,), (0,))
NT = ((1,), (1,))
TN = ((0,), (0,))
VMEM_BYTES = 64 * 2**20 - 2**17
VROWS = 16
MIX, OUT, EXP, SHR = 0, 1, 2, 3
HALF = D // 2
PAIRS = D // 128
EXPAND_TILE = D
SUBS = (4, 1, 2, 2)
LANES = (0, 4, 5, 7)


def dot(left, right, dims):
    return lax.dot_general(left, right, (dims, ((), ())), preferred_element_type=F32)


class Place:
    def __init__(self, count):
        self.count = count
        self.hops = (count // 2, count - 1 - count // 2)
        self.dp = lax.axis_index("dp")
        self.seq = lax.axis_index("seq")
        odd = self.dp % 2
        self.pos = (1 - odd) * (self.dp // 2) + odd * (count - 1 - self.dp // 2)
        self.core = self.seq % 2
        self.x = self.seq // 2
        self.step = 1 - 2 * self.core
        self.sides = ((self.ahead(1), self.seq), (self.behind(1), self.seq))
        self.mate = self.kin(1)
        self.across = self.kin(2)

    def at(self, pos):
        pos = pos % self.count
        upper = pos // (self.count // 2)
        return (1 - upper) * (2 * pos) + upper * (2 * (self.count - 1 - pos) + 1)

    def ahead(self, steps):
        return self.at(self.pos + steps * self.step + self.count)

    def behind(self, steps):
        return self.at(self.pos - steps * self.step + self.count)

    def kin(self, which):
        core = self.core + (1 - 2 * self.core) * (which % 2)
        return (self.dp, 2 * (self.x + (1 - 2 * self.x) * (which // 2)) + core)

    def dp_peer(self, offset):
        return ((self.dp + offset) % self.count, self.seq)

    def greet(self):
        barrier = pltpu.get_barrier_semaphore()
        peers = [self.kin(k) for k in range(1, 4)]
        peers += [self.dp_peer(k) for k in range(1, self.count)]
        for peer in peers:
            pl.semaphore_signal(barrier, inc=1, device_id=peer, device_id_type=MESH)
        return lambda: pl.semaphore_wait(barrier, len(peers))


def describe(src, dst, send, recv, device):
    return pltpu.make_async_remote_copy(
        src_ref=src,
        dst_ref=dst,
        send_sem=send,
        recv_sem=recv,
        device_id=device,
        device_id_type=MESH,
    )


def remote(src, dst, send, recv, device):
    copy = describe(src, dst, send, recv, device)
    copy.start()
    return copy


def local(src, dst, sem):
    copy = pltpu.make_async_copy(src, dst, sem)
    copy.start()
    return copy


def span(start, size, unit):
    return pl.ds(start if isinstance(start, int) else pl.multiple_of(start, unit), size)


def spread(ticks, marks):
    def at(trip, mark, first=0, past=None):
        for n in range(first, len(ticks) // marks if past is None else past):
            here = ticks[n * marks + mark]
            if here:

                def run(here=here):
                    for tick in here:
                        tick()

                pl.when(trip == n)(run)

    return at


class Group:
    def __init__(self, send, recv, of_all_sent, of_all_received, device):
        self.send, self.recv, self.device = send, recv, device
        self.bytes = (of_all_sent, of_all_received)

    def start(self, src, dst, device):
        describe(src, dst, self.send, self.recv, device).start()

    def all(self, which):
        return describe(self.bytes[which], self.bytes[which], self.send, self.recv, self.device)

    def wait_recv(self):
        self.all(1).wait_recv()

    def wait_send(self):
        self.all(0).wait_send()


class Gather:
    def __init__(self, place, full, sems):
        self.place, self.full = place, full
        self.ring_s, self.ring_r, self.mate_s, self.mate_r, self.cross_s, self.cross_r = sems

    def lanes(self, w):
        return ((0, 1, 2), (0,), (self.place.x, 2, 3), (self.place.x, 2, 3))[w]

    def part(self, ref, w, sub):
        rows, columns = ref.shape[-2:]
        lead = (slice(None),) * (len(ref.shape) - 2)
        if w == SHR:
            unit = rows // 4
            return ref.at[lead + (span(sub * unit, unit, 16),)]
        unit = columns // (3, 1, 4)[w]
        return ref.at[lead + (slice(None), span(sub * unit, unit, 128))]

    def cut(self, w, owner, core, sub):
        return self.part(self.full[w].at[owner, core], w, sub)

    def block(self, w, sub, way, t):
        owner = self.place.ahead(t) if way else self.place.behind(t)
        return self.cut(w, owner, self.place.core, sub)

    def copy(self, block, send, recv, device):
        return describe(block, block, send, recv, device)

    def ring(self, w, lane, way, t):
        index = ((0, 3, 4, 7)[w] + lane, t + way * self.place.hops[0])
        block = self.block(w, self.lanes(w)[lane], way, t)
        return self.copy(block, self.ring_s.at[w], self.ring_r.at[index], self.place.sides[way])

    def pair(self, w, sub, way, t):
        block = self.block(w, sub, way, t)
        return self.copy(block, self.mate_s.at[w], self.mate_r.at[w], self.place.mate)

    def over(self, w, way, t):
        recv = self.cross_r.at[w - EXP, t - 1 + way * self.place.hops[0]]
        block = self.block(w, self.place.x, way, t)
        return self.copy(block, self.cross_s.at[w - EXP], recv, self.place.across)

    def start(self, w):
        for lane in range(len(self.lanes(w))):
            for way in range(2):
                self.ring(w, lane, way, 0).start()

    def tick(self, w, lane, way, t):
        self.ring(w, lane, way, t - 1).wait_recv()
        if t < self.place.hops[way]:
            self.ring(w, lane, way, t).start()
        self.pair(w, self.lanes(w)[lane], way, t).start()
        if w >= EXP and lane == 0:
            self.over(w, way, t).start()

    def relay(self, w, way, t):
        self.over(w, way, t).wait_recv()
        self.pair(w, 1 - self.place.x, way, t).start()

    def others(self, w):
        return self.full[w].at[pl.ds(0, self.place.count - 1), self.place.core]

    def arrived(self, w):
        block = self.others(w)
        self.copy(block, self.mate_s.at[w], self.mate_r.at[w], self.place.mate).wait_recv()

    def drain(self, w):
        block = self.others(w)
        self.copy(block, self.mate_s.at[w], self.mate_r.at[w], self.place.mate).wait_send()
        if w >= EXP:
            for lane in range(len(self.lanes(w))):
                part = self.part(block, w, self.lanes(w)[lane])
                self.copy(part, self.ring_s.at[w], self.mate_r.at[w], self.place.mate).wait_send()
            part = self.part(block, w, 0)
            self.copy(part, self.cross_s.at[w - EXP], self.mate_r.at[w], self.place.across).wait_send()
        else:
            self.copy(block, self.ring_s.at[w], self.mate_r.at[w], self.place.mate).wait_send()


class Scatter:
    def __init__(self, place, grads, mates, slots, sums, sems):
        self.place, self.grads, self.mates, self.slots = place, grads, mates, slots
        self.sums = sums
        (
            self.mate_s,
            self.mate_r,
            self.ring_s,
            self.ring_r,
            self.cross_s,
            self.cross_r,
            self.total_s,
            self.total_r,
        ) = sems

    def cut(self, ref, w, sub):
        rows, columns = ref.shape[-2:]
        lead = (slice(None),) * (len(ref.shape) - 2)
        if w == SHR:
            return ref.at[lead + (span(sub * (rows // 2), rows // 2, 16),)]
        if w == MIX:
            rows = self.sums[w].shape[1]
            there = pl.ds((sub - 1) * (rows // 3), rows // 3) if sub else pl.ds(0, rows)
            return ref.at[lead + (there, pl.ds(HALF if sub else 0, HALF))]
        size = columns // SUBS[w]
        return ref.at[lead + (slice(None), span(sub * size, size, 128))]

    def owner(self, way, distance):
        return self.place.behind(distance) if way else self.place.ahead(distance)

    def own(self, w, owner, core, sub):
        return self.cut(self.grads[w].at[owner, core], w, sub)

    def slot(self, w, way, t, sub):
        return self.cut(self.slots(w, t + way * self.place.hops[0]), w, sub)

    def pair(self, w, sub, owner):
        return describe(
            self.own(w, owner, 1 - self.place.core, sub),
            self.cut(self.mates(w, owner), w, sub),
            self.mate_s.at[LANES[w] + sub],
            self.mate_r.at[LANES[w] + sub],
            self.place.mate,
        )

    def pairs(self, w, sub):
        block = self.cut(self.grads[w].at[:, self.place.core], w, sub)
        return describe(
            block, block, self.mate_s.at[LANES[w] + sub], self.mate_r.at[LANES[w] + sub], self.place.mate
        )

    def ring(self, w, sub, way, t):
        if t == 0:
            owner = self.owner(way, self.place.hops[way])
            src = self.own(w, owner, self.place.core, sub)
        else:
            src = self.slot(w, way, t - 1, sub)
        index = (LANES[w] + sub, t + way * self.place.hops[0])
        return describe(
            src,
            self.slot(w, way, t, sub),
            self.ring_s.at[LANES[w] + sub],
            self.ring_r.at[index],
            self.place.sides[way],
        )

    def over(self, w, sub):
        return describe(
            self.own(w, self.place.dp, self.place.core, sub),
            self.cut(self.sums[w].at[self.place.core], w, sub),
            self.cross_s.at[LANES[w] + sub],
            self.cross_r.at[LANES[w] + sub],
            self.place.across,
        )

    def total(self, w, sub):
        block = self.cut(self.sums[w].at[self.place.core], w, sub)
        return describe(
            block, block, self.total_s.at[LANES[w] + sub], self.total_r.at[LANES[w] + sub], self.place.mate
        )

    def hand(self, w, sub):
        for owner in range(self.place.count):
            self.pair(w, sub, owner).start()

    def term(self, w, sub, way, distance):
        owner = self.owner(way, distance)
        mine = self.own(w, owner, self.place.core, sub)[...].astype(F32)
        return mine + self.cut(self.mates(w, owner), w, sub)[...].astype(F32)

    def start(self, w, sub):
        self.pairs(w, sub).wait_recv()
        for way, hops in enumerate(self.place.hops):
            term = self.term(w, sub, way, hops)
            self.own(w, self.owner(way, hops), self.place.core, sub)[...] = term.astype(BF)
            self.ring(w, sub, way, 0).start()

    def tick(self, w, sub, way, t):
        self.ring(w, sub, way, t - 1).wait_recv()
        slot = self.slot(w, way, t - 1, sub)
        term = self.term(w, sub, way, self.place.hops[way] - t)
        slot[...] = (slot[...].astype(F32) + term).astype(BF)
        self.ring(w, sub, way, t).start()

    def finish(self, w, sub):
        total = self.term(w, sub, 0, 0)
        for way, hops in enumerate(self.place.hops):
            self.ring(w, sub, way, hops - 1).wait_recv()
            total = total + self.slot(w, way, hops - 1, sub)[...].astype(F32)
        self.own(w, self.place.dp, self.place.core, sub)[...] = total.astype(BF)
        self.over(w, sub).start()

    def crossed(self, w, sub):
        self.over(w, sub).wait_recv()
        value = self.own(w, self.place.dp, self.place.core, sub)[...].astype(F32)
        there = self.cut(self.sums[w].at[self.place.core], w, sub)
        there[...] = (value + there[...].astype(F32)).astype(BF)
        self.total(w, sub).start()

    def arrived(self, w, sub):
        self.total(w, sub).wait_recv()

    def drain(self, w):
        for sub in range(SUBS[w]):
            self.pairs(w, sub).wait_send()
            sent = self.cut(self.grads[w].at[pl.ds(0, self.place.count - 1), self.place.core], w, sub)
            describe(
                sent, sent, self.ring_s.at[LANES[w] + sub], self.mate_r.at[LANES[w] + sub], self.place.mate
            ).wait_send()
            self.over(w, sub).wait_send()
            self.total(w, sub).wait_send()

    def ticks(self, w, t, subs):
        return [
            partial(self.tick, w, sub, way, t)
            for sub in subs
            for way, hops in enumerate(self.place.hops)
            if t < hops
        ]


def half_lanes(hd):
    lane = lax.broadcasted_iota(jnp.int32, (1, 128), 1)
    return (lane < 64) if hd == 0 else (lane >= 64)


def document_lanes(documents):
    lane = lax.broadcasted_iota(jnp.int32, documents.shape, 1) % 64
    same = jnp.logical_and(documents == lane.astype(F32), lane < 8)
    return jnp.where(same, 1.0, 0.0).astype(BF)


def marked_keys(keys, marked):
    hidden = ((1.0 - marked.astype(F32)) * NEGATIVE).astype(BF)
    return [jnp.where(half_lanes(hd), keys, hidden) for hd in range(2)]


def columns_of(hp):
    first = (hp // 3) * (3 * HALF) + (hp % 3) * 128
    return [span(first + part * HALF, 128, 128) for part in range(3)]


def attend_pair(hp, qkv, marked, causal, out, lse, scores, tick):
    cq, ck, cv = columns_of(hp)
    vt = qkv[:, cv].T
    ones = jnp.ones((8, vt.shape[1]), BF)
    keys = marked_keys(qkv[:, ck], marked[...])
    values = [jnp.concatenate([vt[hd * 64 : (hd + 1) * 64, :], ones], axis=0) for hd in range(2)]
    def rows_of(n):
        return slice(n * BLK, (n + 1) * BLK)

    def score(i, hd):
        kept = rows_of(hd)
        query = jnp.where(half_lanes(hd), qkv[rows_of(i), cq], marked[rows_of(i), :])
        top = None
        for j in range(i + 1):
            s = dot(keys[hd][rows_of(j), :], query, NT)
            if i == j:
                s = s + causal[...]
            scores[rows_of(j), kept] = s
            best = jnp.max(s, axis=0, keepdims=True)
            top = best if top is None else jnp.maximum(top, best)
        return top

    def weigh(i, hd, top):
        parts = [
            jnp.exp(scores[rows_of(j), rows_of(hd)] - top).astype(BF) for j in range(i + 1)
        ]
        return i, hd, top, parts

    outs = []

    def collect(i, hd, top, parts):
        acc = None
        for j, p in enumerate(parts):
            term = dot(values[hd][:, rows_of(j)], p, NN)
            acc = term if acc is None else acc + term
        total = acc[64:65, :]
        lse[pl.ds(hp * 2 + hd, 1), rows_of(i)] = top + jnp.log(total)
        outs.append(acc[0:64, :] * (1.0 / total))
        if hd == 1:
            out[rows_of(i), span(hp * 128, 128, 128)] = (
                jnp.concatenate(outs, axis=0).T.astype(BF)
            )
            outs[:] = []

    chains = [(i, hd) for i in range(qkv.shape[0] // BLK) for hd in range(2)]
    tick(0)
    top = score(*chains[0])
    behind = None
    for n, (i, hd) in enumerate(chains):
        after = None
        if n + 1 < len(chains):
            if hd == 1:
                tick(i + 1)
            after = score(*chains[n + 1])
        if behind is not None:
            collect(*behind)
        behind = weigh(i, hd, top)
        top = after
    collect(*behind)


def attend_back_pair(hp, qkv, marked, causal, out, upstream, lse, sums, tick):
    cq, ck, cv = columns_of(hp)
    co = span(hp * 128, 128, 128)
    in_v, in_k = slice(0, 128), slice(128, 256)
    kt = qkv[:, ck].T
    keys = marked_keys(qkv[:, ck], marked[...])
    def rows_of(n):
        return slice(n * BLK, (n + 1) * BLK)

    def operands(i):
        qb = qkv[rows_of(i), cq]
        db = upstream[rows_of(i), co]
        none = jnp.zeros_like(qb)
        prod = (db.astype(F32) * out[rows_of(i), co].astype(F32)).T
        queries = [jnp.where(half_lanes(hd), qb, marked[rows_of(i), :]) for hd in range(2)]
        grads = [jnp.where(half_lanes(hd), db, none) for hd in range(2)]
        return (
            queries,
            grads,
            [jnp.sum(prod[hd * 64 : (hd + 1) * 64, :], axis=0, keepdims=True) for hd in range(2)],
            [lse[pl.ds(hp * 2 + hd, 1), rows_of(i)] for hd in range(2)],
            jnp.concatenate([jnp.where(half_lanes(hd), qb, none) for hd in range(2)], axis=0),
            jnp.concatenate(grads, axis=0),
        )

    def products(n, ops):
        i, j = blocks[n]
        kept = slice((1 + n % 2) * BLK, (2 + n % 2) * BLK)
        for hd in range(2):
            s = dot(keys[hd][rows_of(j), :], ops[0][hd], NT)
            sums[rows_of(hd), kept] = s + causal[...] if i == j else s
            sums[rows_of(2 + hd), kept] = dot(qkv[rows_of(j), cv], ops[1][hd], NT)

    blocks = [(i, j) for i in range(qkv.shape[0] // BLK) for j in range(i + 1)]
    tick(0)
    ops = operands(0)
    products(0, ops)
    dqs = [None, None]

    def gather_block(i, j, now, ps, dss):
        for hd in range(2):
            term = dot(kt[hd * 64 : (hd + 1) * 64, rows_of(j)], dss[hd], NN)
            dqs[hd] = term if dqs[hd] is None else dqs[hd] + term
        pv = dot(jnp.concatenate(ps, axis=1), now[5], NN)
        pk = dot(jnp.concatenate(dss, axis=1), now[4], NN)
        if i == j:
            sums[rows_of(j), in_v] = pv
            sums[rows_of(j), in_k] = pk
            low = jnp.concatenate(dqs, axis=0).T.astype(BF).astype(F32)
            qkv[rows_of(i), cq] = (low * (1.0 / math.sqrt(HD))).astype(BF)
            dqs[:] = [None, None]
        else:
            sums[rows_of(j), in_v] += pv
            sums[rows_of(j), in_k] += pk

    behind = None
    for n, (i, j) in enumerate(blocks):
        now = ops
        kept = slice((1 + n % 2) * BLK, (2 + n % 2) * BLK)
        if n + 1 < len(blocks):
            if blocks[n + 1][1] == 0:
                tick(i + 1)
                ops = operands(i + 1)
            products(n + 1, ops)
        if behind is not None:
            gather_block(*behind)
        ps, dss = [], []
        for hd in range(2):
            p = jnp.exp(sums[rows_of(hd), kept] - now[3][hd])
            ps.append(p.astype(BF))
            dss.append((p * (sums[rows_of(2 + hd), kept] - now[2][hd])).astype(BF))
        behind = (i, j, now, ps, dss)
    gather_block(*behind)
    qkv[:, ck] = sums[:, in_k].astype(BF)
    qkv[:, cv] = sums[:, in_v].astype(BF)


def normalised(values):
    center = values - jnp.mean(values, axis=-1, keepdims=True)
    inverse = lax.rsqrt(jnp.mean(center * center, axis=-1, keepdims=True) + NORM_EPS)
    return center * inverse, inverse


def norm_grad(values, gain, upstream):
    hat, inverse = normalised(values)
    scaled = upstream * gain
    first = jnp.mean(scaled, axis=-1, keepdims=True)
    second = jnp.mean(scaled * hat, axis=-1, keepdims=True)
    return (
        inverse * (scaled - first - hat * second),
        jnp.sum(upstream * hat, axis=0, keepdims=True),
        jnp.sum(upstream, axis=0, keepdims=True),
    )


def gelu_both(u):
    inner = math.sqrt(2.0 / math.pi)
    cubic = inner * 0.044715
    square = u * u
    half = 0.5 + 0.5 * jnp.tanh(u * (inner + cubic * square))
    value = u * half
    return value, half + value * (1.0 - half) * (2.0 * inner + 6.0 * cubic * square)


def softmax(values):
    e = jnp.exp(values - jnp.max(values, axis=-1, keepdims=True))
    return e * (1.0 / jnp.sum(e, axis=-1, keepdims=True))


def whole(ref):
    return ref[...].reshape(-1, ref.shape[-1])


VEC_PLACES = (("g1", D), ("b1", D), ("bq", D), ("bv", D), ("bo", D), ("g2", D), ("b2", D), ("bf1", FF), ("bf2", D))
VEC_ROW = {name: row for row, (name, _) in enumerate(VEC_PLACES)}
VEC_SIZE = dict(VEC_PLACES)


def block_kernel(count, *refs):
    inputs, teacher, segments, masters, vec_ref = refs[0], refs[1], refs[2], refs[3:7], refs[7]
    sums_out, vec_sum, norm_ref, out_rows, back_rows = refs[8:12], *refs[12:16]
    (
        full0, full1, full2, full3, x, h1, qkv, att, x1, h2, act, slope, dy, low, sent, shrink_grads,
        shr_mate, shr_slot, lse, segs, seg_stage, marked, causal,
        sums0, sums1, sums2, sums3, vec_stage, vec_all, vec, gvec, vec_out, vec_buf, vec_mine, vec_seq, sq_mine, sq_buf,
        load_sem, g_ring_s, g_ring_r, g_mate_s, g_mate_r, g_cross_s, g_cross_r,
        s_mate_s, s_mate_r, s_ring_s, s_ring_r, s_cross_s, s_cross_r, s_total_s, s_total_r,
        row_s, row_r, row_l, vec_s, vec_r, free,
    ) = refs[16:]
    full = (full0, full1, full2, full3)
    sums = (sums0, sums1, sums2, sums3)
    place = Place(count)
    ready = place.greet()
    length = x.shape[0]
    blocks = length // BLK
    scale = 1.0 / math.sqrt(HD)

    def rows(i):
        return span(i * BLK, BLK, BLK)

    loads, pieces, used = [], [], [0, 0]
    for w in (MIX, OUT, EXP, SHR):
        height, width = masters[w].shape
        for column in range(0, width, D):
            which = 0 if used[0] + height <= length else 1
            where = (dy, x1)[which].at[pl.ds(used[which], height)]
            used[which] += height
            source = masters[w].at[:, pl.ds(column, D)]
            loads.append(local(source, where, load_sem.at[len(loads)]))
            pieces.append((w, column, where))

    def stage(w):
        for load, (owner, column, where) in zip(loads, pieces):
            if owner == w:
                load.wait()
                piece = where[...].astype(BF).reshape(full[w].shape[1:3] + (D,))
                if w == MIX:
                    for part in range(2):
                        c = slice(part * HALF, (part + 1) * HALF)
                        there = pl.ds(part * 3 * HALF + column // 2, HALF)
                        full[w][place.dp, :, :, there] = piece[:, :, c]
                else:
                    full[w][place.dp, :, :, pl.ds(column, D)] = piece

    gather = Gather(place, full, (g_ring_s, g_ring_r, g_mate_s, g_mate_r, g_cross_s, g_cross_r))
    stage(MIX)
    ready()
    gather.start(MIX)

    me = rows(place.seq)
    three, seven = pl.ds(0, 3), pl.ds(0, count - 1)
    most = pl.ds(0, 3 * BLK)

    def group(n, sent, received):
        return Group(row_s.at[n], row_r.at[n], sent, received, place.mate)

    row_in = group(0, inputs.at[three], x.at[most])
    seg_in = group(1, seg_stage.at[three], segs.at[three])
    teach_in = group(2, teacher.at[three], low.at[most])
    out_go = group(3, out_rows.at[three], out_rows.at[three])
    back_go = group(4, back_rows.at[three], back_rows.at[three])
    seq_go = group(5, vec_seq.at[three], vec_seq.at[three])
    vec_in = Group(vec_s.at[0], vec_r.at[0], vec_all.at[seven], vec_all.at[seven], place.mate)
    vec_go = Group(vec_s.at[1], vec_r.at[1], vec_buf.at[seven], vec_buf.at[seven], place.mate)
    sq_go = Group(vec_s.at[2], vec_r.at[2], sq_buf.at[seven], sq_buf.at[seven], place.mate)
    for k in (2, 3, 1):
        peer = place.kin(k)
        row_in.start(inputs.at[peer[1]], x.at[me], peer)
    row_local = local(inputs.at[place.seq], x.at[me], row_l.at[0])
    seg_stage[...] = jnp.broadcast_to(segments[...][:, None, :], seg_stage.shape)
    vec_stage[...] = jnp.concatenate(
        [vec_ref[...].astype(BF).astype(F32), jnp.zeros((VROWS - vec_ref.shape[0], 128), F32)],
        axis=0,
    )
    for k in range(1, count):
        vec_in.start(vec_stage, vec_all.at[place.dp], place.dp_peer(k))
    for k in (2, 3, 1):
        peer = place.kin(k)
        seg_in.start(seg_stage.at[peer[1]], segs.at[place.seq], peer)

    def send_teacher(k, part=0, parts=1):
        size = BLK // parts
        there = low.at[span(place.seq * BLK + part * size, size, 16)]
        peer = place.kin(k)
        teach_in.start(teacher.at[peer[1], pl.ds(part * size, size)], there, peer)

    for k in (2, 1):
        send_teacher(k)
    segs[place.seq] = seg_stage[place.seq]
    vec_all[place.dp] = vec_stage[...]
    teach_local = local(teacher.at[place.seq], low.at[me], row_l.at[1])
    for w in (OUT, EXP, SHR):
        stage(w)

    def ring_steps(w, t):
        return [
            partial(gather.tick, w, lane, way, t)
            for lane in range(len(gather.lanes(w)))
            for way in range(2)
            if t <= place.hops[way]
        ]

    def relays(w, t):
        return [partial(gather.relay, w, way, t) for way in range(2) if 1 <= t <= place.hops[way]]

    far = place.hops[0]
    for t in range(1, far + 1):
        for step in ring_steps(MIX, t):
            step()
        if t == far - 2:
            gather.start(OUT)
        if t == far - 1:
            gather.start(EXP)
    for step in ring_steps(OUT, 1):
        step()

    vec_in.wait_recv()
    per = vec_ref.shape[0]
    flat = 0
    for name, size in VEC_PLACES:
        parts = []
        for r in range(flat, flat + size // 128):
            parts.append(vec_all[r // per, r % per : r % per + 1, :])
        vec[VEC_ROW[name] : VEC_ROW[name] + 1, 0:size] = jnp.concatenate(parts, axis=1)
        flat += size // 128

    def of(name):
        return vec[VEC_ROW[name] : VEC_ROW[name] + 1, 0 : VEC_SIZE[name]]

    def add_grad(name, term, start=0):
        gvec[VEC_ROW[name] : VEC_ROW[name] + 1, start : start + term.shape[1]] += term

    gvec[...] = jnp.zeros_like(gvec)
    row_local.wait()
    row_in.wait_recv()
    seg_in.wait_recv()

    for s in range(4):
        documents = jnp.concatenate([segs[s].astype(F32)] * 16, axis=0).T
        marked[s * BLK : (s + 1) * BLK, :] = document_lanes(documents)
    earlier = lax.broadcasted_iota(jnp.int32, (BLK, BLK), 0) <= lax.broadcasted_iota(
        jnp.int32, (BLK, BLK), 1
    )
    causal[...] = jnp.where(earlier, 0.0, NEGATIVE)

    def first_norm(i, _):
        hat, _ = normalised(x[rows(i), :].astype(F32))
        h1[rows(i), :] = (hat * of("g1") + of("b1")).astype(BF)
        return 0

    lax.fori_loop(0, blocks, first_norm, 0)
    gather.arrived(MIX)

    def lane(w, number, t):
        return [partial(gather.tick, w, number, way, t) for way in range(2) if t <= place.hops[way]]

    def piece(n):
        return [partial(send_teacher, 3, n, 4)]

    in_project = spread(
        [[], [], lane(EXP, 0, 1), lane(EXP, 1, 1), piece(0), lane(EXP, 2, 1), [], lane(OUT, 0, 2)],
        2,
    )
    in_forward = spread(
        [
            [],
            lane(EXP, 0, 2) + piece(1),
            lane(EXP, 1, 2) + lane(EXP, 2, 2),
            lane(OUT, 0, 3),
            lane(EXP, 0, 3) + lane(OUT, 0, 4) + piece(2),
            lane(EXP, 1, 3) + lane(EXP, 2, 3) + piece(3) + [partial(gather.start, SHR)],
        ],
        1,
    )
    in_middle = spread([[], lane(EXP, 0, 4), lane(EXP, 1, 4), lane(EXP, 2, 4)], 1)
    before_expand = relays(EXP, 1) + relays(EXP, 2) + lane(SHR, 0, 1) + relays(EXP, 3)
    before_expand += lane(SHR, 1, 1) + relays(EXP, 4)
    in_expand = spread(
        [
            lane(SHR, 2, 1), lane(SHR, 0, 2),
            lane(SHR, 1, 2), lane(SHR, 2, 2),
            lane(SHR, 0, 3), lane(SHR, 1, 3),
            lane(SHR, 2, 3), lane(SHR, 0, 4),
        ],
        2,
    )
    after_expand = lane(SHR, 1, 4) + lane(SHR, 2, 4)
    for t in range(1, far + 1):
        after_expand += relays(SHR, t)

    def project(i, _):
        in_project(i, 0)
        value = dot(h1[rows(i), :], whole(full[MIX]), NN)
        for part in range(2):
            c = slice(part * HALF, (part + 1) * HALF)
            q, k, v = (
                slice(part * 3 * HALF + n * HALF, part * 3 * HALF + (n + 1) * HALF) for n in range(3)
            )
            qkv[rows(i), q] = ((value[:, q] + of("bq")[:, c]) * scale).astype(BF)
            qkv[rows(i), k] = value[:, k].astype(BF)
            qkv[rows(i), v] = (value[:, v] + of("bv")[:, c]).astype(BF)
        in_project(i, 1)
        return 0

    lax.fori_loop(0, blocks, project, 0)
    def forward_pair(hp, _):
        attend_pair(
            hp,
            qkv,
            marked,
            causal,
            att,
            lse,
            dy,
            lambda i: in_forward(hp, 0) if i == 0 else None,
        )
        return 0

    lax.fori_loop(0, PAIRS, forward_pair, 0)
    def middle(i, _):
        in_middle(i, 0)
        value = x[rows(i), :].astype(F32) + dot(att[rows(i), :], whole(full[OUT]), NN) + of("bo")
        x1[rows(i), :] = value
        hat, _ = normalised(value)
        h2[rows(i), :] = (hat * of("g2") + of("b2")).astype(BF)
        return 0

    gather.arrived(OUT)
    lax.fori_loop(0, blocks, middle, 0)

    def target(i, _):
        dy[rows(i), :] = softmax(low[rows(i), :].astype(F32))
        return 0

    for tick in before_expand[:-1]:
        tick()
    teach_local.wait()
    teach_in.wait_recv()
    lax.fori_loop(0, blocks, target, 0)
    before_expand[-1]()
    gather.arrived(EXP)

    def expand(i, _):
        for n in range(FF // EXPAND_TILE):
            if n % 2 == 0:
                in_expand(i, n // 2)
            c = slice(n * EXPAND_TILE, (n + 1) * EXPAND_TILE)
            weight = full[EXP][:, :, :, c].reshape(D, EXPAND_TILE)
            u = dot(h2[rows(i), :], weight, NN) + vec[VEC_ROW["bf1"] : VEC_ROW["bf1"] + 1, c]
            a, s = gelu_both(u)
            act[rows(i), c] = a.astype(BF)
            slope[rows(i), c] = s.astype(BF)
        return 0

    lax.fori_loop(0, blocks, expand, 0)
    for tick in after_expand:
        tick()
    gather.arrived(SHR)

    def shrink(i, _):
        value = x1[rows(i), :] + dot(act[rows(i), :], whole(full[SHR]), NN) + of("bf2")
        sent[rows(i), :] = value.astype(BF)
        grad = D * (softmax(value) - dy[rows(i), :])
        dy[rows(i), :] = grad
        low[rows(i), :] = grad.astype(BF)
        add_grad("bf2", jnp.sum(grad, axis=0, keepdims=True))
        return 0

    lax.fori_loop(0, blocks, shrink, 0)
    for w in (MIX, OUT, EXP, SHR):
        gather.drain(w)

    def send_rows(rows_out, copies, k, first=0, size=BLK):
        peer = place.kin(k)
        source = sent.at[span(peer[1] * BLK + first, size, 128)]
        copies.start(source, rows_out.at[place.seq, pl.ds(first, size)], peer)

    out_local = local(sent.at[me], out_rows.at[place.seq], row_l.at[2])
    for k in (2, 3, 1):
        send_rows(out_rows, out_go, k)

    half, some = full[MIX].shape[2], count // 2

    def part_of(buffer, w, where):
        if w == EXP:
            return act.at[where]
        return slope.at[where, pl.ds(3 * D, D)]

    def third(group, n):
        return slope.at[span(n * 3 * half, 3 * half, 16), span(group * D, D, 128)]

    def mates(w, owner):
        if w == SHR:
            return shr_mate.at[owner]
        if w == MIX:
            return third(owner // (count // 2), owner % (count // 2))
        return part_of(act, w, span(owner * half, half, 16))

    def slots(w, t):
        if w == SHR:
            return shr_slot.at[t]
        if w == MIX:
            return third(2, t)
        return part_of(act, w, span((count + t) * half, half, 16))

    scatter = Scatter(
        place,
        (full3, full1, full2, shrink_grads),
        mates,
        slots,
        sums,
        (s_mate_s, s_mate_r, s_ring_s, s_ring_r, s_cross_s, s_cross_r, s_total_s, s_total_r),
    )

    def offer(which):
        for n, peer in enumerate((place.mate,) + place.sides):
            pl.semaphore_signal(
                free.at[3 * which + n], inc=1, device_id=peer, device_id_type=MESH
            )

    def accept(which, which_sides):
        for n in range(1, 3) if which_sides else range(1):
            pl.semaphore_wait(free.at[3 * which + n], 1)

    def shrink_grad(n, _):
        value = dot(act[:, span(n * D, D, 128)], low[...], TN).astype(BF)
        shrink_grads[pl.ds(2 * n, 2)] = value.reshape((2,) + shrink_grads.shape[1:])
        for owner in range(2):
            for sub in range(2):
                scatter.pair(SHR, sub, 2 * n + owner).start()
        return 0

    lax.fori_loop(0, FF // D, shrink_grad, 0)
    offer(0)

    def hop(w, t, sub):
        return scatter.ticks(w, t, (sub,))

    def end(w, sub):
        return [partial(scatter.finish, w, sub)]

    in_middle_back = spread([hop(SHR, 1, 0), [], hop(SHR, 1, 1), []], 1)
    in_expand_grad = spread([hop(SHR, 2, 0), [], hop(SHR, 2, 1), []], 1)
    in_upstream = spread(
        [[partial(scatter.start, EXP, 0)] + hop(SHR, 3, 0), [], [], []],
        1,
    )
    in_backward = spread(
        [
            hop(SHR, 3, 1), [], [], [],
            [partial(scatter.start, OUT, 0)] + hop(EXP, 1, 0) + end(SHR, 0), [], [], [],
            hop(EXP, 1, 1), [], [], hop(EXP, 2, 0) + hop(OUT, 1, 0) + end(SHR, 1),
            hop(EXP, 2, 1), [], [], hop(OUT, 2, 0) + hop(EXP, 3, 0) + [partial(scatter.start, MIX, 0)],
            [], [], [], hop(EXP, 3, 1) + hop(OUT, 3, 0),
            end(EXP, 0), [], [], hop(MIX, 1, 0) + end(OUT, 0) + end(EXP, 1),
        ],
        4,
    )

    in_expand_back = spread([[], [partial(scatter.start, SHR, sub) for sub in range(2)], [], []], 1)

    def expand_back(i, _):
        in_expand_back(i, 0)
        for n in range(FF // D):
            c = slice(n * D, (n + 1) * D)
            weight = full[SHR][2 * n : 2 * n + 2].reshape(D, D)
            da = dot(low[rows(i), :], weight, NT).astype(BF).astype(F32)
            du = (da * slope[rows(i), c].astype(F32)).astype(BF)
            slope[rows(i), c] = du
            gvec[VEC_ROW["bf1"] : VEC_ROW["bf1"] + 1, c] += jnp.sum(
                du.astype(F32), axis=0, keepdims=True
            )
        return 0

    lax.fori_loop(0, blocks, expand_back, 0)


    def middle_back(i, _):
        in_middle_back(i, 0)
        upstream = dot(slope[rows(i), :], whole(full[EXP]), NT)
        part, gain, shift = norm_grad(x1[rows(i), :], of("g2"), upstream)
        value = dy[rows(i), :] + part
        dy[rows(i), :] = value
        low[rows(i), :] = value.astype(BF)
        add_grad("g2", gain)
        add_grad("b2", shift)
        add_grad("bo", jnp.sum(value, axis=0, keepdims=True))
        return 0

    lax.fori_loop(0, blocks, middle_back, 0)
    accept(0, False)

    def expand_grad(n, _):
        in_expand_grad(n, 0)
        c = span(n * D, D, 128)
        for owners in range(2):
            value = dot(h2[:, owners * HALF : (owners + 1) * HALF], slope[:, c], TN).astype(BF)
            full2[owners * some : (owners + 1) * some, :, :, c] = value.reshape(
                (some,) + full2.shape[1:3] + (D,)
            )
        pl.when(n == FF // D // 2 - 1)(lambda: scatter.hand(EXP, 0))
        return 0

    lax.fori_loop(0, FF // D, expand_grad, 0)
    scatter.hand(EXP, 1)
    offer(1)
    accept(0, True)

    def upstream_rows(i, _):
        in_upstream(i, 0)
        h2[rows(i), :] = dot(low[rows(i), :], whole(full[OUT]), NT).astype(BF)
        return 0

    lax.fori_loop(0, blocks, upstream_rows, 0)
    for owners in range(2):
        if owners:
            scatter.start(EXP, 1)
        value = dot(att[:, owners * HALF : (owners + 1) * HALF], low[...], TN).astype(BF)
        full1[owners * some : (owners + 1) * some] = value.reshape((some,) + full1.shape[1:])
    accept(1, False)
    scatter.hand(OUT, 0)
    accept(1, True)
    def backward_part(part, _):
        def backward_pair(hp, _):
            def tick(i):
                for n in range(2):
                    first = n * (PAIRS // 2)
                    pl.when(part == n)(
                        lambda first=first: in_backward(hp + first, i, first, first + PAIRS // 2)
                    )

            number = part * (PAIRS // 2) + hp
            attend_back_pair(
                number, qkv, marked, causal, att, h2, lse, x1, tick
            )
            return 0

        lax.fori_loop(0, PAIRS // 2, backward_pair, 0)
        c = span(part * 3 * HALF, 3 * HALF, 128)
        for owners in range(2):
            mine = slice(owners * HALF, (owners + 1) * HALF)
            value = dot(h1[:, mine], qkv[:, c], TN).astype(BF)
            for n in range(3):
                there = span(part * HALF, HALF, 128)
                full3[owners * some : (owners + 1) * some, :, n * half : (n + 1) * half, there] = (
                    value[:, n * HALF : (n + 1) * HALF].reshape(some, 2, half, HALF)
                )
            for number in range(2):

                def hand(number=number, owners=owners):
                    for sub in ((0,), (1, 2, 3))[number]:
                        for owner in range(owners * some, (owners + 1) * some):
                            scatter.pair(MIX, sub, owner).start()

                pl.when(part == number)(hand)
        return 0

    lax.fori_loop(0, 2, backward_part, 0)
    for tick in hop(MIX, 2, 0):
        tick()
    out_local.wait()
    out_go.wait_send()
    in_input_back = spread(
        [
            [],
            [partial(scatter.start, MIX, sub) for sub in range(1, 4)],
            hop(MIX, 3, 0),
            hop(MIX, 1, 1),
        ],
        1,
    )
    late = BLK // 2

    def input_back(j, _):
        in_input_back(j, 0)
        core = place.core + (1 - 2 * place.core) * (j % 2)
        i = 2 * (place.x + (1 - 2 * place.x) * (1 - j // 2)) + core
        d = qkv[rows(i), :]
        part, gain, shift = norm_grad(
            x[rows(i), :].astype(F32), of("g1"), dot(d, whole(full[MIX]), NT)
        )
        sent[rows(i), :] = (dy[rows(i), :] + part).astype(BF)
        add_grad("g1", gain)
        add_grad("b1", shift)
        for half_of in range(2):
            first = half_of * 3 * HALF
            for name, start in (("bq", first), ("bv", first + 2 * HALF)):
                term = d[:, start : start + HALF].astype(F32)
                add_grad(name, jnp.sum(term, axis=0, keepdims=True), half_of * HALF)
        pl.when(j == 0)(lambda: send_rows(back_rows, back_go, 2))
        pl.when(j == 1)(lambda: send_rows(back_rows, back_go, 3, 0, late) if late else None)
        pl.when(j == 3)(lambda: send_rows(back_rows, back_go, 1))
        return 0

    lax.fori_loop(0, blocks, input_back, 0)
    back_local = local(sent.at[me], back_rows.at[place.seq], row_l.at[3])
    flat = 0
    vec_out[...] = jnp.zeros_like(vec_out)
    for name, size in VEC_PLACES:
        for n in range(size // 128):
            r = flat + n
            vec_out[r // per, r % per : r % per + 1, :] = gvec[
                VEC_ROW[name] : VEC_ROW[name] + 1, n * 128 : (n + 1) * 128
            ]
        flat += size // 128
    for k in range(1, count):
        peer = place.dp_peer(k)
        vec_go.start(vec_out.at[peer[0]], vec_buf.at[place.dp], peer)
    vec_buf[place.dp] = vec_out[place.dp]
    for tick in hop(MIX, 1, 2) + hop(MIX, 1, 3) + end(MIX, 0) + hop(MIX, 2, 1) + hop(MIX, 2, 2) + hop(MIX, 2, 3):
        tick()
    for w, sub in ((SHR, 0), (SHR, 1), (EXP, 0)):
        scatter.crossed(w, sub)
    for tick in hop(MIX, 3, 1) + hop(MIX, 3, 2) + hop(MIX, 3, 3):
        tick()
    vec_go.wait_recv()
    vec_mine[...] = jnp.sum(vec_buf[...], axis=0)
    vec_seq[place.seq] = vec_mine[...]
    for k in (2, 3, 1):
        seq_go.start(vec_mine, vec_seq.at[place.seq], place.kin(k))
    for sub in range(1, 4):
        scatter.finish(MIX, sub)
    send_rows(back_rows, back_go, 3, late, BLK - late)
    for w, sub in ((EXP, 1), (OUT, 0), (MIX, 0)):
        scatter.crossed(w, sub)

    def squares_of(w, part, total):
        c = slice(None) if part is None else slice(part * HALF, (part + 1) * HALF)
        for core in range(2):
            value = sums[w][core, :, c].astype(F32)
            term = jnp.sum(value * value, axis=0, keepdims=True)
            for n in range(term.shape[1] // 128):
                total = total + term[:, n * 128 : (n + 1) * 128]
        return total

    squares = jnp.zeros((1, 128), F32)
    for w in (SHR, EXP, OUT):
        for sub in range(SUBS[w]):
            scatter.arrived(w, sub)
        squares = squares_of(w, None, squares)
    scatter.arrived(MIX, 0)
    squares = squares_of(MIX, 0, squares)
    seq_go.wait_recv()
    vec_total = jnp.sum(vec_seq[...], axis=0)
    vec_sum[...] = vec_total
    squares = squares + jnp.sum(vec_total * vec_total, axis=0, keepdims=True)
    for sub in range(1, 4):
        scatter.crossed(MIX, sub)
    for sub in range(1, 4):
        scatter.arrived(MIX, sub)
    squares = squares_of(MIX, 1, squares)
    sq_mine[...] = jnp.broadcast_to(squares, sq_mine.shape)
    sq_buf[place.dp] = sq_mine[...]
    for k in range(1, count):
        sq_go.start(sq_mine, sq_buf.at[place.dp], place.dp_peer(k))
    saved = [local(sums[w], sums_out[w], load_sem.at[w]) for w in range(4)]
    for w in (MIX, OUT, EXP, SHR):
        scatter.drain(w)
    for copies in (row_in, seg_in, teach_in, vec_in, vec_go, seq_go, back_go, sq_go):
        copies.wait_send()
    for copy in saved + [back_local]:
        copy.wait()
    out_go.wait_recv()
    back_go.wait_recv()
    sq_go.wait_recv()
    total = jnp.sum(jnp.sum(sq_buf[...], axis=0), axis=1, keepdims=True)
    norm_ref[...] = jnp.broadcast_to(jnp.sqrt(total), norm_ref.shape)


def block_call(count, inputs, teacher, segments, masters, vectors):
    rows, local_len, features = inputs.shape
    length = rows * local_len
    halves = [(2, m.shape[0] // 2, m.shape[1]) for m in masters]
    any_spec = pl.BlockSpec(memory_space=pl.ANY)
    vmem = pl.BlockSpec(memory_space=pltpu.VMEM)
    row_shape = jax.ShapeDtypeStruct(inputs.shape, BF)
    folded = [(2, 3 * halves[MIX][1], D)] + halves[1:]
    out_shape = [jax.ShapeDtypeStruct(h, BF) for h in folded]
    out_shape += [
        jax.ShapeDtypeStruct((VROWS, 128), F32),
        jax.ShapeDtypeStruct((8, 128), F32),
        row_shape,
        row_shape,
    ]

    def low(*shape):
        return pltpu.VMEM(shape, BF)

    def wide(*shape):
        return pltpu.VMEM(shape, F32)

    def dma(*shape):
        return pltpu.SemaphoreType.DMA(shape)

    shrink_half = halves[SHR][1:]
    buffers = [low(count, *h) for h in halves]
    buffers += [
        low(length, D),
        low(length, D),
        low(length, 3 * D),
        low(length, D),
        wide(length, D),
        low(length, D),
        low(length, FF),
        low(length, FF),
        wide(length, D),
        low(length, D),
        low(length, D),
        low(count, *halves[SHR]),
        low(count, *shrink_half),
        low(count - 1, *shrink_half),
    ]
    buffers += [
        wide(16, length),
        pltpu.VMEM((rows, 8, local_len), jnp.int32),
        pltpu.VMEM((rows, 8, local_len), jnp.int32),
        low(length, 128),
        wide(BLK, BLK),
        *(low(*shape) for shape in folded),
        wide(VROWS, 128),
        wide(count, VROWS, 128),
        wide(16, FF),
        wide(16, FF),
        wide(count, VROWS, 128),
        wide(count, VROWS, 128),
        wide(VROWS, 128),
        wide(4, VROWS, 128),
        wide(8, 128),
        wide(count, 8, 128),
    ]
    hops = count - 1
    sems = [dma(9), dma(4), dma(10, hops), dma(4), dma(4), dma(2), dma(2, hops)]
    sems += [dma(9), dma(9), dma(9), dma(9, hops)] + [dma(9)] * 4
    sems += [dma(6), dma(6), dma(4), dma(3), dma(3)]
    sems.append(pltpu.SemaphoreType.REGULAR((6,)))
    return pl.pallas_call(
        partial(block_kernel, count),
        out_shape=out_shape,
        in_specs=[any_spec] * 2 + [vmem] + [any_spec] * 4 + [vmem],
        out_specs=[any_spec] * 4 + [vmem] * 2 + [any_spec] * 2,
        scratch_shapes=buffers + sems,
        compiler_params=pltpu.CompilerParams(
            collective_id=1, has_side_effects=True, vmem_limit_bytes=VMEM_BYTES
        ),
    )(inputs, teacher, segments, *masters, vectors.reshape(-1, 128))


def update_kernel(steps, norm_ref, *refs):
    sums, masters, firsts, seconds = refs[0:5], refs[5:10], refs[10:15], refs[15:20]
    out_from, back_from = refs[20:22]
    updated, first_out, second_out = refs[22:27], refs[27:32], refs[32:37]
    out_to, back_to, norm_out, held, sem = refs[37:42]
    step = pl.program_id(0)
    norm = norm_ref[0:1, 0:1]
    factor = clip_level() / jnp.maximum(norm, clip_level())
    takes = [
        pltpu.make_async_copy(rows, held.at[n], sem.at[n])
        for n, rows in enumerate((out_from, back_from))
    ]
    gives = [
        pltpu.make_async_copy(held.at[n], rows, sem.at[2 + n])
        for n, rows in enumerate((out_to, back_to))
    ]

    @pl.when(step == 0)
    def _():
        for copy in takes:
            copy.start()
        norm_out[...] = norm

    @pl.when(step == steps // 2)
    def _():
        for take, give in zip(takes, gives):
            take.wait()
            give.start()

    def apply(n, gradient):
        rate = learn_rates()[n]
        clipped = gradient * factor
        first = BETA_ONE * firsts[n][...] + (1.0 - BETA_ONE) * clipped
        second = BETA_TWO * seconds[n][...] + (1.0 - BETA_TWO) * (clipped * clipped)
        scale = jnp.sqrt(second * (1.0 / (1.0 - BETA_TWO**STEP))) + ADAM_EPS
        change = first * (rate / (1.0 - BETA_ONE**STEP)) / scale
        updated[n][...] = masters[n][...] * (1.0 - rate * WEIGHT_DECAY) - change
        first_out[n][...] = first
        second_out[n][...] = second

    for w in range(4):
        gradient = sums[w][...].astype(F32)
        if w == MIX:
            gradient = jnp.concatenate([gradient[n] for n in range(3)], axis=1)
        apply(w, gradient)

    @pl.when(step == 0)
    def _():
        apply(4, sums[4][0 : masters[4].shape[0], :])

    @pl.when(step == steps - 1)
    def _():
        for copy in gives:
            copy.wait()


def update_call(results, masters, firsts, seconds):
    half = results[OUT].shape[1]
    parts = 1
    steps = 2 * parts
    mixed = results[MIX].reshape(2, 3, half, D)

    def fixed(shape):
        return pl.BlockSpec(shape, lambda i: (0,) * len(shape))

    any_spec = pl.BlockSpec(memory_space=pl.ANY)
    sum_specs, state_specs, states = [], [], []
    for master in masters[:4]:
        rows, columns = master.shape[0] // steps, master.shape[1]
        sum_specs.append(pl.BlockSpec((None, rows, columns), lambda i: (i // parts, i % parts, 0)))
        state_specs.append(pl.BlockSpec((rows, columns), lambda i: (i, 0)))
    sum_specs[MIX] = pl.BlockSpec(
        (None, 3, half // parts, D), lambda i: (i // parts, 0, i % parts, 0)
    )
    packed = (masters[4].shape[0] // 128, 128)
    state_specs.append(fixed(packed))
    sum_specs.append(fixed(results[4].shape))
    for group in (masters, firsts, seconds):
        states += list(group[:4]) + [group[4].reshape(packed)]
    out_shape = [jax.ShapeDtypeStruct(state.shape, F32) for state in states]
    out_shape += [jax.ShapeDtypeStruct(results[6].shape, BF)] * 2
    out_shape.append(jax.ShapeDtypeStruct((1, 1), F32))
    return pl.pallas_call(
        partial(update_kernel, steps),
        grid=(steps,),
        out_shape=out_shape,
        in_specs=[fixed(results[5].shape)] + sum_specs + state_specs * 3 + [any_spec] * 2,
        out_specs=state_specs * 3 + [any_spec] * 2 + [fixed((1, 1))],
        scratch_shapes=[
            pltpu.VMEM((2,) + results[6].shape, BF),
            pltpu.SemaphoreType.DMA((4,)),
        ],
        compiler_params=pltpu.CompilerParams(vmem_limit_bytes=VMEM_BYTES),
    )(results[5], mixed, *results[1:5], *states, *results[6:8])


def row_body(
    inputs,
    segments,
    teacher,
    mixing_weight,
    output_weight,
    expand_weight,
    shrink_weight,
    vectors,
    mixing_first,
    output_first,
    expand_first,
    shrink_first,
    vectors_first,
    mixing_second,
    output_second,
    expand_second,
    shrink_second,
    vectors_second,
):
    masters = (mixing_weight, output_weight, expand_weight, shrink_weight, vectors)
    firsts = (mixing_first, output_first, expand_first, shrink_first, vectors_first)
    seconds = (mixing_second, output_second, expand_second, shrink_second, vectors_second)
    results = block_call(lax.axis_size("dp"), inputs, teacher, segments, masters[:4], vectors)
    fresh = update_call(results, masters, firsts, seconds)
    states = [
        state.reshape(vectors.shape) if n % 5 == 4 else state for n, state in enumerate(fresh[:15])
    ]
    return (fresh[15], fresh[16], fresh[17].reshape(()), *states)


def whole_rows(mesh):
    return mesh.shape["seq"] == 4 and mesh.shape["dp"] == 8


def solution(mesh):
    in_specs = (
        P("dp", "seq", None),
        P("dp", "seq"),
        P("dp", "seq", None),
        P("dp", None),
        P("dp", None),
        P("dp", None),
        P("dp", None),
        P("dp"),
        P("dp", None),
        P("dp", None),
        P("dp", None),
        P("dp", None),
        P("dp"),
        P("dp", None),
        P("dp", None),
        P("dp", None),
        P("dp", None),
        P("dp"),
    )
    out_specs = (
        P("dp", "seq", None),
        P("dp", "seq", None),
        P(),
        P("dp", None),
        P("dp", None),
        P("dp", None),
        P("dp", None),
        P("dp"),
        P("dp", None),
        P("dp", None),
        P("dp", None),
        P("dp", None),
        P("dp"),
        P("dp", None),
        P("dp", None),
        P("dp", None),
        P("dp", None),
        P("dp"),
    )
    chosen = row_body if whole_rows(mesh) else body
    return jax.shard_map(chosen, mesh=mesh, in_specs=in_specs, out_specs=out_specs, check_vma=False)
```
